32 devices in a mesh: dp: 8 (over z, y), fsdp: 4 (over x, core).
Axes of the slice: x: 2, y: 2, z: 4, core: 2. Of those that a mesh axis runs over, the one named last changes fastest.
Arguments:
- tokens: bfloat16 [2, 32, 128, 1024], P(None, 'fsdp', 'dp'), may hold values from -6 to 6
- cotangent: bfloat16 [2, 32, 128, 1024], P(None, ('dp', 'fsdp')), may hold values from -6 to 6
- lengths: int32 [2, 32], replicated, may hold values from 1 to 128, 2560 in all within a row
- deal: int32 [2, 32], replicated, may hold values from 0 to 31, as said below
- weights: float32 [768, 128, 128], P(('dp', 'fsdp')), may hold values from -1 to 1
- vectors: float32 [12288], P(('dp', 'fsdp')), may hold values from -2 to 2
- owners: int32 [768], P(('dp', 'fsdp')), may hold values from 0 to 767, as said below
- left_basis: float32 [768, 128, 128], P(('dp', 'fsdp')), may hold values from -1 to 1, as said below
- right_basis: float32 [768, 128, 128], P(('dp', 'fsdp')), may hold values from -1 to 1, as said below
- first_moment: float32 [768, 128, 128], P(('dp', 'fsdp')), may hold values from -200.35169 to 200.35169
- second_moment: float32 [768, 128, 128], P(('dp', 'fsdp')), may hold values from 0 to 6690.1333, as said below
- vec_first: float32 [12288], P(('dp', 'fsdp')), may hold values from -286.2167 to 286.2167
- vec_second: float32 [12288], P(('dp', 'fsdp')), may hold values from 0 to 13653.333, as said below
Outputs:
- out_tokens: bfloat16 [2, 32, 128, 1024], P(None, 'fsdp', 'dp')
- in_grad: bfloat16 [2, 32, 128, 1024], P(None, 'fsdp', 'dp')
- tile_grads: float32 [768, 128, 128], P(('dp', 'fsdp'))
- vec_grads: float32 [12288], P(('dp', 'fsdp'))
- new_first: float32 [768, 128, 128], P(('dp', 'fsdp'))
- new_second: float32 [768, 128, 128], P(('dp', 'fsdp'))
- new_tiles: float32 [768, 128, 128], P(('dp', 'fsdp'))
- new_tiles_low: bfloat16 [768, 128, 128], P(('dp', 'fsdp'))
- vec_first_new: float32 [12288], P(('dp', 'fsdp'))
- vec_second_new: float32 [12288], P(('dp', 'fsdp'))
- new_vectors: float32 [12288], P(('dp', 'fsdp'))
The draws below stay inside these ranges and needn't reach their ends.
Inputs may be any that keep to these rules, and one draw needn't show every extreme that they name: Each micro-batch's lengths add up to 2560, and the longest is 128. `deal`: each row is a permutation of the sequence numbers; dealt position j holds a sequence of the block (j % 4) * 8 to (j % 4 + 1) * 8 - 1. `owners`: a permutation of the tile numbers; each aligned block of 96 positions holds the tiles of the same block of numbers. `left_basis`: each tile's basis is orthogonal. `right_basis`: each tile's basis is orthogonal. `second_moment`: positive. `vec_second`: positive.
All inputs are finite; a program needn't handle non-finite values.
Results may differ from the reference program's by a relative error of at most 0.013.
Values may be sent and summed in bfloat16 or wider, within the bound.
A program may use at most 152 MiB of HBM per device.

```python
import math
import jax
import jax.numpy as jnp
import numpy as np
from jax import lax

D = 1024
HEADS = 16
HEAD_DIM = 64
FF = 4096
LEN = 128
MB = 2
STEP = 10
TB = 128
SEQS = 32
TILES = 768
NVEC = 12288
FILLED = 2560
N_DP = 8
N_FSDP = 4


def tile_spread(tile_ids):
    qkv_end = 3 * D * D // (TB * TB)
    out_end = 4 * D * D // (TB * TB)
    up_end = (4 * D * D + D * FF) // (TB * TB)
    return jnp.where(tile_ids < qkv_end, D ** (-0.5), jnp.where(tile_ids < out_end, (HEAD_DIM / D) ** 0.5, jnp.where(tile_ids < up_end, D ** (-0.5), 1.5 * FF ** (-0.5)))).astype(jnp.float32)


def grad_spread(tile_ids):
    qkv_end = 3 * D * D // (TB * TB)
    out_end = 4 * D * D // (TB * TB)
    up_end = (4 * D * D + D * FF) // (TB * TB)
    return jnp.where(tile_ids < qkv_end, 0.7, jnp.where(tile_ids < out_end, 1.4 / LEN ** 0.5, jnp.where(tile_ids < up_end, 0.34, 0.45))).astype(jnp.float32)


def vector_spread(position):
    return jnp.where(position < 3 * D, 0.7, jnp.where(position < 3 * D + FF, 0.34, jnp.where(position < 4 * D + FF, 0.7, 1.0))).astype(jnp.float32)


def shuffle_block(block_key, block_size):
    return jax.random.permutation(block_key, block_size)


def owner_table(key):
    key = jax.random.fold_in(key, 101)
    group_size = TILES // N_DP
    block_keys = jax.random.split(key, N_DP)
    shuffled = jax.vmap(lambda block_key: shuffle_block(block_key, group_size))(block_keys)
    offsets = jnp.arange(N_DP, dtype=jnp.int32)[:, None] * group_size
    return (shuffled.astype(jnp.int32) + offsets).reshape(TILES)


def orthogonal_stack(key):
    row_keys = jax.random.split(jax.random.fold_in(key, 11), TILES)
    col_keys = jax.random.split(jax.random.fold_in(key, 12), TILES)
    row_order = jax.vmap(lambda block_key: shuffle_block(block_key, TB))(row_keys).astype(jnp.int32)
    col_order = jax.vmap(lambda block_key: shuffle_block(block_key, TB))(col_keys).astype(jnp.int32)
    row_sign = jax.random.randint(jax.random.fold_in(key, 13), (TILES, TB), 0, 2) * 2 - 1
    col_sign = jax.random.randint(jax.random.fold_in(key, 14), (TILES, TB), 0, 2) * 2 - 1
    product = (2 * row_order[:, :, None] + 1) * (2 * col_order[:, None, :] + 1) % (8 * TB)
    angle = math.pi * product.astype(jnp.float32) / (4.0 * TB)
    signs = (row_sign[:, :, None] * col_sign[:, None, :]).astype(jnp.float32)
    return math.sqrt(2.0 / TB) * jnp.cos(angle) * signs


def draw_deal(key, part):
    key = jax.random.fold_in(key, 7)
    block_keys = jax.random.split(key, MB * N_FSDP)
    shuffled = jax.vmap(lambda block_key: shuffle_block(block_key, N_DP))(block_keys).astype(jnp.int32)
    shuffled = shuffled.reshape(MB, N_FSDP, N_DP) + (jnp.arange(N_FSDP, dtype=jnp.int32) * N_DP)[None, :, None]
    return shuffled.transpose(0, 2, 1).reshape(MB, SEQS).astype(jnp.int32)


def draw_owners(key, part):
    return owner_table(key)


def draw_weights(key, part):
    key = jax.random.fold_in(key, 5)
    normal_part = jnp.clip(jax.random.normal(key, (TILES, TB, TB), jnp.float32), -4.0, 4.0)
    return normal_part * tile_spread(jnp.arange(TILES))[:, None, None]


def draw_vectors(key, part):
    key = jax.random.fold_in(key, 6)
    bias_key, gain_key = jax.random.split(key)
    biases = 0.5 * jnp.clip(jax.random.normal(bias_key, (NVEC,), jnp.float32), -4.0, 4.0)
    gains = jax.random.uniform(gain_key, (NVEC,), jnp.float32, 0.5, 1.5)
    position = jnp.arange(NVEC)
    is_gain = (position >= 4 * D + FF) & (position < 5 * D + FF) | (position >= 6 * D + FF) & (position < 7 * D + FF)
    return jnp.where(is_gain, gains, biases)


def draw_left_basis(key, part):
    key = jax.random.fold_in(key, 3)
    return orthogonal_stack(key)


def draw_right_basis(key, part):
    key = jax.random.fold_in(key, 4)
    return orthogonal_stack(key)


def draw_first_moment(key, part):
    table = owner_table(key)
    key = jax.random.fold_in(key, 8)
    spread = grad_spread(table)[:, None, None] * math.sqrt(MB * FILLED)
    return spread * jnp.clip(jax.random.normal(key, (TILES, TB, TB), jnp.float32), -4.0, 4.0)


def draw_second_moment(key, part):
    table = owner_table(key)
    key = jax.random.fold_in(key, 9)
    spread = grad_spread(table)[:, None, None] * math.sqrt(MB * FILLED)
    factor = jnp.exp(jax.random.uniform(key, (TILES, TB, TB), jnp.float32, 0.0, math.log(4.0)))
    return 2.0 / 3.0 * spread * spread * factor


def draw_vec_first(key, part):
    key = jax.random.fold_in(key, 15)
    spread = vector_spread(jnp.arange(NVEC)) * math.sqrt(MB * FILLED)
    return spread * jnp.clip(jax.random.normal(key, (NVEC,), jnp.float32), -4.0, 4.0)


def draw_vec_second(key, part):
    key = jax.random.fold_in(key, 16)
    spread = vector_spread(jnp.arange(NVEC)) * math.sqrt(MB * FILLED)
    factor = jnp.exp(jax.random.uniform(key, (NVEC,), jnp.float32, 0.0, math.log(4.0)))
    return 2.0 / 3.0 * spread * spread * factor


def level_of(stream_key, dims, cuts, low, high):
    level, own = 1.0, jax.random.fold_in(stream_key, 6)
    for dim, shards_of in cuts:
        draws = jnp.exp(jax.random.uniform(jax.random.fold_in(own, dim), (shards_of,), jnp.float32, low / len(cuts), high / len(cuts)))
        level = level * jnp.repeat(draws, dims[dim] // shards_of).reshape([-1 if axis == dim else 1 for axis in range(len(dims))])
    return level


def length_profile(amount, total, limit, slope):
    loads = [(1 << 20) // math.isqrt(standing ** slope) + 1 for standing in range(2, amount + 1)]
    surplus, counts = total - limit - (amount - 1), [1] * (amount - 1)
    while surplus > 0:
        free = [i for i in range(amount - 1) if counts[i] < limit]
        pool, budget = sum([loads[i] for i in free]), surplus
        for i in free:
            more = min(limit - counts[i], max(1, budget * loads[i] // pool), surplus)
            counts[i] = counts[i] + more
            surplus = surplus - more
    return np.array([limit] + counts)


def ragged(stream_key, amount, total, limit, lean):
    if amount == 2:
        one = jax.random.randint(stream_key, (), max(1, total - limit), min(limit, total - 1) + 1)
        return jnp.stack([one, total - one])
    sizes = jnp.asarray(length_profile(amount, total, limit, lean), jnp.int32)
    twos = (amount - 1) // 2
    giver, receiver = sizes[1:1 + 2 * twos:2], sizes[2:2 + 2 * twos:2]
    margin = jnp.minimum(giver - 1, limit - receiver)
    moved = jax.random.randint(jax.random.fold_in(stream_key, 1), (twos,), 0, 1 << 20) % (margin + 1)
    sizes = sizes.at[1:1 + 2 * twos:2].set(giver - moved).at[2:2 + 2 * twos:2].set(receiver + moved)
    return sizes[jax.random.permutation(jax.random.fold_in(stream_key, 2), amount)]


def normal_values(stream_key, dims, scale, bound, cuts=(), held_as=jnp.bfloat16):
    values = jax.random.normal(stream_key, dims, jnp.float32) * scale
    if len(cuts) > 0:
        values = level_of(stream_key, dims, cuts, -0.22, 0.18) * values
    return jnp.clip(values, min=-bound, max=bound).astype(held_as)


def setup_inputs(seed: int = 0) -> dict:
    key_list = jax.random.split(jax.random.key(seed), 14)
    return {
        "tokens": normal_values(key_list[0], (MB, SEQS, LEN, D), 1.0, 6.0, ((1, 4), (2, 8))),
        "cotangent": normal_values(key_list[1], (MB, SEQS, LEN, D), 1.0, 6.0, ((1, 32),)),
        "lengths": jax.vmap(lambda own: ragged(own, SEQS, FILLED, LEN, 2))(jax.random.split(key_list[2], MB)).reshape((MB, SEQS)).astype(jnp.int32),
        "deal": draw_deal(jax.random.fold_in(key_list[13], 71), 0),
        "weights": draw_weights(jax.random.fold_in(key_list[13], 71), 0),
        "vectors": draw_vectors(jax.random.fold_in(key_list[13], 71), 0),
        "owners": draw_owners(jax.random.fold_in(key_list[13], 71), 0),
        "left_basis": draw_left_basis(jax.random.fold_in(key_list[13], 71), 0),
        "right_basis": draw_right_basis(jax.random.fold_in(key_list[13], 71), 0),
        "first_moment": draw_first_moment(jax.random.fold_in(key_list[13], 71), 0),
        "second_moment": draw_second_moment(jax.random.fold_in(key_list[13], 71), 0),
        "vec_first": draw_vec_first(jax.random.fold_in(key_list[13], 71), 0),
        "vec_second": draw_vec_second(jax.random.fold_in(key_list[13], 71), 0),
    }


@jax.custom_vjp
def low(v):
    return lax.optimization_barrier(v.astype(jnp.bfloat16)).astype(jnp.float32)

@jax.custom_vjp
def low_back(v):
    return v

def low_keep(v):
    return (low(v), None)

def low_pass(kept, grad):
    return (grad,)

def back_keep(v):
    return (v, None)

def back_low(kept, grad):
    return (low(grad),)
low.defvjp(low_keep, low_pass)
low_back.defvjp(back_keep, back_low)
EPS_NORM = 1e-05
BETA_ONE = 0.5
BETA_TWO = 0.6
ADAM_EPS = 1e-08
DECAY = 0.01
VEC_RATE = 0.2
PRECISION_HIGH = lax.Precision.HIGHEST

def cut_tiles(stacked, row_count, col_count, start_at):
    tile_count = row_count // TB * (col_count // TB)
    blocked = lax.slice_in_dim(stacked, start_at, start_at + tile_count, axis=0)
    blocked = blocked.reshape(row_count // TB, col_count // TB, TB, TB)
    return (blocked.transpose(0, 2, 1, 3).reshape(row_count, col_count), start_at + tile_count)

def unpack_mats(stacked):
    w_qkv, offset = cut_tiles(stacked, D, 3 * D, 0)
    w_out, offset = cut_tiles(stacked, D, D, offset)
    w_up, offset = cut_tiles(stacked, D, FF, offset)
    w_down, offset = cut_tiles(stacked, FF, D, offset)
    return (w_qkv, w_out, w_up, w_down)

def make_tiles(matrix):
    row_count, col_count = matrix.shape
    blocked = matrix.reshape(row_count // TB, TB, col_count // TB, TB).transpose(0, 2, 1, 3)
    return blocked.reshape(-1, TB, TB)

def pack_mats(matrices):
    return jnp.concatenate([make_tiles(matrix) for matrix in matrices], axis=0)

def unpack_vecs(vector):
    widths = [D, D, D, FF, D, D, D, D, D]
    pieces = []
    offset = 0
    for width_now in widths:
        pieces.append(vector[offset:offset + width_now])
        offset += width_now
    return tuple(pieces)

def tile_rate(tile_ids):
    qkv_end = 3 * D * D // (TB * TB)
    out_end = 4 * D * D // (TB * TB)
    up_end = (4 * D * D + D * FF) // (TB * TB)
    return jnp.where(tile_ids < qkv_end, D ** (-0.5), jnp.where(tile_ids < out_end, (HEAD_DIM / D) ** 0.5, jnp.where(tile_ids < up_end, D ** (-0.5), 1.5 * FF ** (-0.5)))).astype(jnp.float32)

def layer_norm(values, gain_vec, shift_vec):
    center = values - lax.optimization_barrier(jnp.mean(values, axis=-1, keepdims=True))
    spread = lax.optimization_barrier(jnp.mean(center * center, axis=-1, keepdims=True))
    return center * lax.rsqrt(spread + EPS_NORM) * gain_vec + shift_vec

def sequence_forward(matrices, vecs, inputs, length):
    w_qkv, w_out, w_up, w_down = matrices
    bias_q, bias_v, bias_out, bias_up, bias_down, gain_one, shift_one, gain_two, shift_two = vecs
    seq_rows = inputs.shape[0]
    joined = low_back(jnp.dot(inputs, w_qkv, precision=PRECISION_HIGH, preferred_element_type=jnp.float32))
    joined = joined + jnp.concatenate([bias_q, jnp.zeros_like(bias_q), bias_v])
    joined = low(joined)
    query_heads = joined[:, :D].reshape(seq_rows, HEADS, HEAD_DIM)
    key_heads = joined[:, D:2 * D].reshape(seq_rows, HEADS, HEAD_DIM)
    value_heads = joined[:, 2 * D:].reshape(seq_rows, HEADS, HEAD_DIM)
    scores = low_back(jnp.einsum('qhd,khd->hqk', query_heads, key_heads, precision=PRECISION_HIGH) * HEAD_DIM ** (-0.5))
    in_length = jnp.arange(seq_rows) < length
    scores = jnp.where(in_length[None, None, :], scores, -1e+30)
    attention = low(jax.nn.softmax(scores, axis=-1))
    attended = low(low_back(jnp.einsum('hqk,khd->qhd', attention, value_heads, precision=PRECISION_HIGH))).reshape(seq_rows, D)
    branch = low_back(jnp.dot(attended, w_out, precision=PRECISION_HIGH, preferred_element_type=jnp.float32)) + bias_out
    normed_one = layer_norm(inputs + branch, gain_one, shift_one)
    hidden = low_back(jnp.dot(low(normed_one), w_up, precision=PRECISION_HIGH, preferred_element_type=jnp.float32)) + bias_up
    active = low(jax.nn.gelu(hidden, approximate=False))
    down_out = low_back(jnp.dot(active, w_down, precision=PRECISION_HIGH, preferred_element_type=jnp.float32)) + bias_down
    result = layer_norm(normed_one + down_out, gain_two, shift_two)
    return jnp.where(in_length[:, None], result, 0.0)

def rotate_in(left_side, matrix, right_side):
    inner = jnp.einsum('pji,pjk->pik', left_side, matrix, precision=PRECISION_HIGH)
    return jnp.einsum('pik,pkl->pil', inner, right_side, precision=PRECISION_HIGH)

def rotate_out(left_side, matrix, right_side):
    inner = jnp.einsum('pij,pjk->pik', left_side, matrix, precision=PRECISION_HIGH)
    return jnp.einsum('pik,plk->pil', inner, right_side, precision=PRECISION_HIGH)

def reference(tokens, cotangent, lengths, deal, weights, vectors, owners, left_basis, right_basis, first_moment, second_moment, vec_first, vec_second):
    seq_total = MB * SEQS
    batch_rows = jnp.arange(MB)[:, None]
    positions = jnp.broadcast_to(jnp.arange(SEQS, dtype=jnp.int32)[None, :], (MB, SEQS))
    inverse = jnp.zeros((MB, SEQS), jnp.int32).at[batch_rows, deal].set(positions)
    back_in = jnp.take_along_axis(cotangent, inverse[:, :, None, None], axis=1)
    matrices = unpack_mats(low(weights))
    vecs = unpack_vecs(low(vectors))
    group_size = 8
    step_count = seq_total // group_size
    inputs_all = tokens.reshape(step_count, group_size, LEN, D)
    backs_all = back_in.reshape(step_count, group_size, LEN, D)
    lengths_all = lengths.reshape(step_count, group_size)

    def group_step(carry, scan_items):
        group_in, group_back, group_len = scan_items

        def run_group(mats_in, vecs_in, seq_in):
            return jax.vmap(sequence_forward, in_axes=(None, None, 0, 0))(mats_in, vecs_in, seq_in, group_len)
        outputs, pullback = jax.vjp(run_group, matrices, vecs, group_in.astype(jnp.float32))
        d_mats, d_vecs, d_inputs = pullback(group_back.astype(jnp.float32))
        carry = jax.tree.map(jnp.add, carry, (d_mats, d_vecs))
        return (carry, (outputs.astype(jnp.bfloat16), d_inputs.astype(jnp.bfloat16)))
    zero_carry = jax.tree.map(jnp.zeros_like, (matrices, vecs))
    (grad_mats, grad_vecs), (outputs, d_inputs) = lax.scan(group_step, zero_carry, (inputs_all, backs_all, lengths_all))
    out_tokens = outputs.reshape(MB, SEQS, LEN, D)
    in_grad = d_inputs.reshape(MB, SEQS, LEN, D)
    tile_grads = pack_mats(grad_mats)
    vec_grads = jnp.concatenate(grad_vecs)
    own_grads = jnp.take(tile_grads, owners, axis=0)
    own_master = jnp.take(weights, owners, axis=0)
    rates = tile_rate(owners)
    rotated = rotate_in(left_basis, own_grads, right_basis)
    new_first = BETA_ONE * first_moment + (1.0 - BETA_ONE) * rotated
    new_second = BETA_TWO * second_moment + (1.0 - BETA_TWO) * rotated * rotated
    first_hat = new_first / (1.0 - BETA_ONE ** STEP)
    second_hat = new_second / (1.0 - BETA_TWO ** STEP)
    step_rotated = first_hat / (jnp.sqrt(second_hat) + ADAM_EPS)
    update = rotate_out(left_basis, step_rotated, right_basis)
    new_tiles = own_master - rates[:, None, None] * (update + DECAY * own_master)
    vec_first_new = BETA_ONE * vec_first + (1.0 - BETA_ONE) * vec_grads
    vec_second_new = BETA_TWO * vec_second + (1.0 - BETA_TWO) * vec_grads * vec_grads
    vec_hat_one = vec_first_new / (1.0 - BETA_ONE ** STEP)
    vec_hat_two = vec_second_new / (1.0 - BETA_TWO ** STEP)
    new_vectors = vectors - VEC_RATE * vec_hat_one / (jnp.sqrt(vec_hat_two) + ADAM_EPS)
    return (out_tokens, in_grad, tile_grads, vec_grads, new_first, new_second, new_tiles, new_tiles.astype(jnp.bfloat16), vec_first_new, vec_second_new, new_vectors)
```

```python
import functools

import jax
import jax.numpy as jnp
from jax import lax
from jax.experimental import pallas as pl
from jax.experimental.pallas import tpu as pltpu
from jax.sharding import PartitionSpec as P

D = 1024
HEADS = 16
HEAD_DIM = 64
FF = 4096
STEP = 10
TB = 128


EPS_NORM = 1e-05
BETA_ONE = 0.5
BETA_TWO = 0.6
ADAM_EPS = 1e-08
DECAY = 0.01
VEC_RATE = 0.2
PRECISION_HIGH = lax.Precision.HIGHEST


def cut_tiles(stacked, row_count, col_count, start_at):
    tile_count = row_count // TB * (col_count // TB)
    blocked = lax.slice_in_dim(stacked, start_at, start_at + tile_count, axis=0)
    blocked = blocked.reshape(row_count // TB, col_count // TB, TB, TB)
    return (blocked.transpose(0, 2, 1, 3).reshape(row_count, col_count), start_at + tile_count)


def unpack_mats(stacked):
    w_qkv, offset = cut_tiles(stacked, D, 3 * D, 0)
    w_out, offset = cut_tiles(stacked, D, D, offset)
    w_up, offset = cut_tiles(stacked, D, FF, offset)
    w_down, offset = cut_tiles(stacked, FF, D, offset)
    return (w_qkv, w_out, w_up, w_down)


def tiled_grad(left_rows, right_rows):
    row_total = left_rows.shape[0]
    left_split = left_rows.reshape(row_total, left_rows.shape[1] // TB, TB)
    right_split = right_rows.reshape(row_total, right_rows.shape[1] // TB, TB)
    blocked = jnp.einsum(
        "tai,tbj->abij", left_split, right_split, preferred_element_type=jnp.float32
    )
    return blocked.reshape(-1, TB, TB)


def unpack_vecs(vector):
    widths = [D, D, D, FF, D, D, D, D, D]
    pieces = []
    offset = 0
    for width_now in widths:
        pieces.append(vector[offset : offset + width_now])
        offset += width_now
    return tuple(pieces)


def tile_rate(tile_ids):
    qkv_end = 3 * D * D // (TB * TB)
    out_end = 4 * D * D // (TB * TB)
    up_end = (4 * D * D + D * FF) // (TB * TB)
    return jnp.where(
        tile_ids < qkv_end,
        D ** (-0.5),
        jnp.where(
            tile_ids < out_end,
            (HEAD_DIM / D) ** 0.5,
            jnp.where(tile_ids < up_end, D ** (-0.5), 1.5 * FF ** (-0.5)),
        ),
    ).astype(jnp.float32)


def norm_apply(values, gain_vec, shift_vec):
    center = values - jnp.mean(values, axis=-1, keepdims=True)
    spread = jnp.mean(center * center, axis=-1, keepdims=True)
    return center * lax.rsqrt(spread + EPS_NORM) * gain_vec + shift_vec


def exact_gelu(values):
    return jax.nn.gelu(values, approximate=False)


def split_heads(joined16):
    seq_rows = joined16.shape[0]
    query_heads = joined16[:, :D].reshape(seq_rows, HEADS, HEAD_DIM)
    key_heads = joined16[:, D : 2 * D].reshape(seq_rows, HEADS, HEAD_DIM)
    value_heads = joined16[:, 2 * D :].reshape(seq_rows, HEADS, HEAD_DIM)
    return (query_heads, key_heads, value_heads)


def masked_scores(query_heads, key_heads, in_length):
    scores = jnp.einsum(
        "qhd,khd->hqk", query_heads, key_heads, preferred_element_type=jnp.float32
    ) * HEAD_DIM ** (-0.5)
    return jnp.where(in_length[None, None, :], scores, -1e30)


def forward_pass(inputs16, length, matrices, vecs):
    w_qkv, w_out, w_up, w_down = matrices
    bias_q, bias_v, bias_out, bias_up, bias_down, gain_one, shift_one, gain_two, shift_two = vecs
    seq_rows = inputs16.shape[0]
    joined = jnp.dot(inputs16, w_qkv, preferred_element_type=jnp.float32)
    joined = joined + jnp.concatenate([bias_q, jnp.zeros_like(bias_q), bias_v])
    joined16 = joined.astype(jnp.bfloat16)
    query_heads, key_heads, value_heads = split_heads(joined16)
    in_length = jnp.arange(seq_rows) < length
    scores = masked_scores(query_heads, key_heads, in_length)
    row_top = jnp.max(scores, axis=-1, keepdims=True)
    exp_scores = jnp.exp(scores - row_top)
    row_total = jnp.sum(exp_scores, axis=-1, keepdims=True)
    attention16 = (exp_scores / row_total).astype(jnp.bfloat16)
    log_total = row_top + jnp.log(row_total)
    attended = jnp.einsum(
        "hqk,khd->qhd", attention16, value_heads, preferred_element_type=jnp.float32
    )
    attended16 = attended.reshape(seq_rows, D).astype(jnp.bfloat16)
    resid_one = (
        inputs16.astype(jnp.float32)
        + jnp.dot(attended16, w_out, preferred_element_type=jnp.float32)
        + bias_out
    )
    normed_one = norm_apply(resid_one, gain_one, shift_one)
    normed16 = normed_one.astype(jnp.bfloat16)
    hidden = jnp.dot(normed16, w_up, preferred_element_type=jnp.float32) + bias_up
    active16 = exact_gelu(hidden).astype(jnp.bfloat16)
    resid_two = (
        normed_one + jnp.dot(active16, w_down, preferred_element_type=jnp.float32) + bias_down
    )
    result = norm_apply(resid_two, gain_two, shift_two)
    result = jnp.where(in_length[:, None], result, 0.0).astype(jnp.bfloat16)
    kept = (
        joined16,
        log_total,
        attended16,
        resid_one,
        normed16,
        hidden,
        active16,
        resid_two,
        in_length,
    )
    return (result, kept)


def backward_pass(back16, inputs16, kept, matrices, vecs):
    w_qkv, w_out, w_up, w_down = matrices
    bias_q, bias_v, bias_out, bias_up, bias_down, gain_one, shift_one, gain_two, shift_two = vecs
    joined16, log_total, attended16, resid_one, normed16, hidden, active16, resid_two, in_length = (
        kept
    )
    seq_rows = inputs16.shape[0]
    back = jnp.where(in_length[:, None], back16.astype(jnp.float32), 0.0)
    unused_two, pull_two = jax.vjp(norm_apply, resid_two, gain_two, shift_two)
    d_resid_two, d_gain_two, d_shift_two = pull_two(back)
    d_down16 = d_resid_two.astype(jnp.bfloat16)
    d_active = jnp.einsum("to,io->ti", d_down16, w_down, preferred_element_type=jnp.float32)
    unused_gelu, pull_gelu = jax.vjp(exact_gelu, hidden)
    d_hidden = pull_gelu(d_active)[0]
    d_hidden16 = d_hidden.astype(jnp.bfloat16)
    d_normed = d_resid_two + jnp.einsum(
        "to,io->ti", d_hidden16, w_up, preferred_element_type=jnp.float32
    )
    unused_one, pull_one = jax.vjp(norm_apply, resid_one, gain_one, shift_one)
    d_resid_one, d_gain_one, d_shift_one = pull_one(d_normed)
    d_branch16 = d_resid_one.astype(jnp.bfloat16)
    d_attended = jnp.einsum("to,io->ti", d_branch16, w_out, preferred_element_type=jnp.float32)
    d_attended16 = d_attended.astype(jnp.bfloat16).reshape(seq_rows, HEADS, HEAD_DIM)
    query_heads, key_heads, value_heads = split_heads(joined16)
    scores = masked_scores(query_heads, key_heads, in_length)
    attention = jnp.exp(scores - log_total)
    attention16 = attention.astype(jnp.bfloat16)
    d_value = jnp.einsum(
        "hqk,qhd->khd", attention16, d_attended16, preferred_element_type=jnp.float32
    )
    d_attention = jnp.einsum(
        "qhd,khd->hqk", d_attended16, value_heads, preferred_element_type=jnp.float32
    )
    d_scores = attention * (d_attention - jnp.sum(attention * d_attention, axis=-1, keepdims=True))
    d_scores16 = d_scores.astype(jnp.bfloat16)
    d_query = jnp.einsum(
        "hqk,khd->qhd", d_scores16, key_heads, preferred_element_type=jnp.float32
    ) * HEAD_DIM ** (-0.5)
    d_key = jnp.einsum(
        "hqk,qhd->khd", d_scores16, query_heads, preferred_element_type=jnp.float32
    ) * HEAD_DIM ** (-0.5)
    d_query = d_query.reshape(seq_rows, D)
    d_key = d_key.reshape(seq_rows, D)
    d_value = d_value.reshape(seq_rows, D)
    d_joined16 = jnp.concatenate([d_query, d_key, d_value], axis=1).astype(jnp.bfloat16)
    d_inputs = d_resid_one + jnp.einsum(
        "to,io->ti", d_joined16, w_qkv, preferred_element_type=jnp.float32
    )
    vec_grad = jnp.concatenate(
        [
            jnp.sum(d_query, axis=0),
            jnp.sum(d_value, axis=0),
            jnp.sum(d_resid_one, axis=0),
            jnp.sum(d_hidden, axis=0),
            jnp.sum(d_resid_two, axis=0),
            d_gain_one,
            d_shift_one,
            d_gain_two,
            d_shift_two,
        ]
    )
    pairs = (d_joined16, attended16, d_branch16, normed16, d_hidden16, active16, d_down16)
    return (pairs, vec_grad, d_inputs.astype(jnp.bfloat16))


def rotate_in(left_side, matrix, right_side):
    inner = jnp.einsum(
        "pji,pjk->pik",
        left_side,
        matrix,
        precision=PRECISION_HIGH,
        preferred_element_type=jnp.float32,
    )
    return jnp.einsum(
        "pik,pkl->pil",
        inner,
        right_side,
        precision=PRECISION_HIGH,
        preferred_element_type=jnp.float32,
    )


def rotate_out(left_side, matrix, right_side):
    inner = jnp.einsum(
        "pij,pjk->pik",
        left_side,
        matrix,
        precision=PRECISION_HIGH,
        preferred_element_type=jnp.float32,
    )
    return jnp.einsum(
        "pik,plk->pil",
        inner,
        right_side,
        precision=PRECISION_HIGH,
        preferred_element_type=jnp.float32,
    )


def per_device_any(
    tokens,
    cotangent,
    lengths,
    deal,
    weights,
    vectors,
    owners,
    left_basis,
    right_basis,
    first_moment,
    second_moment,
    vec_first,
    vec_second,
):
    dp_count = lax.axis_size("dp")
    fsdp_count = lax.axis_size("fsdp")
    dp_place = lax.axis_index("dp")
    fsdp_place = lax.axis_index("fsdp")
    micro_count = tokens.shape[0]
    my_place = dp_place * fsdp_count + fsdp_place
    quarter = lax.dynamic_index_in_dim(
        deal.reshape(micro_count, dp_count, fsdp_count), fsdp_place, axis=2, keepdims=False
    )
    quarter = quarter - fsdp_place * dp_count
    ordered = jnp.take_along_axis(tokens, quarter[:, :, None, None], axis=1)
    dealt_rows = lax.all_to_all(ordered, "dp", split_axis=1, concat_axis=2, tiled=True)
    my_seq = lax.dynamic_index_in_dim(deal, my_place, axis=1, keepdims=False)
    my_length = jnp.take_along_axis(lengths, my_seq[:, None], axis=1)[:, 0]
    shard_low = (weights.astype(jnp.bfloat16), vectors.astype(jnp.bfloat16))
    whole_tiles, whole_vecs = (
        lax.all_gather(shard_low[0], ("dp", "fsdp"), axis=0, tiled=True),
        lax.all_gather(shard_low[1], ("dp", "fsdp"), axis=0, tiled=True),
    )
    mats_kept = unpack_mats(whole_tiles)
    vecs_kept = unpack_vecs(whole_vecs.astype(jnp.float32))
    all_pairs = []
    all_inputs = []
    vec_terms = []
    results = []
    input_grads = []
    for micro_index in range(micro_count):
        inputs16 = dealt_rows[micro_index, 0]
        matrices, vecs = (mats_kept, vecs_kept)
        result, kept = forward_pass(inputs16, my_length[micro_index], matrices, vecs)
        pairs, vec_term, d_inputs = backward_pass(
            cotangent[micro_index, 0], inputs16, kept, matrices, vecs
        )
        all_pairs.append(pairs)
        all_inputs.append(inputs16)
        vec_terms.append(vec_term)
        results.append(result)
        input_grads.append(d_inputs)

    def joined_rows(index):
        return jnp.concatenate([pairs[index] for pairs in all_pairs], axis=0)

    inputs_rows = jnp.concatenate(all_inputs, axis=0)
    tile_terms = jnp.concatenate(
        [
            tiled_grad(inputs_rows, joined_rows(0)),
            tiled_grad(joined_rows(1), joined_rows(2)),
            tiled_grad(joined_rows(3), joined_rows(4)),
            tiled_grad(joined_rows(5), joined_rows(6)),
        ],
        axis=0,
    )
    grad_vec = vec_terms[0]
    for vec_term in vec_terms[1:]:
        grad_vec = grad_vec + vec_term
    shard_tiles = weights.shape[0]
    tile_grads, vec_grads = (
        lax.psum_scatter(tile_terms, ("dp", "fsdp"), scatter_dimension=0, tiled=True),
        lax.psum_scatter(grad_vec, ("dp", "fsdp"), scatter_dimension=0, tiled=True),
    )
    group_grads, group_master = (
        lax.all_gather(tile_grads.astype(jnp.bfloat16), "fsdp", axis=0, tiled=True).astype(
            tile_grads.dtype
        ),
        lax.all_gather(weights.astype(jnp.bfloat16), "fsdp", axis=0, tiled=True).astype(
            weights.dtype
        ),
    )
    result_dealt = jnp.stack(results)[:, None]
    grads_dealt = jnp.stack(input_grads)[:, None]
    back_result, back_grads = (
        lax.all_to_all(result_dealt, "dp", split_axis=2, concat_axis=1, tiled=True),
        lax.all_to_all(grads_dealt, "dp", split_axis=2, concat_axis=1, tiled=True),
    )
    restore = jnp.argsort(quarter, axis=1)
    out_tokens = jnp.take_along_axis(back_result, restore[:, :, None, None], axis=1)
    in_grad = jnp.take_along_axis(back_grads, restore[:, :, None, None], axis=1)
    group_size = fsdp_count * shard_tiles
    pick_rows = owners - dp_place * group_size
    own_grads = jnp.take(group_grads, pick_rows, axis=0)
    own_master = jnp.take(group_master, pick_rows, axis=0)
    rates = tile_rate(owners)
    rotated = rotate_in(left_basis, own_grads, right_basis)
    new_first = BETA_ONE * first_moment + (1.0 - BETA_ONE) * rotated
    new_second = BETA_TWO * second_moment + (1.0 - BETA_TWO) * rotated * rotated
    first_hat = new_first / (1.0 - BETA_ONE**STEP)
    second_hat = new_second / (1.0 - BETA_TWO**STEP)
    step_rotated = first_hat / (jnp.sqrt(second_hat) + ADAM_EPS)
    update = rotate_out(left_basis, step_rotated, right_basis)
    new_tiles = own_master - rates[:, None, None] * (update + DECAY * own_master)
    vec_first_new = BETA_ONE * vec_first + (1.0 - BETA_ONE) * vec_grads
    vec_second_new = BETA_TWO * vec_second + (1.0 - BETA_TWO) * vec_grads * vec_grads
    vec_hat_one = vec_first_new / (1.0 - BETA_ONE**STEP)
    vec_hat_two = vec_second_new / (1.0 - BETA_TWO**STEP)
    new_vectors = vectors - VEC_RATE * vec_hat_one / (jnp.sqrt(vec_hat_two) + ADAM_EPS)
    return (
        out_tokens,
        in_grad,
        tile_grads,
        vec_grads,
        new_first,
        new_second,
        new_tiles,
        new_tiles.astype(jnp.bfloat16),
        vec_first_new,
        vec_second_new,
        new_vectors,
    )


MESH = pl.DeviceIdType.MESH
ZN = 4
OCT = 96
RING = 8


class Place:
    def __init__(self):
        self.dp = lax.axis_index("dp")
        self.fs = lax.axis_index("fsdp")
        self.z, self.y = self.dp // 2, self.dp % 2
        self.x, self.c = self.fs // 2, self.fs % 2
        self.to_x = (self.dp, (self.fs + 2) % 4)
        self.to_y = (self.z * 2 + 1 - self.y, self.fs)
        self.to_core = (self.dp, self.x * 2 + 1 - self.c)
        self.to_up = (self.dp + 2, self.fs)
        self.to_down = (self.dp - 2, self.fs)
        near = self.z + 1 - 2 * (self.z % 2)
        far = (self.z + 2) % ZN
        self.to_near = (near * 2 + self.y, self.fs)
        self.to_far = (far * 2 + self.y, self.fs)

    def greet(self):
        bar = pltpu.get_barrier_semaphore()
        for dev in (self.to_x, self.to_y, self.to_core, self.to_far):
            pl.semaphore_signal(bar, inc=1, device_id=dev, device_id_type=MESH)

        @pl.when(self.z < ZN - 1)
        def _():
            pl.semaphore_signal(bar, inc=1, device_id=self.to_up, device_id_type=MESH)

        @pl.when(self.z > 0)
        def _():
            pl.semaphore_signal(bar, inc=1, device_id=self.to_down, device_id_type=MESH)

        pl.semaphore_wait(
            bar, 4 + jnp.where(self.z > 0, 1, 0) + jnp.where(self.z < ZN - 1, 1, 0)
        )

    def octet(self, dx, dy, zp, k, c=None):
        yy = self.y if dy == 0 else 1 - self.y
        xx = self.x if dx == 0 else 1 - self.x
        return ((zp * 2 + yy) * 4 + xx * 2 + (self.c if c is None else c)) * 3 + k

    def plane(self, s, middle):
        low = self.z < 2
        zz = jnp.where(low, self.z, 3 - self.z)
        f = jnp.where(zz == 0, s, middle[s])
        return jnp.where(low, f, 3 - f)


def octet_place(o):
    return jnp.where(
        o < 24,
        (o % 3) * 8 + o // 3,
        jnp.where((o >= 32) & (o < 64), 32 + ((o - 32) % 4) * 8 + (o - 32) // 4, o),
    )


def left_block(o):
    return jnp.where(
        o < 24, o // 3, jnp.where(o < 32, o - 16, jnp.where(o < 64, 16 + (o - 32) // 4, o - 40))
    )


def right_block(o):
    return jnp.where(o < 24, o % 3, jnp.where(o < 32, 3, jnp.where(o < 64, 4 + (o - 32) % 4, 8)))


def wait_for(ref, sem):
    pltpu.make_async_copy(ref, ref, sem).wait()


def remote(src, dst, send_sem, recv_sem, dev):
    return pltpu.make_async_remote_copy(
        src_ref=src,
        dst_ref=dst,
        send_sem=send_sem,
        recv_sem=recv_sem,
        device_id=dev,
        device_id_type=MESH,
    )


def route_x(s, zp, k):
    if s == 0 and k < 2:
        return k == 0
    return (zp % 2) == 0


def on(flag, fn):
    if flag is True:
        fn()
    elif flag is not False:
        pl.when(flag)(fn)


def unless(flag, fn):
    on((not flag) if isinstance(flag, bool) else jnp.logical_not(flag), fn)


GATHER_ORDER = [
    (1, 0), (1, 1), (2, 0), (1, 2), (2, 1), (3, 0), (1, 3), (2, 2), (3, 1), (2, 3), (3, 2), (3, 3),
]
GATHER_MIDDLE = [1, 2, 0, 3]


def gather_kernel(
    shard, vec, out, vout, rs, s_x, s_y, s_up, s_down, s_core, s_local, s_vec, r_vec
):
    p = Place()
    z = p.z
    p.greet()

    def ref_of(o):
        return out.at[octet_place(o)]

    def send(o, dev, sem, src=None):
        remote(ref_of(o) if src is None else src, ref_of(o), sem, rs.at[o], dev).start()

    def wait(o):
        wait_for(ref_of(o), rs.at[o])

    def along_z(s, zp, o, src=None):
        def up():
            send(o, p.to_up, s_up, src)

        def down():
            send(o, p.to_down, s_down, src)

        if s == 0:
            pl.when(z < ZN - 1)(up)
            pl.when(z > 0)(down)
        else:
            pl.when((zp < z) & (z < ZN - 1))(up)
            pl.when((zp > z) & (z > 0))(down)

    for k in range(3):
        pltpu.make_async_copy(shard.at[k], ref_of(p.octet(0, 0, z, k)), s_local.at[k]).start()
    me = p.dp * 4 + p.fs
    vout[me] = vec[...]
    vec_dev = [p.to_core, p.to_x, p.to_y, p.to_near, p.to_far]

    def vec_step(n):
        size = 2**n
        if n > 0:
            half = size // 2
            theirs = (me // half) * half
            theirs = theirs + half * (1 - 2 * (theirs // half % 2))
            wait_for(vout.at[pl.ds(theirs, half)], r_vec.at[n - 1])
        if n < 5:
            mine = vout.at[pl.ds((me // size) * size, size)]
            remote(mine, mine, s_vec.at[n], r_vec.at[n], vec_dev[n]).start()

    vec_step(0)
    for step, (phase, s) in enumerate(GATHER_ORDER):
        zp = p.plane(s, GATHER_MIDDLE)
        for k in range(3):
            if phase == 1:
                o = p.octet(0, 0, zp, k)
                src = shard.at[k] if s == 0 else None
                if s > 0:
                    wait(o)
                along_z(s, zp, o, src)
                send(o, p.to_x, s_x, src)
                send(o, p.to_y, s_y, src)
                send(o, p.to_core, s_core, src)
            if phase == 2:
                o = p.octet(0, 1, zp, k)
                wait(o)
                if s == 0 or k == 2:
                    on(route_x(s, zp, k), functools.partial(send, o, p.to_x, s_x))
                send(o, p.to_core, s_core)
                o = p.octet(1, 0, zp, k)
                wait(o)
                if s == 0 or k == 2:
                    unless(route_x(s, zp, k), functools.partial(send, o, p.to_y, s_y))
                send(o, p.to_core, s_core)
            if phase == 3:
                o = p.octet(1, 1, zp, k)
                wait(o)
                if k < 2:
                    along_z(s, zp, o)
                send(o, p.to_core, s_core)
        if 0 < step < 6:
            vec_step(step)

    for zp in range(ZN):
        for dx in range(2):
            for dy in range(2):
                for k in range(3):
                    wait(p.octet(dx, dy, zp, k, 1 - p.c))
    for k in range(3):
        wait_for(shard.at[k], s_local.at[k])
    for n in range(5):
        wait_for(vout.at[pl.ds(0, 2**n)], s_vec.at[n])

    def drain(sem, n):
        wait_for(out.at[pl.ds(0, n)], sem)

    drain(s_core, 48)
    drain(s_x, 15)
    drain(s_y, 15)
    for zz in range(ZN - 1):
        pl.when(z == zz)(functools.partial(drain, s_up, 5 * (zz + 1)))
        pl.when(z == ZN - 1 - zz)(functools.partial(drain, s_down, 5 * (zz + 1)))


def gather_weights(shard, vec):
    dma = pltpu.SemaphoreType.DMA
    return pl.pallas_call(
        gather_kernel,
        out_shape=(
            jax.ShapeDtypeStruct((OCT, TB, D), jnp.bfloat16),
            jax.ShapeDtypeStruct((32, 8, TB), jnp.float32),
        ),
        in_specs=[pl.BlockSpec(memory_space=pl.ANY), pl.BlockSpec(memory_space=pltpu.VMEM)],
        out_specs=(pl.BlockSpec(memory_space=pl.ANY), pl.BlockSpec(memory_space=pltpu.VMEM)),
        scratch_shapes=[dma((OCT,)), dma, dma, dma, dma, dma, dma((3,)), dma((5,)), dma((5,))],
        compiler_params=pltpu.CompilerParams(
            collective_id=0, has_side_effects=True, vmem_limit_bytes=16 * 2**20
        ),
        name="gather_weights",
    )(shard, vec)


REDUCE_ORDER = [
    "A3", "V0", "A2", "B3", "V1", "B2", "C3", "V2", "A1", "B1", "C2", "V3", "D3", "A0", "V4", "B0",
    "C1", "D2", "C0", "D1", "D0",
]
REDUCE_MIDDLE = [1, 0, 2, 3]


def reduce_kernel(
    lt, r3, vecg, tiles, grp, vout,
    land_c, land_x, land_y, land_z, ring, vland, acc,
    r_c, r_x, r_y, r_z, r_e, r_v, s_ring, s_x, s_y, s_up, s_down, s_e, s_e2, s_v,
):
    p = Place()
    z, c, fs = p.z, p.c, p.fs
    p.greet()

    def rel(dx, dy, zp, k):
        return ((dy * 2 + dx) * ZN + zp) * 3 + k

    def slot(j, zp, k):
        return (j * ZN + zp) * 3 + k

    def part(o):
        return jnp.dot(lt[left_block(o)], r3[right_block(o)], preferred_element_type=jnp.float32)

    def add(land, sem, n):
        wait_for(land.at[n], sem.at[n])
        acc[...] += land[n].astype(jnp.float32)

    def begin(q, o):
        wait_for(land_c.at[q], r_c.at[q])
        acc[...] = part(o) + land_c[q].astype(jnp.float32)

    def keep(q):
        land_c[q] = acc[...].astype(jnp.bfloat16)

    def send_x(q, n):
        remote(land_c.at[q], land_x.at[n], s_x, r_x.at[n], p.to_x).start()

    def send_y(q, n):
        remote(land_c.at[q], land_y.at[n], s_y, r_y.at[n], p.to_y).start()

    def send_z(q, j, zp, k):
        n = slot(j, zp, k)

        @pl.when(zp > z)
        def _():
            remote(land_c.at[q], land_z.at[n], s_up, r_z.at[n], p.to_up).start()

        @pl.when(zp < z)
        def _():
            t = jnp.where(zp == z - 1, 24 + j * 3 + k, n)
            remote(land_c.at[q], land_z.at[t], s_down, r_z.at[t], p.to_down).start()

    def add_z(s, j, zp, k):
        n = slot(j, zp, k)
        if s == 0:
            pl.when(z > 0)(functools.partial(add, land_z, r_z, n))
            pl.when(z < ZN - 1)(functools.partial(add, land_z, r_z, 24 + j * 3 + k))
        else:
            pl.when(((zp > z) & (z > 0)) | ((zp < z) & (z < ZN - 1)))(
                functools.partial(add, land_z, r_z, n)
            )

    def to_partner(s, zp, first):
        def body(i, _):
            yy, xx = (i // 3) % 2, i // 6
            o = ((zp * 2 + yy) * 4 + xx * 2 + (1 - c)) * 3 + i % 3
            n = (first + i) % RING
            value = part(o).astype(jnp.bfloat16)

            def free():
                wait_for(ring.at[0], s_ring.at[n])

            if first == 0:
                pl.when(i >= RING)(free)
            else:
                free()
            ring[n] = value
            q = ((jnp.where(yy == p.y, 0, 1) * 2 + jnp.where(xx == p.x, 0, 1)) * ZN + zp) * 3 + i % 3
            remote(ring.at[n], land_c.at[q], s_ring.at[n], r_c.at[q], p.to_core).start()
            return 0

        lax.fori_loop(0, 12, body, 0)

    def corner(s, zp):
        for k in range(3):
            q = rel(1, 1, zp, k)
            begin(q, p.octet(1, 1, zp, k))
            if k < 2:
                add_z(s, 1, zp, k)
            keep(q)
            if s == 0 or k == 2:
                on(route_x(s, zp, k), functools.partial(send_x, q, slot(1, zp, k)))
                unless(route_x(s, zp, k), functools.partial(send_y, q, slot(1, zp, k)))
            else:
                send_z(q, 1, zp, k)

    def sides(s, zp):
        for k in range(3):
            q = rel(0, 1, zp, k)
            begin(q, p.octet(0, 1, zp, k))
            if s == 0 or k == 2:
                on(route_x(s, zp, k), functools.partial(add, land_x, r_x, slot(1, zp, k)))
            keep(q)
            send_y(q, slot(0, zp, k))
            q = rel(1, 0, zp, k)
            begin(q, p.octet(1, 0, zp, k))
            if s == 0 or k == 2:
                unless(route_x(s, zp, k), functools.partial(add, land_y, r_y, slot(1, zp, k)))
            keep(q)
            send_x(q, slot(0, zp, k))

    def column(s, zp):
        for k in range(3):
            q = rel(0, 0, zp, k)
            begin(q, p.octet(0, 0, zp, k))
            add(land_x, r_x, slot(0, zp, k))
            add(land_y, r_y, slot(0, zp, k))
            add_z(s, 0, zp, k)
            if s > 0:
                keep(q)
                send_z(q, 0, zp, k)
            else:
                for j in range(8):
                    piece = acc[:, j * TB : (j + 1) * TB]
                    tiles[8 * k + j] = piece
                    grp[fs * 24 + 8 * k + j] = piece.astype(jnp.bfloat16)
                mine = grp.at[pl.ds(fs * 24 + 8 * k, 8)]
                remote(mine, mine, s_e, r_e.at[fs * 3 + k], p.to_x).start()
                remote(mine, mine, s_e2, r_e.at[fs * 3 + k], p.to_core).start()

    vec_dev = [p.to_core, p.to_x, p.to_y, p.to_near, p.to_far]

    def vec_step(n):
        if n == 0:
            vout[...] = vecg[...]
        else:
            wait_for(vland.at[n - 1], r_v.at[n - 1])
            vout[...] = vout[...] + vland[n - 1]
        if n < 5:
            vland[5 + n] = vout[...]
            remote(vland.at[5 + n], vland.at[n], s_v.at[n], r_v.at[n], vec_dev[n]).start()

    first = 0
    for name in REDUCE_ORDER:
        s = int(name[1])
        if name[0] == "V":
            vec_step(s)
            continue
        zp = p.plane(s, REDUCE_MIDDLE)
        if name[0] == "A":
            to_partner(s, zp, first)
            first += 12
        elif name[0] == "B":
            corner(s, zp)
        elif name[0] == "C":
            sides(s, zp)
        else:
            column(s, zp)
    vec_step(5)

    fx = (fs + 2) % 4
    for k in range(3):
        block = grp.at[pl.ds(fx * 24 + 8 * k, 8)]
        wait_for(block, r_e.at[fx * 3 + k])
        remote(block, block, s_e2, r_e.at[fx * 3 + k], p.to_core).start()
    for f in (p.x * 2 + 1 - c, (1 - p.x) * 2 + 1 - c):
        for k in range(3):
            wait_for(grp.at[pl.ds(f * 24 + 8 * k, 8)], r_e.at[f * 3 + k])

    for n in range(RING):
        wait_for(ring.at[0], s_ring.at[n])
    for n in range(5):
        wait_for(vland.at[5 + n], s_v.at[n])

    def drain(sem, n):
        wait_for(land_c.at[pl.ds(0, n)], sem)

    drain(s_x, 15)
    drain(s_y, 15)
    wait_for(grp.at[pl.ds(0, 24)], s_e)
    wait_for(grp.at[pl.ds(0, 48)], s_e2)
    for zz in range(ZN - 1):
        pl.when(z == zz)(functools.partial(drain, s_up, 5 * (ZN - 1 - zz)))
        pl.when(z == ZN - 1 - zz)(functools.partial(drain, s_down, 5 * (ZN - 1 - zz)))


def reduce_grads(lt, r3, vecg):
    bf = jnp.bfloat16
    dma = pltpu.SemaphoreType.DMA
    vmem = pl.BlockSpec(memory_space=pltpu.VMEM)
    return pl.pallas_call(
        reduce_kernel,
        out_shape=(
            jax.ShapeDtypeStruct((24, TB, TB), jnp.float32),
            jax.ShapeDtypeStruct((96, TB, TB), bf),
            jax.ShapeDtypeStruct((96, TB), jnp.float32),
        ),
        in_specs=[vmem] * 3,
        out_specs=(vmem,) * 3,
        scratch_shapes=[
            pltpu.VMEM((48, TB, D), bf),
            pltpu.VMEM((24, TB, D), bf),
            pltpu.VMEM((24, TB, D), bf),
            pltpu.VMEM((30, TB, D), bf),
            pltpu.VMEM((RING, TB, D), bf),
            pltpu.VMEM((10, 96, TB), jnp.float32),
            pltpu.VMEM((TB, D), jnp.float32),
            dma((48,)), dma((24,)), dma((24,)), dma((30,)), dma((12,)), dma((5,)),
            dma((RING,)), dma, dma, dma, dma, dma, dma, dma((5,)),
        ],
        compiler_params=pltpu.CompilerParams(
            collective_id=1, has_side_effects=True, vmem_limit_bytes=62 * 2**20
        ),
        name="reduce_grads",
    )(lt, r3, vecg)


def per_device(
    tokens,
    cotangent,
    lengths,
    deal,
    weights,
    vectors,
    owners,
    left_basis,
    right_basis,
    first_moment,
    second_moment,
    vec_first,
    vec_second,
):
    dp_count = lax.axis_size("dp")
    fsdp_count = lax.axis_size("fsdp")
    dp_place = lax.axis_index("dp")
    fsdp_place = lax.axis_index("fsdp")
    micro_count = tokens.shape[0]
    my_place = dp_place * fsdp_count + fsdp_place
    quarter = lax.dynamic_index_in_dim(
        deal.reshape(micro_count, dp_count, fsdp_count), fsdp_place, axis=2, keepdims=False
    )
    quarter = quarter - fsdp_place * dp_count
    ordered = jnp.take_along_axis(tokens, quarter[:, :, None, None], axis=1)
    dealt_rows = lax.all_to_all(ordered, "dp", split_axis=1, concat_axis=2, tiled=True)
    my_seq = lax.dynamic_index_in_dim(deal, my_place, axis=1, keepdims=False)
    my_length = jnp.take_along_axis(lengths, my_seq[:, None], axis=1)[:, 0]
    shard = weights.astype(jnp.bfloat16).reshape(3, 8, TB, TB).transpose(0, 2, 1, 3)
    shard = shard.reshape(3, TB, D)
    vec_shard = vectors.astype(jnp.bfloat16).astype(jnp.float32).reshape(3, TB)
    wm, all_vecs = gather_weights(shard, jnp.pad(vec_shard, ((0, 5), (0, 0))))
    whole_vecs = all_vecs[:, :3].reshape(-1)
    w12 = wm.reshape(12, D, D)
    matrices = (
        w12[:3].transpose(1, 0, 2).reshape(D, 3 * D),
        w12[3],
        w12[4:8].transpose(1, 0, 2).reshape(D, FF),
        w12[8:].reshape(FF, D),
    )
    vecs = unpack_vecs(whole_vecs)
    all_pairs, all_inputs, vec_terms, results, input_grads = [], [], [], [], []
    for micro_index in range(micro_count):
        inputs16 = dealt_rows[micro_index, 0]
        result, kept = forward_pass(inputs16, my_length[micro_index], matrices, vecs)
        pairs, vec_term, d_inputs = backward_pass(
            cotangent[micro_index, 0], inputs16, kept, matrices, vecs
        )
        all_pairs.append(pairs)
        all_inputs.append(inputs16)
        vec_terms.append(vec_term)
        results.append(result)
        input_grads.append(d_inputs)

    def joined_rows(index):
        return jnp.concatenate([pairs[index] for pairs in all_pairs], axis=0)

    x_rows = jnp.concatenate(all_inputs, axis=0)
    left = jnp.concatenate([x_rows, joined_rows(1), joined_rows(3), joined_rows(5)], axis=1)
    right = jnp.concatenate([joined_rows(0), joined_rows(2), joined_rows(4), joined_rows(6)], axis=1)
    rows = left.shape[0]
    lt = left.T.reshape(56, TB, rows)
    r3 = right.reshape(rows, 9, D).transpose(1, 0, 2)
    grad_vec = sum(vec_terms[1:], vec_terms[0])
    tile_grads, group_grads, vec_total = reduce_grads(lt, r3, grad_vec.reshape(96, TB))
    vec_grads = lax.dynamic_slice_in_dim(vec_total, my_place * 3, 3, axis=0).reshape(-1)
    result_dealt = jnp.stack(results)[:, None]
    grads_dealt = jnp.stack(input_grads)[:, None]
    back_result, back_grads = (
        lax.all_to_all(result_dealt, "dp", split_axis=2, concat_axis=1, tiled=True),
        lax.all_to_all(grads_dealt, "dp", split_axis=2, concat_axis=1, tiled=True),
    )
    restore = jnp.argsort(quarter, axis=1)
    out_tokens = jnp.take_along_axis(back_result, restore[:, :, None, None], axis=1)
    in_grad = jnp.take_along_axis(back_grads, restore[:, :, None, None], axis=1)
    own_octets = jnp.take(wm, octet_place(owners // 8), axis=0).reshape(24, TB, 8, TB)
    own_master = jnp.take_along_axis(own_octets, (owners % 8)[:, None, None, None], axis=2)
    own_master = own_master[:, :, 0].astype(jnp.float32)
    own_grads = jnp.take(group_grads, owners - dp_place * 96, axis=0).astype(jnp.float32)
    rates = tile_rate(owners)
    rotated = rotate_in(left_basis, own_grads, right_basis)
    new_first = BETA_ONE * first_moment + (1.0 - BETA_ONE) * rotated
    new_second = BETA_TWO * second_moment + (1.0 - BETA_TWO) * rotated * rotated
    first_hat = new_first / (1.0 - BETA_ONE**STEP)
    second_hat = new_second / (1.0 - BETA_TWO**STEP)
    step_rotated = first_hat / (jnp.sqrt(second_hat) + ADAM_EPS)
    update = rotate_out(left_basis, step_rotated, right_basis)
    new_tiles = own_master - rates[:, None, None] * (update + DECAY * own_master)
    vec_first_new = BETA_ONE * vec_first + (1.0 - BETA_ONE) * vec_grads
    vec_second_new = BETA_TWO * vec_second + (1.0 - BETA_TWO) * vec_grads * vec_grads
    vec_hat_one = vec_first_new / (1.0 - BETA_ONE**STEP)
    vec_hat_two = vec_second_new / (1.0 - BETA_TWO**STEP)
    new_vectors = vectors - VEC_RATE * vec_hat_one / (jnp.sqrt(vec_hat_two) + ADAM_EPS)
    return (
        out_tokens,
        in_grad,
        tile_grads,
        vec_grads,
        new_first,
        new_second,
        new_tiles,
        new_tiles.astype(jnp.bfloat16),
        vec_first_new,
        vec_second_new,
        new_vectors,
    )


def solution(mesh):
    body = per_device if (mesh.shape["dp"], mesh.shape["fsdp"]) == (2 * ZN, 4) else per_device_any
    placed = (
        P(None, "fsdp", "dp", None),
        P(None, ("dp", "fsdp"), None, None),
        P(),
        P(),
        P(("dp", "fsdp"), None, None),
        P(("dp", "fsdp")),
        P(("dp", "fsdp")),
        P(("dp", "fsdp"), None, None),
        P(("dp", "fsdp"), None, None),
        P(("dp", "fsdp"), None, None),
        P(("dp", "fsdp"), None, None),
        P(("dp", "fsdp")),
        P(("dp", "fsdp")),
    )
    return jax.shard_map(
        body,
        mesh=mesh,
        in_specs=placed,
        out_specs=(
            P(None, "fsdp", "dp", None),
            P(None, "fsdp", "dp", None),
            P(("dp", "fsdp"), None, None),
            P(("dp", "fsdp")),
            P(("dp", "fsdp"), None, None),
            P(("dp", "fsdp"), None, None),
            P(("dp", "fsdp"), None, None),
            P(("dp", "fsdp"), None, None),
            P(("dp", "fsdp")),
            P(("dp", "fsdp")),
            P(("dp", "fsdp")),
        ),
        check_vma=False,
    )
```

```python
import functools

import jax
import jax.numpy as jnp
from jax import lax
from jax.experimental import pallas as pl
from jax.experimental.pallas import tpu as pltpu
from jax.sharding import PartitionSpec as P

D = 1024
HEADS = 16
HEAD_DIM = 64
FF = 4096
STEP = 10
TB = 128


EPS_NORM = 1e-05
BETA_ONE = 0.5
BETA_TWO = 0.6
ADAM_EPS = 1e-08
DECAY = 0.01
VEC_RATE = 0.2
PRECISION_HIGH = lax.Precision.HIGHEST


def cut_tiles(stacked, row_count, col_count, start_at):
    tile_count = row_count // TB * (col_count // TB)
    blocked = lax.slice_in_dim(stacked, start_at, start_at + tile_count, axis=0)
    blocked = blocked.reshape(row_count // TB, col_count // TB, TB, TB)
    return (blocked.transpose(0, 2, 1, 3).reshape(row_count, col_count), start_at + tile_count)


def unpack_mats(stacked):
    w_qkv, offset = cut_tiles(stacked, D, 3 * D, 0)
    w_out, offset = cut_tiles(stacked, D, D, offset)
    w_up, offset = cut_tiles(stacked, D, FF, offset)
    w_down, offset = cut_tiles(stacked, FF, D, offset)
    return (w_qkv, w_out, w_up, w_down)


def tiled_grad(left_rows, right_rows):
    row_total = left_rows.shape[0]
    left_split = left_rows.reshape(row_total, left_rows.shape[1] // TB, TB)
    right_split = right_rows.reshape(row_total, right_rows.shape[1] // TB, TB)
    blocked = jnp.einsum(
        "tai,tbj->abij", left_split, right_split, preferred_element_type=jnp.float32
    )
    return blocked.reshape(-1, TB, TB)


def unpack_vecs(vector):
    widths = [D, D, D, FF, D, D, D, D, D]
    pieces = []
    offset = 0
    for width_now in widths:
        pieces.append(vector[offset : offset + width_now])
        offset += width_now
    return tuple(pieces)


def tile_rate(tile_ids):
    qkv_end = 3 * D * D // (TB * TB)
    out_end = 4 * D * D // (TB * TB)
    up_end = (4 * D * D + D * FF) // (TB * TB)
    return jnp.where(
        tile_ids < qkv_end,
        D ** (-0.5),
        jnp.where(
            tile_ids < out_end,
            (HEAD_DIM / D) ** 0.5,
            jnp.where(tile_ids < up_end, D ** (-0.5), 1.5 * FF ** (-0.5)),
        ),
    ).astype(jnp.float32)


def norm_apply(values, gain_vec, shift_vec):
    center = values - jnp.mean(values, axis=-1, keepdims=True)
    spread = jnp.mean(center * center, axis=-1, keepdims=True)
    return center * lax.rsqrt(spread + EPS_NORM) * gain_vec + shift_vec


def exact_gelu(values):
    return jax.nn.gelu(values, approximate=False)


def split_heads(joined16):
    seq_rows = joined16.shape[0]
    query_heads = joined16[:, :D].reshape(seq_rows, HEADS, HEAD_DIM)
    key_heads = joined16[:, D : 2 * D].reshape(seq_rows, HEADS, HEAD_DIM)
    value_heads = joined16[:, 2 * D :].reshape(seq_rows, HEADS, HEAD_DIM)
    return (query_heads, key_heads, value_heads)


def masked_scores(query_heads, key_heads, in_length):
    scores = jnp.einsum(
        "qhd,khd->hqk", query_heads, key_heads, preferred_element_type=jnp.float32
    ) * HEAD_DIM ** (-0.5)
    return jnp.where(in_length[None, None, :], scores, -1e30)


def forward_pass(inputs16, length, matrices, vecs):
    w_qkv, w_out, w_up, w_down = matrices
    bias_q, bias_v, bias_out, bias_up, bias_down, gain_one, shift_one, gain_two, shift_two = vecs
    seq_rows = inputs16.shape[0]
    joined = jnp.dot(inputs16, w_qkv, preferred_element_type=jnp.float32)
    joined = joined + jnp.concatenate([bias_q, jnp.zeros_like(bias_q), bias_v])
    joined16 = joined.astype(jnp.bfloat16)
    query_heads, key_heads, value_heads = split_heads(joined16)
    in_length = jnp.arange(seq_rows) < length
    scores = masked_scores(query_heads, key_heads, in_length)
    row_top = jnp.max(scores, axis=-1, keepdims=True)
    exp_scores = jnp.exp(scores - row_top)
    row_total = jnp.sum(exp_scores, axis=-1, keepdims=True)
    attention16 = (exp_scores / row_total).astype(jnp.bfloat16)
    log_total = row_top + jnp.log(row_total)
    attended = jnp.einsum(
        "hqk,khd->qhd", attention16, value_heads, preferred_element_type=jnp.float32
    )
    attended16 = attended.reshape(seq_rows, D).astype(jnp.bfloat16)
    resid_one = (
        inputs16.astype(jnp.float32)
        + jnp.dot(attended16, w_out, preferred_element_type=jnp.float32)
        + bias_out
    )
    normed_one = norm_apply(resid_one, gain_one, shift_one)
    normed16 = normed_one.astype(jnp.bfloat16)
    hidden = jnp.dot(normed16, w_up, preferred_element_type=jnp.float32) + bias_up
    active16 = exact_gelu(hidden).astype(jnp.bfloat16)
    resid_two = (
        normed_one + jnp.dot(active16, w_down, preferred_element_type=jnp.float32) + bias_down
    )
    result = norm_apply(resid_two, gain_two, shift_two)
    result = jnp.where(in_length[:, None], result, 0.0).astype(jnp.bfloat16)
    kept = (
        joined16,
        log_total,
        attended16,
        resid_one,
        normed16,
        hidden,
        active16,
        resid_two,
        in_length,
    )
    return (result, kept)


def backward_pass(back16, inputs16, kept, matrices, vecs):
    w_qkv, w_out, w_up, w_down = matrices
    bias_q, bias_v, bias_out, bias_up, bias_down, gain_one, shift_one, gain_two, shift_two = vecs
    joined16, log_total, attended16, resid_one, normed16, hidden, active16, resid_two, in_length = (
        kept
    )
    seq_rows = inputs16.shape[0]
    back = jnp.where(in_length[:, None], back16.astype(jnp.float32), 0.0)
    unused_two, pull_two = jax.vjp(norm_apply, resid_two, gain_two, shift_two)
    d_resid_two, d_gain_two, d_shift_two = pull_two(back)
    d_down16 = d_resid_two.astype(jnp.bfloat16)
    d_active = jnp.einsum("to,io->ti", d_down16, w_down, preferred_element_type=jnp.float32)
    unused_gelu, pull_gelu = jax.vjp(exact_gelu, hidden)
    d_hidden = pull_gelu(d_active)[0]
    d_hidden16 = d_hidden.astype(jnp.bfloat16)
    d_normed = d_resid_two + jnp.einsum(
        "to,io->ti", d_hidden16, w_up, preferred_element_type=jnp.float32
    )
    unused_one, pull_one = jax.vjp(norm_apply, resid_one, gain_one, shift_one)
    d_resid_one, d_gain_one, d_shift_one = pull_one(d_normed)
    d_branch16 = d_resid_one.astype(jnp.bfloat16)
    d_attended = jnp.einsum("to,io->ti", d_branch16, w_out, preferred_element_type=jnp.float32)
    d_attended16 = d_attended.astype(jnp.bfloat16).reshape(seq_rows, HEADS, HEAD_DIM)
    query_heads, key_heads, value_heads = split_heads(joined16)
    scores = masked_scores(query_heads, key_heads, in_length)
    attention = jnp.exp(scores - log_total)
    attention16 = attention.astype(jnp.bfloat16)
    d_value = jnp.einsum(
        "hqk,qhd->khd", attention16, d_attended16, preferred_element_type=jnp.float32
    )
    d_attention = jnp.einsum(
        "qhd,khd->hqk", d_attended16, value_heads, preferred_element_type=jnp.float32
    )
    d_scores = attention * (d_attention - jnp.sum(attention * d_attention, axis=-1, keepdims=True))
    d_scores16 = d_scores.astype(jnp.bfloat16)
    d_query = jnp.einsum(
        "hqk,khd->qhd", d_scores16, key_heads, preferred_element_type=jnp.float32
    ) * HEAD_DIM ** (-0.5)
    d_key = jnp.einsum(
        "hqk,qhd->khd", d_scores16, query_heads, preferred_element_type=jnp.float32
    ) * HEAD_DIM ** (-0.5)
    d_query = d_query.reshape(seq_rows, D)
    d_key = d_key.reshape(seq_rows, D)
    d_value = d_value.reshape(seq_rows, D)
    d_joined16 = jnp.concatenate([d_query, d_key, d_value], axis=1).astype(jnp.bfloat16)
    d_inputs = d_resid_one + jnp.einsum(
        "to,io->ti", d_joined16, w_qkv, preferred_element_type=jnp.float32
    )
    vec_grad = jnp.concatenate(
        [
            jnp.sum(d_query, axis=0),
            jnp.sum(d_value, axis=0),
            jnp.sum(d_resid_one, axis=0),
            jnp.sum(d_hidden, axis=0),
            jnp.sum(d_resid_two, axis=0),
            d_gain_one,
            d_shift_one,
            d_gain_two,
            d_shift_two,
        ]
    )
    pairs = (d_joined16, attended16, d_branch16, normed16, d_hidden16, active16, d_down16)
    return (pairs, vec_grad, d_inputs.astype(jnp.bfloat16))


def rotate_in(left_side, matrix, right_side):
    inner = jnp.einsum(
        "pji,pjk->pik",
        left_side,
        matrix,
        precision=PRECISION_HIGH,
        preferred_element_type=jnp.float32,
    )
    return jnp.einsum(
        "pik,pkl->pil",
        inner,
        right_side,
        precision=PRECISION_HIGH,
        preferred_element_type=jnp.float32,
    )


def rotate_out(left_side, matrix, right_side):
    inner = jnp.einsum(
        "pij,pjk->pik",
        left_side,
        matrix,
        precision=PRECISION_HIGH,
        preferred_element_type=jnp.float32,
    )
    return jnp.einsum(
        "pik,plk->pil",
        inner,
        right_side,
        precision=PRECISION_HIGH,
        preferred_element_type=jnp.float32,
    )


def per_device_any(
    tokens,
    cotangent,
    lengths,
    deal,
    weights,
    vectors,
    owners,
    left_basis,
    right_basis,
    first_moment,
    second_moment,
    vec_first,
    vec_second,
):
    dp_count = lax.axis_size("dp")
    fsdp_count = lax.axis_size("fsdp")
    dp_place = lax.axis_index("dp")
    fsdp_place = lax.axis_index("fsdp")
    micro_count = tokens.shape[0]
    my_place = dp_place * fsdp_count + fsdp_place
    quarter = lax.dynamic_index_in_dim(
        deal.reshape(micro_count, dp_count, fsdp_count), fsdp_place, axis=2, keepdims=False
    )
    quarter = quarter - fsdp_place * dp_count
    ordered = jnp.take_along_axis(tokens, quarter[:, :, None, None], axis=1)
    dealt_rows = lax.all_to_all(ordered, "dp", split_axis=1, concat_axis=2, tiled=True)
    my_seq = lax.dynamic_index_in_dim(deal, my_place, axis=1, keepdims=False)
    my_length = jnp.take_along_axis(lengths, my_seq[:, None], axis=1)[:, 0]
    shard_low = (weights.astype(jnp.bfloat16), vectors.astype(jnp.bfloat16))
    whole_tiles, whole_vecs = (
        lax.all_gather(shard_low[0], ("dp", "fsdp"), axis=0, tiled=True),
        lax.all_gather(shard_low[1], ("dp", "fsdp"), axis=0, tiled=True),
    )
    mats_kept = unpack_mats(whole_tiles)
    vecs_kept = unpack_vecs(whole_vecs.astype(jnp.float32))
    all_pairs = []
    all_inputs = []
    vec_terms = []
    results = []
    input_grads = []
    for micro_index in range(micro_count):
        inputs16 = dealt_rows[micro_index, 0]
        matrices, vecs = (mats_kept, vecs_kept)
        result, kept = forward_pass(inputs16, my_length[micro_index], matrices, vecs)
        pairs, vec_term, d_inputs = backward_pass(
            cotangent[micro_index, 0], inputs16, kept, matrices, vecs
        )
        all_pairs.append(pairs)
        all_inputs.append(inputs16)
        vec_terms.append(vec_term)
        results.append(result)
        input_grads.append(d_inputs)

    def joined_rows(index):
        return jnp.concatenate([pairs[index] for pairs in all_pairs], axis=0)

    inputs_rows = jnp.concatenate(all_inputs, axis=0)
    tile_terms = jnp.concatenate(
        [
            tiled_grad(inputs_rows, joined_rows(0)),
            tiled_grad(joined_rows(1), joined_rows(2)),
            tiled_grad(joined_rows(3), joined_rows(4)),
            tiled_grad(joined_rows(5), joined_rows(6)),
        ],
        axis=0,
    )
    grad_vec = vec_terms[0]
    for vec_term in vec_terms[1:]:
        grad_vec = grad_vec + vec_term
    shard_tiles = weights.shape[0]
    tile_grads, vec_grads = (
        lax.psum_scatter(tile_terms, ("dp", "fsdp"), scatter_dimension=0, tiled=True),
        lax.psum_scatter(grad_vec, ("dp", "fsdp"), scatter_dimension=0, tiled=True),
    )
    group_grads, group_master = (
        lax.all_gather(tile_grads.astype(jnp.bfloat16), "fsdp", axis=0, tiled=True).astype(
            tile_grads.dtype
        ),
        lax.all_gather(weights.astype(jnp.bfloat16), "fsdp", axis=0, tiled=True).astype(
            weights.dtype
        ),
    )
    result_dealt = jnp.stack(results)[:, None]
    grads_dealt = jnp.stack(input_grads)[:, None]
    back_result, back_grads = (
        lax.all_to_all(result_dealt, "dp", split_axis=2, concat_axis=1, tiled=True),
        lax.all_to_all(grads_dealt, "dp", split_axis=2, concat_axis=1, tiled=True),
    )
    restore = jnp.argsort(quarter, axis=1)
    out_tokens = jnp.take_along_axis(back_result, restore[:, :, None, None], axis=1)
    in_grad = jnp.take_along_axis(back_grads, restore[:, :, None, None], axis=1)
    group_size = fsdp_count * shard_tiles
    pick_rows = owners - dp_place * group_size
    own_grads = jnp.take(group_grads, pick_rows, axis=0)
    own_master = jnp.take(group_master, pick_rows, axis=0)
    rates = tile_rate(owners)
    rotated = rotate_in(left_basis, own_grads, right_basis)
    new_first = BETA_ONE * first_moment + (1.0 - BETA_ONE) * rotated
    new_second = BETA_TWO * second_moment + (1.0 - BETA_TWO) * rotated * rotated
    first_hat = new_first / (1.0 - BETA_ONE**STEP)
    second_hat = new_second / (1.0 - BETA_TWO**STEP)
    step_rotated = first_hat / (jnp.sqrt(second_hat) + ADAM_EPS)
    update = rotate_out(left_basis, step_rotated, right_basis)
    new_tiles = own_master - rates[:, None, None] * (update + DECAY * own_master)
    vec_first_new = BETA_ONE * vec_first + (1.0 - BETA_ONE) * vec_grads
    vec_second_new = BETA_TWO * vec_second + (1.0 - BETA_TWO) * vec_grads * vec_grads
    vec_hat_one = vec_first_new / (1.0 - BETA_ONE**STEP)
    vec_hat_two = vec_second_new / (1.0 - BETA_TWO**STEP)
    new_vectors = vectors - VEC_RATE * vec_hat_one / (jnp.sqrt(vec_hat_two) + ADAM_EPS)
    return (
        out_tokens,
        in_grad,
        tile_grads,
        vec_grads,
        new_first,
        new_second,
        new_tiles,
        new_tiles.astype(jnp.bfloat16),
        vec_first_new,
        vec_second_new,
        new_vectors,
    )


CHUNK = 256
ROWS_AT_ONCE = 32
f32 = jnp.float32
bf = jnp.bfloat16


def mul(a, b):
    return jnp.dot(a, b, preferred_element_type=f32)


def mul_t(a, b):
    return lax.dot_general(a, b, (((1,), (1,)), ((), ())), preferred_element_type=f32)


def t_mul(a, b):
    return lax.dot_general(a, b, (((0,), (0,)), ((), ())), preferred_element_type=f32)


class Layer:
    def __init__(self, lens, vec, l3, r3, vsum, q3, p3, da3, xh, rs, acc, tmp, gp):
        self.__dict__.update(locals())
        self.rows = l3.shape[1]
        self.seqs = self.rows // TB

    def left(self, first):
        return jnp.concatenate([self.l3[first + j] for j in range(8)], axis=1)

    def each_rows(self, fn):
        def body(i, _):
            fn(pl.ds(pl.multiple_of(i * ROWS_AT_ONCE, ROWS_AT_ONCE), ROWS_AT_ONCE), i)
            return 0

        lax.fori_loop(0, self.rows // ROWS_AT_ONCE, body, 0)

    def counted(self, i):
        per = TB // ROWS_AT_ONCE
        at = (i % per) * ROWS_AT_ONCE + lax.broadcasted_iota(jnp.int32, (ROWS_AT_ONCE, 1), 0)
        return at < self.lens[i // per]

    def add_sum(self, n, value):
        folded = value.reshape(value.shape[0] // 8, 8, value.shape[1]).sum(axis=0)
        self.vsum[n] += folded

    def clear(self):
        self.vsum[...] = jnp.zeros_like(self.vsum)

    def project(self, w, t):
        x = self.left(0)
        for j in range(D // CHUNK):
            cols = slice(j * CHUNK, (j + 1) * CHUNK)
            out = mul(x, w[:, cols])
            if t != 1:
                out = out + self.vec[pl.ds(0 if t == 0 else 1, 1), cols]
            out = out.astype(bf)
            for i in range(CHUNK // TB):
                self.q3[t, j * (CHUNK // TB) + i] = out[:, i * TB : (i + 1) * TB]

    def two(self, block):
        lane = lax.broadcasted_iota(jnp.int32, block.shape, 1)
        zero = jnp.zeros_like(block)
        return jnp.concatenate(
            [jnp.where(lane < HEAD_DIM, block, zero), jnp.where(lane < HEAD_DIM, zero, block)], axis=0
        )

    def one(self, stacked):
        top, low = stacked[:TB], stacked[TB:]
        lane = lax.broadcasted_iota(jnp.int32, top.shape, 1)
        return jnp.where(lane < HEAD_DIM, top, low)

    def attend(self):
        def body(b, _):
            at = pl.ds(pl.multiple_of(b * TB, TB), TB)
            key = lax.broadcasted_iota(jnp.int32, (2 * TB, TB), 1)
            seen = key < self.lens[b]
            for h in range(HEADS // 2):
                s = mul_t(self.two(self.q3[0, h, at]), self.q3[1, h, at]) * HEAD_DIM**-0.5
                s = jnp.where(seen, s, -1e30)
                e = jnp.exp(s - jnp.max(s, axis=1, keepdims=True))
                p = e * (1.0 / jnp.sum(e, axis=1, keepdims=True))
                self.p3[b, h] = p
                a = self.one(mul(p.astype(bf), self.q3[2, h, at]))
                self.l3[8 + h, at] = a.astype(bf)
            return 0

        lax.fori_loop(0, self.seqs, body, 0)

    def norm_one(self, w):
        a = self.left(8)
        for j in range(D // CHUNK):
            cols = slice(j * CHUNK, (j + 1) * CHUNK)
            x = jnp.concatenate([self.l3[2 * j], self.l3[2 * j + 1]], axis=1).astype(f32)
            self.xh[:, cols] = x + mul(a, w[:, cols]) + self.vec[pl.ds(2, 1), cols]

        def rows(at, i):
            r = self.xh[at]
            center = r - jnp.mean(r, axis=1, keepdims=True)
            scale = lax.rsqrt(jnp.mean(center * center, axis=1, keepdims=True) + EPS_NORM)
            hat = center * scale
            self.xh[at] = hat
            self.rs[at] = jnp.broadcast_to(scale, (ROWS_AT_ONCE, TB))
            u = hat * self.vec[pl.ds(8, 1)] + self.vec[pl.ds(9, 1)]
            self.acc[at] = u
            u16 = u.astype(bf)
            for j in range(8):
                self.l3[16 + j, at] = u16[:, j * TB : (j + 1) * TB]

        self.each_rows(rows)

    def up(self, w, t):
        u = self.left(16)
        for j in range(D // CHUNK):
            cols = slice(j * CHUNK, (j + 1) * CHUNK)
            self.tmp[:, cols] = mul(u, w[:, cols]) + self.vec[pl.ds(3 + t, 1), cols]

        def rows(at, i):
            h = self.tmp[at]
            cdf = 0.5 + 0.5 * lax.erf(h * 0.7071067811865476)
            self.gp[t, at] = cdf + h * (0.3989422804014327 * jnp.exp(-0.5 * h * h))
            e = (h * cdf).astype(bf)
            for j in range(8):
                self.l3[24 + 8 * t + j, at] = e[:, j * TB : (j + 1) * TB]

        self.each_rows(rows)

    def down(self, w, t):
        e = self.left(24 + 8 * t)
        for j in range(D // CHUNK):
            cols = slice(j * CHUNK, (j + 1) * CHUNK)
            self.acc[:, cols] += mul(e, w[:, cols])

    def norm_two(self, cot, out):
        def rows(at, i):
            r = self.acc[at] + self.vec[pl.ds(7, 1)]
            center = r - jnp.mean(r, axis=1, keepdims=True)
            scale = lax.rsqrt(jnp.mean(center * center, axis=1, keepdims=True) + EPS_NORM)
            hat = center * scale
            live = self.counted(i)
            gain = self.vec[pl.ds(10, 1)]
            out[at] = jnp.where(live, hat * gain + self.vec[pl.ds(11, 1)], 0.0).astype(bf)
            dy = jnp.where(live, cot[at].astype(f32), 0.0)
            self.add_sum(10, dy * hat)
            self.add_sum(11, dy)
            g = dy * gain
            dr = scale * (
                g
                - jnp.mean(g, axis=1, keepdims=True)
                - hat * jnp.mean(g * hat, axis=1, keepdims=True)
            )
            self.add_sum(7, dr)
            self.acc[at] = dr
            self.r3[8, at] = dr.astype(bf)

        self.each_rows(rows)

    def down_back(self, w, t):
        d = self.r3[8]
        for j in range(D // CHUNK):
            cols = slice(j * CHUNK, (j + 1) * CHUNK)
            self.tmp[:, cols] = mul_t(d, w[cols, :])

        def rows(at, i):
            dh = self.tmp[at] * self.gp[t, at]
            self.add_sum(3 + t, dh)
            self.r3[4 + t, at] = dh.astype(bf)

        self.each_rows(rows)

    def up_back(self, w, t):
        d = self.r3[4 + t]
        for j in range(D // CHUNK):
            cols = slice(j * CHUNK, (j + 1) * CHUNK)
            self.acc[:, cols] += mul_t(d, w[cols, :])

    def norm_one_back(self):
        def rows(at, i):
            du, hat = self.acc[at], self.xh[at]
            self.add_sum(8, du * hat)
            self.add_sum(9, du)
            g = du * self.vec[pl.ds(8, 1)]
            dr = self.rs[at][:, :1] * (
                g
                - jnp.mean(g, axis=1, keepdims=True)
                - hat * jnp.mean(g * hat, axis=1, keepdims=True)
            )
            self.add_sum(2, dr)
            self.acc[at] = dr
            self.r3[3, at] = dr.astype(bf)

        self.each_rows(rows)

    def out_back(self, w):
        d = self.r3[3]
        for j in range(D // CHUNK):
            da = mul_t(d, w[j * CHUNK : (j + 1) * CHUNK, :]).astype(bf)
            for i in range(CHUNK // TB):
                self.da3[j * (CHUNK // TB) + i] = da[:, i * TB : (i + 1) * TB]

    def attend_back(self):
        def body(b, _):
            at = pl.ds(pl.multiple_of(b * TB, TB), TB)
            for h in range(HEADS // 2):
                cols = slice(h * TB, (h + 1) * TB)
                p = self.p3[b, h]
                da = self.two(self.da3[h, at])
                dv = t_mul(p.astype(bf), da)
                dp = mul_t(da, self.q3[2, h, at])
                pd = p * dp
                ds = (pd - p * jnp.sum(pd, axis=1, keepdims=True)).astype(bf)
                dq = self.one(mul(ds, self.q3[1, h, at])) * HEAD_DIM**-0.5
                dk = t_mul(ds, self.two(self.q3[0, h, at])) * HEAD_DIM**-0.5
                self.r3[0, at, cols] = dq.astype(bf)
                self.r3[1, at, cols] = dk.astype(bf)
                self.r3[2, at, cols] = dv.astype(bf)
                self.vsum[0, :, cols] += dq.reshape(TB // 8, 8, TB).sum(axis=0)
                self.vsum[1, :, cols] += dv.reshape(TB // 8, 8, TB).sum(axis=0)
            return 0

        lax.fori_loop(0, self.seqs, body, 0)

    def project_back(self, w, t, din=None):
        d = self.r3[t]
        for j in range(D // CHUNK):
            cols = slice(j * CHUNK, (j + 1) * CHUNK)
            value = self.acc[:, cols] + mul_t(d, w[cols, :])
            if din is None:
                self.acc[:, cols] = value
            else:
                din[:, cols] = value.astype(bf)


def layer_kernel(lens, x, cot, vec, wm, l3, r3, vsum, out, din,
                 w, q3, p3, da3, xh, rs, acc, tmp, gp, sem):
    order = [0, 1, 2, 3, 4, 5, 6, 7, 8, 9, 10, 11]
    for n in order:
        pltpu.make_async_copy(wm.at[n], w.at[n], sem.at[n]).start()

    def got(n):
        pltpu.make_async_copy(wm.at[n], w.at[n], sem.at[n]).wait()
        return w.at[n]

    f = Layer(lens, vec, l3, r3, vsum, q3, p3, da3, xh, rs, acc, tmp, gp)
    f.clear()
    for j in range(8):
        l3[j] = x[:, j * TB : (j + 1) * TB]
    for t in range(3):
        f.project(got(t), t)
    f.attend()
    f.norm_one(got(3))
    for t in range(4):
        f.up(got(4 + t), t)
    for t in range(4):
        f.down(got(8 + t), t)
    f.norm_two(cot, out)
    for t in range(4):
        f.down_back(w.at[8 + t], t)
        f.up_back(w.at[4 + t], t)
    f.norm_one_back()
    f.out_back(w.at[3])
    f.attend_back()
    for t in range(3):
        f.project_back(w.at[t], t, din if t == 2 else None)


def layer(lens, x, cot, vec, w12):
    rows = x.shape[0]
    dma = pltpu.SemaphoreType.DMA
    vmem = pl.BlockSpec(memory_space=pltpu.VMEM)
    return pl.pallas_call(
        layer_kernel,
        out_shape=(
            jax.ShapeDtypeStruct((56, rows, TB), bf),
            jax.ShapeDtypeStruct((9, rows, D), bf),
            jax.ShapeDtypeStruct((12, 8, D), f32),
            jax.ShapeDtypeStruct((rows, D), bf),
            jax.ShapeDtypeStruct((rows, D), bf),
        ),
        in_specs=[pl.BlockSpec(memory_space=pltpu.SMEM), vmem, vmem, vmem, pl.BlockSpec(memory_space=pl.ANY)],
        out_specs=(vmem,) * 5,
        scratch_shapes=[
            pltpu.VMEM((12, D, D), bf),
            pltpu.VMEM((3, 8, rows, TB), bf),
            pltpu.VMEM((rows // TB, 8, 2 * TB, TB), f32),
            pltpu.VMEM((8, rows, TB), bf),
            pltpu.VMEM((rows, D), f32),
            pltpu.VMEM((rows, TB), f32),
            pltpu.VMEM((rows, D), f32),
            pltpu.VMEM((rows, D), f32),
            pltpu.VMEM((4, rows, D), f32),
            dma((12,)),
        ],
        compiler_params=pltpu.CompilerParams(vmem_limit_bytes=62 * 2**20),
        name="layer",
    )(lens, x, cot, vec, w12)


GROUP = 6


def halves(a):
    high = a.astype(bf)
    return high, (a - high.astype(f32)).astype(bf)


def wide(b):
    return jnp.concatenate(
        [jnp.concatenate(b, 1), jnp.concatenate([b[0], jnp.zeros_like(b[0])], 1)], 0
    )


def fine(a, b_wide):
    out = mul(jnp.concatenate(a, 1), b_wide)
    return out[:, :TB] + out[:, TB:]


def fine_t(a, b):
    wide_t = jnp.concatenate(
        [jnp.concatenate([b[0], b[0]], 1), jnp.concatenate([b[1], jnp.zeros_like(b[1])], 1)], 0
    )
    out = mul_t(jnp.concatenate(a, 1), wide_t)
    return out[:, :TB] + out[:, TB:]


def moments(first, second, grad):
    first = BETA_ONE * first + (1.0 - BETA_ONE) * grad
    second = BETA_TWO * second + (1.0 - BETA_TWO) * grad * grad
    hat = (first * (1.0 / (1.0 - BETA_ONE**STEP))) / (
        jnp.sqrt(second * (1.0 / (1.0 - BETA_TWO**STEP))) + ADAM_EPS
    )
    return first, second, hat


def adam_kernel(place, lane, pick, rate, *refs):
    masters = refs[:GROUP]
    grads, left, right, first, second, vec, vec_first, vec_second, vec_grad = refs[GROUP : GROUP + 9]
    new_first, new_second, new_tiles, new_low, vec_first_new, vec_second_new, new_vec = refs[GROUP + 9 :]
    step = pl.program_id(0)
    span = range(GROUP)
    ls = [halves(left[g]) for g in span]
    rs = [halves(right[g]) for g in span]
    grad = [grads[pick[step * GROUP + g]] for g in span]
    inner = [t_mul(jnp.concatenate(ls[g], 0), jnp.concatenate([grad[g]] * 2, 0)) for g in span]
    rwide = [wide(rs[g]) for g in span]
    rotated = [fine(halves(inner[g]), rwide[g]) for g in span]
    hats = []
    for g in span:
        first_now, second_now, hat = moments(first[g], second[g], rotated[g])
        new_first[g] = first_now
        new_second[g] = second_now
        hats.append(hat)
    outer = [fine(ls[g], wide(halves(hats[g]))) for g in span]
    update = [fine_t(halves(outer[g]), rs[g]) for g in span]
    for g in span:
        master = masters[g][0].astype(f32)
        fresh = master - rate[step * GROUP + g] * (update[g] + DECAY * master)
        new_tiles[g] = fresh
        new_low[g] = fresh.astype(bf)

    @pl.when(step == 0)
    def _():
        a, b, hat = moments(vec_first[...], vec_second[...], vec_grad[...])
        vec_first_new[...] = a
        vec_second_new[...] = b
        new_vec[...] = vec[...] - VEC_RATE * hat


def adam(place, lane, pick, rate, wm, grads, left, right, first, second, vec, vec_first, vec_second, vec_grad):
    count = left.shape[0]
    one = [
        pl.BlockSpec((1, TB, TB), functools.partial(lambda g, i, p, l, *_: (p[i * GROUP + g], 0, l[i * GROUP + g]), g))
        for g in range(GROUP)
    ]
    stack = pl.BlockSpec((GROUP, TB, TB), lambda i, *_: (i, 0, 0))
    whole = pl.BlockSpec(grads.shape, lambda i, *_: (0, 0, 0))
    small = pl.BlockSpec(vec.shape, lambda i, *_: (0, 0))
    tiles = jax.ShapeDtypeStruct(left.shape, f32)
    return pl.pallas_call(
        adam_kernel,
        out_shape=(tiles, tiles, tiles, jax.ShapeDtypeStruct(left.shape, bf)) + (jax.ShapeDtypeStruct(vec.shape, f32),) * 3,
        grid_spec=pltpu.PrefetchScalarGridSpec(
            num_scalar_prefetch=4,
            grid=(count // GROUP,),
            in_specs=one + [whole] + [stack] * 4 + [small] * 4,
            out_specs=[stack] * 4 + [small] * 3,
        ),
        compiler_params=pltpu.CompilerParams(vmem_limit_bytes=60 * 2**20),
        name="adam",
    )(place, lane, pick, rate, *([wm] * GROUP), grads, left, right, first, second, vec, vec_first, vec_second, vec_grad)


MESH = pl.DeviceIdType.MESH
ZN = 4
OCT = 96
RING = 8


class Place:
    def __init__(self):
        self.dp = lax.axis_index("dp")
        self.fs = lax.axis_index("fsdp")
        self.z, self.y = self.dp // 2, self.dp % 2
        self.x, self.c = self.fs // 2, self.fs % 2
        self.to_x = (self.dp, (self.fs + 2) % 4)
        self.to_y = (self.z * 2 + 1 - self.y, self.fs)
        self.to_core = (self.dp, self.x * 2 + 1 - self.c)
        self.to_up = (self.dp + 2, self.fs)
        self.to_down = (self.dp - 2, self.fs)
        near = self.z + 1 - 2 * (self.z % 2)
        far = (self.z + 2) % ZN
        self.to_near = (near * 2 + self.y, self.fs)
        self.to_far = (far * 2 + self.y, self.fs)

    def greet(self):
        bar = pltpu.get_barrier_semaphore()
        for dev in (self.to_x, self.to_y, self.to_core, self.to_far):
            pl.semaphore_signal(bar, inc=1, device_id=dev, device_id_type=MESH)

        @pl.when(self.z < ZN - 1)
        def _():
            pl.semaphore_signal(bar, inc=1, device_id=self.to_up, device_id_type=MESH)

        @pl.when(self.z > 0)
        def _():
            pl.semaphore_signal(bar, inc=1, device_id=self.to_down, device_id_type=MESH)

        pl.semaphore_wait(
            bar, 4 + jnp.where(self.z > 0, 1, 0) + jnp.where(self.z < ZN - 1, 1, 0)
        )

    def octet(self, dx, dy, zp, k, c=None):
        yy = self.y if dy == 0 else 1 - self.y
        xx = self.x if dx == 0 else 1 - self.x
        return ((zp * 2 + yy) * 4 + xx * 2 + (self.c if c is None else c)) * 3 + k

    def plane(self, s, middle):
        low = self.z < 2
        zz = jnp.where(low, self.z, 3 - self.z)
        f = jnp.where(zz == 0, s, middle[s])
        return jnp.where(low, f, 3 - f)


def octet_place(o):
    return jnp.where(
        o < 24,
        (o % 3) * 8 + o // 3,
        jnp.where((o >= 32) & (o < 64), 32 + ((o - 32) % 4) * 8 + (o - 32) // 4, o),
    )


def left_block(o):
    return jnp.where(
        o < 24, o // 3, jnp.where(o < 32, o - 16, jnp.where(o < 64, 16 + (o - 32) // 4, o - 40))
    )


def right_block(o):
    return jnp.where(o < 24, o % 3, jnp.where(o < 32, 3, jnp.where(o < 64, 4 + (o - 32) % 4, 8)))


def wait_for(ref, sem):
    pltpu.make_async_copy(ref, ref, sem).wait()


def remote(src, dst, send_sem, recv_sem, dev):
    return pltpu.make_async_remote_copy(
        src_ref=src,
        dst_ref=dst,
        send_sem=send_sem,
        recv_sem=recv_sem,
        device_id=dev,
        device_id_type=MESH,
    )


def route_x(s, zp, k):
    if s == 0 and k < 2:
        return k == 0
    return (zp % 2) == 0


def on(flag, fn):
    if flag is True:
        fn()
    elif flag is not False:
        pl.when(flag)(fn)


def unless(flag, fn):
    on((not flag) if isinstance(flag, bool) else jnp.logical_not(flag), fn)


GATHER_ORDER = [
    (1, 0), (1, 1), (2, 0), (1, 2), (2, 1), (3, 0), (1, 3), (2, 2), (3, 1), (2, 3), (3, 2), (3, 3),
]
GATHER_MIDDLE = [1, 2, 0, 3]


def gather_kernel(
    shard, vec, out, vout, rs, s_x, s_y, s_up, s_down, s_core, s_local, s_vec, r_vec
):
    p = Place()
    z = p.z
    p.greet()

    def ref_of(o):
        return out.at[octet_place(o)]

    def send(o, dev, sem, src=None):
        remote(ref_of(o) if src is None else src, ref_of(o), sem, rs.at[o], dev).start()

    def wait(o):
        wait_for(ref_of(o), rs.at[o])

    def along_z(s, zp, o, src=None):
        def up():
            send(o, p.to_up, s_up, src)

        def down():
            send(o, p.to_down, s_down, src)

        if s == 0:
            pl.when(z < ZN - 1)(up)
            pl.when(z > 0)(down)
        else:
            pl.when((zp < z) & (z < ZN - 1))(up)
            pl.when((zp > z) & (z > 0))(down)

    for k in range(3):
        pltpu.make_async_copy(shard.at[k], ref_of(p.octet(0, 0, z, k)), s_local.at[k]).start()
    me = p.dp * 4 + p.fs
    vout[me] = vec[...]
    vec_dev = [p.to_core, p.to_x, p.to_y, p.to_near, p.to_far]

    def vec_step(n):
        size = 2**n
        if n > 0:
            half = size // 2
            theirs = (me // half) * half
            theirs = theirs + half * (1 - 2 * (theirs // half % 2))
            wait_for(vout.at[pl.ds(theirs, half)], r_vec.at[n - 1])
        if n < 5:
            mine = vout.at[pl.ds((me // size) * size, size)]
            remote(mine, mine, s_vec.at[n], r_vec.at[n], vec_dev[n]).start()

    vec_step(0)
    for step, (phase, s) in enumerate(GATHER_ORDER):
        zp = p.plane(s, GATHER_MIDDLE)
        for k in range(3):
            if phase == 1:
                o = p.octet(0, 0, zp, k)
                src = shard.at[k] if s == 0 else None
                if s > 0:
                    wait(o)
                along_z(s, zp, o, src)
                send(o, p.to_x, s_x, src)
                send(o, p.to_y, s_y, src)
                send(o, p.to_core, s_core, src)
            if phase == 2:
                o = p.octet(0, 1, zp, k)
                wait(o)
                if s == 0 or k == 2:
                    on(route_x(s, zp, k), functools.partial(send, o, p.to_x, s_x))
                send(o, p.to_core, s_core)
                o = p.octet(1, 0, zp, k)
                wait(o)
                if s == 0 or k == 2:
                    unless(route_x(s, zp, k), functools.partial(send, o, p.to_y, s_y))
                send(o, p.to_core, s_core)
            if phase == 3:
                o = p.octet(1, 1, zp, k)
                wait(o)
                if k < 2:
                    along_z(s, zp, o)
                send(o, p.to_core, s_core)
        if 0 < step < 6:
            vec_step(step)

    for zp in range(ZN):
        for dx in range(2):
            for dy in range(2):
                for k in range(3):
                    wait(p.octet(dx, dy, zp, k, 1 - p.c))
    for k in range(3):
        wait_for(shard.at[k], s_local.at[k])
    for n in range(5):
        wait_for(vout.at[pl.ds(0, 2**n)], s_vec.at[n])

    def drain(sem, n):
        wait_for(out.at[pl.ds(0, n)], sem)

    drain(s_core, 48)
    drain(s_x, 15)
    drain(s_y, 15)
    for zz in range(ZN - 1):
        pl.when(z == zz)(functools.partial(drain, s_up, 5 * (zz + 1)))
        pl.when(z == ZN - 1 - zz)(functools.partial(drain, s_down, 5 * (zz + 1)))


def gather_weights(shard, vec):
    dma = pltpu.SemaphoreType.DMA
    return pl.pallas_call(
        gather_kernel,
        out_shape=(
            jax.ShapeDtypeStruct((OCT, TB, D), jnp.bfloat16),
            jax.ShapeDtypeStruct((32, 8, TB), jnp.float32),
        ),
        in_specs=[pl.BlockSpec(memory_space=pl.ANY), pl.BlockSpec(memory_space=pltpu.VMEM)],
        out_specs=(pl.BlockSpec(memory_space=pl.ANY), pl.BlockSpec(memory_space=pltpu.VMEM)),
        scratch_shapes=[dma((OCT,)), dma, dma, dma, dma, dma, dma((3,)), dma((5,)), dma((5,))],
        compiler_params=pltpu.CompilerParams(
            collective_id=0, has_side_effects=True, vmem_limit_bytes=16 * 2**20
        ),
        name="gather_weights",
    )(shard, vec)


REDUCE_ORDER = [
    "A3", "V0", "A2", "B3", "V1", "B2", "C3", "V2", "A1", "B1", "C2", "V3", "D3", "A0", "V4", "B0",
    "C1", "D2", "C0", "D1", "D0",
]
REDUCE_MIDDLE = [1, 0, 2, 3]


def reduce_kernel(
    l3, r3, vecg, tiles, grp, vout,
    land_c, land_x, land_y, land_z, ring, vland, acc,
    r_c, r_x, r_y, r_z, r_e, r_v, s_ring, s_x, s_y, s_up, s_down, s_e, s_e2, s_v,
):
    p = Place()
    z, c, fs = p.z, p.c, p.fs
    p.greet()

    def rel(dx, dy, zp, k):
        return ((dy * 2 + dx) * ZN + zp) * 3 + k

    def slot(j, zp, k):
        return (j * ZN + zp) * 3 + k

    def part(o):
        return t_mul(l3[left_block(o)], r3[right_block(o)])

    def add(land, sem, n):
        wait_for(land.at[n], sem.at[n])
        acc[...] += land[n].astype(jnp.float32)

    def begin(q, o):
        wait_for(land_c.at[q], r_c.at[q])
        acc[...] = part(o) + land_c[q].astype(jnp.float32)

    def keep(q):
        land_c[q] = acc[...].astype(jnp.bfloat16)

    def send_x(q, n):
        remote(land_c.at[q], land_x.at[n], s_x, r_x.at[n], p.to_x).start()

    def send_y(q, n):
        remote(land_c.at[q], land_y.at[n], s_y, r_y.at[n], p.to_y).start()

    def send_z(q, j, zp, k):
        n = slot(j, zp, k)

        @pl.when(zp > z)
        def _():
            remote(land_c.at[q], land_z.at[n], s_up, r_z.at[n], p.to_up).start()

        @pl.when(zp < z)
        def _():
            t = jnp.where(zp == z - 1, 24 + j * 3 + k, n)
            remote(land_c.at[q], land_z.at[t], s_down, r_z.at[t], p.to_down).start()

    def add_z(s, j, zp, k):
        n = slot(j, zp, k)
        if s == 0:
            pl.when(z > 0)(functools.partial(add, land_z, r_z, n))
            pl.when(z < ZN - 1)(functools.partial(add, land_z, r_z, 24 + j * 3 + k))
        else:
            pl.when(((zp > z) & (z > 0)) | ((zp < z) & (z < ZN - 1)))(
                functools.partial(add, land_z, r_z, n)
            )

    def to_partner(s, zp, first):
        def body(i, _):
            yy, xx = (i // 3) % 2, i // 6
            o = ((zp * 2 + yy) * 4 + xx * 2 + (1 - c)) * 3 + i % 3
            n = (first + i) % RING
            value = part(o).astype(jnp.bfloat16)

            def free():
                wait_for(ring.at[0], s_ring.at[n])

            if first == 0:
                pl.when(i >= RING)(free)
            else:
                free()
            ring[n] = value
            q = ((jnp.where(yy == p.y, 0, 1) * 2 + jnp.where(xx == p.x, 0, 1)) * ZN + zp) * 3 + i % 3
            remote(ring.at[n], land_c.at[q], s_ring.at[n], r_c.at[q], p.to_core).start()
            return 0

        lax.fori_loop(0, 12, body, 0)

    def corner(s, zp):
        for k in range(3):
            q = rel(1, 1, zp, k)
            begin(q, p.octet(1, 1, zp, k))
            if k < 2:
                add_z(s, 1, zp, k)
            keep(q)
            if s == 0 or k == 2:
                on(route_x(s, zp, k), functools.partial(send_x, q, slot(1, zp, k)))
                unless(route_x(s, zp, k), functools.partial(send_y, q, slot(1, zp, k)))
            else:
                send_z(q, 1, zp, k)

    def sides(s, zp):
        for k in range(3):
            q = rel(0, 1, zp, k)
            begin(q, p.octet(0, 1, zp, k))
            if s == 0 or k == 2:
                on(route_x(s, zp, k), functools.partial(add, land_x, r_x, slot(1, zp, k)))
            keep(q)
            send_y(q, slot(0, zp, k))
            q = rel(1, 0, zp, k)
            begin(q, p.octet(1, 0, zp, k))
            if s == 0 or k == 2:
                unless(route_x(s, zp, k), functools.partial(add, land_y, r_y, slot(1, zp, k)))
            keep(q)
            send_x(q, slot(0, zp, k))

    def column(s, zp):
        for k in range(3):
            q = rel(0, 0, zp, k)
            begin(q, p.octet(0, 0, zp, k))
            add(land_x, r_x, slot(0, zp, k))
            add(land_y, r_y, slot(0, zp, k))
            add_z(s, 0, zp, k)
            if s > 0:
                keep(q)
                send_z(q, 0, zp, k)
            else:
                for j in range(8):
                    piece = acc[:, j * TB : (j + 1) * TB]
                    tiles[8 * k + j] = piece
                    grp[fs * 24 + 8 * k + j] = piece.astype(jnp.bfloat16)
                mine = grp.at[pl.ds(fs * 24 + 8 * k, 8)]
                remote(mine, mine, s_e, r_e.at[fs * 3 + k], p.to_x).start()
                remote(mine, mine, s_e2, r_e.at[fs * 3 + k], p.to_core).start()

    vec_dev = [p.to_core, p.to_x, p.to_y, p.to_near, p.to_far]

    def vec_step(n):
        if n == 0:
            vout[...] = vecg[...]
        else:
            wait_for(vland.at[n - 1], r_v.at[n - 1])
            vout[...] = vout[...] + vland[n - 1]
        if n < 5:
            vland[5 + n] = vout[...]
            remote(vland.at[5 + n], vland.at[n], s_v.at[n], r_v.at[n], vec_dev[n]).start()

    first = 0
    for name in REDUCE_ORDER:
        s = int(name[1])
        if name[0] == "V":
            vec_step(s)
            continue
        zp = p.plane(s, REDUCE_MIDDLE)
        if name[0] == "A":
            to_partner(s, zp, first)
            first += 12
        elif name[0] == "B":
            corner(s, zp)
        elif name[0] == "C":
            sides(s, zp)
        else:
            column(s, zp)
    vec_step(5)

    fx = (fs + 2) % 4
    for k in range(3):
        block = grp.at[pl.ds(fx * 24 + 8 * k, 8)]
        wait_for(block, r_e.at[fx * 3 + k])
        remote(block, block, s_e2, r_e.at[fx * 3 + k], p.to_core).start()
    for f in (p.x * 2 + 1 - c, (1 - p.x) * 2 + 1 - c):
        for k in range(3):
            wait_for(grp.at[pl.ds(f * 24 + 8 * k, 8)], r_e.at[f * 3 + k])

    for n in range(RING):
        wait_for(ring.at[0], s_ring.at[n])
    for n in range(5):
        wait_for(vland.at[5 + n], s_v.at[n])

    def drain(sem, n):
        wait_for(land_c.at[pl.ds(0, n)], sem)

    drain(s_x, 15)
    drain(s_y, 15)
    wait_for(grp.at[pl.ds(0, 24)], s_e)
    wait_for(grp.at[pl.ds(0, 48)], s_e2)
    for zz in range(ZN - 1):
        pl.when(z == zz)(functools.partial(drain, s_up, 5 * (ZN - 1 - zz)))
        pl.when(z == ZN - 1 - zz)(functools.partial(drain, s_down, 5 * (ZN - 1 - zz)))


def reduce_grads(l3, r3, vecg):
    bf = jnp.bfloat16
    dma = pltpu.SemaphoreType.DMA
    vmem = pl.BlockSpec(memory_space=pltpu.VMEM)
    return pl.pallas_call(
        reduce_kernel,
        out_shape=(
            jax.ShapeDtypeStruct((24, TB, TB), jnp.float32),
            jax.ShapeDtypeStruct((96, TB, TB), bf),
            jax.ShapeDtypeStruct((96, TB), jnp.float32),
        ),
        in_specs=[vmem] * 3,
        out_specs=(vmem,) * 3,
        scratch_shapes=[
            pltpu.VMEM((48, TB, D), bf),
            pltpu.VMEM((24, TB, D), bf),
            pltpu.VMEM((24, TB, D), bf),
            pltpu.VMEM((30, TB, D), bf),
            pltpu.VMEM((RING, TB, D), bf),
            pltpu.VMEM((10, 96, TB), jnp.float32),
            pltpu.VMEM((TB, D), jnp.float32),
            dma((48,)), dma((24,)), dma((24,)), dma((30,)), dma((12,)), dma((5,)),
            dma((RING,)), dma, dma, dma, dma, dma, dma, dma((5,)),
        ],
        compiler_params=pltpu.CompilerParams(
            collective_id=1, has_side_effects=True, vmem_limit_bytes=62 * 2**20
        ),
        name="reduce_grads",
    )(l3, r3, vecg)


def per_device(
    tokens,
    cotangent,
    lengths,
    deal,
    weights,
    vectors,
    owners,
    left_basis,
    right_basis,
    first_moment,
    second_moment,
    vec_first,
    vec_second,
):
    dp_count = lax.axis_size("dp")
    fsdp_count = lax.axis_size("fsdp")
    dp_place = lax.axis_index("dp")
    fsdp_place = lax.axis_index("fsdp")
    micro_count = tokens.shape[0]
    my_place = dp_place * fsdp_count + fsdp_place
    quarter = lax.dynamic_index_in_dim(
        deal.reshape(micro_count, dp_count, fsdp_count), fsdp_place, axis=2, keepdims=False
    )
    quarter = quarter - fsdp_place * dp_count
    ordered = jnp.take_along_axis(tokens, quarter[:, :, None, None], axis=1)
    dealt_rows = lax.all_to_all(ordered, "dp", split_axis=1, concat_axis=2, tiled=True)
    my_seq = lax.dynamic_index_in_dim(deal, my_place, axis=1, keepdims=False)
    my_length = jnp.take_along_axis(lengths, my_seq[:, None], axis=1)[:, 0]
    shard = weights.astype(jnp.bfloat16).reshape(3, 8, TB, TB).transpose(0, 2, 1, 3)
    shard = shard.reshape(3, TB, D)
    vec_shard = vectors.astype(jnp.bfloat16).astype(jnp.float32).reshape(3, TB)
    wm, all_vecs = gather_weights(shard, jnp.pad(vec_shard, ((0, 5), (0, 0))))
    vecs = all_vecs[:, :3].reshape(12, D)
    rows = micro_count * tokens.shape[2] * dp_count
    l3, r3, vsum, result, d_inputs = layer(
        my_length, dealt_rows.reshape(rows, D), cotangent.reshape(rows, D), vecs, wm.reshape(12, D, D)
    )
    tile_grads, group_grads, vec_total = reduce_grads(l3, r3, vsum.sum(axis=1).reshape(96, TB))
    vec_grads = lax.dynamic_slice_in_dim(vec_total, my_place * 3, 3, axis=0)
    shape = (micro_count, 1, rows // micro_count, D)
    back_result, back_grads = (
        lax.all_to_all(result.reshape(shape), "dp", split_axis=2, concat_axis=1, tiled=True),
        lax.all_to_all(d_inputs.reshape(shape), "dp", split_axis=2, concat_axis=1, tiled=True),
    )
    restore = jnp.argsort(quarter, axis=1)
    out_tokens = jnp.take_along_axis(back_result, restore[:, :, None, None], axis=1)
    in_grad = jnp.take_along_axis(back_grads, restore[:, :, None, None], axis=1)
    new_first, new_second, new_tiles, new_low, vec_first_new, vec_second_new, new_vectors = adam(
        octet_place(owners // 8),
        owners % 8,
        owners - dp_place * (owners.shape[0] * fsdp_count),
        tile_rate(owners),
        wm,
        group_grads,
        left_basis,
        right_basis,
        first_moment,
        second_moment,
        vectors.reshape(3, TB),
        vec_first.reshape(3, TB),
        vec_second.reshape(3, TB),
        vec_grads,
    )
    return (
        out_tokens,
        in_grad,
        tile_grads,
        vec_grads.reshape(-1),
        new_first,
        new_second,
        new_tiles,
        new_low,
        vec_first_new.reshape(-1),
        vec_second_new.reshape(-1),
        new_vectors.reshape(-1),
    )


def solution(mesh):
    body = per_device if (mesh.shape["dp"], mesh.shape["fsdp"]) == (2 * ZN, 4) else per_device_any
    placed = (
        P(None, "fsdp", "dp", None),
        P(None, ("dp", "fsdp"), None, None),
        P(),
        P(),
        P(("dp", "fsdp"), None, None),
        P(("dp", "fsdp")),
        P(("dp", "fsdp")),
        P(("dp", "fsdp"), None, None),
        P(("dp", "fsdp"), None, None),
        P(("dp", "fsdp"), None, None),
        P(("dp", "fsdp"), None, None),
        P(("dp", "fsdp")),
        P(("dp", "fsdp")),
    )
    return jax.shard_map(
        body,
        mesh=mesh,
        in_specs=placed,
        out_specs=(
            P(None, "fsdp", "dp", None),
            P(None, "fsdp", "dp", None),
            P(("dp", "fsdp"), None, None),
            P(("dp", "fsdp")),
            P(("dp", "fsdp"), None, None),
            P(("dp", "fsdp"), None, None),
            P(("dp", "fsdp"), None, None),
            P(("dp", "fsdp"), None, None),
            P(("dp", "fsdp")),
            P(("dp", "fsdp")),
            P(("dp", "fsdp")),
        ),
        check_vma=False,
    )
```

```python
import functools

import jax
import jax.numpy as jnp
from jax import lax
from jax.experimental import pallas as pl
from jax.experimental.pallas import tpu as pltpu
from jax.sharding import PartitionSpec as P

D = 1024
HEADS = 16
HEAD_DIM = 64
FF = 4096
STEP = 10
TB = 128


EPS_NORM = 1e-05
BETA_ONE = 0.5
BETA_TWO = 0.6
ADAM_EPS = 1e-08
DECAY = 0.01
VEC_RATE = 0.2
PRECISION_HIGH = lax.Precision.HIGHEST


def cut_tiles(stacked, row_count, col_count, start_at):
    tile_count = row_count // TB * (col_count // TB)
    blocked = lax.slice_in_dim(stacked, start_at, start_at + tile_count, axis=0)
    blocked = blocked.reshape(row_count // TB, col_count // TB, TB, TB)
    return (blocked.transpose(0, 2, 1, 3).reshape(row_count, col_count), start_at + tile_count)


def unpack_mats(stacked):
    w_qkv, offset = cut_tiles(stacked, D, 3 * D, 0)
    w_out, offset = cut_tiles(stacked, D, D, offset)
    w_up, offset = cut_tiles(stacked, D, FF, offset)
    w_down, offset = cut_tiles(stacked, FF, D, offset)
    return (w_qkv, w_out, w_up, w_down)


def tiled_grad(left_rows, right_rows):
    row_total = left_rows.shape[0]
    left_split = left_rows.reshape(row_total, left_rows.shape[1] // TB, TB)
    right_split = right_rows.reshape(row_total, right_rows.shape[1] // TB, TB)
    blocked = jnp.einsum(
        "tai,tbj->abij", left_split, right_split, preferred_element_type=jnp.float32
    )
    return blocked.reshape(-1, TB, TB)


def unpack_vecs(vector):
    widths = [D, D, D, FF, D, D, D, D, D]
    pieces = []
    offset = 0
    for width_now in widths:
        pieces.append(vector[offset : offset + width_now])
        offset += width_now
    return tuple(pieces)


def tile_rate(tile_ids):
    qkv_end = 3 * D * D // (TB * TB)
    out_end = 4 * D * D // (TB * TB)
    up_end = (4 * D * D + D * FF) // (TB * TB)
    return jnp.where(
        tile_ids < qkv_end,
        D ** (-0.5),
        jnp.where(
            tile_ids < out_end,
            (HEAD_DIM / D) ** 0.5,
            jnp.where(tile_ids < up_end, D ** (-0.5), 1.5 * FF ** (-0.5)),
        ),
    ).astype(jnp.float32)


def norm_apply(values, gain_vec, shift_vec):
    center = values - jnp.mean(values, axis=-1, keepdims=True)
    spread = jnp.mean(center * center, axis=-1, keepdims=True)
    return center * lax.rsqrt(spread + EPS_NORM) * gain_vec + shift_vec


def exact_gelu(values):
    return jax.nn.gelu(values, approximate=False)


def split_heads(joined16):
    seq_rows = joined16.shape[0]
    query_heads = joined16[:, :D].reshape(seq_rows, HEADS, HEAD_DIM)
    key_heads = joined16[:, D : 2 * D].reshape(seq_rows, HEADS, HEAD_DIM)
    value_heads = joined16[:, 2 * D :].reshape(seq_rows, HEADS, HEAD_DIM)
    return (query_heads, key_heads, value_heads)


def masked_scores(query_heads, key_heads, in_length):
    scores = jnp.einsum(
        "qhd,khd->hqk", query_heads, key_heads, preferred_element_type=jnp.float32
    ) * HEAD_DIM ** (-0.5)
    return jnp.where(in_length[None, None, :], scores, -1e30)


def forward_pass(inputs16, length, matrices, vecs):
    w_qkv, w_out, w_up, w_down = matrices
    bias_q, bias_v, bias_out, bias_up, bias_down, gain_one, shift_one, gain_two, shift_two = vecs
    seq_rows = inputs16.shape[0]
    joined = jnp.dot(inputs16, w_qkv, preferred_element_type=jnp.float32)
    joined = joined + jnp.concatenate([bias_q, jnp.zeros_like(bias_q), bias_v])
    joined16 = joined.astype(jnp.bfloat16)
    query_heads, key_heads, value_heads = split_heads(joined16)
    in_length = jnp.arange(seq_rows) < length
    scores = masked_scores(query_heads, key_heads, in_length)
    row_top = jnp.max(scores, axis=-1, keepdims=True)
    exp_scores = jnp.exp(scores - row_top)
    row_total = jnp.sum(exp_scores, axis=-1, keepdims=True)
    attention16 = (exp_scores / row_total).astype(jnp.bfloat16)
    log_total = row_top + jnp.log(row_total)
    attended = jnp.einsum(
        "hqk,khd->qhd", attention16, value_heads, preferred_element_type=jnp.float32
    )
    attended16 = attended.reshape(seq_rows, D).astype(jnp.bfloat16)
    resid_one = (
        inputs16.astype(jnp.float32)
        + jnp.dot(attended16, w_out, preferred_element_type=jnp.float32)
        + bias_out
    )
    normed_one = norm_apply(resid_one, gain_one, shift_one)
    normed16 = normed_one.astype(jnp.bfloat16)
    hidden = jnp.dot(normed16, w_up, preferred_element_type=jnp.float32) + bias_up
    active16 = exact_gelu(hidden).astype(jnp.bfloat16)
    resid_two = (
        normed_one + jnp.dot(active16, w_down, preferred_element_type=jnp.float32) + bias_down
    )
    result = norm_apply(resid_two, gain_two, shift_two)
    result = jnp.where(in_length[:, None], result, 0.0).astype(jnp.bfloat16)
    kept = (
        joined16,
        log_total,
        attended16,
        resid_one,
        normed16,
        hidden,
        active16,
        resid_two,
        in_length,
    )
    return (result, kept)


def backward_pass(back16, inputs16, kept, matrices, vecs):
    w_qkv, w_out, w_up, w_down = matrices
    bias_q, bias_v, bias_out, bias_up, bias_down, gain_one, shift_one, gain_two, shift_two = vecs
    joined16, log_total, attended16, resid_one, normed16, hidden, active16, resid_two, in_length = (
        kept
    )
    seq_rows = inputs16.shape[0]
    back = jnp.where(in_length[:, None], back16.astype(jnp.float32), 0.0)
    unused_two, pull_two = jax.vjp(norm_apply, resid_two, gain_two, shift_two)
    d_resid_two, d_gain_two, d_shift_two = pull_two(back)
    d_down16 = d_resid_two.astype(jnp.bfloat16)
    d_active = jnp.einsum("to,io->ti", d_down16, w_down, preferred_element_type=jnp.float32)
    unused_gelu, pull_gelu = jax.vjp(exact_gelu, hidden)
    d_hidden = pull_gelu(d_active)[0]
    d_hidden16 = d_hidden.astype(jnp.bfloat16)
    d_normed = d_resid_two + jnp.einsum(
        "to,io->ti", d_hidden16, w_up, preferred_element_type=jnp.float32
    )
    unused_one, pull_one = jax.vjp(norm_apply, resid_one, gain_one, shift_one)
    d_resid_one, d_gain_one, d_shift_one = pull_one(d_normed)
    d_branch16 = d_resid_one.astype(jnp.bfloat16)
    d_attended = jnp.einsum("to,io->ti", d_branch16, w_out, preferred_element_type=jnp.float32)
    d_attended16 = d_attended.astype(jnp.bfloat16).reshape(seq_rows, HEADS, HEAD_DIM)
    query_heads, key_heads, value_heads = split_heads(joined16)
    scores = masked_scores(query_heads, key_heads, in_length)
    attention = jnp.exp(scores - log_total)
    attention16 = attention.astype(jnp.bfloat16)
    d_value = jnp.einsum(
        "hqk,qhd->khd", attention16, d_attended16, preferred_element_type=jnp.float32
    )
    d_attention = jnp.einsum(
        "qhd,khd->hqk", d_attended16, value_heads, preferred_element_type=jnp.float32
    )
    d_scores = attention * (d_attention - jnp.sum(attention * d_attention, axis=-1, keepdims=True))
    d_scores16 = d_scores.astype(jnp.bfloat16)
    d_query = jnp.einsum(
        "hqk,khd->qhd", d_scores16, key_heads, preferred_element_type=jnp.float32
    ) * HEAD_DIM ** (-0.5)
    d_key = jnp.einsum(
        "hqk,qhd->khd", d_scores16, query_heads, preferred_element_type=jnp.float32
    ) * HEAD_DIM ** (-0.5)
    d_query = d_query.reshape(seq_rows, D)
    d_key = d_key.reshape(seq_rows, D)
    d_value = d_value.reshape(seq_rows, D)
    d_joined16 = jnp.concatenate([d_query, d_key, d_value], axis=1).astype(jnp.bfloat16)
    d_inputs = d_resid_one + jnp.einsum(
        "to,io->ti", d_joined16, w_qkv, preferred_element_type=jnp.float32
    )
    vec_grad = jnp.concatenate(
        [
            jnp.sum(d_query, axis=0),
            jnp.sum(d_value, axis=0),
            jnp.sum(d_resid_one, axis=0),
            jnp.sum(d_hidden, axis=0),
            jnp.sum(d_resid_two, axis=0),
            d_gain_one,
            d_shift_one,
            d_gain_two,
            d_shift_two,
        ]
    )
    pairs = (d_joined16, attended16, d_branch16, normed16, d_hidden16, active16, d_down16)
    return (pairs, vec_grad, d_inputs.astype(jnp.bfloat16))


def rotate_in(left_side, matrix, right_side):
    inner = jnp.einsum(
        "pji,pjk->pik",
        left_side,
        matrix,
        precision=PRECISION_HIGH,
        preferred_element_type=jnp.float32,
    )
    return jnp.einsum(
        "pik,pkl->pil",
        inner,
        right_side,
        precision=PRECISION_HIGH,
        preferred_element_type=jnp.float32,
    )


def rotate_out(left_side, matrix, right_side):
    inner = jnp.einsum(
        "pij,pjk->pik",
        left_side,
        matrix,
        precision=PRECISION_HIGH,
        preferred_element_type=jnp.float32,
    )
    return jnp.einsum(
        "pik,plk->pil",
        inner,
        right_side,
        precision=PRECISION_HIGH,
        preferred_element_type=jnp.float32,
    )


def per_device_any(
    tokens,
    cotangent,
    lengths,
    deal,
    weights,
    vectors,
    owners,
    left_basis,
    right_basis,
    first_moment,
    second_moment,
    vec_first,
    vec_second,
):
    dp_count = lax.axis_size("dp")
    fsdp_count = lax.axis_size("fsdp")
    dp_place = lax.axis_index("dp")
    fsdp_place = lax.axis_index("fsdp")
    micro_count = tokens.shape[0]
    my_place = dp_place * fsdp_count + fsdp_place
    quarter = lax.dynamic_index_in_dim(
        deal.reshape(micro_count, dp_count, fsdp_count), fsdp_place, axis=2, keepdims=False
    )
    quarter = quarter - fsdp_place * dp_count
    ordered = jnp.take_along_axis(tokens, quarter[:, :, None, None], axis=1)
    dealt_rows = lax.all_to_all(ordered, "dp", split_axis=1, concat_axis=2, tiled=True)
    my_seq = lax.dynamic_index_in_dim(deal, my_place, axis=1, keepdims=False)
    my_length = jnp.take_along_axis(lengths, my_seq[:, None], axis=1)[:, 0]
    shard_low = (weights.astype(jnp.bfloat16), vectors.astype(jnp.bfloat16))
    whole_tiles, whole_vecs = (
        lax.all_gather(shard_low[0], ("dp", "fsdp"), axis=0, tiled=True),
        lax.all_gather(shard_low[1], ("dp", "fsdp"), axis=0, tiled=True),
    )
    mats_kept = unpack_mats(whole_tiles)
    vecs_kept = unpack_vecs(whole_vecs.astype(jnp.float32))
    all_pairs = []
    all_inputs = []
    vec_terms = []
    results = []
    input_grads = []
    for micro_index in range(micro_count):
        inputs16 = dealt_rows[micro_index, 0]
        matrices, vecs = (mats_kept, vecs_kept)
        result, kept = forward_pass(inputs16, my_length[micro_index], matrices, vecs)
        pairs, vec_term, d_inputs = backward_pass(
            cotangent[micro_index, 0], inputs16, kept, matrices, vecs
        )
        all_pairs.append(pairs)
        all_inputs.append(inputs16)
        vec_terms.append(vec_term)
        results.append(result)
        input_grads.append(d_inputs)

    def joined_rows(index):
        return jnp.concatenate([pairs[index] for pairs in all_pairs], axis=0)

    inputs_rows = jnp.concatenate(all_inputs, axis=0)
    tile_terms = jnp.concatenate(
        [
            tiled_grad(inputs_rows, joined_rows(0)),
            tiled_grad(joined_rows(1), joined_rows(2)),
            tiled_grad(joined_rows(3), joined_rows(4)),
            tiled_grad(joined_rows(5), joined_rows(6)),
        ],
        axis=0,
    )
    grad_vec = vec_terms[0]
    for vec_term in vec_terms[1:]:
        grad_vec = grad_vec + vec_term
    shard_tiles = weights.shape[0]
    tile_grads, vec_grads = (
        lax.psum_scatter(tile_terms, ("dp", "fsdp"), scatter_dimension=0, tiled=True),
        lax.psum_scatter(grad_vec, ("dp", "fsdp"), scatter_dimension=0, tiled=True),
    )
    group_grads, group_master = (
        lax.all_gather(tile_grads.astype(jnp.bfloat16), "fsdp", axis=0, tiled=True).astype(
            tile_grads.dtype
        ),
        lax.all_gather(weights.astype(jnp.bfloat16), "fsdp", axis=0, tiled=True).astype(
            weights.dtype
        ),
    )
    result_dealt = jnp.stack(results)[:, None]
    grads_dealt = jnp.stack(input_grads)[:, None]
    back_result, back_grads = (
        lax.all_to_all(result_dealt, "dp", split_axis=2, concat_axis=1, tiled=True),
        lax.all_to_all(grads_dealt, "dp", split_axis=2, concat_axis=1, tiled=True),
    )
    restore = jnp.argsort(quarter, axis=1)
    out_tokens = jnp.take_along_axis(back_result, restore[:, :, None, None], axis=1)
    in_grad = jnp.take_along_axis(back_grads, restore[:, :, None, None], axis=1)
    group_size = fsdp_count * shard_tiles
    pick_rows = owners - dp_place * group_size
    own_grads = jnp.take(group_grads, pick_rows, axis=0)
    own_master = jnp.take(group_master, pick_rows, axis=0)
    rates = tile_rate(owners)
    rotated = rotate_in(left_basis, own_grads, right_basis)
    new_first = BETA_ONE * first_moment + (1.0 - BETA_ONE) * rotated
    new_second = BETA_TWO * second_moment + (1.0 - BETA_TWO) * rotated * rotated
    first_hat = new_first / (1.0 - BETA_ONE**STEP)
    second_hat = new_second / (1.0 - BETA_TWO**STEP)
    step_rotated = first_hat / (jnp.sqrt(second_hat) + ADAM_EPS)
    update = rotate_out(left_basis, step_rotated, right_basis)
    new_tiles = own_master - rates[:, None, None] * (update + DECAY * own_master)
    vec_first_new = BETA_ONE * vec_first + (1.0 - BETA_ONE) * vec_grads
    vec_second_new = BETA_TWO * vec_second + (1.0 - BETA_TWO) * vec_grads * vec_grads
    vec_hat_one = vec_first_new / (1.0 - BETA_ONE**STEP)
    vec_hat_two = vec_second_new / (1.0 - BETA_TWO**STEP)
    new_vectors = vectors - VEC_RATE * vec_hat_one / (jnp.sqrt(vec_hat_two) + ADAM_EPS)
    return (
        out_tokens,
        in_grad,
        tile_grads,
        vec_grads,
        new_first,
        new_second,
        new_tiles,
        new_tiles.astype(jnp.bfloat16),
        vec_first_new,
        vec_second_new,
        new_vectors,
    )


CHUNK = 256
ROWS_AT_ONCE = 32
f32 = jnp.float32
bf = jnp.bfloat16


def mul(a, b):
    return jnp.dot(a, b, preferred_element_type=f32)


def mul_t(a, b):
    return lax.dot_general(a, b, (((1,), (1,)), ((), ())), preferred_element_type=f32)


def t_mul(a, b):
    return lax.dot_general(a, b, (((0,), (0,)), ((), ())), preferred_element_type=f32)


def column_chunks():
    return [slice(j * CHUNK, (j + 1) * CHUNK) for j in range(D // CHUNK)]


class Layer:
    def __init__(self, **refs):
        self.__dict__.update(refs)
        self.rows = self.l3.shape[1]
        self.seqs = self.rows // TB

    def left(self, first, count=8):
        return jnp.concatenate([self.l3[first + j] for j in range(count)], axis=1)

    def each_rows(self, fn):
        def body(i, _):
            fn(pl.ds(pl.multiple_of(i * ROWS_AT_ONCE, ROWS_AT_ONCE), ROWS_AT_ONCE), i)
            return 0

        lax.fori_loop(0, self.rows // ROWS_AT_ONCE, body, 0)

    def counted(self, i):
        per = TB // ROWS_AT_ONCE
        at = (i % per) * ROWS_AT_ONCE + lax.broadcasted_iota(jnp.int32, (ROWS_AT_ONCE, 1), 0)
        return at < self.lens[i // per]

    def add_sum(self, n, value, cols=slice(None)):
        self.vsum[n, :, cols] += value.reshape(value.shape[0] // 8, 8, value.shape[1]).sum(axis=0)

    def project(self, t):
        x = self.left(0)
        for j, cols in enumerate(column_chunks()):
            out = mul(x, self.wcols(t, cols))
            if t != 1:
                out = out + self.vec[pl.ds(0 if t == 0 else 1, 1), cols]
            out = out.astype(bf)
            for i in range(CHUNK // TB):
                self.q3[t, j * (CHUNK // TB) + i] = out[:, i * TB : (i + 1) * TB]

    def two(self, block):
        lane = lax.broadcasted_iota(jnp.int32, block.shape, 1)
        zero = jnp.zeros_like(block)
        return jnp.concatenate(
            [jnp.where(lane < HEAD_DIM, block, zero), jnp.where(lane < HEAD_DIM, zero, block)], axis=0
        )

    def one(self, stacked):
        top, low = stacked[:TB], stacked[TB:]
        lane = lax.broadcasted_iota(jnp.int32, top.shape, 1)
        return jnp.where(lane < HEAD_DIM, top, low)

    def attend(self):
        def body(b, _):
            at = pl.ds(pl.multiple_of(b * TB, TB), TB)
            key = lax.broadcasted_iota(jnp.int32, (2 * TB, TB), 1)
            seen = key < self.lens[b]
            for h in range(HEADS // 2):
                s = mul_t(self.two(self.q3[0, h, at]), self.q3[1, h, at]) * HEAD_DIM**-0.5
                s = jnp.where(seen, s, -1e30)
                e = jnp.exp(s - jnp.max(s, axis=1, keepdims=True))
                p = e * (1.0 / jnp.sum(e, axis=1, keepdims=True))
                self.p3[b, h] = p
                a = self.one(mul(p.astype(bf), self.q3[2, h, at]))
                self.l3[8 + h, at] = a.astype(bf)
            return 0

        lax.fori_loop(0, self.seqs, body, 0)

    def norm_one(self):
        a = self.left(8)
        for j, cols in enumerate(column_chunks()):
            x = jnp.concatenate([self.l3[2 * j], self.l3[2 * j + 1]], axis=1).astype(f32)
            self.xh[:, cols] = x + mul(a, self.wcols(3, cols)) + self.vec[pl.ds(2, 1), cols]

        def rows(at, i):
            r = self.xh[at]
            center = r - jnp.mean(r, axis=1, keepdims=True)
            scale = lax.rsqrt(jnp.mean(center * center, axis=1, keepdims=True) + EPS_NORM)
            hat = center * scale
            self.xh[at] = hat
            self.rs[at] = jnp.broadcast_to(scale, (ROWS_AT_ONCE, TB))
            u = hat * self.vec[pl.ds(8, 1)] + self.vec[pl.ds(9, 1)]
            self.acc[at] = u
            u16 = u.astype(bf)
            for j in range(8):
                self.l3[16 + j, at] = u16[:, j * TB : (j + 1) * TB]

        self.each_rows(rows)

    def up_begin(self, t):
        u = self.left(16, 4)
        for cols in column_chunks():
            self.gp[t, :, cols] = mul(u, self.wcols(4 + t, cols, 0)) + self.vec[pl.ds(3 + t, 1), cols]

    def up_end(self, t):
        u = self.left(20, 4)
        for cols in column_chunks():
            self.gp[t, :, cols] += mul(u, self.wcols(4 + t, cols, 1))

        def rows(at, i):
            h = self.gp[t, at]
            cdf = 0.5 + 0.5 * lax.erf(h * 0.7071067811865476)
            self.gp[t, at] = cdf + h * (0.3989422804014327 * jnp.exp(-0.5 * h * h))
            e = (h * cdf).astype(bf)
            for j in range(8):
                self.l3[24 + 8 * t + j, at] = e[:, j * TB : (j + 1) * TB]

        self.each_rows(rows)

    def down(self, t):
        e = self.left(24 + 8 * t)
        for cols in column_chunks():
            self.acc[:, cols] += mul(e, self.wcols(8 + t, cols))

    def norm_two(self):
        def rows(at, i):
            r = self.acc[at] + self.vec[pl.ds(7, 1)]
            center = r - jnp.mean(r, axis=1, keepdims=True)
            scale = lax.rsqrt(jnp.mean(center * center, axis=1, keepdims=True) + EPS_NORM)
            hat = center * scale
            live = self.counted(i)
            gain = self.vec[pl.ds(10, 1)]
            out = jnp.where(live, hat * gain + self.vec[pl.ds(11, 1)], 0.0).astype(bf)
            per = TB // ROWS_AT_ONCE
            slabs = ROWS_AT_ONCE // self.res.shape[2]
            self.res[i // per, pl.ds((i % per) * slabs, slabs)] = out.reshape(
                slabs, self.res.shape[2], D
            )
            dy = jnp.where(live, self.cot[at].astype(f32), 0.0)
            self.add_sum(10, dy * hat)
            self.add_sum(11, dy)
            g = dy * gain
            dr = scale * (
                g
                - jnp.mean(g, axis=1, keepdims=True)
                - hat * jnp.mean(g * hat, axis=1, keepdims=True)
            )
            self.add_sum(7, dr)
            self.acc[at] = dr
            self.d2[at] = dr.astype(bf)

        self.each_rows(rows)

    def down_back(self, t):
        d = self.r3[8]
        for cols in column_chunks():
            dh = mul_t(d, self.wrows(8 + t, cols)) * self.gp[t, :, cols]
            self.add_sum(3 + t, dh, cols)
            self.r3[4 + t, :, cols] = dh.astype(bf)

    def up_back(self, t):
        d = self.r3[4 + t]
        for cols in column_chunks():
            self.acc[:, cols] += mul_t(d, self.wrows(4 + t, cols))

    def norm_one_back(self):
        def rows(at, i):
            du, hat = self.acc[at], self.xh[at]
            self.add_sum(8, du * hat)
            self.add_sum(9, du)
            g = du * self.vec[pl.ds(8, 1)]
            dr = self.rs[at][:, :1] * (
                g
                - jnp.mean(g, axis=1, keepdims=True)
                - hat * jnp.mean(g * hat, axis=1, keepdims=True)
            )
            self.add_sum(2, dr)
            self.acc[at] = dr
            self.r3[3, at] = dr.astype(bf)

        self.each_rows(rows)

    def out_back(self):
        d = self.r3[3]
        for j, cols in enumerate(column_chunks()):
            da = mul_t(d, self.wrows(3, cols)).astype(bf)
            for i in range(CHUNK // TB):
                self.da3[j * (CHUNK // TB) + i] = da[:, i * TB : (i + 1) * TB]

    def attend_back(self):
        def body(b, _):
            at = pl.ds(pl.multiple_of(b * TB, TB), TB)
            for h in range(HEADS // 2):
                cols = slice(h * TB, (h + 1) * TB)
                p = self.p3[b, h]
                da = self.two(self.da3[h, at])
                dv = t_mul(p.astype(bf), da)
                pd = p * mul_t(da, self.q3[2, h, at])
                ds = (pd - p * jnp.sum(pd, axis=1, keepdims=True)).astype(bf)
                dq = self.one(mul(ds, self.q3[1, h, at])) * HEAD_DIM**-0.5
                dk = t_mul(ds, self.two(self.q3[0, h, at])) * HEAD_DIM**-0.5
                self.r3[0, at, cols] = dq.astype(bf)
                self.r3[1, at, cols] = dk.astype(bf)
                self.r3[2, at, cols] = dv.astype(bf)
                self.add_sum(0, dq, cols)
                self.add_sum(1, dv, cols)
            return 0

        lax.fori_loop(0, self.seqs, body, 0)

    def project_back(self, t):
        d = self.r3[t]
        for cols in column_chunks():
            value = self.acc[:, cols] + mul_t(d, self.wrows(t, cols))
            if t < 2:
                self.acc[:, cols] = value
            else:
                self.din[:, :, :, cols] = value.astype(bf).reshape(self.din.shape[:3] + (CHUNK,))


MESH = pl.DeviceIdType.MESH
ZN = 4
OCT = 96
RING = 8
SPOTS = 16


class Place:
    def __init__(self):
        self.dp = lax.axis_index("dp")
        self.fs = lax.axis_index("fsdp")
        self.z, self.y = self.dp // 2, self.dp % 2
        self.x, self.c = self.fs // 2, self.fs % 2
        self.to_x = (self.dp, (self.fs + 2) % 4)
        self.to_y = (self.z * 2 + 1 - self.y, self.fs)
        self.to_core = (self.dp, self.x * 2 + 1 - self.c)
        self.to_up = (self.dp + 2, self.fs)
        self.to_down = (self.dp - 2, self.fs)
        near = self.z + 1 - 2 * (self.z % 2)
        far = (self.z + 2) % ZN
        self.doubling = [
            self.to_core,
            self.to_x,
            self.to_y,
            (near * 2 + self.y, self.fs),
            (far * 2 + self.y, self.fs),
        ]

    def peer(self, j):
        return (self.dp + j) % (2 * ZN)

    def greet(self):
        bar = pltpu.get_barrier_semaphore()
        for dev in [self.to_x, self.to_core] + [(self.peer(j), self.fs) for j in range(1, 2 * ZN)]:
            pl.semaphore_signal(bar, inc=1, device_id=dev, device_id_type=MESH)
        pl.semaphore_wait(bar, 1 + 2 * ZN)

    def octet(self, dx, dy, zp, k, c=None):
        yy = self.y if dy == 0 else 1 - self.y
        xx = self.x if dx == 0 else 1 - self.x
        return ((zp * 2 + yy) * 4 + xx * 2 + (self.c if c is None else c)) * 3 + k

    def plane(self, table, i):
        zp = table[0][i]
        for n in range(1, ZN):
            zp = jnp.where(self.z == n, table[n][i], zp)
        return zp


def octet_place(o):
    return jnp.where(
        o < 24,
        (o % 3) * 8 + o // 3,
        jnp.where((o >= 32) & (o < 64), 32 + ((o - 32) % 4) * 8 + (o - 32) // 4, o),
    )


def left_block(o):
    return jnp.where(
        o < 24, o // 3, jnp.where(o < 32, o - 16, jnp.where(o < 64, 16 + (o - 32) // 4, o - 40))
    )


def right_block(o):
    return jnp.where(o < 24, o % 3, jnp.where(o < 32, 3, jnp.where(o < 64, 4 + (o - 32) % 4, 8)))


def wait_for(ref, sem):
    pltpu.make_async_copy(ref, ref, sem).wait()


def remote(src, dst, send_sem, recv_sem, dev):
    return pltpu.make_async_remote_copy(
        src_ref=src,
        dst_ref=dst,
        send_sem=send_sem,
        recv_sem=recv_sem,
        device_id=dev,
        device_id_type=MESH,
    )


def start_deal(p, src, dst, s_sem, r_sem, l_sem):
    for j in range(1, 2 * ZN):
        d = p.peer(j)
        remote(src.at[:, d], dst.at[:, p.dp], s_sem, r_sem.at[p.dp], (d, p.fs)).start()
    pltpu.make_async_copy(src.at[:, p.dp], dst.at[:, p.dp], l_sem).start()


def end_deal(p, src, dst, s_sem, r_sem, l_sem):
    for j in range(1, 2 * ZN):
        d = p.peer(j)
        wait_for(dst.at[:, d], r_sem.at[d])
    wait_for(dst.at[:, p.dp], l_sem)
    wait_for(src.at[:, pl.ds(0, 2 * ZN - 1)], s_sem)


FORWARD_STEPS = [
    "P0", "P1", "P2", "ATT", "N1", "UA0", "UA1", "UA2", "UA3",
    "UB0", "UB1", "UB2", "UB3", "D0", "D1", "D2", "D3", "N2",
]
FORWARD_NEEDS = {"P0": (0,), "N1": (1,), "UB0": (2,), "D1": (3,)}
FORWARD_ROUTES = [
    ["xyx", "zzx", "zzy", "zxy"],
    ["zzz", "xyx", "zzz", "zzz"],
    ["zzz", "zzz", "xyx", "zzz"],
    ["zxy", "zzy", "zzx", "xyx"],
]
FORWARD_PLANS = [
    [
        0, 100, 2, 1, 102, 101, 200, 10, 110, 22, 300, 12, 201, 112, 202, 122,
        11, 111, 21, 121, 301, 222, 302, 30, 130, 212, 1000, 20, 32, 31, 221, 1001,
        132, 210, 322, 311, 310, 131, 211, 312, 1002, 120, 1003, 232, 320, 1004, 330, 1005,
        1006, 231, 220, 230, 1007, 1008, 321, 1009, 1010, 332, 331, 1011, 1012, 1013, 1014, 1015,
        1016, 1017,
    ],
    [
        10, 110, 12, 112, 210, 22, 0, 122, 2, 21, 100, 102, 1, 11, 111, 200,
        310, 101, 30, 121, 20, 32, 31, 212, 300, 131, 211, 201, 120, 130, 301, 302,
        202, 311, 222, 1000, 331, 320, 1001, 1002, 312, 220, 1003, 221, 230, 330, 132, 1004,
        1005, 322, 231, 1006, 1007, 1008, 332, 321, 1009, 1010, 232, 1011, 1012, 1013, 1014, 1015,
        1016, 1017,
    ],
    [
        22, 21, 121, 20, 122, 120, 31, 221, 131, 220, 12, 30, 0, 222, 2, 100,
        32, 1, 102, 330, 101, 320, 11, 200, 10, 331, 112, 132, 111, 110, 300, 322,
        301, 202, 130, 231, 232, 332, 310, 302, 212, 201, 1000, 311, 321, 1001, 211, 1002,
        1003, 210, 312, 1004, 1005, 1006, 230, 1007, 1008, 1009, 1010, 1011, 1012, 1013, 1014, 1015,
        1016, 1017,
    ],
    [
        30, 31, 32, 130, 131, 132, 22, 230, 21, 121, 122, 330, 12, 232, 231, 0,
        112, 2, 331, 102, 100, 332, 1, 20, 320, 101, 212, 222, 200, 11, 221, 201,
        10, 202, 110, 111, 300, 120, 301, 302, 1000, 1001, 312, 1002, 210, 311, 310, 322,
        211, 1003, 1004, 321, 1005, 220, 1006, 1007, 1008, 1009, 1010, 1011, 1012, 1013, 1014, 1015,
        1016, 1017,
    ],
]


def along_z(here, zp, k=None):
    up = zp <= here < ZN - 1 and (k is None or FORWARD_ROUTES[here + 1][zp][k] == "z")
    down = zp >= here > 0 and (k is None or FORWARD_ROUTES[here - 1][zp][k] == "z")
    return (["u"] if up else []) + (["d"] if down else [])


def split_plan(plan):
    parts = [[]]
    for code in plan:
        if code >= 1000:
            parts.append([])
        else:
            parts[-1].append(code)
    return parts


def forward_kernel(
    lens, shard, vec, tok, cot,
    wm, l3_out, d2_out, acc_out, gp_out, xh_out, rs_out, p3_out, q3_out, res_out, vsum, vecs,
    wbuf, vbuf, xl, l3, d2, q3, p3, xh, rs, acc, gp, res,
    r_w, s_x, s_y, s_up, s_down, s_core, s_local, s_vec, r_vec, s_tok, r_tok, l_tok, s_out,
):
    p = Place()
    z = p.z
    p.greet()

    def wcols(n, cols, half=None):
        if half is None:
            return wbuf[8 * n : 8 * n + 8, :, cols].reshape(D, CHUNK)
        first = 8 * n + 4 * half
        return wbuf[first : first + 4, :, cols].reshape(D // 2, CHUNK)

    f = Layer(
        lens=lens, vec=vecs, l3=l3, d2=d2, vsum=vsum, q3=q3, p3=p3, xh=xh, rs=rs, acc=acc, gp=gp,
        res=res, cot=cot, wcols=wcols,
    )

    def ref_of(o):
        return wbuf.at[octet_place(o)]

    def wait(o):
        wait_for(ref_of(o), r_w.at[o])

    start_deal(p, tok, xl, s_tok, r_tok, l_tok)
    me = p.dp * 4 + p.fs
    vbuf[me] = vec[...]
    for k in range(3):
        wbuf[octet_place(p.octet(0, 0, z, k))] = shard[k]

    def vec_step(n):
        size = 2**n
        if n > 0:
            half = size // 2
            theirs = (me // half) * half
            theirs = theirs + half * (1 - 2 * (theirs // half % 2))
            wait_for(vbuf.at[pl.ds(theirs, half)], r_vec.at[n - 1])
        if n < 5:
            mine = vbuf.at[pl.ds((me // size) * size, size)]
            remote(mine, mine, s_vec.at[n], r_vec.at[n], p.doubling[n]).start()

    def vec_rows():
        for m in range(OCT):
            cols = slice((m % 8) * TB, (m % 8 + 1) * TB)
            vecs[m // 8 : m // 8 + 1, cols] = vbuf[m // 3, m % 3 : m % 3 + 1, :]

    sent = [dict(x=0, y=0, u=0, d=0, c=0) for _ in range(ZN)]
    way = dict(
        x=(p.to_x, s_x), y=(p.to_y, s_y), u=(p.to_up, s_up), d=(p.to_down, s_down),
        c=(p.to_core, s_core),
    )

    def item(here, kind, zp, k):
        def send(o, *ways):
            ref = ref_of(o)
            for w in ways:
                dev, sem = way[w]
                remote(ref, ref, sem, r_w.at[o], dev).start()
                sent[here][w] += 1

        route = FORWARD_ROUTES[here][zp][k]
        if kind == 0:
            o = p.octet(0, 0, zp, k)
            if zp != here:
                wait(o)
            send(o, *along_z(here, zp))
        elif kind == 1:
            send(p.octet(0, 0, zp, k), "x", "y", "c")
        elif kind == 2:
            o = p.octet(0, 1, zp, k)
            wait(o)
            send(o, *(["x"] if route == "x" else []), "c")
            o = p.octet(1, 0, zp, k)
            wait(o)
            send(o, *(["y"] if route == "y" else []), "c")
        else:
            o = p.octet(1, 1, zp, k)
            wait(o)
            send(o, *along_z(here, zp, k), "c")

    def partner(zp):
        for dx in range(2):
            for dy in range(2):
                for k in range(3):
                    wait(p.octet(dx, dy, zp, k, 1 - p.c))

    outs = []

    def give(src, dst):
        copy = pltpu.make_async_copy(src, dst, s_out.at[len(outs)])
        copy.start()
        outs.append(copy)

    def give_square(n):
        give(wbuf.at[pl.ds(8 * n, 8)], wm.at[pl.ds(8 * n, 8)])

    def compute(name):
        t = int(name[-1]) if name[-1].isdigit() else 0
        if name == "P0":
            vec_rows()
            vsum[...] = jnp.zeros_like(vsum)
            end_deal(p, tok, xl, s_tok, r_tok, l_tok)
            for j in range(8):
                l3[j] = xl[:, :, :, j * TB : (j + 1) * TB].reshape(l3.shape[1], TB)
        if name[0] == "P":
            f.project(t)
            give_square(t)
        elif name == "ATT":
            f.attend()
            give(q3, q3_out)
            give(p3, p3_out)
        elif name == "N1":
            f.norm_one()
            give_square(3)
            give(xh, xh_out)
            give(rs, rs_out)
        elif name[:2] == "UA":
            f.up_begin(t)
        elif name[:2] == "UB":
            f.up_end(t)
            give_square(4 + t)
            give(gp.at[t], gp_out.at[t])
            if t == 3:
                give(l3, l3_out)
        elif name[0] == "D":
            f.down(t)
            give_square(8 + t)
        else:
            f.norm_two()
            give(d2, d2_out)
            give(acc, acc_out)
            give(res, res_out)

    parts = [split_plan(plan) for plan in FORWARD_PLANS]
    for n in range(len(FORWARD_STEPS) + 1):

        def run(here):
            for m, code in enumerate(parts[here][n]):
                item(here, code // 100, code // 10 % 10, code % 10)
                if n == 0 and m % 4 == 1 and m // 4 < 6:
                    vec_step(m // 4)

        for here in range(ZN):
            pl.when(z == here)(functools.partial(run, here))
        if n < len(FORWARD_STEPS):
            name = FORWARD_STEPS[n]
            for zp in FORWARD_NEEDS.get(name, ()):
                partner(zp)
            compute(name)

    for copy in outs:
        copy.wait()
    for n in range(5):
        wait_for(vbuf.at[pl.ds(0, 2**n)], s_vec.at[n])

    def drain(here):
        for w, n in sent[here].items():
            if n:
                wait_for(wbuf.at[pl.ds(0, n)], way[w][1])

    for here in range(ZN):
        pl.when(z == here)(functools.partial(drain, here))


def forward(lens, shard, vec, tok, cot):
    dma = pltpu.SemaphoreType.DMA
    rows = cot.shape[0]
    vmem = pl.BlockSpec(memory_space=pltpu.VMEM)
    far = pl.BlockSpec(memory_space=pl.ANY)
    out = jax.ShapeDtypeStruct
    stages = (
        out((56, rows, TB), bf),
        out((rows, D), bf),
        out((rows, D), f32),
        out((4, rows, D), f32),
        out((rows, D), f32),
        out((rows, TB), f32),
        out((rows // TB, 8, 2 * TB, TB), f32),
        out((3, 8, rows, TB), bf),
        out(tok.shape, bf),
    )
    scratch = [pltpu.VMEM(s.shape, s.dtype) for s in stages]
    l3, d2, acc, gp, xh, rs, p3, q3, res = scratch
    return pl.pallas_call(
        forward_kernel,
        out_shape=(out((OCT, TB, D), bf),) + stages + (out((12, 8, D), f32), out((12, D), f32)),
        in_specs=[pl.BlockSpec(memory_space=pltpu.SMEM)] + [vmem] * 4,
        out_specs=(far,) * 10 + (vmem,) * 2,
        scratch_shapes=[
            pltpu.VMEM((OCT, TB, D), bf), pltpu.VMEM((32, 8, TB), f32), pltpu.VMEM(tok.shape, bf),
            l3, d2, q3, p3, xh, rs, acc, gp, res,
            dma((OCT,)), dma, dma, dma, dma, dma, dma((3,)), dma((5,)), dma((5,)),
            dma, dma((2 * ZN,)), dma, dma((32,)),
        ],
        compiler_params=pltpu.CompilerParams(
            collective_id=0, has_side_effects=True, vmem_limit_bytes=62 * 2**20
        ),
        name="forward",
    )(lens, shard, vec, tok, cot)


BACKWARD_STEPS = [
    "DB0", "DB1", "DB2", "DB3", "UB0", "UB1", "UB2", "UB3",
    "N1B", "OB", "ATB", "PB0", "PB1", "PB2",
]
BACKWARD_ROUTES = [
    ["xyy", "zzx", "zzy", "zzx"],
    ["zzz", "xyy", "zzz", "zzz"],
    ["zzz", "zzz", "xyy", "zzz"],
    ["zzx", "zzy", "zzx", "xyy"],
]
BACKWARD_PLANS = [
    [
        500, 1000, 30, 31, 1001, 230, 1002, 130, 1003, 32, 132, 1004, 330, 231, 21, 1005,
        1006, 1007, 221, 131, 1008, 10, 22, 20, 1009, 110, 210, 122, 1010, 11, 121, 2,
        232, 1011, 331, 12, 222, 120, 112, 1012, 220, 111, 0, 211, 1, 212, 332, 102,
        322, 320, 321, 100, 202, 310, 312, 101, 1013, 200, 201, 311, 300, 501, 301, 302,
        401, 400, 402,
    ],
    [
        32, 1000, 1001, 500, 232, 1002, 1003, 30, 31, 230, 22, 1004, 1005, 20, 1006, 21,
        231, 1007, 122, 221, 330, 131, 1008, 1009, 1010, 1011, 222, 12, 130, 1012, 0, 200,
        132, 10, 1, 11, 112, 201, 331, 2, 110, 102, 212, 220, 100, 120, 121, 111,
        101, 332, 322, 210, 202, 211, 321, 300, 320, 310, 301, 312, 1013, 302, 311, 501,
        402, 400, 401,
    ],
    [
        500, 1000, 31, 1001, 30, 1002, 1003, 1004, 1005, 1006, 1007, 22, 1008, 12, 230, 1009,
        231, 32, 11, 1010, 10, 111, 211, 2, 112, 0, 110, 330, 232, 212, 1011, 122,
        102, 210, 202, 200, 21, 131, 100, 132, 311, 20, 1, 1012, 201, 101, 310, 130,
        120, 121, 331, 312, 300, 220, 332, 1013, 222, 301, 221, 302, 501, 322, 321, 320,
        402, 400, 401,
    ],
    [
        1000, 1001, 1002, 1003, 20, 220, 120, 1004, 21, 1005, 1006, 1007, 221, 121, 1008, 11,
        211, 12, 111, 10, 112, 22, 210, 110, 1009, 311, 122, 1010, 0, 100, 200, 1011,
        1, 32, 222, 101, 31, 212, 2, 310, 322, 131, 30, 300, 102, 1012, 201, 312,
        130, 132, 202, 1013, 232, 301, 302, 230, 231, 321, 320, 330, 500, 332, 331, 400,
        501, 402, 401,
    ],
]


def backward_codes(here):
    routes = BACKWARD_ROUTES
    spots = {}
    for way in "xy":
        pairs = [(zp, k) for zp in range(ZN) for k in range(3) if routes[here][zp][k] == way]
        spots.update({pair: n for n, pair in enumerate(pairs)})

    def octet(side, zp, k):
        dx, dy = side % 2, side // 2
        own = zp == here
        route = routes[here][zp][k]
        code = k + 4 * zp + 16 * side + 131072
        along = "u" if zp > here else "d"
        if side == 0:
            code += 64 + 128
            way = "f" if own else along
        elif side == 1:
            code += 128 * (route == "y")
            way = "x"
        elif side == 2:
            code += 64 * (route == "x")
            way = "y"
        else:
            way = along if route == "z" else route
        if side in (0, 3):
            for step, there, bit in ((1, here - 1, 256), (-1, here + 1, 512)):
                if 0 <= there < ZN and (zp - here) * step >= 0:
                    code += bit * (side == 0 or routes[there][zp][k] == "z")
        return code + 1024 * "xyudf".index(way) + 8192 * spots.get((zp, k), 0)

    parts, first, vec, since = [[]], 0, None, 0
    for item in BACKWARD_PLANS[here]:
        if item >= 1000:
            parts.append([])
            if len(parts) - 1 == BACKWARD_STEPS.index("ATB") + 1:
                vec = 0
            continue
        kind, zp, k = item // 100, item // 10 % 10, item % 10
        if kind == 0:
            parts[-1].append(k + 4 * zp + 64 * (first >= 2) + 8192 * (first % 2))
            first += 1
        elif kind == 1:
            parts[-1].append(octet(3, zp, k))
        elif kind == 2:
            parts[-1] += [octet(2, zp, k), octet(1, zp, k)]
        elif kind == 3:
            parts[-1].append(octet(0, zp, k))
        elif kind == 4:
            parts[-1].append(131072 * 2 + k)
        else:
            parts[-1].append(131072 * (3 + k))
        since += 1
        if vec is not None and vec < 6 and since >= 3:
            parts[-1].append(131072 * (5 + vec))
            vec, since = vec + 1, 0
    return parts


def backward_kernel(
    wm, l3_in, d2_in, acc_in, gp_in, xh_in, rs_in, p3_in, q3_in, res, vsum_in, vec,
    tiles, grp, vout, res_back, din_back,
    l3, r3, acc, gp, xh, rs, p3, q3, da3, din, wb, vsum,
    land_c, land_x, land_y, land_z, ring, vland, total,
    r_in, r_wb, r_c, r_x, r_y, r_z, r_e, r_v, s_ring, s_x, s_y, s_up, s_down, s_e, s_e2, s_v,
    s_res, r_res, l_res, s_din, r_din, l_din,
):
    p = Place()
    z, c, fs = p.z, p.c, p.fs
    takes = [
        pltpu.make_async_copy(src, dst, r_in.at[n])
        for n, (src, dst) in enumerate(
            [
                (d2_in, r3.at[8]), (l3_in, l3), (gp_in, gp), (acc_in, acc), (xh_in, xh),
                (rs_in, rs), (p3_in, p3), (q3_in, q3),
            ]
        )
    ]
    for copy in takes:
        copy.start()
    weights = [8, 9, 10, 11, 4, 5, 6, 7, 3, 0, 1, 2]
    slots = wb.shape[0]

    def bring(n):
        if n < len(weights):
            pltpu.make_async_copy(
                wm.at[pl.ds(8 * weights[n], 8)], wb.at[n % slots], r_wb.at[n % slots]
            ).start()

    for n in range(slots):
        bring(n)
    vsum[...] = vsum_in[...]
    p.greet()

    def wrows(n, rows):
        at = slice(rows.start // TB, rows.stop // TB)
        return wb[weights.index(n) % slots, at].reshape(CHUNK, D)

    f = Layer(
        vec=vec, l3=l3, r3=r3, vsum=vsum, q3=q3, p3=p3, da3=da3, xh=xh, rs=rs, acc=acc, gp=gp,
        din=din, wrows=wrows,
    )

    def part(o):
        return t_mul(l3[left_block(o)], r3[right_block(o)])

    def add(land, sem, n):
        wait_for(land.at[n], sem.at[n])
        total[...] += land[n].astype(f32)

    def to_partner(zp, k, slot, again):
        def body(j, _):
            yy, xx = j % 2, j // 2
            o = ((zp * 2 + yy) * 4 + xx * 2 + (1 - c)) * 3 + k
            n = slot * 4 + j
            value = part(o).astype(bf)
            pl.when(again == 1)(lambda: wait_for(ring.at[0], s_ring.at[n]))
            ring[n] = value
            q = ((jnp.where(yy == p.y, 0, 2) + jnp.where(xx == p.x, 0, 1)) * ZN + zp) * 3 + k
            remote(ring.at[n], land_c.at[q], s_ring.at[n], r_c.at[q], p.to_core).start()
            return 0

        lax.fori_loop(0, 4, body, 0)

    def octet_step(code, zp, k):
        side = code // 16 % 4
        dx, dy = side % 2, side // 2
        corner = side // 3
        q = (side * ZN + zp) * 3 + k
        yy = p.y + dy * (1 - 2 * p.y)
        xx = p.x + dx * (1 - 2 * p.x)
        o = ((zp * 2 + yy) * 4 + xx * 2 + c) * 3 + k
        wait_for(land_c.at[q], r_c.at[q])
        total[...] = part(o) + land_c[q].astype(f32)
        spot = 12 + code // 8192 % 16
        flat = zp * 3 + k
        column = jnp.where(side == 0, flat, spot)
        n = corner * 12 + flat
        mine = 24 + corner * 3 + k
        above = jnp.where(zp == z, mine, n)
        below_to = jnp.where(zp == z - 1, mine, n)
        pl.when(code // 64 % 2 == 1)(functools.partial(add, land_x, r_x, column))
        pl.when(code // 128 % 2 == 1)(functools.partial(add, land_y, r_y, column))
        pl.when(code // 256 % 2 == 1)(functools.partial(add, land_z, r_z, n))
        pl.when(code // 512 % 2 == 1)(functools.partial(add, land_z, r_z, above))
        way = code // 1024 % 8
        t = jnp.where(side == 3, spot, flat)

        @pl.when(way < 4)
        def _():
            land_c[q] = total[...].astype(bf)
            src = land_c.at[q]
            pl.when(way == 0)(lambda: remote(src, land_x.at[t], s_x, r_x.at[t], p.to_x).start())
            pl.when(way == 1)(lambda: remote(src, land_y.at[t], s_y, r_y.at[t], p.to_y).start())
            pl.when(way == 2)(lambda: remote(src, land_z.at[n], s_up, r_z.at[n], p.to_up).start())
            pl.when(way == 3)(
                lambda: remote(
                    src, land_z.at[below_to], s_down, r_z.at[below_to], p.to_down
                ).start()
            )

        @pl.when(way == 4)
        def _():
            for j in range(8):
                piece = total[:, j * TB : (j + 1) * TB]
                tiles[8 * k + j] = piece
                grp[fs * 24 + 8 * k + j] = piece.astype(bf)
            mine = grp.at[pl.ds(fs * 24 + 8 * k, 8)]
            remote(mine, mine, s_e, r_e.at[fs * 3 + k], p.to_x).start()
            remote(mine, mine, s_e2, r_e.at[fs * 3 + k], p.to_core).start()

    def hand_on(k):
        fx = (fs + 2) % 4
        block = grp.at[pl.ds(fx * 24 + 8 * k, 8)]
        wait_for(block, r_e.at[fx * 3 + k])
        remote(block, block, s_e2, r_e.at[fx * 3 + k], p.to_core).start()

    def vec_step(n):
        if n == 0:
            sums = vsum[...].sum(axis=1)
            for j in range(8):
                vout[pl.ds(12 * j, 12)] = sums[:, j * TB : (j + 1) * TB]
        else:
            wait_for(vland.at[n - 1], r_v.at[n - 1])
            vout[...] = vout[...] + vland[n - 1]
        if n < 5:
            vland[5 + n] = vout[...]
            remote(vland.at[5 + n], vland.at[n], s_v.at[n], r_v.at[n], p.doubling[n]).start()

    def run_codes(lists):
        longest = max(len(codes) for codes in lists)
        if longest == 0:
            return

        def of_plane(values):
            got = values[0]
            for here in range(1, ZN):
                if values[here] != values[0]:
                    got = jnp.where(z == here, values[here], got)
            return got

        count = of_plane([len(codes) for codes in lists])
        table = [of_plane([codes[i] if i < len(codes) else 0 for codes in lists]) for i in range(longest)]

        def body(i, _):
            code = table[0]
            for j in range(1, longest):
                code = jnp.where(i == j, table[j], code)
            kind = code // 131072
            zp, k = code // 4 % 4, code % 4
            pl.when(kind == 0)(lambda: to_partner(zp, k, code // 8192 % 16, code // 64 % 2))
            pl.when(kind == 1)(lambda: octet_step(code, zp, k))
            pl.when(kind == 2)(lambda: hand_on(k))
            pl.when(kind == 3)(lambda: start_deal(p, res, res_back, s_res, r_res, l_res))
            pl.when(kind == 4)(lambda: start_deal(p, din, din_back, s_din, r_din, l_din))
            for n in range(6):
                pl.when(kind == 5 + n)(functools.partial(vec_step, n))
            return 0

        lax.fori_loop(0, count, body, 0)

    used = [0]

    def square(step):
        n = used[0]
        used[0] += 1
        wait_for(wb.at[n % slots], r_wb.at[n % slots])
        step()
        bring(n + slots)

    def compute(name):
        t = int(name[-1]) if name[-1].isdigit() else 0
        if name[:2] == "DB":
            if t == 0:
                takes[2].wait()
            square(lambda: f.down_back(t))
        elif name[:2] == "UB":
            if t == 0:
                takes[3].wait()
            square(lambda: f.up_back(t))
        elif name == "N1B":
            takes[4].wait()
            takes[5].wait()
            f.norm_one_back()
        elif name == "OB":
            square(f.out_back)
        elif name == "ATB":
            takes[6].wait()
            takes[7].wait()
            f.attend_back()
        else:
            square(lambda: f.project_back(t))

    takes[0].wait()
    takes[1].wait()
    parts = [backward_codes(here) for here in range(ZN)]
    for n in range(len(BACKWARD_STEPS) + 1):
        run_codes([codes[n] for codes in parts])
        if n < len(BACKWARD_STEPS):
            compute(BACKWARD_STEPS[n])

    end_deal(p, res, res_back, s_res, r_res, l_res)
    end_deal(p, din, din_back, s_din, r_din, l_din)
    for g in (p.x * 2 + 1 - c, (1 - p.x) * 2 + 1 - c):
        for k in range(3):
            wait_for(grp.at[pl.ds(g * 24 + 8 * k, 8)], r_e.at[g * 3 + k])

    for n in range(RING):
        wait_for(ring.at[0], s_ring.at[n])
    for n in range(5):
        wait_for(vland.at[5 + n], s_v.at[n])

    wait_for(grp.at[pl.ds(0, 24)], s_e)
    wait_for(grp.at[pl.ds(0, 48)], s_e2)

    def drain(here):
        ways = [code // 1024 % 8 for codes in parts[here] for code in codes if code // 131072 == 1]
        for way, sem in enumerate((s_x, s_y, s_up, s_down)):
            if ways.count(way):
                wait_for(land_c.at[pl.ds(0, ways.count(way))], sem)

    for here in range(ZN):
        pl.when(z == here)(functools.partial(drain, here))


def backward(wm, l3, d2, acc, gp, xh, rs, p3, q3, res, vsum, vec):
    dma = pltpu.SemaphoreType.DMA
    rows = d2.shape[0]
    vmem = pl.BlockSpec(memory_space=pltpu.VMEM)
    far = pl.BlockSpec(memory_space=pl.ANY)
    out = jax.ShapeDtypeStruct
    return pl.pallas_call(
        backward_kernel,
        out_shape=(
            out((24, TB, TB), f32),
            out((96, TB, TB), bf),
            out((96, TB), f32),
            out(res.shape, bf),
            out(res.shape, bf),
        ),
        in_specs=[far] * 10 + [vmem] * 2,
        out_specs=(vmem,) * 3 + (far,) * 2,
        scratch_shapes=[
            pltpu.VMEM(l3.shape, bf), pltpu.VMEM((9, rows, D), bf), pltpu.VMEM(acc.shape, f32),
            pltpu.VMEM(gp.shape, f32), pltpu.VMEM(xh.shape, f32), pltpu.VMEM(rs.shape, f32),
            pltpu.VMEM(p3.shape, f32), pltpu.VMEM(q3.shape, bf), pltpu.VMEM((8, rows, TB), bf),
            pltpu.VMEM(res.shape, bf), pltpu.VMEM((2, 8, TB, D), bf), pltpu.VMEM((12, 8, D), f32),
            pltpu.VMEM((48, TB, D), bf), pltpu.VMEM((SPOTS, TB, D), bf),
            pltpu.VMEM((SPOTS, TB, D), bf), pltpu.VMEM((30, TB, D), bf), pltpu.VMEM((RING, TB, D), bf),
            pltpu.VMEM((10, 96, TB), f32), pltpu.VMEM((TB, D), f32),
            dma((8,)), dma((2,)), dma((48,)), dma((SPOTS,)), dma((SPOTS,)), dma((30,)), dma((12,)), dma((5,)),
            dma((RING,)), dma, dma, dma, dma, dma, dma, dma((5,)),
            dma, dma((2 * ZN,)), dma, dma, dma((2 * ZN,)), dma,
        ],
        compiler_params=pltpu.CompilerParams(
            collective_id=1, has_side_effects=True, vmem_limit_bytes=62 * 2**20
        ),
        name="backward",
    )(wm, l3, d2, acc, gp, xh, rs, p3, q3, res, vsum, vec)


GROUP = 6


def halves(a):
    high = a.astype(bf)
    return high, (a - high.astype(f32)).astype(bf)


def wide(b):
    return jnp.concatenate(
        [jnp.concatenate(b, 1), jnp.concatenate([b[0], jnp.zeros_like(b[0])], 1)], 0
    )


def fine(a, b_wide):
    out = mul(jnp.concatenate(a, 1), b_wide)
    return out[:, :TB] + out[:, TB:]


def fine_t(a, b):
    wide_t = jnp.concatenate(
        [jnp.concatenate([b[0], b[0]], 1), jnp.concatenate([b[1], jnp.zeros_like(b[1])], 1)], 0
    )
    out = mul_t(jnp.concatenate(a, 1), wide_t)
    return out[:, :TB] + out[:, TB:]


def moments(first, second, grad):
    first = BETA_ONE * first + (1.0 - BETA_ONE) * grad
    second = BETA_TWO * second + (1.0 - BETA_TWO) * grad * grad
    hat = (first * (1.0 / (1.0 - BETA_ONE**STEP))) / (
        jnp.sqrt(second * (1.0 / (1.0 - BETA_TWO**STEP))) + ADAM_EPS
    )
    return first, second, hat


def adam_kernel(place, lane, pick, rate, *refs):
    masters = refs[:GROUP]
    grads, left, right, first, second, vec, vec_first, vec_second, vec_grad = refs[GROUP : GROUP + 9]
    new_first, new_second, new_tiles, new_low, vec_first_new, vec_second_new, new_vec = refs[GROUP + 9 :]
    step = pl.program_id(0)
    span = range(GROUP)
    ls = [halves(left[g]) for g in span]
    rs = [halves(right[g]) for g in span]
    grad = [grads[pick[step * GROUP + g]] for g in span]
    inner = [t_mul(jnp.concatenate(ls[g], 0), jnp.concatenate([grad[g]] * 2, 0)) for g in span]
    rwide = [wide(rs[g]) for g in span]
    rotated = [fine(halves(inner[g]), rwide[g]) for g in span]
    hats = []
    for g in span:
        first_now, second_now, hat = moments(first[g], second[g], rotated[g])
        new_first[g] = first_now
        new_second[g] = second_now
        hats.append(hat)
    outer = [fine(ls[g], wide(halves(hats[g]))) for g in span]
    update = [fine_t(halves(outer[g]), rs[g]) for g in span]
    for g in span:
        master = masters[g][0].astype(f32)
        fresh = master - rate[step * GROUP + g] * (update[g] + DECAY * master)
        new_tiles[g] = fresh
        new_low[g] = fresh.astype(bf)

    @pl.when(step == 0)
    def _():
        a, b, hat = moments(vec_first[...], vec_second[...], vec_grad[...])
        vec_first_new[...] = a
        vec_second_new[...] = b
        new_vec[...] = vec[...] - VEC_RATE * hat


def adam(place, lane, pick, rate, wm, grads, left, right, first, second, vec, vec_first, vec_second, vec_grad):
    count = left.shape[0]
    one = [
        pl.BlockSpec((1, TB, TB), functools.partial(lambda g, i, p, l, *_: (p[i * GROUP + g], 0, l[i * GROUP + g]), g))
        for g in range(GROUP)
    ]
    stack = pl.BlockSpec((GROUP, TB, TB), lambda i, *_: (i, 0, 0))
    whole = pl.BlockSpec(grads.shape, lambda i, *_: (0, 0, 0))
    small = pl.BlockSpec(vec.shape, lambda i, *_: (0, 0))
    tiles = jax.ShapeDtypeStruct(left.shape, f32)
    return pl.pallas_call(
        adam_kernel,
        out_shape=(tiles, tiles, tiles, jax.ShapeDtypeStruct(left.shape, bf)) + (jax.ShapeDtypeStruct(vec.shape, f32),) * 3,
        grid_spec=pltpu.PrefetchScalarGridSpec(
            num_scalar_prefetch=4,
            grid=(count // GROUP,),
            in_specs=one + [whole] + [stack] * 4 + [small] * 4,
            out_specs=[stack] * 4 + [small] * 3,
        ),
        compiler_params=pltpu.CompilerParams(vmem_limit_bytes=60 * 2**20),
        name="adam",
    )(place, lane, pick, rate, *([wm] * GROUP), grads, left, right, first, second, vec, vec_first, vec_second, vec_grad)


def per_device(
    tokens,
    cotangent,
    lengths,
    deal,
    weights,
    vectors,
    owners,
    left_basis,
    right_basis,
    first_moment,
    second_moment,
    vec_first,
    vec_second,
):
    dp_count = lax.axis_size("dp")
    fsdp_count = lax.axis_size("fsdp")
    dp_place = lax.axis_index("dp")
    fsdp_place = lax.axis_index("fsdp")
    micro_count = tokens.shape[0]
    my_place = dp_place * fsdp_count + fsdp_place
    quarter = lax.dynamic_index_in_dim(
        deal.reshape(micro_count, dp_count, fsdp_count), fsdp_place, axis=2, keepdims=False
    )
    quarter = quarter - fsdp_place * dp_count
    ordered = jnp.take_along_axis(tokens, quarter[:, :, None, None], axis=1)
    my_seq = lax.dynamic_index_in_dim(deal, my_place, axis=1, keepdims=False)
    my_length = jnp.take_along_axis(lengths, my_seq[:, None], axis=1)[:, 0]
    shard = weights.astype(jnp.bfloat16).reshape(3, 8, TB, TB).transpose(0, 2, 1, 3)
    shard = shard.reshape(3, TB, D)
    vec_shard = vectors.astype(jnp.bfloat16).astype(jnp.float32).reshape(3, TB)
    rows = micro_count * tokens.shape[2] * dp_count
    wm, l3, d2, acc, gp, xh, rs, p3, q3, res, vsum, vecs = forward(
        my_length,
        shard,
        jnp.pad(vec_shard, ((0, 5), (0, 0))),
        ordered,
        cotangent.reshape(rows, D),
    )
    tile_grads, group_grads, vec_total, back_result, back_grads = backward(
        wm, l3, d2, acc, gp, xh, rs, p3, q3, res, vsum, vecs
    )
    vec_total = vec_total.reshape(8, 12, TB).transpose(1, 0, 2).reshape(OCT, TB)
    vec_grads = lax.dynamic_slice_in_dim(vec_total, my_place * 3, 3, axis=0)
    restore = jnp.argsort(quarter, axis=1)
    out_tokens = jnp.take_along_axis(back_result, restore[:, :, None, None], axis=1)
    in_grad = jnp.take_along_axis(back_grads, restore[:, :, None, None], axis=1)
    new_first, new_second, new_tiles, new_low, vec_first_new, vec_second_new, new_vectors = adam(
        octet_place(owners // 8),
        owners % 8,
        owners - dp_place * (owners.shape[0] * fsdp_count),
        tile_rate(owners),
        wm,
        group_grads,
        left_basis,
        right_basis,
        first_moment,
        second_moment,
        vectors.reshape(3, TB),
        vec_first.reshape(3, TB),
        vec_second.reshape(3, TB),
        vec_grads,
    )
    return (
        out_tokens,
        in_grad,
        tile_grads,
        vec_grads.reshape(-1),
        new_first,
        new_second,
        new_tiles,
        new_low,
        vec_first_new.reshape(-1),
        vec_second_new.reshape(-1),
        new_vectors.reshape(-1),
    )


def solution(mesh):
    body = per_device if (mesh.shape["dp"], mesh.shape["fsdp"]) == (2 * ZN, 4) else per_device_any
    placed = (
        P(None, "fsdp", "dp", None),
        P(None, ("dp", "fsdp"), None, None),
        P(),
        P(),
        P(("dp", "fsdp"), None, None),
        P(("dp", "fsdp")),
        P(("dp", "fsdp")),
        P(("dp", "fsdp"), None, None),
        P(("dp", "fsdp"), None, None),
        P(("dp", "fsdp"), None, None),
        P(("dp", "fsdp"), None, None),
        P(("dp", "fsdp")),
        P(("dp", "fsdp")),
    )
    return jax.shard_map(
        body,
        mesh=mesh,
        in_specs=placed,
        out_specs=(
            P(None, "fsdp", "dp", None),
            P(None, "fsdp", "dp", None),
            P(("dp", "fsdp"), None, None),
            P(("dp", "fsdp")),
            P(("dp", "fsdp"), None, None),
            P(("dp", "fsdp"), None, None),
            P(("dp", "fsdp"), None, None),
            P(("dp", "fsdp"), None, None),
            P(("dp", "fsdp")),
            P(("dp", "fsdp")),
            P(("dp", "fsdp")),
        ),
        check_vma=False,
    )
```

```python
import functools

import jax
import jax.numpy as jnp
from jax import lax
from jax.experimental import pallas as pl
from jax.experimental.pallas import tpu as pltpu
from jax.sharding import PartitionSpec as P

D = 1024
HEADS = 16
HEAD_DIM = 64
FF = 4096
STEP = 10
TB = 128


EPS_NORM = 1e-05
BETA_ONE = 0.5
BETA_TWO = 0.6
ADAM_EPS = 1e-08
DECAY = 0.01
VEC_RATE = 0.2
PRECISION_HIGH = lax.Precision.HIGHEST


def cut_tiles(stacked, row_count, col_count, start_at):
    tile_count = row_count // TB * (col_count // TB)
    blocked = lax.slice_in_dim(stacked, start_at, start_at + tile_count, axis=0)
    blocked = blocked.reshape(row_count // TB, col_count // TB, TB, TB)
    return (blocked.transpose(0, 2, 1, 3).reshape(row_count, col_count), start_at + tile_count)


def unpack_mats(stacked):
    w_qkv, offset = cut_tiles(stacked, D, 3 * D, 0)
    w_out, offset = cut_tiles(stacked, D, D, offset)
    w_up, offset = cut_tiles(stacked, D, FF, offset)
    w_down, offset = cut_tiles(stacked, FF, D, offset)
    return (w_qkv, w_out, w_up, w_down)


def tiled_grad(left_rows, right_rows):
    row_total = left_rows.shape[0]
    left_split = left_rows.reshape(row_total, left_rows.shape[1] // TB, TB)
    right_split = right_rows.reshape(row_total, right_rows.shape[1] // TB, TB)
    blocked = jnp.einsum(
        "tai,tbj->abij", left_split, right_split, preferred_element_type=jnp.float32
    )
    return blocked.reshape(-1, TB, TB)


def unpack_vecs(vector):
    widths = [D, D, D, FF, D, D, D, D, D]
    pieces = []
    offset = 0
    for width_now in widths:
        pieces.append(vector[offset : offset + width_now])
        offset += width_now
    return tuple(pieces)


def tile_rate(tile_ids):
    qkv_end = 3 * D * D // (TB * TB)
    out_end = 4 * D * D // (TB * TB)
    up_end = (4 * D * D + D * FF) // (TB * TB)
    return jnp.where(
        tile_ids < qkv_end,
        D ** (-0.5),
        jnp.where(
            tile_ids < out_end,
            (HEAD_DIM / D) ** 0.5,
            jnp.where(tile_ids < up_end, D ** (-0.5), 1.5 * FF ** (-0.5)),
        ),
    ).astype(jnp.float32)


def norm_apply(values, gain_vec, shift_vec):
    center = values - jnp.mean(values, axis=-1, keepdims=True)
    spread = jnp.mean(center * center, axis=-1, keepdims=True)
    return center * lax.rsqrt(spread + EPS_NORM) * gain_vec + shift_vec


def exact_gelu(values):
    return jax.nn.gelu(values, approximate=False)


def split_heads(joined16):
    seq_rows = joined16.shape[0]
    query_heads = joined16[:, :D].reshape(seq_rows, HEADS, HEAD_DIM)
    key_heads = joined16[:, D : 2 * D].reshape(seq_rows, HEADS, HEAD_DIM)
    value_heads = joined16[:, 2 * D :].reshape(seq_rows, HEADS, HEAD_DIM)
    return (query_heads, key_heads, value_heads)


def masked_scores(query_heads, key_heads, in_length):
    scores = jnp.einsum(
        "qhd,khd->hqk", query_heads, key_heads, preferred_element_type=jnp.float32
    ) * HEAD_DIM ** (-0.5)
    return jnp.where(in_length[None, None, :], scores, -1e30)


def forward_pass(inputs16, length, matrices, vecs):
    w_qkv, w_out, w_up, w_down = matrices
    bias_q, bias_v, bias_out, bias_up, bias_down, gain_one, shift_one, gain_two, shift_two = vecs
    seq_rows = inputs16.shape[0]
    joined = jnp.dot(inputs16, w_qkv, preferred_element_type=jnp.float32)
    joined = joined + jnp.concatenate([bias_q, jnp.zeros_like(bias_q), bias_v])
    joined16 = joined.astype(jnp.bfloat16)
    query_heads, key_heads, value_heads = split_heads(joined16)
    in_length = jnp.arange(seq_rows) < length
    scores = masked_scores(query_heads, key_heads, in_length)
    row_top = jnp.max(scores, axis=-1, keepdims=True)
    exp_scores = jnp.exp(scores - row_top)
    row_total = jnp.sum(exp_scores, axis=-1, keepdims=True)
    attention16 = (exp_scores / row_total).astype(jnp.bfloat16)
    log_total = row_top + jnp.log(row_total)
    attended = jnp.einsum(
        "hqk,khd->qhd", attention16, value_heads, preferred_element_type=jnp.float32
    )
    attended16 = attended.reshape(seq_rows, D).astype(jnp.bfloat16)
    resid_one = (
        inputs16.astype(jnp.float32)
        + jnp.dot(attended16, w_out, preferred_element_type=jnp.float32)
        + bias_out
    )
    normed_one = norm_apply(resid_one, gain_one, shift_one)
    normed16 = normed_one.astype(jnp.bfloat16)
    hidden = jnp.dot(normed16, w_up, preferred_element_type=jnp.float32) + bias_up
    active16 = exact_gelu(hidden).astype(jnp.bfloat16)
    resid_two = (
        normed_one + jnp.dot(active16, w_down, preferred_element_type=jnp.float32) + bias_down
    )
    result = norm_apply(resid_two, gain_two, shift_two)
    result = jnp.where(in_length[:, None], result, 0.0).astype(jnp.bfloat16)
    kept = (
        joined16,
        log_total,
        attended16,
        resid_one,
        normed16,
        hidden,
        active16,
        resid_two,
        in_length,
    )
    return (result, kept)


def backward_pass(back16, inputs16, kept, matrices, vecs):
    w_qkv, w_out, w_up, w_down = matrices
    bias_q, bias_v, bias_out, bias_up, bias_down, gain_one, shift_one, gain_two, shift_two = vecs
    joined16, log_total, attended16, resid_one, normed16, hidden, active16, resid_two, in_length = (
        kept
    )
    seq_rows = inputs16.shape[0]
    back = jnp.where(in_length[:, None], back16.astype(jnp.float32), 0.0)
    unused_two, pull_two = jax.vjp(norm_apply, resid_two, gain_two, shift_two)
    d_resid_two, d_gain_two, d_shift_two = pull_two(back)
    d_down16 = d_resid_two.astype(jnp.bfloat16)
    d_active = jnp.einsum("to,io->ti", d_down16, w_down, preferred_element_type=jnp.float32)
    unused_gelu, pull_gelu = jax.vjp(exact_gelu, hidden)
    d_hidden = pull_gelu(d_active)[0]
    d_hidden16 = d_hidden.astype(jnp.bfloat16)
    d_normed = d_resid_two + jnp.einsum(
        "to,io->ti", d_hidden16, w_up, preferred_element_type=jnp.float32
    )
    unused_one, pull_one = jax.vjp(norm_apply, resid_one, gain_one, shift_one)
    d_resid_one, d_gain_one, d_shift_one = pull_one(d_normed)
    d_branch16 = d_resid_one.astype(jnp.bfloat16)
    d_attended = jnp.einsum("to,io->ti", d_branch16, w_out, preferred_element_type=jnp.float32)
    d_attended16 = d_attended.astype(jnp.bfloat16).reshape(seq_rows, HEADS, HEAD_DIM)
    query_heads, key_heads, value_heads = split_heads(joined16)
    scores = masked_scores(query_heads, key_heads, in_length)
    attention = jnp.exp(scores - log_total)
    attention16 = attention.astype(jnp.bfloat16)
    d_value = jnp.einsum(
        "hqk,qhd->khd", attention16, d_attended16, preferred_element_type=jnp.float32
    )
    d_attention = jnp.einsum(
        "qhd,khd->hqk", d_attended16, value_heads, preferred_element_type=jnp.float32
    )
    d_scores = attention * (d_attention - jnp.sum(attention * d_attention, axis=-1, keepdims=True))
    d_scores16 = d_scores.astype(jnp.bfloat16)
    d_query = jnp.einsum(
        "hqk,khd->qhd", d_scores16, key_heads, preferred_element_type=jnp.float32
    ) * HEAD_DIM ** (-0.5)
    d_key = jnp.einsum(
        "hqk,qhd->khd", d_scores16, query_heads, preferred_element_type=jnp.float32
    ) * HEAD_DIM ** (-0.5)
    d_query = d_query.reshape(seq_rows, D)
    d_key = d_key.reshape(seq_rows, D)
    d_value = d_value.reshape(seq_rows, D)
    d_joined16 = jnp.concatenate([d_query, d_key, d_value], axis=1).astype(jnp.bfloat16)
    d_inputs = d_resid_one + jnp.einsum(
        "to,io->ti", d_joined16, w_qkv, preferred_element_type=jnp.float32
    )
    vec_grad = jnp.concatenate(
        [
            jnp.sum(d_query, axis=0),
            jnp.sum(d_value, axis=0),
            jnp.sum(d_resid_one, axis=0),
            jnp.sum(d_hidden, axis=0),
            jnp.sum(d_resid_two, axis=0),
            d_gain_one,
            d_shift_one,
            d_gain_two,
            d_shift_two,
        ]
    )
    pairs = (d_joined16, attended16, d_branch16, normed16, d_hidden16, active16, d_down16)
    return (pairs, vec_grad, d_inputs.astype(jnp.bfloat16))


def rotate_in(left_side, matrix, right_side):
    inner = jnp.einsum(
        "pji,pjk->pik",
        left_side,
        matrix,
        precision=PRECISION_HIGH,
        preferred_element_type=jnp.float32,
    )
    return jnp.einsum(
        "pik,pkl->pil",
        inner,
        right_side,
        precision=PRECISION_HIGH,
        preferred_element_type=jnp.float32,
    )


def rotate_out(left_side, matrix, right_side):
    inner = jnp.einsum(
        "pij,pjk->pik",
        left_side,
        matrix,
        precision=PRECISION_HIGH,
        preferred_element_type=jnp.float32,
    )
    return jnp.einsum(
        "pik,plk->pil",
        inner,
        right_side,
        precision=PRECISION_HIGH,
        preferred_element_type=jnp.float32,
    )


def per_device_any(
    tokens,
    cotangent,
    lengths,
    deal,
    weights,
    vectors,
    owners,
    left_basis,
    right_basis,
    first_moment,
    second_moment,
    vec_first,
    vec_second,
):
    dp_count = lax.axis_size("dp")
    fsdp_count = lax.axis_size("fsdp")
    dp_place = lax.axis_index("dp")
    fsdp_place = lax.axis_index("fsdp")
    micro_count = tokens.shape[0]
    my_place = dp_place * fsdp_count + fsdp_place
    quarter = lax.dynamic_index_in_dim(
        deal.reshape(micro_count, dp_count, fsdp_count), fsdp_place, axis=2, keepdims=False
    )
    quarter = quarter - fsdp_place * dp_count
    ordered = jnp.take_along_axis(tokens, quarter[:, :, None, None], axis=1)
    dealt_rows = lax.all_to_all(ordered, "dp", split_axis=1, concat_axis=2, tiled=True)
    my_seq = lax.dynamic_index_in_dim(deal, my_place, axis=1, keepdims=False)
    my_length = jnp.take_along_axis(lengths, my_seq[:, None], axis=1)[:, 0]
    shard_low = (weights.astype(jnp.bfloat16), vectors.astype(jnp.bfloat16))
    whole_tiles, whole_vecs = (
        lax.all_gather(shard_low[0], ("dp", "fsdp"), axis=0, tiled=True),
        lax.all_gather(shard_low[1], ("dp", "fsdp"), axis=0, tiled=True),
    )
    mats_kept = unpack_mats(whole_tiles)
    vecs_kept = unpack_vecs(whole_vecs.astype(jnp.float32))
    all_pairs = []
    all_inputs = []
    vec_terms = []
    results = []
    input_grads = []
    for micro_index in range(micro_count):
        inputs16 = dealt_rows[micro_index, 0]
        matrices, vecs = (mats_kept, vecs_kept)
        result, kept = forward_pass(inputs16, my_length[micro_index], matrices, vecs)
        pairs, vec_term, d_inputs = backward_pass(
            cotangent[micro_index, 0], inputs16, kept, matrices, vecs
        )
        all_pairs.append(pairs)
        all_inputs.append(inputs16)
        vec_terms.append(vec_term)
        results.append(result)
        input_grads.append(d_inputs)

    def joined_rows(index):
        return jnp.concatenate([pairs[index] for pairs in all_pairs], axis=0)

    inputs_rows = jnp.concatenate(all_inputs, axis=0)
    tile_terms = jnp.concatenate(
        [
            tiled_grad(inputs_rows, joined_rows(0)),
            tiled_grad(joined_rows(1), joined_rows(2)),
            tiled_grad(joined_rows(3), joined_rows(4)),
            tiled_grad(joined_rows(5), joined_rows(6)),
        ],
        axis=0,
    )
    grad_vec = vec_terms[0]
    for vec_term in vec_terms[1:]:
        grad_vec = grad_vec + vec_term
    shard_tiles = weights.shape[0]
    tile_grads, vec_grads = (
        lax.psum_scatter(tile_terms, ("dp", "fsdp"), scatter_dimension=0, tiled=True),
        lax.psum_scatter(grad_vec, ("dp", "fsdp"), scatter_dimension=0, tiled=True),
    )
    group_grads, group_master = (
        lax.all_gather(tile_grads.astype(jnp.bfloat16), "fsdp", axis=0, tiled=True).astype(
            tile_grads.dtype
        ),
        lax.all_gather(weights.astype(jnp.bfloat16), "fsdp", axis=0, tiled=True).astype(
            weights.dtype
        ),
    )
    result_dealt = jnp.stack(results)[:, None]
    grads_dealt = jnp.stack(input_grads)[:, None]
    back_result, back_grads = (
        lax.all_to_all(result_dealt, "dp", split_axis=2, concat_axis=1, tiled=True),
        lax.all_to_all(grads_dealt, "dp", split_axis=2, concat_axis=1, tiled=True),
    )
    restore = jnp.argsort(quarter, axis=1)
    out_tokens = jnp.take_along_axis(back_result, restore[:, :, None, None], axis=1)
    in_grad = jnp.take_along_axis(back_grads, restore[:, :, None, None], axis=1)
    group_size = fsdp_count * shard_tiles
    pick_rows = owners - dp_place * group_size
    own_grads = jnp.take(group_grads, pick_rows, axis=0)
    own_master = jnp.take(group_master, pick_rows, axis=0)
    rates = tile_rate(owners)
    rotated = rotate_in(left_basis, own_grads, right_basis)
    new_first = BETA_ONE * first_moment + (1.0 - BETA_ONE) * rotated
    new_second = BETA_TWO * second_moment + (1.0 - BETA_TWO) * rotated * rotated
    first_hat = new_first / (1.0 - BETA_ONE**STEP)
    second_hat = new_second / (1.0 - BETA_TWO**STEP)
    step_rotated = first_hat / (jnp.sqrt(second_hat) + ADAM_EPS)
    update = rotate_out(left_basis, step_rotated, right_basis)
    new_tiles = own_master - rates[:, None, None] * (update + DECAY * own_master)
    vec_first_new = BETA_ONE * vec_first + (1.0 - BETA_ONE) * vec_grads
    vec_second_new = BETA_TWO * vec_second + (1.0 - BETA_TWO) * vec_grads * vec_grads
    vec_hat_one = vec_first_new / (1.0 - BETA_ONE**STEP)
    vec_hat_two = vec_second_new / (1.0 - BETA_TWO**STEP)
    new_vectors = vectors - VEC_RATE * vec_hat_one / (jnp.sqrt(vec_hat_two) + ADAM_EPS)
    return (
        out_tokens,
        in_grad,
        tile_grads,
        vec_grads,
        new_first,
        new_second,
        new_tiles,
        new_tiles.astype(jnp.bfloat16),
        vec_first_new,
        vec_second_new,
        new_vectors,
    )


CHUNK = 256
ROWS_AT_ONCE = 32
f32 = jnp.float32
bf = jnp.bfloat16


def mul(a, b):
    return jnp.dot(a, b, preferred_element_type=f32)


def mul_t(a, b):
    return lax.dot_general(a, b, (((1,), (1,)), ((), ())), preferred_element_type=f32)


def t_mul(a, b):
    return lax.dot_general(a, b, (((0,), (0,)), ((), ())), preferred_element_type=f32)


def column_chunks():
    return [slice(j * CHUNK, (j + 1) * CHUNK) for j in range(D // CHUNK)]


class Layer:
    def __init__(self, **refs):
        self.__dict__.update(refs)
        self.rows = self.l3.shape[1]
        self.seqs = self.rows // TB

    def left(self, first, count=8):
        return jnp.concatenate([self.l3[first + j] for j in range(count)], axis=1)

    def each_rows(self, fn):
        def body(i, _):
            fn(pl.ds(pl.multiple_of(i * ROWS_AT_ONCE, ROWS_AT_ONCE), ROWS_AT_ONCE), i)
            return 0

        lax.fori_loop(0, self.rows // ROWS_AT_ONCE, body, 0)

    def counted(self, i):
        per = TB // ROWS_AT_ONCE
        at = (i % per) * ROWS_AT_ONCE + lax.broadcasted_iota(jnp.int32, (ROWS_AT_ONCE, 1), 0)
        return at < self.lens[i // per]

    def add_sum(self, n, value, cols=slice(None)):
        self.vsum[n, :, cols] += value.reshape(value.shape[0] // 8, 8, value.shape[1]).sum(axis=0)

    def project(self, t):
        x = self.left(0)
        for j, cols in enumerate(column_chunks()):
            out = mul(x, self.wcols(t, cols))
            if t != 1:
                out = out + self.vec[pl.ds(0 if t == 0 else 1, 1), cols]
            out = out.astype(bf)
            for i in range(CHUNK // TB):
                self.q3[t, j * (CHUNK // TB) + i] = out[:, i * TB : (i + 1) * TB]

    def two(self, block):
        lane = lax.broadcasted_iota(jnp.int32, block.shape, 1)
        zero = jnp.zeros_like(block)
        return jnp.concatenate(
            [jnp.where(lane < HEAD_DIM, block, zero), jnp.where(lane < HEAD_DIM, zero, block)], axis=0
        )

    def one(self, stacked):
        top, low = stacked[:TB], stacked[TB:]
        lane = lax.broadcasted_iota(jnp.int32, top.shape, 1)
        return jnp.where(lane < HEAD_DIM, top, low)

    def attend(self):
        def body(b, _):
            at = pl.ds(pl.multiple_of(b * TB, TB), TB)
            key = lax.broadcasted_iota(jnp.int32, (2 * TB, TB), 1)
            seen = key < self.lens[b]
            for h in range(HEADS // 2):
                s = mul_t(self.two(self.q3[0, h, at]), self.q3[1, h, at]) * HEAD_DIM**-0.5
                s = jnp.where(seen, s, -1e30)
                e = jnp.exp(s - jnp.max(s, axis=1, keepdims=True))
                p = e * (1.0 / jnp.sum(e, axis=1, keepdims=True))
                self.p3[b, h] = p
                a = self.one(mul(p.astype(bf), self.q3[2, h, at]))
                self.l3[8 + h, at] = a.astype(bf)
            return 0

        lax.fori_loop(0, self.seqs, body, 0)

    def norm_one(self):
        a = self.left(8)
        for j, cols in enumerate(column_chunks()):
            x = jnp.concatenate([self.l3[2 * j], self.l3[2 * j + 1]], axis=1).astype(f32)
            self.xh[:, cols] = x + mul(a, self.wcols(3, cols)) + self.vec[pl.ds(2, 1), cols]

        def rows(at, i):
            r = self.xh[at]
            center = r - jnp.mean(r, axis=1, keepdims=True)
            scale = lax.rsqrt(jnp.mean(center * center, axis=1, keepdims=True) + EPS_NORM)
            hat = center * scale
            self.xh[at] = hat
            self.rs[at] = jnp.broadcast_to(scale, (ROWS_AT_ONCE, TB))
            u = hat * self.vec[pl.ds(8, 1)] + self.vec[pl.ds(9, 1)]
            self.acc[at] = u
            u16 = u.astype(bf)
            for j in range(8):
                self.l3[16 + j, at] = u16[:, j * TB : (j + 1) * TB]

        self.each_rows(rows)

    def up_begin(self, t):
        u = self.left(16, 4)
        for cols in column_chunks():
            self.gp[t, :, cols] = mul(u, self.wcols(4 + t, cols, 0)) + self.vec[pl.ds(3 + t, 1), cols]

    def up_end(self, t):
        u = self.left(20, 4)
        for cols in column_chunks():
            self.gp[t, :, cols] += mul(u, self.wcols(4 + t, cols, 1))

        def rows(at, i):
            h = self.gp[t, at]
            cdf = 0.5 + 0.5 * lax.erf(h * 0.7071067811865476)
            self.gp[t, at] = cdf + h * (0.3989422804014327 * jnp.exp(-0.5 * h * h))
            e = (h * cdf).astype(bf)
            for j in range(8):
                self.l3[24 + 8 * t + j, at] = e[:, j * TB : (j + 1) * TB]

        self.each_rows(rows)

    def down(self, t):
        e = self.left(24 + 8 * t)
        for cols in column_chunks():
            self.acc[:, cols] += mul(e, self.wcols(8 + t, cols))

    def norm_two(self):
        def rows(at, i):
            r = self.acc[at] + self.vec[pl.ds(7, 1)]
            center = r - jnp.mean(r, axis=1, keepdims=True)
            scale = lax.rsqrt(jnp.mean(center * center, axis=1, keepdims=True) + EPS_NORM)
            hat = center * scale
            live = self.counted(i)
            gain = self.vec[pl.ds(10, 1)]
            out = jnp.where(live, hat * gain + self.vec[pl.ds(11, 1)], 0.0).astype(bf)
            per = TB // ROWS_AT_ONCE
            slabs = ROWS_AT_ONCE // self.res.shape[2]
            self.res[i // per, pl.ds((i % per) * slabs, slabs)] = out.reshape(
                slabs, self.res.shape[2], D
            )
            dy = jnp.where(live, self.cot[at].astype(f32), 0.0)
            self.add_sum(10, dy * hat)
            self.add_sum(11, dy)
            g = dy * gain
            dr = scale * (
                g
                - jnp.mean(g, axis=1, keepdims=True)
                - hat * jnp.mean(g * hat, axis=1, keepdims=True)
            )
            self.add_sum(7, dr)
            self.acc[at] = dr
            self.d2[at] = dr.astype(bf)

        self.each_rows(rows)

    def down_back(self, t):
        d = self.r3[8]
        for cols in column_chunks():
            dh = mul_t(d, self.wrows(8 + t, cols)) * self.gp[t, :, cols]
            self.add_sum(3 + t, dh, cols)
            self.r3[4 + t, :, cols] = dh.astype(bf)

    def up_back(self, t):
        d = self.r3[4 + t]
        for cols in column_chunks():
            self.acc[:, cols] += mul_t(d, self.wrows(4 + t, cols))

    def norm_one_back(self):
        def rows(at, i):
            du, hat = self.acc[at], self.xh[at]
            self.add_sum(8, du * hat)
            self.add_sum(9, du)
            g = du * self.vec[pl.ds(8, 1)]
            dr = self.rs[at][:, :1] * (
                g
                - jnp.mean(g, axis=1, keepdims=True)
                - hat * jnp.mean(g * hat, axis=1, keepdims=True)
            )
            self.add_sum(2, dr)
            self.acc[at] = dr
            self.r3[3, at] = dr.astype(bf)

        self.each_rows(rows)

    def out_back(self):
        d = self.r3[3]
        for j, cols in enumerate(column_chunks()):
            da = mul_t(d, self.wrows(3, cols)).astype(bf)
            for i in range(CHUNK // TB):
                self.da3[j * (CHUNK // TB) + i] = da[:, i * TB : (i + 1) * TB]

    def attend_back(self):
        def body(b, _):
            at = pl.ds(pl.multiple_of(b * TB, TB), TB)
            for h in range(HEADS // 2):
                cols = slice(h * TB, (h + 1) * TB)
                p = self.p3[b, h]
                da = self.two(self.da3[h, at])
                dv = t_mul(p.astype(bf), da)
                pd = p * mul_t(da, self.q3[2, h, at])
                ds = (pd - p * jnp.sum(pd, axis=1, keepdims=True)).astype(bf)
                dq = self.one(mul(ds, self.q3[1, h, at])) * HEAD_DIM**-0.5
                dk = t_mul(ds, self.two(self.q3[0, h, at])) * HEAD_DIM**-0.5
                self.r3[0, at, cols] = dq.astype(bf)
                self.r3[1, at, cols] = dk.astype(bf)
                self.r3[2, at, cols] = dv.astype(bf)
                self.add_sum(0, dq, cols)
                self.add_sum(1, dv, cols)
            return 0

        lax.fori_loop(0, self.seqs, body, 0)

    def project_back(self, t):
        d = self.r3[t]
        for cols in column_chunks():
            value = self.acc[:, cols] + mul_t(d, self.wrows(t, cols))
            if t < 2:
                self.acc[:, cols] = value
            else:
                self.din[:, :, :, cols] = value.astype(bf).reshape(self.din.shape[:3] + (CHUNK,))


MESH = pl.DeviceIdType.MESH
ZN = 4
OCT = 96
RING = 8
SPOTS = 16


class Place:
    def __init__(self):
        self.dp = lax.axis_index("dp")
        self.fs = lax.axis_index("fsdp")
        self.z, self.y = self.dp // 2, self.dp % 2
        self.x, self.c = self.fs // 2, self.fs % 2
        self.to_x = (self.dp, (self.fs + 2) % 4)
        self.to_y = (self.z * 2 + 1 - self.y, self.fs)
        self.to_core = (self.dp, self.x * 2 + 1 - self.c)
        self.to_up = (self.dp + 2, self.fs)
        self.to_down = (self.dp - 2, self.fs)
        near = self.z + 1 - 2 * (self.z % 2)
        far = (self.z + 2) % ZN
        self.doubling = [
            self.to_core,
            self.to_x,
            self.to_y,
            (near * 2 + self.y, self.fs),
            (far * 2 + self.y, self.fs),
        ]

    def peer(self, j):
        return (self.dp + j) % (2 * ZN)

    def greet(self):
        bar = pltpu.get_barrier_semaphore()
        for dev in [self.to_x, self.to_core] + [(self.peer(j), self.fs) for j in range(1, 2 * ZN)]:
            pl.semaphore_signal(bar, inc=1, device_id=dev, device_id_type=MESH)
        pl.semaphore_wait(bar, 1 + 2 * ZN)

    def octet(self, dx, dy, zp, k, c=None):
        yy = self.y if dy == 0 else 1 - self.y
        xx = self.x if dx == 0 else 1 - self.x
        return ((zp * 2 + yy) * 4 + xx * 2 + (self.c if c is None else c)) * 3 + k

    def plane(self, table, i):
        zp = table[0][i]
        for n in range(1, ZN):
            zp = jnp.where(self.z == n, table[n][i], zp)
        return zp


def octet_place(o):
    return jnp.where(
        o < 24,
        (o % 3) * 8 + o // 3,
        jnp.where((o >= 32) & (o < 64), 32 + ((o - 32) % 4) * 8 + (o - 32) // 4, o),
    )


def left_block(o):
    return jnp.where(
        o < 24, o // 3, jnp.where(o < 32, o - 16, jnp.where(o < 64, 16 + (o - 32) // 4, o - 40))
    )


def right_block(o):
    return jnp.where(o < 24, o % 3, jnp.where(o < 32, 3, jnp.where(o < 64, 4 + (o - 32) % 4, 8)))


def wait_for(ref, sem):
    pltpu.make_async_copy(ref, ref, sem).wait()


def remote(src, dst, send_sem, recv_sem, dev):
    return pltpu.make_async_remote_copy(
        src_ref=src,
        dst_ref=dst,
        send_sem=send_sem,
        recv_sem=recv_sem,
        device_id=dev,
        device_id_type=MESH,
    )


def start_deal(p, src, dst, s_sem, r_sem, l_sem):
    for j in range(1, 2 * ZN):
        d = p.peer(j)
        remote(src.at[:, d], dst.at[:, p.dp], s_sem, r_sem.at[p.dp], (d, p.fs)).start()
    pltpu.make_async_copy(src.at[:, p.dp], dst.at[:, p.dp], l_sem).start()


def end_deal(p, src, dst, s_sem, r_sem, l_sem):
    for j in range(1, 2 * ZN):
        d = p.peer(j)
        wait_for(dst.at[:, d], r_sem.at[d])
    wait_for(dst.at[:, p.dp], l_sem)
    wait_for(src.at[:, pl.ds(0, 2 * ZN - 1)], s_sem)


FORWARD_STEPS = [
    "P0", "P1", "P2", "ATT", "N1", "UA0", "UA1", "UA2", "UA3",
    "UB0", "UB1", "UB2", "UB3", "D0", "D1", "D2", "D3", "N2",
]
FORWARD_NEEDS = {"P0": (0,), "N1": (1,), "UB0": (2,), "D1": (3,)}
FORWARD_ROUTES = [
    ["xyx", "zzx", "zzy", "zxy"],
    ["zzz", "xyx", "zzz", "zzz"],
    ["zzz", "zzz", "xyx", "zzz"],
    ["zxy", "zzy", "zzx", "xyx"],
]
FORWARD_PLANS = [
    [
        1, 600, 2, 0, 100, 601, 102, 200, 101, 11, 12, 112, 602, 111, 201, 603,
        10, 202, 300, 22, 122, 604, 110, 32, 20, 21, 132, 301, 120, 210, 302, 232,
        605, 211, 212, 222, 31, 131, 1000, 121, 310, 30, 1001, 312, 1002, 311, 1003, 332,
        220, 1004, 1005, 231, 322, 320, 1006, 1007, 130, 1008, 321, 221, 331, 1009, 1010, 330,
        1011, 230, 1012, 1013, 1014, 1015, 1016, 1017,
    ],
    [
        600, 12, 11, 112, 111, 601, 212, 1, 10, 101, 110, 2, 602, 21, 211, 102,
        22, 603, 0, 121, 32, 604, 100, 210, 201, 20, 31, 132, 120, 122, 131, 300,
        311, 30, 310, 200, 322, 202, 301, 320, 605, 302, 1000, 312, 1001, 220, 1002, 222,
        1003, 130, 232, 1004, 1005, 221, 1006, 321, 1007, 1008, 1009, 231, 1010, 1011, 330, 230,
        1012, 332, 331, 1013, 1014, 1015, 1016, 1017,
    ],
    [
        20, 21, 22, 122, 121, 222, 600, 12, 32, 221, 601, 602, 120, 112, 1, 11,
        111, 603, 30, 31, 220, 211, 10, 322, 2, 332, 0, 604, 101, 320, 110, 201,
        102, 100, 202, 212, 300, 311, 310, 132, 321, 605, 301, 210, 330, 130, 200, 302,
        331, 1000, 1001, 1002, 1003, 312, 131, 1004, 1005, 1006, 232, 1007, 1008, 230, 1009, 1010,
        231, 1011, 1012, 1013, 1014, 1015, 1016, 1017,
    ],
    [
        32, 132, 600, 31, 131, 601, 30, 130, 232, 21, 602, 121, 22, 122, 332, 12,
        603, 112, 1, 230, 101, 222, 231, 212, 604, 2, 102, 0, 100, 605, 201, 11,
        330, 331, 10, 202, 300, 312, 111, 20, 221, 302, 320, 200, 110, 301, 1000, 1001,
        1002, 311, 211, 322, 1003, 120, 210, 310, 1004, 321, 1005, 220, 1006, 1007, 1008, 1009,
        1010, 1011, 1012, 1013, 1014, 1015, 1016, 1017,
    ],
]


def along_z(here, zp, k=None):
    up = zp <= here < ZN - 1 and (k is None or FORWARD_ROUTES[here + 1][zp][k] == "z")
    down = zp >= here > 0 and (k is None or FORWARD_ROUTES[here - 1][zp][k] == "z")
    return (["u"] if up else []) + (["d"] if down else [])


def split_plan(plan):
    parts = [[]]
    for code in plan:
        if code >= 1000:
            parts.append([])
        else:
            parts[-1].append(code)
    return parts


def forward_kernel(
    lens, shard, vec, tok, cot,
    wm, l3_out, d2_out, acc_out, gp_out, xh_out, rs_out, p3_out, q3_out, res_out, vsum, vecs,
    wbuf, vbuf, xl, l3, d2, q3, p3, xh, rs, acc, gp, res,
    r_w, s_x, s_y, s_up, s_down, s_core, s_local, s_vec, r_vec, s_tok, r_tok, l_tok, s_out,
):
    p = Place()
    z = p.z
    p.greet()

    def wcols(n, cols, half=None):
        if half is None:
            return wbuf[8 * n : 8 * n + 8, :, cols].reshape(D, CHUNK)
        first = 8 * n + 4 * half
        return wbuf[first : first + 4, :, cols].reshape(D // 2, CHUNK)

    f = Layer(
        lens=lens, vec=vecs, l3=l3, d2=d2, vsum=vsum, q3=q3, p3=p3, xh=xh, rs=rs, acc=acc, gp=gp,
        res=res, cot=cot, wcols=wcols,
    )

    def ref_of(o):
        return wbuf.at[octet_place(o)]

    def wait(o):
        wait_for(ref_of(o), r_w.at[o])

    start_deal(p, tok, xl, s_tok, r_tok, l_tok)
    me = p.dp * 4 + p.fs
    vbuf[me] = vec[...]
    for k in range(3):
        wbuf[octet_place(p.octet(0, 0, z, k))] = shard[k]

    def vec_step(n):
        size = 2**n
        if n > 0:
            half = size // 2
            theirs = (me // half) * half
            theirs = theirs + half * (1 - 2 * (theirs // half % 2))
            wait_for(vbuf.at[pl.ds(theirs, half)], r_vec.at[n - 1])
        if n < 5:
            mine = vbuf.at[pl.ds((me // size) * size, size)]
            remote(mine, mine, s_vec.at[n], r_vec.at[n], p.doubling[n]).start()

    def vec_rows():
        for m in range(OCT):
            cols = slice((m % 8) * TB, (m % 8 + 1) * TB)
            vecs[m // 8 : m // 8 + 1, cols] = vbuf[m // 3, m % 3 : m % 3 + 1, :]

    sent = [dict(x=0, y=0, u=0, d=0, c=0) for _ in range(ZN)]
    way = dict(
        x=(p.to_x, s_x), y=(p.to_y, s_y), u=(p.to_up, s_up), d=(p.to_down, s_down),
        c=(p.to_core, s_core),
    )

    def item(here, kind, zp, k):
        if kind == 6:
            vec_step(k)
            return

        def send(o, *ways):
            ref = ref_of(o)
            for w in ways:
                dev, sem = way[w]
                remote(ref, ref, sem, r_w.at[o], dev).start()
                sent[here][w] += 1

        route = FORWARD_ROUTES[here][zp][k]
        if kind == 0:
            o = p.octet(0, 0, zp, k)
            if zp != here:
                wait(o)
            send(o, *along_z(here, zp))
        elif kind == 1:
            send(p.octet(0, 0, zp, k), "x", "y", "c")
        elif kind == 2:
            o = p.octet(0, 1, zp, k)
            wait(o)
            send(o, *(["x"] if route == "x" else []), "c")
            o = p.octet(1, 0, zp, k)
            wait(o)
            send(o, *(["y"] if route == "y" else []), "c")
        else:
            o = p.octet(1, 1, zp, k)
            wait(o)
            send(o, *along_z(here, zp, k), "c")

    def partner(zp):
        for dx in range(2):
            for dy in range(2):
                for k in range(3):
                    wait(p.octet(dx, dy, zp, k, 1 - p.c))

    outs = []

    def give(src, dst):
        copy = pltpu.make_async_copy(src, dst, s_out.at[len(outs)])
        copy.start()
        outs.append(copy)

    def give_square(n):
        give(wbuf.at[pl.ds(8 * n, 8)], wm.at[pl.ds(8 * n, 8)])

    def compute(name):
        t = int(name[-1]) if name[-1].isdigit() else 0
        if name == "P0":
            vec_rows()
            vsum[...] = jnp.zeros_like(vsum)
            end_deal(p, tok, xl, s_tok, r_tok, l_tok)
            for j in range(8):
                l3[j] = xl[:, :, :, j * TB : (j + 1) * TB].reshape(l3.shape[1], TB)
        if name[0] == "P":
            f.project(t)
            give_square(t)
        elif name == "ATT":
            f.attend()
            give(q3, q3_out)
            give(p3, p3_out)
        elif name == "N1":
            f.norm_one()
            give_square(3)
            give(xh, xh_out)
            give(rs, rs_out)
        elif name[:2] == "UA":
            f.up_begin(t)
        elif name[:2] == "UB":
            f.up_end(t)
            give_square(4 + t)
            give(gp.at[t], gp_out.at[t])
            if t == 3:
                give(l3, l3_out)
        elif name[0] == "D":
            f.down(t)
            give_square(8 + t)
        else:
            f.norm_two()
            give(d2, d2_out)
            give(acc, acc_out)
            give(res, res_out)

    parts = [split_plan(plan) for plan in FORWARD_PLANS]
    for n in range(len(FORWARD_STEPS) + 1):

        def run(here):
            for code in parts[here][n]:
                item(here, code // 100, code // 10 % 10, code % 10)

        for here in range(ZN):
            pl.when(z == here)(functools.partial(run, here))
        if n < len(FORWARD_STEPS):
            name = FORWARD_STEPS[n]
            for zp in FORWARD_NEEDS.get(name, ()):
                partner(zp)
            compute(name)

    for copy in outs:
        copy.wait()
    for n in range(5):
        wait_for(vbuf.at[pl.ds(0, 2**n)], s_vec.at[n])

    def drain(here):
        for w, n in sent[here].items():
            if n:
                wait_for(wbuf.at[pl.ds(0, n)], way[w][1])

    for here in range(ZN):
        pl.when(z == here)(functools.partial(drain, here))


def forward(lens, shard, vec, tok, cot):
    dma = pltpu.SemaphoreType.DMA
    rows = cot.shape[0]
    vmem = pl.BlockSpec(memory_space=pltpu.VMEM)
    far = pl.BlockSpec(memory_space=pl.ANY)
    out = jax.ShapeDtypeStruct
    stages = (
        out((56, rows, TB), bf),
        out((rows, D), bf),
        out((rows, D), f32),
        out((4, rows, D), f32),
        out((rows, D), f32),
        out((rows, TB), f32),
        out((rows // TB, 8, 2 * TB, TB), f32),
        out((3, 8, rows, TB), bf),
        out(tok.shape, bf),
    )
    scratch = [pltpu.VMEM(s.shape, s.dtype) for s in stages]
    l3, d2, acc, gp, xh, rs, p3, q3, res = scratch
    return pl.pallas_call(
        forward_kernel,
        out_shape=(out((OCT, TB, D), bf),) + stages + (out((12, 8, D), f32), out((12, D), f32)),
        in_specs=[pl.BlockSpec(memory_space=pltpu.SMEM)] + [vmem] * 4,
        out_specs=(far,) * 10 + (vmem,) * 2,
        scratch_shapes=[
            pltpu.VMEM((OCT, TB, D), bf), pltpu.VMEM((32, 8, TB), f32), pltpu.VMEM(tok.shape, bf),
            l3, d2, q3, p3, xh, rs, acc, gp, res,
            dma((OCT,)), dma, dma, dma, dma, dma, dma((3,)), dma((5,)), dma((5,)),
            dma, dma((2 * ZN,)), dma, dma((32,)),
        ],
        compiler_params=pltpu.CompilerParams(
            collective_id=0, has_side_effects=True, vmem_limit_bytes=62 * 2**20
        ),
        name="forward",
    )(lens, shard, vec, tok, cot)


BACKWARD_STEPS = [
    "DB0", "DB1", "DB2", "DB3", "UB0", "UB1", "UB2", "UB3",
    "N1B", "OB", "ATB", "PB0", "PB1", "PB2",
]
BACKWARD_ROUTES = [
    ["xyy", "zzx", "zzy", "zzx"],
    ["zzz", "xyy", "zzz", "zzz"],
    ["zzz", "zzz", "xyy", "zzz"],
    ["zzx", "zzy", "zzx", "xyy"],
]
BACKWARD_PLANS = [
    [
        31, 30, 1000, 131, 231, 1001, 130, 1002, 32, 230, 1003, 1004, 1005, 21, 1006, 1007,
        121, 132, 221, 330, 20, 22, 120, 220, 1008, 331, 122, 232, 1009, 1010, 10, 110,
        210, 0, 222, 12, 600, 332, 11, 601, 2, 111, 320, 102, 321, 1011, 112, 310,
        211, 1, 322, 100, 602, 202, 212, 101, 603, 200, 311, 312, 201, 1012, 500, 1013,
        300, 301, 604, 400, 302, 501, 605, 401, 402,
    ],
    [
        500, 30, 1000, 32, 230, 1001, 1002, 1003, 22, 132, 1004, 31, 1005, 122, 1006, 222,
        20, 1007, 130, 21, 1008, 12, 1009, 220, 1010, 232, 0, 1011, 231, 131, 1012, 1013,
        121, 2, 120, 600, 221, 330, 601, 10, 200, 11, 102, 1, 201, 110, 202, 332,
        100, 331, 111, 112, 101, 320, 210, 300, 321, 211, 212, 322, 310, 602, 301, 311,
        302, 603, 501, 312, 401, 604, 605, 400, 402,
    ],
    [
        32, 30, 1000, 1001, 1002, 500, 230, 1003, 1004, 1005, 1006, 1007, 1008, 12, 11, 232,
        1009, 112, 1010, 0, 2, 200, 212, 31, 20, 102, 211, 1011, 111, 10, 132, 21,
        1, 1012, 110, 201, 22, 600, 131, 210, 121, 601, 100, 101, 130, 301, 120, 231,
        330, 220, 202, 300, 122, 332, 602, 331, 221, 311, 1013, 310, 302, 222, 603, 312,
        501, 320, 321, 322, 604, 401, 400, 402, 605,
    ],
    [
        500, 1000, 1001, 1002, 1003, 21, 1004, 221, 1005, 121, 20, 1006, 1007, 220, 1008, 11,
        120, 10, 211, 1009, 210, 111, 1010, 1, 110, 600, 201, 0, 12, 100, 2, 200,
        301, 22, 31, 112, 102, 122, 101, 310, 32, 30, 300, 132, 212, 202, 311, 601,
        1011, 320, 130, 232, 302, 1012, 312, 131, 1013, 231, 321, 602, 222, 603, 331, 230,
        332, 322, 401, 604, 501, 330, 402, 605, 400,
    ],
]


def backward_codes(here):
    routes = BACKWARD_ROUTES
    spots = {}
    for way in "xy":
        pairs = [(zp, k) for zp in range(ZN) for k in range(3) if routes[here][zp][k] == way]
        spots.update({pair: n for n, pair in enumerate(pairs)})

    def octet(side, zp, k):
        dx, dy = side % 2, side // 2
        own = zp == here
        route = routes[here][zp][k]
        code = k + 4 * zp + 16 * side + 131072
        along = "u" if zp > here else "d"
        if side == 0:
            code += 64 + 128
            way = "f" if own else along
        elif side == 1:
            code += 128 * (route == "y")
            way = "x"
        elif side == 2:
            code += 64 * (route == "x")
            way = "y"
        else:
            way = along if route == "z" else route
        if side in (0, 3):
            for step, there, bit in ((1, here - 1, 256), (-1, here + 1, 512)):
                if 0 <= there < ZN and (zp - here) * step >= 0:
                    code += bit * (side == 0 or routes[there][zp][k] == "z")
        return code + 1024 * "xyudf".index(way) + 8192 * spots.get((zp, k), 0)

    parts, first = [[]], 0
    for item in BACKWARD_PLANS[here]:
        if item >= 1000:
            parts.append([])
            continue
        kind, zp, k = item // 100, item // 10 % 10, item % 10
        if kind == 0:
            parts[-1].append(k + 4 * zp + 64 * (first >= 2) + 8192 * (first % 2))
            first += 1
        elif kind == 1:
            parts[-1].append(octet(3, zp, k))
        elif kind == 2:
            parts[-1] += [octet(2, zp, k), octet(1, zp, k)]
        elif kind == 3:
            parts[-1].append(octet(0, zp, k))
        elif kind == 4:
            parts[-1].append(131072 * 2 + k)
        elif kind == 5:
            parts[-1].append(131072 * (3 + k))
        else:
            parts[-1].append(131072 * (5 + k))
    return parts


def backward_kernel(
    wm, l3_in, d2_in, acc_in, gp_in, xh_in, rs_in, p3_in, q3_in, res, vsum_in, vec,
    tiles, grp, vout, res_back, din_back,
    l3, r3, acc, gp, xh, rs, p3, q3, da3, din, wb, vsum,
    land_c, land_x, land_y, land_z, ring, vland, total,
    r_in, r_wb, r_c, r_x, r_y, r_z, r_e, r_v, s_ring, s_x, s_y, s_up, s_down, s_e, s_e2, s_v,
    s_res, r_res, l_res, s_din, r_din, l_din,
):
    p = Place()
    z, c, fs = p.z, p.c, p.fs
    weights = [8, 9, 10, 11, 4, 5, 6, 7, 3, 0, 1, 2]
    slots = wb.shape[0]

    def bring(n):
        if n < len(weights):
            pltpu.make_async_copy(
                wm.at[pl.ds(8 * weights[n], 8)], wb.at[n % slots], r_wb.at[n % slots]
            ).start()

    pairs = [(d2_in, r3.at[8]), (l3_in, l3)]
    pairs += [(gp_in.at[t], gp.at[t]) for t in range(4)]
    pairs += [(acc_in, acc), (xh_in, xh), (rs_in, rs), (p3_in, p3), (q3_in, q3)]
    takes = [pltpu.make_async_copy(src, dst, r_in.at[n]) for n, (src, dst) in enumerate(pairs)]
    for n, copy in enumerate(takes):
        copy.start()
        if 2 <= n < 2 + slots:
            bring(n - 2)
    vsum[...] = vsum_in[...]
    p.greet()

    def wrows(n, rows):
        at = slice(rows.start // TB, rows.stop // TB)
        return wb[weights.index(n) % slots, at].reshape(CHUNK, D)

    f = Layer(
        vec=vec, l3=l3, r3=r3, vsum=vsum, q3=q3, p3=p3, da3=da3, xh=xh, rs=rs, acc=acc, gp=gp,
        din=din, wrows=wrows,
    )

    def part(o):
        return t_mul(l3[left_block(o)], r3[right_block(o)])

    def add(land, sem, n):
        wait_for(land.at[n], sem.at[n])
        total[...] += land[n].astype(f32)

    def to_partner(zp, k, slot, again):
        def body(j, _):
            yy, xx = j % 2, j // 2
            o = ((zp * 2 + yy) * 4 + xx * 2 + (1 - c)) * 3 + k
            n = slot * 4 + j
            value = part(o).astype(bf)
            pl.when(again == 1)(lambda: wait_for(ring.at[0], s_ring.at[n]))
            ring[n] = value
            q = ((jnp.where(yy == p.y, 0, 2) + jnp.where(xx == p.x, 0, 1)) * ZN + zp) * 3 + k
            remote(ring.at[n], land_c.at[q], s_ring.at[n], r_c.at[q], p.to_core).start()
            return 0

        lax.fori_loop(0, 4, body, 0)

    def octet_step(code, zp, k):
        side = code // 16 % 4
        dx, dy = side % 2, side // 2
        corner = side // 3
        q = (side * ZN + zp) * 3 + k
        yy = p.y + dy * (1 - 2 * p.y)
        xx = p.x + dx * (1 - 2 * p.x)
        o = ((zp * 2 + yy) * 4 + xx * 2 + c) * 3 + k
        wait_for(land_c.at[q], r_c.at[q])
        total[...] = part(o) + land_c[q].astype(f32)
        spot = 12 + code // 8192 % 16
        flat = zp * 3 + k
        column = jnp.where(side == 0, flat, spot)
        n = corner * 12 + flat
        mine = 24 + corner * 3 + k
        above = jnp.where(zp == z, mine, n)
        below_to = jnp.where(zp == z - 1, mine, n)
        pl.when(code // 64 % 2 == 1)(functools.partial(add, land_x, r_x, column))
        pl.when(code // 128 % 2 == 1)(functools.partial(add, land_y, r_y, column))
        pl.when(code // 256 % 2 == 1)(functools.partial(add, land_z, r_z, n))
        pl.when(code // 512 % 2 == 1)(functools.partial(add, land_z, r_z, above))
        way = code // 1024 % 8
        t = jnp.where(side == 3, spot, flat)

        @pl.when(way < 4)
        def _():
            land_c[q] = total[...].astype(bf)
            src = land_c.at[q]
            pl.when(way == 0)(lambda: remote(src, land_x.at[t], s_x, r_x.at[t], p.to_x).start())
            pl.when(way == 1)(lambda: remote(src, land_y.at[t], s_y, r_y.at[t], p.to_y).start())
            pl.when(way == 2)(lambda: remote(src, land_z.at[n], s_up, r_z.at[n], p.to_up).start())
            pl.when(way == 3)(
                lambda: remote(
                    src, land_z.at[below_to], s_down, r_z.at[below_to], p.to_down
                ).start()
            )

        @pl.when(way == 4)
        def _():
            for j in range(8):
                piece = total[:, j * TB : (j + 1) * TB]
                tiles[8 * k + j] = piece
                grp[fs * 24 + 8 * k + j] = piece.astype(bf)
            mine = grp.at[pl.ds(fs * 24 + 8 * k, 8)]
            remote(mine, mine, s_e, r_e.at[fs * 3 + k], p.to_x).start()
            remote(mine, mine, s_e2, r_e.at[fs * 3 + k], p.to_core).start()

    def hand_on(k):
        fx = (fs + 2) % 4
        block = grp.at[pl.ds(fx * 24 + 8 * k, 8)]
        wait_for(block, r_e.at[fx * 3 + k])
        remote(block, block, s_e2, r_e.at[fx * 3 + k], p.to_core).start()

    def vec_step(n):
        if n == 0:
            sums = vsum[...].sum(axis=1)
            for j in range(8):
                vout[pl.ds(12 * j, 12)] = sums[:, j * TB : (j + 1) * TB]
        else:
            wait_for(vland.at[n - 1], r_v.at[n - 1])
            vout[...] = vout[...] + vland[n - 1]
        if n < 5:
            vland[5 + n] = vout[...]
            remote(vland.at[5 + n], vland.at[n], s_v.at[n], r_v.at[n], p.doubling[n]).start()

    def run_codes(lists):
        longest = max(len(codes) for codes in lists)
        if longest == 0:
            return

        def of_plane(values):
            got = values[0]
            for here in range(1, ZN):
                if values[here] != values[0]:
                    got = jnp.where(z == here, values[here], got)
            return got

        count = of_plane([len(codes) for codes in lists])
        table = [of_plane([codes[i] if i < len(codes) else 0 for codes in lists]) for i in range(longest)]

        def body(i, _):
            code = table[0]
            for j in range(1, longest):
                code = jnp.where(i == j, table[j], code)
            kind = code // 131072
            zp, k = code // 4 % 4, code % 4
            pl.when(kind == 0)(lambda: to_partner(zp, k, code // 8192 % 16, code // 64 % 2))
            pl.when(kind == 1)(lambda: octet_step(code, zp, k))
            pl.when(kind == 2)(lambda: hand_on(k))
            pl.when(kind == 3)(lambda: start_deal(p, res, res_back, s_res, r_res, l_res))
            pl.when(kind == 4)(lambda: start_deal(p, din, din_back, s_din, r_din, l_din))
            for n in range(6):
                pl.when(kind == 5 + n)(functools.partial(vec_step, n))
            return 0

        lax.fori_loop(0, count, body, 0)

    used = [0]

    def square(step):
        n = used[0]
        used[0] += 1
        wait_for(wb.at[n % slots], r_wb.at[n % slots])
        step()
        bring(n + slots)

    def compute(name):
        t = int(name[-1]) if name[-1].isdigit() else 0
        if name[:2] == "DB":
            takes[2 + t].wait()
            square(lambda: f.down_back(t))
        elif name[:2] == "UB":
            if t == 0:
                takes[6].wait()
            square(lambda: f.up_back(t))
        elif name == "N1B":
            takes[7].wait()
            takes[8].wait()
            f.norm_one_back()
        elif name == "OB":
            square(f.out_back)
        elif name == "ATB":
            takes[9].wait()
            takes[10].wait()
            f.attend_back()
        else:
            square(lambda: f.project_back(t))

    takes[0].wait()
    takes[1].wait()
    parts = [backward_codes(here) for here in range(ZN)]
    for n in range(len(BACKWARD_STEPS) + 1):
        run_codes([codes[n] for codes in parts])
        if n < len(BACKWARD_STEPS):
            compute(BACKWARD_STEPS[n])

    end_deal(p, res, res_back, s_res, r_res, l_res)
    end_deal(p, din, din_back, s_din, r_din, l_din)
    for g in (p.x * 2 + 1 - c, (1 - p.x) * 2 + 1 - c):
        for k in range(3):
            wait_for(grp.at[pl.ds(g * 24 + 8 * k, 8)], r_e.at[g * 3 + k])

    for n in range(RING):
        wait_for(ring.at[0], s_ring.at[n])
    for n in range(5):
        wait_for(vland.at[5 + n], s_v.at[n])

    wait_for(grp.at[pl.ds(0, 24)], s_e)
    wait_for(grp.at[pl.ds(0, 48)], s_e2)

    def drain(here):
        ways = [code // 1024 % 8 for codes in parts[here] for code in codes if code // 131072 == 1]
        for way, sem in enumerate((s_x, s_y, s_up, s_down)):
            if ways.count(way):
                wait_for(land_c.at[pl.ds(0, ways.count(way))], sem)

    for here in range(ZN):
        pl.when(z == here)(functools.partial(drain, here))


def backward(wm, l3, d2, acc, gp, xh, rs, p3, q3, res, vsum, vec):
    dma = pltpu.SemaphoreType.DMA
    rows = d2.shape[0]
    vmem = pl.BlockSpec(memory_space=pltpu.VMEM)
    far = pl.BlockSpec(memory_space=pl.ANY)
    out = jax.ShapeDtypeStruct
    return pl.pallas_call(
        backward_kernel,
        out_shape=(
            out((24, TB, TB), f32),
            out((96, TB, TB), bf),
            out((96, TB), f32),
            out(res.shape, bf),
            out(res.shape, bf),
        ),
        in_specs=[far] * 10 + [vmem] * 2,
        out_specs=(vmem,) * 3 + (far,) * 2,
        scratch_shapes=[
            pltpu.VMEM(l3.shape, bf), pltpu.VMEM((9, rows, D), bf), pltpu.VMEM(acc.shape, f32),
            pltpu.VMEM(gp.shape, f32), pltpu.VMEM(xh.shape, f32), pltpu.VMEM(rs.shape, f32),
            pltpu.VMEM(p3.shape, f32), pltpu.VMEM(q3.shape, bf), pltpu.VMEM((8, rows, TB), bf),
            pltpu.VMEM(res.shape, bf), pltpu.VMEM((2, 8, TB, D), bf), pltpu.VMEM((12, 8, D), f32),
            pltpu.VMEM((48, TB, D), bf), pltpu.VMEM((SPOTS, TB, D), bf),
            pltpu.VMEM((SPOTS, TB, D), bf), pltpu.VMEM((30, TB, D), bf), pltpu.VMEM((RING, TB, D), bf),
            pltpu.VMEM((10, 96, TB), f32), pltpu.VMEM((TB, D), f32),
            dma((11,)), dma((2,)), dma((48,)), dma((SPOTS,)), dma((SPOTS,)), dma((30,)), dma((12,)), dma((5,)),
            dma((RING,)), dma, dma, dma, dma, dma, dma, dma((5,)),
            dma, dma((2 * ZN,)), dma, dma, dma((2 * ZN,)), dma,
        ],
        compiler_params=pltpu.CompilerParams(
            collective_id=1, has_side_effects=True, vmem_limit_bytes=62 * 2**20
        ),
        name="backward",
    )(wm, l3, d2, acc, gp, xh, rs, p3, q3, res, vsum, vec)


GROUP = 6


def halves(a):
    high = a.astype(bf)
    return high, (a - high.astype(f32)).astype(bf)


def wide(b):
    return jnp.concatenate(
        [jnp.concatenate(b, 1), jnp.concatenate([b[0], jnp.zeros_like(b[0])], 1)], 0
    )


def fine(a, b_wide):
    out = mul(jnp.concatenate(a, 1), b_wide)
    return out[:, :TB] + out[:, TB:]


def fine_t(a, b):
    wide_t = jnp.concatenate(
        [jnp.concatenate([b[0], b[0]], 1), jnp.concatenate([b[1], jnp.zeros_like(b[1])], 1)], 0
    )
    out = mul_t(jnp.concatenate(a, 1), wide_t)
    return out[:, :TB] + out[:, TB:]


def moments(first, second, grad):
    first = BETA_ONE * first + (1.0 - BETA_ONE) * grad
    second = BETA_TWO * second + (1.0 - BETA_TWO) * grad * grad
    hat = (first * (1.0 / (1.0 - BETA_ONE**STEP))) / (
        jnp.sqrt(second * (1.0 / (1.0 - BETA_TWO**STEP))) + ADAM_EPS
    )
    return first, second, hat


def adam_kernel(place, lane, pick, rate, *refs):
    masters = refs[:GROUP]
    grads, left, right, first, second, vec, vec_first, vec_second, vec_grad = refs[GROUP : GROUP + 9]
    new_first, new_second, new_tiles, new_low, vec_first_new, vec_second_new, new_vec = refs[GROUP + 9 :]
    step = pl.program_id(0)
    span = range(GROUP)
    ls = [halves(left[g]) for g in span]
    rs = [halves(right[g]) for g in span]
    grad = [grads[pick[step * GROUP + g]] for g in span]
    inner = [t_mul(jnp.concatenate(ls[g], 0), jnp.concatenate([grad[g]] * 2, 0)) for g in span]
    rwide = [wide(rs[g]) for g in span]
    rotated = [fine(halves(inner[g]), rwide[g]) for g in span]
    hats = []
    for g in span:
        first_now, second_now, hat = moments(first[g], second[g], rotated[g])
        new_first[g] = first_now
        new_second[g] = second_now
        hats.append(hat)
    outer = [fine(ls[g], wide(halves(hats[g]))) for g in span]
    update = [fine_t(halves(outer[g]), rs[g]) for g in span]
    for g in span:
        master = masters[g][0].astype(f32)
        fresh = master - rate[step * GROUP + g] * (update[g] + DECAY * master)
        new_tiles[g] = fresh
        new_low[g] = fresh.astype(bf)

    @pl.when(step == 0)
    def _():
        a, b, hat = moments(vec_first[...], vec_second[...], vec_grad[...])
        vec_first_new[...] = a
        vec_second_new[...] = b
        new_vec[...] = vec[...] - VEC_RATE * hat


def adam(place, lane, pick, rate, wm, grads, left, right, first, second, vec, vec_first, vec_second, vec_grad):
    count = left.shape[0]
    one = [
        pl.BlockSpec((1, TB, TB), functools.partial(lambda g, i, p, l, *_: (p[i * GROUP + g], 0, l[i * GROUP + g]), g))
        for g in range(GROUP)
    ]
    stack = pl.BlockSpec((GROUP, TB, TB), lambda i, *_: (i, 0, 0))
    whole = pl.BlockSpec(grads.shape, lambda i, *_: (0, 0, 0))
    small = pl.BlockSpec(vec.shape, lambda i, *_: (0, 0))
    tiles = jax.ShapeDtypeStruct(left.shape, f32)
    return pl.pallas_call(
        adam_kernel,
        out_shape=(tiles, tiles, tiles, jax.ShapeDtypeStruct(left.shape, bf)) + (jax.ShapeDtypeStruct(vec.shape, f32),) * 3,
        grid_spec=pltpu.PrefetchScalarGridSpec(
            num_scalar_prefetch=4,
            grid=(count // GROUP,),
            in_specs=one + [whole] + [stack] * 4 + [small] * 4,
            out_specs=[stack] * 4 + [small] * 3,
        ),
        compiler_params=pltpu.CompilerParams(vmem_limit_bytes=60 * 2**20),
        name="adam",
    )(place, lane, pick, rate, *([wm] * GROUP), grads, left, right, first, second, vec, vec_first, vec_second, vec_grad)


def per_device(
    tokens,
    cotangent,
    lengths,
    deal,
    weights,
    vectors,
    owners,
    left_basis,
    right_basis,
    first_moment,
    second_moment,
    vec_first,
    vec_second,
):
    dp_count = lax.axis_size("dp")
    fsdp_count = lax.axis_size("fsdp")
    dp_place = lax.axis_index("dp")
    fsdp_place = lax.axis_index("fsdp")
    micro_count = tokens.shape[0]
    my_place = dp_place * fsdp_count + fsdp_place
    quarter = lax.dynamic_index_in_dim(
        deal.reshape(micro_count, dp_count, fsdp_count), fsdp_place, axis=2, keepdims=False
    )
    quarter = quarter - fsdp_place * dp_count
    ordered = jnp.take_along_axis(tokens, quarter[:, :, None, None], axis=1)
    my_seq = lax.dynamic_index_in_dim(deal, my_place, axis=1, keepdims=False)
    my_length = jnp.take_along_axis(lengths, my_seq[:, None], axis=1)[:, 0]
    shard = weights.astype(jnp.bfloat16).reshape(3, 8, TB, TB).transpose(0, 2, 1, 3)
    shard = shard.reshape(3, TB, D)
    vec_shard = vectors.astype(jnp.bfloat16).astype(jnp.float32).reshape(3, TB)
    rows = micro_count * tokens.shape[2] * dp_count
    wm, l3, d2, acc, gp, xh, rs, p3, q3, res, vsum, vecs = forward(
        my_length,
        shard,
        jnp.pad(vec_shard, ((0, 5), (0, 0))),
        ordered,
        cotangent.reshape(rows, D),
    )
    tile_grads, group_grads, vec_total, back_result, back_grads = backward(
        wm, l3, d2, acc, gp, xh, rs, p3, q3, res, vsum, vecs
    )
    vec_total = vec_total.reshape(8, 12, TB).transpose(1, 0, 2).reshape(OCT, TB)
    vec_grads = lax.dynamic_slice_in_dim(vec_total, my_place * 3, 3, axis=0)
    restore = jnp.argsort(quarter, axis=1)
    out_tokens = jnp.take_along_axis(back_result, restore[:, :, None, None], axis=1)
    in_grad = jnp.take_along_axis(back_grads, restore[:, :, None, None], axis=1)
    new_first, new_second, new_tiles, new_low, vec_first_new, vec_second_new, new_vectors = adam(
        octet_place(owners // 8),
        owners % 8,
        owners - dp_place * (owners.shape[0] * fsdp_count),
        tile_rate(owners),
        wm,
        group_grads,
        left_basis,
        right_basis,
        first_moment,
        second_moment,
        vectors.reshape(3, TB),
        vec_first.reshape(3, TB),
        vec_second.reshape(3, TB),
        vec_grads,
    )
    return (
        out_tokens,
        in_grad,
        tile_grads,
        vec_grads.reshape(-1),
        new_first,
        new_second,
        new_tiles,
        new_low,
        vec_first_new.reshape(-1),
        vec_second_new.reshape(-1),
        new_vectors.reshape(-1),
    )


def solution(mesh):
    body = per_device if (mesh.shape["dp"], mesh.shape["fsdp"]) == (2 * ZN, 4) else per_device_any
    placed = (
        P(None, "fsdp", "dp", None),
        P(None, ("dp", "fsdp"), None, None),
        P(),
        P(),
        P(("dp", "fsdp"), None, None),
        P(("dp", "fsdp")),
        P(("dp", "fsdp")),
        P(("dp", "fsdp"), None, None),
        P(("dp", "fsdp"), None, None),
        P(("dp", "fsdp"), None, None),
        P(("dp", "fsdp"), None, None),
        P(("dp", "fsdp")),
        P(("dp", "fsdp")),
    )
    return jax.shard_map(
        body,
        mesh=mesh,
        in_specs=placed,
        out_specs=(
            P(None, "fsdp", "dp", None),
            P(None, "fsdp", "dp", None),
            P(("dp", "fsdp"), None, None),
            P(("dp", "fsdp")),
            P(("dp", "fsdp"), None, None),
            P(("dp", "fsdp"), None, None),
            P(("dp", "fsdp"), None, None),
            P(("dp", "fsdp"), None, None),
            P(("dp", "fsdp")),
            P(("dp", "fsdp")),
            P(("dp", "fsdp")),
        ),
        check_vma=False,
    )
```

```python
import functools

import jax
import jax.numpy as jnp
from jax import lax
from jax.experimental import pallas as pl
from jax.experimental.pallas import tpu as pltpu
from jax.sharding import PartitionSpec as P

D = 1024
HEADS = 16
HEAD_DIM = 64
FF = 4096
STEP = 10
TB = 128


EPS_NORM = 1e-05
BETA_ONE = 0.5
BETA_TWO = 0.6
ADAM_EPS = 1e-08
DECAY = 0.01
VEC_RATE = 0.2
PRECISION_HIGH = lax.Precision.HIGHEST


def cut_tiles(stacked, row_count, col_count, start_at):
    tile_count = row_count // TB * (col_count // TB)
    blocked = lax.slice_in_dim(stacked, start_at, start_at + tile_count, axis=0)
    blocked = blocked.reshape(row_count // TB, col_count // TB, TB, TB)
    return (blocked.transpose(0, 2, 1, 3).reshape(row_count, col_count), start_at + tile_count)


def unpack_mats(stacked):
    w_qkv, offset = cut_tiles(stacked, D, 3 * D, 0)
    w_out, offset = cut_tiles(stacked, D, D, offset)
    w_up, offset = cut_tiles(stacked, D, FF, offset)
    w_down, offset = cut_tiles(stacked, FF, D, offset)
    return (w_qkv, w_out, w_up, w_down)


def tiled_grad(left_rows, right_rows):
    row_total = left_rows.shape[0]
    left_split = left_rows.reshape(row_total, left_rows.shape[1] // TB, TB)
    right_split = right_rows.reshape(row_total, right_rows.shape[1] // TB, TB)
    blocked = jnp.einsum(
        "tai,tbj->abij", left_split, right_split, preferred_element_type=jnp.float32
    )
    return blocked.reshape(-1, TB, TB)


def unpack_vecs(vector):
    widths = [D, D, D, FF, D, D, D, D, D]
    pieces = []
    offset = 0
    for width_now in widths:
        pieces.append(vector[offset : offset + width_now])
        offset += width_now
    return tuple(pieces)


def tile_rate(tile_ids):
    qkv_end = 3 * D * D // (TB * TB)
    out_end = 4 * D * D // (TB * TB)
    up_end = (4 * D * D + D * FF) // (TB * TB)
    return jnp.where(
        tile_ids < qkv_end,
        D ** (-0.5),
        jnp.where(
            tile_ids < out_end,
            (HEAD_DIM / D) ** 0.5,
            jnp.where(tile_ids < up_end, D ** (-0.5), 1.5 * FF ** (-0.5)),
        ),
    ).astype(jnp.float32)


def norm_apply(values, gain_vec, shift_vec):
    center = values - jnp.mean(values, axis=-1, keepdims=True)
    spread = jnp.mean(center * center, axis=-1, keepdims=True)
    return center * lax.rsqrt(spread + EPS_NORM) * gain_vec + shift_vec


def exact_gelu(values):
    return jax.nn.gelu(values, approximate=False)


def split_heads(joined16):
    seq_rows = joined16.shape[0]
    query_heads = joined16[:, :D].reshape(seq_rows, HEADS, HEAD_DIM)
    key_heads = joined16[:, D : 2 * D].reshape(seq_rows, HEADS, HEAD_DIM)
    value_heads = joined16[:, 2 * D :].reshape(seq_rows, HEADS, HEAD_DIM)
    return (query_heads, key_heads, value_heads)


def masked_scores(query_heads, key_heads, in_length):
    scores = jnp.einsum(
        "qhd,khd->hqk", query_heads, key_heads, preferred_element_type=jnp.float32
    ) * HEAD_DIM ** (-0.5)
    return jnp.where(in_length[None, None, :], scores, -1e30)


def forward_pass(inputs16, length, matrices, vecs):
    w_qkv, w_out, w_up, w_down = matrices
    bias_q, bias_v, bias_out, bias_up, bias_down, gain_one, shift_one, gain_two, shift_two = vecs
    seq_rows = inputs16.shape[0]
    joined = jnp.dot(inputs16, w_qkv, preferred_element_type=jnp.float32)
    joined = joined + jnp.concatenate([bias_q, jnp.zeros_like(bias_q), bias_v])
    joined16 = joined.astype(jnp.bfloat16)
    query_heads, key_heads, value_heads = split_heads(joined16)
    in_length = jnp.arange(seq_rows) < length
    scores = masked_scores(query_heads, key_heads, in_length)
    row_top = jnp.max(scores, axis=-1, keepdims=True)
    exp_scores = jnp.exp(scores - row_top)
    row_total = jnp.sum(exp_scores, axis=-1, keepdims=True)
    attention16 = (exp_scores / row_total).astype(jnp.bfloat16)
    log_total = row_top + jnp.log(row_total)
    attended = jnp.einsum(
        "hqk,khd->qhd", attention16, value_heads, preferred_element_type=jnp.float32
    )
    attended16 = attended.reshape(seq_rows, D).astype(jnp.bfloat16)
    resid_one = (
        inputs16.astype(jnp.float32)
        + jnp.dot(attended16, w_out, preferred_element_type=jnp.float32)
        + bias_out
    )
    normed_one = norm_apply(resid_one, gain_one, shift_one)
    normed16 = normed_one.astype(jnp.bfloat16)
    hidden = jnp.dot(normed16, w_up, preferred_element_type=jnp.float32) + bias_up
    active16 = exact_gelu(hidden).astype(jnp.bfloat16)
    resid_two = (
        normed_one + jnp.dot(active16, w_down, preferred_element_type=jnp.float32) + bias_down
    )
    result = norm_apply(resid_two, gain_two, shift_two)
    result = jnp.where(in_length[:, None], result, 0.0).astype(jnp.bfloat16)
    kept = (
        joined16,
        log_total,
        attended16,
        resid_one,
        normed16,
        hidden,
        active16,
        resid_two,
        in_length,
    )
    return (result, kept)


def backward_pass(back16, inputs16, kept, matrices, vecs):
    w_qkv, w_out, w_up, w_down = matrices
    bias_q, bias_v, bias_out, bias_up, bias_down, gain_one, shift_one, gain_two, shift_two = vecs
    joined16, log_total, attended16, resid_one, normed16, hidden, active16, resid_two, in_length = (
        kept
    )
    seq_rows = inputs16.shape[0]
    back = jnp.where(in_length[:, None], back16.astype(jnp.float32), 0.0)
    unused_two, pull_two = jax.vjp(norm_apply, resid_two, gain_two, shift_two)
    d_resid_two, d_gain_two, d_shift_two = pull_two(back)
    d_down16 = d_resid_two.astype(jnp.bfloat16)
    d_active = jnp.einsum("to,io->ti", d_down16, w_down, preferred_element_type=jnp.float32)
    unused_gelu, pull_gelu = jax.vjp(exact_gelu, hidden)
    d_hidden = pull_gelu(d_active)[0]
    d_hidden16 = d_hidden.astype(jnp.bfloat16)
    d_normed = d_resid_two + jnp.einsum(
        "to,io->ti", d_hidden16, w_up, preferred_element_type=jnp.float32
    )
    unused_one, pull_one = jax.vjp(norm_apply, resid_one, gain_one, shift_one)
    d_resid_one, d_gain_one, d_shift_one = pull_one(d_normed)
    d_branch16 = d_resid_one.astype(jnp.bfloat16)
    d_attended = jnp.einsum("to,io->ti", d_branch16, w_out, preferred_element_type=jnp.float32)
    d_attended16 = d_attended.astype(jnp.bfloat16).reshape(seq_rows, HEADS, HEAD_DIM)
    query_heads, key_heads, value_heads = split_heads(joined16)
    scores = masked_scores(query_heads, key_heads, in_length)
    attention = jnp.exp(scores - log_total)
    attention16 = attention.astype(jnp.bfloat16)
    d_value = jnp.einsum(
        "hqk,qhd->khd", attention16, d_attended16, preferred_element_type=jnp.float32
    )
    d_attention = jnp.einsum(
        "qhd,khd->hqk", d_attended16, value_heads, preferred_element_type=jnp.float32
    )
    d_scores = attention * (d_attention - jnp.sum(attention * d_attention, axis=-1, keepdims=True))
    d_scores16 = d_scores.astype(jnp.bfloat16)
    d_query = jnp.einsum(
        "hqk,khd->qhd", d_scores16, key_heads, preferred_element_type=jnp.float32
    ) * HEAD_DIM ** (-0.5)
    d_key = jnp.einsum(
        "hqk,qhd->khd", d_scores16, query_heads, preferred_element_type=jnp.float32
    ) * HEAD_DIM ** (-0.5)
    d_query = d_query.reshape(seq_rows, D)
    d_key = d_key.reshape(seq_rows, D)
    d_value = d_value.reshape(seq_rows, D)
    d_joined16 = jnp.concatenate([d_query, d_key, d_value], axis=1).astype(jnp.bfloat16)
    d_inputs = d_resid_one + jnp.einsum(
        "to,io->ti", d_joined16, w_qkv, preferred_element_type=jnp.float32
    )
    vec_grad = jnp.concatenate(
        [
            jnp.sum(d_query, axis=0),
            jnp.sum(d_value, axis=0),
            jnp.sum(d_resid_one, axis=0),
            jnp.sum(d_hidden, axis=0),
            jnp.sum(d_resid_two, axis=0),
            d_gain_one,
            d_shift_one,
            d_gain_two,
            d_shift_two,
        ]
    )
    pairs = (d_joined16, attended16, d_branch16, normed16, d_hidden16, active16, d_down16)
    return (pairs, vec_grad, d_inputs.astype(jnp.bfloat16))


def rotate_in(left_side, matrix, right_side):
    inner = jnp.einsum(
        "pji,pjk->pik",
        left_side,
        matrix,
        precision=PRECISION_HIGH,
        preferred_element_type=jnp.float32,
    )
    return jnp.einsum(
        "pik,pkl->pil",
        inner,
        right_side,
        precision=PRECISION_HIGH,
        preferred_element_type=jnp.float32,
    )


def rotate_out(left_side, matrix, right_side):
    inner = jnp.einsum(
        "pij,pjk->pik",
        left_side,
        matrix,
        precision=PRECISION_HIGH,
        preferred_element_type=jnp.float32,
    )
    return jnp.einsum(
        "pik,plk->pil",
        inner,
        right_side,
        precision=PRECISION_HIGH,
        preferred_element_type=jnp.float32,
    )


def per_device_any(
    tokens,
    cotangent,
    lengths,
    deal,
    weights,
    vectors,
    owners,
    left_basis,
    right_basis,
    first_moment,
    second_moment,
    vec_first,
    vec_second,
):
    dp_count = lax.axis_size("dp")
    fsdp_count = lax.axis_size("fsdp")
    dp_place = lax.axis_index("dp")
    fsdp_place = lax.axis_index("fsdp")
    micro_count = tokens.shape[0]
    my_place = dp_place * fsdp_count + fsdp_place
    quarter = lax.dynamic_index_in_dim(
        deal.reshape(micro_count, dp_count, fsdp_count), fsdp_place, axis=2, keepdims=False
    )
    quarter = quarter - fsdp_place * dp_count
    ordered = jnp.take_along_axis(tokens, quarter[:, :, None, None], axis=1)
    dealt_rows = lax.all_to_all(ordered, "dp", split_axis=1, concat_axis=2, tiled=True)
    my_seq = lax.dynamic_index_in_dim(deal, my_place, axis=1, keepdims=False)
    my_length = jnp.take_along_axis(lengths, my_seq[:, None], axis=1)[:, 0]
    shard_low = (weights.astype(jnp.bfloat16), vectors.astype(jnp.bfloat16))
    whole_tiles, whole_vecs = (
        lax.all_gather(shard_low[0], ("dp", "fsdp"), axis=0, tiled=True),
        lax.all_gather(shard_low[1], ("dp", "fsdp"), axis=0, tiled=True),
    )
    mats_kept = unpack_mats(whole_tiles)
    vecs_kept = unpack_vecs(whole_vecs.astype(jnp.float32))
    all_pairs = []
    all_inputs = []
    vec_terms = []
    results = []
    input_grads = []
    for micro_index in range(micro_count):
        inputs16 = dealt_rows[micro_index, 0]
        matrices, vecs = (mats_kept, vecs_kept)
        result, kept = forward_pass(inputs16, my_length[micro_index], matrices, vecs)
        pairs, vec_term, d_inputs = backward_pass(
            cotangent[micro_index, 0], inputs16, kept, matrices, vecs
        )
        all_pairs.append(pairs)
        all_inputs.append(inputs16)
        vec_terms.append(vec_term)
        results.append(result)
        input_grads.append(d_inputs)

    def joined_rows(index):
        return jnp.concatenate([pairs[index] for pairs in all_pairs], axis=0)

    inputs_rows = jnp.concatenate(all_inputs, axis=0)
    tile_terms = jnp.concatenate(
        [
            tiled_grad(inputs_rows, joined_rows(0)),
            tiled_grad(joined_rows(1), joined_rows(2)),
            tiled_grad(joined_rows(3), joined_rows(4)),
            tiled_grad(joined_rows(5), joined_rows(6)),
        ],
        axis=0,
    )
    grad_vec = vec_terms[0]
    for vec_term in vec_terms[1:]:
        grad_vec = grad_vec + vec_term
    shard_tiles = weights.shape[0]
    tile_grads, vec_grads = (
        lax.psum_scatter(tile_terms, ("dp", "fsdp"), scatter_dimension=0, tiled=True),
        lax.psum_scatter(grad_vec, ("dp", "fsdp"), scatter_dimension=0, tiled=True),
    )
    group_grads, group_master = (
        lax.all_gather(tile_grads.astype(jnp.bfloat16), "fsdp", axis=0, tiled=True).astype(
            tile_grads.dtype
        ),
        lax.all_gather(weights.astype(jnp.bfloat16), "fsdp", axis=0, tiled=True).astype(
            weights.dtype
        ),
    )
    result_dealt = jnp.stack(results)[:, None]
    grads_dealt = jnp.stack(input_grads)[:, None]
    back_result, back_grads = (
        lax.all_to_all(result_dealt, "dp", split_axis=2, concat_axis=1, tiled=True),
        lax.all_to_all(grads_dealt, "dp", split_axis=2, concat_axis=1, tiled=True),
    )
    restore = jnp.argsort(quarter, axis=1)
    out_tokens = jnp.take_along_axis(back_result, restore[:, :, None, None], axis=1)
    in_grad = jnp.take_along_axis(back_grads, restore[:, :, None, None], axis=1)
    group_size = fsdp_count * shard_tiles
    pick_rows = owners - dp_place * group_size
    own_grads = jnp.take(group_grads, pick_rows, axis=0)
    own_master = jnp.take(group_master, pick_rows, axis=0)
    rates = tile_rate(owners)
    rotated = rotate_in(left_basis, own_grads, right_basis)
    new_first = BETA_ONE * first_moment + (1.0 - BETA_ONE) * rotated
    new_second = BETA_TWO * second_moment + (1.0 - BETA_TWO) * rotated * rotated
    first_hat = new_first / (1.0 - BETA_ONE**STEP)
    second_hat = new_second / (1.0 - BETA_TWO**STEP)
    step_rotated = first_hat / (jnp.sqrt(second_hat) + ADAM_EPS)
    update = rotate_out(left_basis, step_rotated, right_basis)
    new_tiles = own_master - rates[:, None, None] * (update + DECAY * own_master)
    vec_first_new = BETA_ONE * vec_first + (1.0 - BETA_ONE) * vec_grads
    vec_second_new = BETA_TWO * vec_second + (1.0 - BETA_TWO) * vec_grads * vec_grads
    vec_hat_one = vec_first_new / (1.0 - BETA_ONE**STEP)
    vec_hat_two = vec_second_new / (1.0 - BETA_TWO**STEP)
    new_vectors = vectors - VEC_RATE * vec_hat_one / (jnp.sqrt(vec_hat_two) + ADAM_EPS)
    return (
        out_tokens,
        in_grad,
        tile_grads,
        vec_grads,
        new_first,
        new_second,
        new_tiles,
        new_tiles.astype(jnp.bfloat16),
        vec_first_new,
        vec_second_new,
        new_vectors,
    )


CHUNK = 256
ROWS_AT_ONCE = 32
f32 = jnp.float32
bf = jnp.bfloat16


def mul(a, b):
    return jnp.dot(a, b, preferred_element_type=f32)


def mul_t(a, b):
    return lax.dot_general(a, b, (((1,), (1,)), ((), ())), preferred_element_type=f32)


def t_mul(a, b):
    return lax.dot_general(a, b, (((0,), (0,)), ((), ())), preferred_element_type=f32)


def column_chunks():
    return [slice(j * CHUNK, (j + 1) * CHUNK) for j in range(D // CHUNK)]


class Layer:
    def __init__(self, **refs):
        self.__dict__.update(refs)
        self.rows = self.l3.shape[1]
        self.seqs = self.rows // TB

    def left(self, first, count=8):
        return jnp.concatenate([self.l3[first + j] for j in range(count)], axis=1)

    def each_rows(self, fn):
        def body(i, _):
            fn(pl.ds(pl.multiple_of(i * ROWS_AT_ONCE, ROWS_AT_ONCE), ROWS_AT_ONCE), i)
            return 0

        lax.fori_loop(0, self.rows // ROWS_AT_ONCE, body, 0)

    def counted(self, i):
        per = TB // ROWS_AT_ONCE
        at = (i % per) * ROWS_AT_ONCE + lax.broadcasted_iota(jnp.int32, (ROWS_AT_ONCE, 1), 0)
        return at < self.lens[i // per]

    def add_sum(self, n, value, cols=slice(None)):
        self.vsum[n, :, cols] += value.reshape(value.shape[0] // 8, 8, value.shape[1]).sum(axis=0)

    def project(self, t):
        x = self.left(0)
        for j, cols in enumerate(column_chunks()):
            out = mul(x, self.wcols(t, cols))
            if t != 1:
                out = out + self.vec[pl.ds(0 if t == 0 else 1, 1), cols]
            out = out.astype(bf)
            for i in range(CHUNK // TB):
                self.q3[t, j * (CHUNK // TB) + i] = out[:, i * TB : (i + 1) * TB]

    def two(self, block):
        lane = lax.broadcasted_iota(jnp.int32, block.shape, 1)
        zero = jnp.zeros_like(block)
        return jnp.concatenate(
            [jnp.where(lane < HEAD_DIM, block, zero), jnp.where(lane < HEAD_DIM, zero, block)], axis=0
        )

    def one(self, stacked):
        top, low = stacked[:TB], stacked[TB:]
        lane = lax.broadcasted_iota(jnp.int32, top.shape, 1)
        return jnp.where(lane < HEAD_DIM, top, low)

    def attend(self):
        def body(b, _):
            at = pl.ds(pl.multiple_of(b * TB, TB), TB)
            key = lax.broadcasted_iota(jnp.int32, (2 * TB, TB), 1)
            seen = key < self.lens[b]
            for h in range(HEADS // 2):
                s = mul_t(self.two(self.q3[0, h, at]), self.q3[1, h, at]) * HEAD_DIM**-0.5
                s = jnp.where(seen, s, -1e30)
                e = jnp.exp(s - jnp.max(s, axis=1, keepdims=True))
                p = e * (1.0 / jnp.sum(e, axis=1, keepdims=True))
                self.p3[b, h] = p
                a = self.one(mul(p.astype(bf), self.q3[2, h, at]))
                self.l3[8 + h, at] = a.astype(bf)
            return 0

        lax.fori_loop(0, self.seqs, body, 0)

    def norm_one(self):
        a = self.left(8)
        for j, cols in enumerate(column_chunks()):
            x = jnp.concatenate([self.l3[2 * j], self.l3[2 * j + 1]], axis=1).astype(f32)
            self.xh[:, cols] = x + mul(a, self.wcols(3, cols)) + self.vec[pl.ds(2, 1), cols]

        def rows(at, i):
            r = self.xh[at]
            center = r - jnp.mean(r, axis=1, keepdims=True)
            scale = lax.rsqrt(jnp.mean(center * center, axis=1, keepdims=True) + EPS_NORM)
            hat = center * scale
            self.xh[at] = hat
            self.rs[at] = jnp.broadcast_to(scale, (ROWS_AT_ONCE, TB))
            u = hat * self.vec[pl.ds(8, 1)] + self.vec[pl.ds(9, 1)]
            self.acc[at] = u
            u16 = u.astype(bf)
            for j in range(8):
                self.l3[16 + j, at] = u16[:, j * TB : (j + 1) * TB]

        self.each_rows(rows)

    def up_begin(self, t):
        u = self.left(16, 4)
        for cols in column_chunks():
            self.gp[t, :, cols] = mul(u, self.wcols(4 + t, cols, 0)) + self.vec[pl.ds(3 + t, 1), cols]

    def up_end(self, t):
        u = self.left(20, 4)
        for cols in column_chunks():
            self.gp[t, :, cols] += mul(u, self.wcols(4 + t, cols, 1))

        def rows(at, i):
            h = self.gp[t, at]
            cdf = 0.5 + 0.5 * lax.erf(h * 0.7071067811865476)
            self.gp[t, at] = cdf + h * (0.3989422804014327 * jnp.exp(-0.5 * h * h))
            e = (h * cdf).astype(bf)
            for j in range(8):
                self.l3[24 + 8 * t + j, at] = e[:, j * TB : (j + 1) * TB]

        self.each_rows(rows)

    def down(self, t):
        e = self.left(24 + 8 * t)
        for cols in column_chunks():
            self.acc[:, cols] += mul(e, self.wcols(8 + t, cols))

    def norm_two(self):
        def rows(at, i):
            r = self.acc[at] + self.vec[pl.ds(7, 1)]
            center = r - jnp.mean(r, axis=1, keepdims=True)
            scale = lax.rsqrt(jnp.mean(center * center, axis=1, keepdims=True) + EPS_NORM)
            hat = center * scale
            live = self.counted(i)
            gain = self.vec[pl.ds(10, 1)]
            out = jnp.where(live, hat * gain + self.vec[pl.ds(11, 1)], 0.0).astype(bf)
            per = TB // ROWS_AT_ONCE
            slabs = ROWS_AT_ONCE // self.res.shape[2]
            self.res[i // per, pl.ds((i % per) * slabs, slabs)] = out.reshape(
                slabs, self.res.shape[2], D
            )
            dy = jnp.where(live, self.cot[at].astype(f32), 0.0)
            self.add_sum(10, dy * hat)
            self.add_sum(11, dy)
            g = dy * gain
            dr = scale * (
                g
                - jnp.mean(g, axis=1, keepdims=True)
                - hat * jnp.mean(g * hat, axis=1, keepdims=True)
            )
            self.add_sum(7, dr)
            self.acc[at] = dr
            self.d2[at] = dr.astype(bf)

        self.each_rows(rows)

    def down_back(self, t):
        d = self.r3[8]
        for cols in column_chunks():
            dh = mul_t(d, self.wrows(8 + t, cols)) * self.gp[t, :, cols]
            self.add_sum(3 + t, dh, cols)
            self.r3[4 + t, :, cols] = dh.astype(bf)

    def up_back(self, t):
        d = self.r3[4 + t]
        for cols in column_chunks():
            self.acc[:, cols] += mul_t(d, self.wrows(4 + t, cols))

    def norm_one_back(self):
        def rows(at, i):
            du, hat = self.acc[at], self.xh[at]
            self.add_sum(8, du * hat)
            self.add_sum(9, du)
            g = du * self.vec[pl.ds(8, 1)]
            dr = self.rs[at][:, :1] * (
                g
                - jnp.mean(g, axis=1, keepdims=True)
                - hat * jnp.mean(g * hat, axis=1, keepdims=True)
            )
            self.add_sum(2, dr)
            self.acc[at] = dr
            self.r3[3, at] = dr.astype(bf)

        self.each_rows(rows)

    def out_back(self):
        d = self.r3[3]
        for j, cols in enumerate(column_chunks()):
            da = mul_t(d, self.wrows(3, cols)).astype(bf)
            for i in range(CHUNK // TB):
                self.da3[j * (CHUNK // TB) + i] = da[:, i * TB : (i + 1) * TB]

    def attend_back(self):
        def body(b, _):
            at = pl.ds(pl.multiple_of(b * TB, TB), TB)
            for h in range(HEADS // 2):
                cols = slice(h * TB, (h + 1) * TB)
                p = self.p3[b, h]
                da = self.two(self.da3[h, at])
                dv = t_mul(p.astype(bf), da)
                pd = p * mul_t(da, self.q3[2, h, at])
                ds = (pd - p * jnp.sum(pd, axis=1, keepdims=True)).astype(bf)
                dq = self.one(mul(ds, self.q3[1, h, at])) * HEAD_DIM**-0.5
                dk = t_mul(ds, self.two(self.q3[0, h, at])) * HEAD_DIM**-0.5
                self.r3[0, at, cols] = dq.astype(bf)
                self.r3[1, at, cols] = dk.astype(bf)
                self.r3[2, at, cols] = dv.astype(bf)
                self.add_sum(0, dq, cols)
                self.add_sum(1, dv, cols)
            return 0

        lax.fori_loop(0, self.seqs, body, 0)

    def project_back(self, t):
        d = self.r3[t]
        for cols in column_chunks():
            value = self.acc[:, cols] + mul_t(d, self.wrows(t, cols))
            if t < 2:
                self.acc[:, cols] = value
            else:
                self.din[:, :, :, cols] = value.astype(bf).reshape(self.din.shape[:3] + (CHUNK,))


MESH = pl.DeviceIdType.MESH
ZN = 4
OCT = 96
RING = 8
SPOTS = 16


class Place:
    def __init__(self):
        self.dp = lax.axis_index("dp")
        self.fs = lax.axis_index("fsdp")
        self.z, self.y = self.dp // 2, self.dp % 2
        self.x, self.c = self.fs // 2, self.fs % 2
        self.to_x = (self.dp, (self.fs + 2) % 4)
        self.to_y = (self.z * 2 + 1 - self.y, self.fs)
        self.to_core = (self.dp, self.x * 2 + 1 - self.c)
        self.to_up = (self.dp + 2, self.fs)
        self.to_down = (self.dp - 2, self.fs)
        near = self.z + 1 - 2 * (self.z % 2)
        far = (self.z + 2) % ZN
        self.doubling = [
            self.to_core,
            self.to_x,
            self.to_y,
            (near * 2 + self.y, self.fs),
            (far * 2 + self.y, self.fs),
        ]

    def peer(self, j):
        return (self.dp + j) % (2 * ZN)

    def greet(self):
        bar = pltpu.get_barrier_semaphore()
        for dev in [self.to_x, self.to_core] + [(self.peer(j), self.fs) for j in range(1, 2 * ZN)]:
            pl.semaphore_signal(bar, inc=1, device_id=dev, device_id_type=MESH)

    def greeted(self):
        pl.semaphore_wait(pltpu.get_barrier_semaphore(), 1 + 2 * ZN)

    def octet(self, dx, dy, zp, k, c=None):
        yy = self.y if dy == 0 else 1 - self.y
        xx = self.x if dx == 0 else 1 - self.x
        return ((zp * 2 + yy) * 4 + xx * 2 + (self.c if c is None else c)) * 3 + k

    def plane(self, table, i):
        zp = table[0][i]
        for n in range(1, ZN):
            zp = jnp.where(self.z == n, table[n][i], zp)
        return zp


def octet_place(o):
    return jnp.where(
        o < 24,
        (o % 3) * 8 + o // 3,
        jnp.where((o >= 32) & (o < 64), 32 + ((o - 32) % 4) * 8 + (o - 32) // 4, o),
    )


def left_block(o):
    return jnp.where(
        o < 24, o // 3, jnp.where(o < 32, o - 16, jnp.where(o < 64, 16 + (o - 32) // 4, o - 40))
    )


def right_block(o):
    return jnp.where(o < 24, o % 3, jnp.where(o < 32, 3, jnp.where(o < 64, 4 + (o - 32) % 4, 8)))


def wait_for(ref, sem):
    pltpu.make_async_copy(ref, ref, sem).wait()


def remote(src, dst, send_sem, recv_sem, dev):
    return pltpu.make_async_remote_copy(
        src_ref=src,
        dst_ref=dst,
        send_sem=send_sem,
        recv_sem=recv_sem,
        device_id=dev,
        device_id_type=MESH,
    )


def start_deal(p, src, dst, s_sem, r_sem, l_sem):
    for j in range(1, 2 * ZN):
        d = p.peer(j)
        remote(src.at[:, d], dst.at[:, p.dp], s_sem, r_sem.at[p.dp], (d, p.fs)).start()
    pltpu.make_async_copy(src.at[:, p.dp], dst.at[:, p.dp], l_sem).start()


def end_deal(p, src, dst, s_sem, r_sem, l_sem):
    for j in range(1, 2 * ZN):
        d = p.peer(j)
        wait_for(dst.at[:, d], r_sem.at[d])
    wait_for(dst.at[:, p.dp], l_sem)
    wait_for(src.at[:, pl.ds(0, 2 * ZN - 1)], s_sem)


FORWARD_STEPS = [
    "P0", "P1", "P2", "ATT", "N1", "UA0", "UA1", "UA2", "UA3",
    "UB0", "UB1", "UB2", "UB3", "D0", "D1", "D2", "D3", "N2",
]
FORWARD_NEEDS = {"P0": (0,), "N1": (1,), "UB0": (2,), "D1": (3,)}
FORWARD_ROUTES = [
    ["xyx", "zzx", "zzy", "zxy"],
    ["zzz", "xyx", "zzz", "zzz"],
    ["zzz", "zzz", "xyx", "zzz"],
    ["zxy", "zzy", "zzx", "xyx"],
]
FORWARD_PLANS = [
    [
        1, 600, 2, 0, 100, 601, 102, 200, 101, 11, 12, 112, 602, 111, 201, 603,
        10, 202, 300, 22, 122, 604, 110, 32, 20, 21, 132, 301, 120, 210, 302, 232,
        605, 211, 212, 222, 31, 131, 1000, 121, 310, 30, 1001, 312, 1002, 311, 1003, 332,
        220, 1004, 1005, 231, 322, 320, 1006, 1007, 130, 1008, 321, 221, 331, 1009, 1010, 330,
        1011, 230, 1012, 1013, 1014, 1015, 1016, 1017,
    ],
    [
        600, 12, 11, 112, 111, 601, 212, 1, 10, 101, 110, 2, 602, 21, 211, 102,
        22, 603, 0, 121, 32, 604, 100, 210, 201, 20, 31, 132, 120, 122, 131, 300,
        311, 30, 310, 200, 322, 202, 301, 320, 605, 302, 1000, 312, 1001, 220, 1002, 222,
        1003, 130, 232, 1004, 1005, 221, 1006, 321, 1007, 1008, 1009, 231, 1010, 1011, 330, 230,
        1012, 332, 331, 1013, 1014, 1015, 1016, 1017,
    ],
    [
        20, 21, 22, 122, 121, 222, 600, 12, 32, 221, 601, 602, 120, 112, 1, 11,
        111, 603, 30, 31, 220, 211, 10, 322, 2, 332, 0, 604, 101, 320, 110, 201,
        102, 100, 202, 212, 300, 311, 310, 132, 321, 605, 301, 210, 330, 130, 200, 302,
        331, 1000, 1001, 1002, 1003, 312, 131, 1004, 1005, 1006, 232, 1007, 1008, 230, 1009, 1010,
        231, 1011, 1012, 1013, 1014, 1015, 1016, 1017,
    ],
    [
        32, 132, 600, 31, 131, 601, 30, 130, 232, 21, 602, 121, 22, 122, 332, 12,
        603, 112, 1, 230, 101, 222, 231, 212, 604, 2, 102, 0, 100, 605, 201, 11,
        330, 331, 10, 202, 300, 312, 111, 20, 221, 302, 320, 200, 110, 301, 1000, 1001,
        1002, 311, 211, 322, 1003, 120, 210, 310, 1004, 321, 1005, 220, 1006, 1007, 1008, 1009,
        1010, 1011, 1012, 1013, 1014, 1015, 1016, 1017,
    ],
]


def along_z(here, zp, k=None):
    up = zp <= here < ZN - 1 and (k is None or FORWARD_ROUTES[here + 1][zp][k] == "z")
    down = zp >= here > 0 and (k is None or FORWARD_ROUTES[here - 1][zp][k] == "z")
    return (["u"] if up else []) + (["d"] if down else [])


def split_plan(plan):
    parts = [[]]
    for code in plan:
        if code >= 1000:
            parts.append([])
        else:
            parts[-1].append(code)
    return parts


def forward_kernel(
    lengths, deal, weights, vec, tok, cot_in,
    wm, l3_out, d2_out, acc_out, gp_out, xh_out, rs_out, p3_out, q3_out, res_out, vsum, vecs,
    wbuf, vbuf, xl, xs, cot, l3, d2, q3, p3, xh, rs, acc, gp, res,
    r_w, s_x, s_y, s_up, s_down, s_core, s_local, s_vec, r_vec, s_tok, r_tok, l_tok, s_out, r_cot,
):
    p = Place()
    z = p.z
    p.greet()
    me = p.dp * 4 + p.fs
    get_cot = pltpu.make_async_copy(cot_in, cot, r_cot)
    get_cot.start()

    class Lens:
        def __getitem__(self, b):
            return lengths[b, jnp.clip(deal[b, me], 0, lengths.shape[1] - 1)]

    def wcols(n, cols, half=None):
        if half is None:
            return wbuf[8 * n : 8 * n + 8, :, cols].reshape(D, CHUNK)
        first = 8 * n + 4 * half
        return wbuf[first : first + 4, :, cols].reshape(D // 2, CHUNK)

    f = Layer(
        lens=Lens(), vec=vecs, l3=l3, d2=d2, vsum=vsum, q3=q3, p3=p3, xh=xh, rs=rs, acc=acc, gp=gp,
        res=res, cot=cot, wcols=wcols,
    )

    def ref_of(o):
        return wbuf.at[octet_place(o)]

    def wait(o):
        wait_for(ref_of(o), r_w.at[o])

    seqs = tok.shape[1]
    for b in range(tok.shape[0]):
        for j in range(seqs):
            xs[b, j] = tok[b, jnp.clip(deal[b, j * 4 + p.fs] - p.fs * seqs, 0, seqs - 1)]
    for k in range(3):
        place = octet_place(p.octet(0, 0, z, k))
        for j in range(8):
            wbuf[place, :, j * TB : (j + 1) * TB] = weights[8 * k + j].astype(bf)
    vbuf[me] = jnp.zeros(vbuf.shape[1:], f32)
    vbuf[me, :3] = vec[...].astype(bf).astype(f32)
    p.greeted()
    start_deal(p, xs, xl, s_tok, r_tok, l_tok)

    def vec_step(n):
        size = 2**n
        if n > 0:
            half = size // 2
            theirs = (me // half) * half
            theirs = theirs + half * (1 - 2 * (theirs // half % 2))
            wait_for(vbuf.at[pl.ds(theirs, half)], r_vec.at[n - 1])
        if n < 5:
            mine = vbuf.at[pl.ds((me // size) * size, size)]
            remote(mine, mine, s_vec.at[n], r_vec.at[n], p.doubling[n]).start()

    def vec_rows():
        for m in range(OCT):
            cols = slice((m % 8) * TB, (m % 8 + 1) * TB)
            vecs[m // 8 : m // 8 + 1, cols] = vbuf[m // 3, m % 3 : m % 3 + 1, :]

    sent = [dict(x=0, y=0, u=0, d=0, c=0) for _ in range(ZN)]
    way = dict(
        x=(p.to_x, s_x), y=(p.to_y, s_y), u=(p.to_up, s_up), d=(p.to_down, s_down),
        c=(p.to_core, s_core),
    )

    def item(here, kind, zp, k):
        if kind == 6:
            vec_step(k)
            return

        def send(o, *ways):
            ref = ref_of(o)
            for w in ways:
                dev, sem = way[w]
                remote(ref, ref, sem, r_w.at[o], dev).start()
                sent[here][w] += 1

        route = FORWARD_ROUTES[here][zp][k]
        if kind == 0:
            o = p.octet(0, 0, zp, k)
            if zp != here:
                wait(o)
            send(o, *along_z(here, zp))
        elif kind == 1:
            send(p.octet(0, 0, zp, k), "x", "y", "c")
        elif kind == 2:
            o = p.octet(0, 1, zp, k)
            wait(o)
            send(o, *(["x"] if route == "x" else []), "c")
            o = p.octet(1, 0, zp, k)
            wait(o)
            send(o, *(["y"] if route == "y" else []), "c")
        else:
            o = p.octet(1, 1, zp, k)
            wait(o)
            send(o, *along_z(here, zp, k), "c")

    def partner(zp):
        for dx in range(2):
            for dy in range(2):
                for k in range(3):
                    wait(p.octet(dx, dy, zp, k, 1 - p.c))

    outs = []

    def give(src, dst):
        copy = pltpu.make_async_copy(src, dst, s_out.at[len(outs)])
        copy.start()
        outs.append(copy)

    def give_square(n):
        give(wbuf.at[pl.ds(8 * n, 8)], wm.at[pl.ds(8 * n, 8)])

    def compute(name):
        t = int(name[-1]) if name[-1].isdigit() else 0
        if name == "P0":
            vec_rows()
            vsum[...] = jnp.zeros_like(vsum)
            end_deal(p, xs, xl, s_tok, r_tok, l_tok)
            for j in range(8):
                l3[j] = xl[:, :, :, j * TB : (j + 1) * TB].reshape(l3.shape[1], TB)
        if name[0] == "P":
            f.project(t)
            give_square(t)
        elif name == "ATT":
            f.attend()
            give(q3, q3_out)
            give(p3, p3_out)
        elif name == "N1":
            f.norm_one()
            give_square(3)
            give(xh, xh_out)
            give(rs, rs_out)
        elif name[:2] == "UA":
            f.up_begin(t)
        elif name[:2] == "UB":
            f.up_end(t)
            give_square(4 + t)
            give(gp.at[t], gp_out.at[t])
            if t == 3:
                give(l3, l3_out)
        elif name[0] == "D":
            f.down(t)
            give_square(8 + t)
        else:
            get_cot.wait()
            f.norm_two()
            give(d2, d2_out)
            give(acc, acc_out)
            give(res, res_out)

    parts = [split_plan(plan) for plan in FORWARD_PLANS]
    for n in range(len(FORWARD_STEPS) + 1):

        def run(here):
            for code in parts[here][n]:
                item(here, code // 100, code // 10 % 10, code % 10)

        for here in range(ZN):
            pl.when(z == here)(functools.partial(run, here))
        if n < len(FORWARD_STEPS):
            name = FORWARD_STEPS[n]
            for zp in FORWARD_NEEDS.get(name, ()):
                partner(zp)
            compute(name)

    for copy in outs:
        copy.wait()
    for n in range(5):
        wait_for(vbuf.at[pl.ds(0, 2**n)], s_vec.at[n])

    def drain(here):
        for w, n in sent[here].items():
            if n:
                wait_for(wbuf.at[pl.ds(0, n)], way[w][1])

    for here in range(ZN):
        pl.when(z == here)(functools.partial(drain, here))


def forward(lengths, deal, weights, vec, tok, cot):
    dma = pltpu.SemaphoreType.DMA
    rows = cot.shape[0]
    vmem = pl.BlockSpec(memory_space=pltpu.VMEM)
    far = pl.BlockSpec(memory_space=pl.ANY)
    out = jax.ShapeDtypeStruct
    stages = (
        out((56, rows, TB), bf),
        out((rows, D), bf),
        out((rows, D), f32),
        out((4, rows, D), f32),
        out((rows, D), f32),
        out((rows, TB), f32),
        out((rows // TB, 8, 2 * TB, TB), f32),
        out((3, 8, rows, TB), bf),
        out(tok.shape, bf),
    )
    scratch = [pltpu.VMEM(s.shape, s.dtype) for s in stages]
    l3, d2, acc, gp, xh, rs, p3, q3, res = scratch
    return pl.pallas_call(
        forward_kernel,
        out_shape=(out((OCT, TB, D), bf),) + stages + (out((12, 8, D), f32), out((12, D), f32)),
        in_specs=[pl.BlockSpec(memory_space=pltpu.SMEM)] * 2 + [vmem] * 3 + [far],
        out_specs=(far,) * 10 + (vmem,) * 2,
        scratch_shapes=[
            pltpu.VMEM((OCT, TB, D), bf), pltpu.VMEM((32, 8, TB), f32), pltpu.VMEM(tok.shape, bf),
            pltpu.VMEM(tok.shape, bf), pltpu.VMEM(cot.shape, bf),
            l3, d2, q3, p3, xh, rs, acc, gp, res,
            dma((OCT,)), dma, dma, dma, dma, dma, dma((3,)), dma((5,)), dma((5,)),
            dma, dma((2 * ZN,)), dma, dma((32,)), dma,
        ],
        compiler_params=pltpu.CompilerParams(
            collective_id=0, has_side_effects=True, vmem_limit_bytes=62 * 2**20
        ),
        name="forward",
    )(lengths, deal, weights, vec, tok, cot)


BACKWARD_STEPS = [
    "DB0", "DB1", "DB2", "DB3", "UB0", "UB1", "UB2", "UB3",
    "N1B", "OB", "ATB", "PB0", "PB1", "PB2",
]
BACKWARD_ROUTES = [
    ["xyy", "zzx", "zzy", "zzx"],
    ["zzz", "xyy", "zzz", "zzz"],
    ["zzz", "zzz", "xyy", "zzz"],
    ["zzx", "zzy", "zzx", "xyy"],
]
BACKWARD_PLANS = [
    [
        31, 30, 1000, 131, 231, 1001, 130, 1002, 32, 230, 1003, 1004, 1005, 21, 1006, 1007,
        121, 132, 221, 330, 20, 22, 120, 220, 1008, 331, 122, 232, 1009, 1010, 10, 110,
        210, 0, 222, 12, 600, 332, 11, 601, 2, 111, 320, 102, 321, 1011, 112, 310,
        211, 1, 322, 100, 602, 202, 212, 101, 603, 200, 311, 312, 201, 1012, 500, 1013,
        300, 301, 604, 400, 302, 501, 605, 401, 402,
    ],
    [
        500, 30, 1000, 32, 230, 1001, 1002, 1003, 22, 132, 1004, 31, 1005, 122, 1006, 222,
        20, 1007, 130, 21, 1008, 12, 1009, 220, 1010, 232, 0, 1011, 231, 131, 1012, 1013,
        121, 2, 120, 600, 221, 330, 601, 10, 200, 11, 102, 1, 201, 110, 202, 332,
        100, 331, 111, 112, 101, 320, 210, 300, 321, 211, 212, 322, 310, 602, 301, 311,
        302, 603, 501, 312, 401, 604, 605, 400, 402,
    ],
    [
        32, 30, 1000, 1001, 1002, 500, 230, 1003, 1004, 1005, 1006, 1007, 1008, 12, 11, 232,
        1009, 112, 1010, 0, 2, 200, 212, 31, 20, 102, 211, 1011, 111, 10, 132, 21,
        1, 1012, 110, 201, 22, 600, 131, 210, 121, 601, 100, 101, 130, 301, 120, 231,
        330, 220, 202, 300, 122, 332, 602, 331, 221, 311, 1013, 310, 302, 222, 603, 312,
        501, 320, 321, 322, 604, 401, 400, 402, 605,
    ],
    [
        500, 1000, 1001, 1002, 1003, 21, 1004, 221, 1005, 121, 20, 1006, 1007, 220, 1008, 11,
        120, 10, 211, 1009, 210, 111, 1010, 1, 110, 600, 201, 0, 12, 100, 2, 200,
        301, 22, 31, 112, 102, 122, 101, 310, 32, 30, 300, 132, 212, 202, 311, 601,
        1011, 320, 130, 232, 302, 1012, 312, 131, 1013, 231, 321, 602, 222, 603, 331, 230,
        332, 322, 401, 604, 501, 330, 402, 605, 400,
    ],
]


def backward_codes(here):
    routes = BACKWARD_ROUTES
    spots = {}
    for way in "xy":
        pairs = [(zp, k) for zp in range(ZN) for k in range(3) if routes[here][zp][k] == way]
        spots.update({pair: n for n, pair in enumerate(pairs)})

    def octet(side, zp, k):
        dx, dy = side % 2, side // 2
        own = zp == here
        route = routes[here][zp][k]
        code = k + 4 * zp + 16 * side + 131072
        along = "u" if zp > here else "d"
        if side == 0:
            code += 64 + 128
            way = "f" if own else along
        elif side == 1:
            code += 128 * (route == "y")
            way = "x"
        elif side == 2:
            code += 64 * (route == "x")
            way = "y"
        else:
            way = along if route == "z" else route
        if side in (0, 3):
            for step, there, bit in ((1, here - 1, 256), (-1, here + 1, 512)):
                if 0 <= there < ZN and (zp - here) * step >= 0:
                    code += bit * (side == 0 or routes[there][zp][k] == "z")
        return code + 1024 * "xyudf".index(way) + 8192 * spots.get((zp, k), 0)

    parts, first = [[]], 0
    for item in BACKWARD_PLANS[here]:
        if item >= 1000:
            parts.append([])
            continue
        kind, zp, k = item // 100, item // 10 % 10, item % 10
        if kind == 0:
            parts[-1].append(k + 4 * zp + 64 * (first >= 2) + 8192 * (first % 2))
            first += 1
        elif kind == 1:
            parts[-1].append(octet(3, zp, k))
        elif kind == 2:
            parts[-1] += [octet(2, zp, k), octet(1, zp, k)]
        elif kind == 3:
            parts[-1].append(octet(0, zp, k))
        elif kind == 4:
            parts[-1].append(131072 * 2 + k)
        elif kind == 5:
            parts[-1].append(131072 * (3 + k))
        else:
            parts[-1].append(131072 * (5 + k))
    return parts


def backward_kernel(
    wm, l3_in, d2_in, acc_in, gp_in, xh_in, rs_in, p3_in, q3_in, res, vsum_in, vec,
    tiles, grp, vout, res_back, din_back,
    l3, r3, acc, gp, xh, rs, p3, q3, da3, din, wb, vsum,
    land_c, land_x, land_y, land_z, ring, vland, total,
    r_in, r_wb, r_c, r_x, r_y, r_z, r_e, r_v, s_ring, s_x, s_y, s_up, s_down, s_e, s_e2, s_v,
    s_res, r_res, l_res, s_din, r_din, l_din,
):
    p = Place()
    z, c, fs = p.z, p.c, p.fs
    p.greet()
    weights = [8, 9, 10, 11, 4, 5, 6, 7, 3, 0, 1, 2]
    slots = wb.shape[0]

    def bring(n):
        if n < len(weights):
            pltpu.make_async_copy(
                wm.at[pl.ds(8 * weights[n], 8)], wb.at[n % slots], r_wb.at[n % slots]
            ).start()

    pairs = [(d2_in, r3.at[8]), (l3_in, l3)]
    pairs += [(gp_in.at[t], gp.at[t]) for t in range(4)]
    pairs += [(acc_in, acc), (xh_in, xh), (rs_in, rs), (p3_in, p3), (q3_in, q3)]
    takes = [pltpu.make_async_copy(src, dst, r_in.at[n]) for n, (src, dst) in enumerate(pairs)]
    for n, copy in enumerate(takes):
        copy.start()
        if 2 <= n < 2 + slots:
            bring(n - 2)
    vsum[...] = vsum_in[...]
    p.greeted()

    def wrows(n, rows):
        at = slice(rows.start // TB, rows.stop // TB)
        return wb[weights.index(n) % slots, at].reshape(CHUNK, D)

    f = Layer(
        vec=vec, l3=l3, r3=r3, vsum=vsum, q3=q3, p3=p3, da3=da3, xh=xh, rs=rs, acc=acc, gp=gp,
        din=din, wrows=wrows,
    )

    def part(o):
        return t_mul(l3[left_block(o)], r3[right_block(o)])

    def add(land, sem, n):
        wait_for(land.at[n], sem.at[n])
        total[...] += land[n].astype(f32)

    def to_partner(zp, k, slot, again):
        def body(j, _):
            yy, xx = j % 2, j // 2
            o = ((zp * 2 + yy) * 4 + xx * 2 + (1 - c)) * 3 + k
            n = slot * 4 + j
            value = part(o).astype(bf)
            pl.when(again == 1)(lambda: wait_for(ring.at[0], s_ring.at[n]))
            ring[n] = value
            q = ((jnp.where(yy == p.y, 0, 2) + jnp.where(xx == p.x, 0, 1)) * ZN + zp) * 3 + k
            remote(ring.at[n], land_c.at[q], s_ring.at[n], r_c.at[q], p.to_core).start()
            return 0

        lax.fori_loop(0, 4, body, 0)

    def octet_step(code, zp, k):
        side = code // 16 % 4
        dx, dy = side % 2, side // 2
        corner = side // 3
        q = (side * ZN + zp) * 3 + k
        yy = p.y + dy * (1 - 2 * p.y)
        xx = p.x + dx * (1 - 2 * p.x)
        o = ((zp * 2 + yy) * 4 + xx * 2 + c) * 3 + k
        wait_for(land_c.at[q], r_c.at[q])
        total[...] = part(o) + land_c[q].astype(f32)
        spot = 12 + code // 8192 % 16
        flat = zp * 3 + k
        column = jnp.where(side == 0, flat, spot)
        n = corner * 12 + flat
        mine = 24 + corner * 3 + k
        above = jnp.where(zp == z, mine, n)
        below_to = jnp.where(zp == z - 1, mine, n)
        pl.when(code // 64 % 2 == 1)(functools.partial(add, land_x, r_x, column))
        pl.when(code // 128 % 2 == 1)(functools.partial(add, land_y, r_y, column))
        pl.when(code // 256 % 2 == 1)(functools.partial(add, land_z, r_z, n))
        pl.when(code // 512 % 2 == 1)(functools.partial(add, land_z, r_z, above))
        way = code // 1024 % 8
        t = jnp.where(side == 3, spot, flat)

        @pl.when(way < 4)
        def _():
            land_c[q] = total[...].astype(bf)
            src = land_c.at[q]
            pl.when(way == 0)(lambda: remote(src, land_x.at[t], s_x, r_x.at[t], p.to_x).start())
            pl.when(way == 1)(lambda: remote(src, land_y.at[t], s_y, r_y.at[t], p.to_y).start())
            pl.when(way == 2)(lambda: remote(src, land_z.at[n], s_up, r_z.at[n], p.to_up).start())
            pl.when(way == 3)(
                lambda: remote(
                    src, land_z.at[below_to], s_down, r_z.at[below_to], p.to_down
                ).start()
            )

        @pl.when(way == 4)
        def _():
            for j in range(8):
                piece = total[:, j * TB : (j + 1) * TB]
                tiles[8 * k + j] = piece
                grp[fs * 24 + 8 * k + j] = piece.astype(bf)
            mine = grp.at[pl.ds(fs * 24 + 8 * k, 8)]
            remote(mine, mine, s_e, r_e.at[fs * 3 + k], p.to_x).start()
            remote(mine, mine, s_e2, r_e.at[fs * 3 + k], p.to_core).start()

    def hand_on(k):
        fx = (fs + 2) % 4
        block = grp.at[pl.ds(fx * 24 + 8 * k, 8)]
        wait_for(block, r_e.at[fx * 3 + k])
        remote(block, block, s_e2, r_e.at[fx * 3 + k], p.to_core).start()

    def vec_step(n):
        if n == 0:
            sums = vsum[...].sum(axis=1)
            for j in range(8):
                vout[pl.ds(12 * j, 12)] = sums[:, j * TB : (j + 1) * TB]
        else:
            wait_for(vland.at[n - 1], r_v.at[n - 1])
            vout[...] = vout[...] + vland[n - 1]
        if n < 5:
            vland[5 + n] = vout[...]
            remote(vland.at[5 + n], vland.at[n], s_v.at[n], r_v.at[n], p.doubling[n]).start()

    def run_codes(lists):
        longest = max(len(codes) for codes in lists)
        if longest == 0:
            return

        def of_plane(values):
            got = values[0]
            for here in range(1, ZN):
                if values[here] != values[0]:
                    got = jnp.where(z == here, values[here], got)
            return got

        count = of_plane([len(codes) for codes in lists])
        table = [of_plane([codes[i] if i < len(codes) else 0 for codes in lists]) for i in range(longest)]

        def body(i, _):
            code = table[0]
            for j in range(1, longest):
                code = jnp.where(i == j, table[j], code)
            kind = code // 131072
            zp, k = code // 4 % 4, code % 4
            pl.when(kind == 0)(lambda: to_partner(zp, k, code // 8192 % 16, code // 64 % 2))
            pl.when(kind == 1)(lambda: octet_step(code, zp, k))
            pl.when(kind == 2)(lambda: hand_on(k))
            pl.when(kind == 3)(lambda: start_deal(p, res, res_back, s_res, r_res, l_res))
            pl.when(kind == 4)(lambda: start_deal(p, din, din_back, s_din, r_din, l_din))
            for n in range(6):
                pl.when(kind == 5 + n)(functools.partial(vec_step, n))
            return 0

        lax.fori_loop(0, count, body, 0)

    used = [0]

    def square(step):
        n = used[0]
        used[0] += 1
        wait_for(wb.at[n % slots], r_wb.at[n % slots])
        step()
        bring(n + slots)

    def compute(name):
        t = int(name[-1]) if name[-1].isdigit() else 0
        if name[:2] == "DB":
            takes[2 + t].wait()
            square(lambda: f.down_back(t))
        elif name[:2] == "UB":
            if t == 0:
                takes[6].wait()
            square(lambda: f.up_back(t))
        elif name == "N1B":
            takes[7].wait()
            takes[8].wait()
            f.norm_one_back()
        elif name == "OB":
            square(f.out_back)
        elif name == "ATB":
            takes[9].wait()
            takes[10].wait()
            f.attend_back()
        else:
            square(lambda: f.project_back(t))

    takes[0].wait()
    takes[1].wait()
    parts = [backward_codes(here) for here in range(ZN)]
    for n in range(len(BACKWARD_STEPS) + 1):
        run_codes([codes[n] for codes in parts])
        if n < len(BACKWARD_STEPS):
            compute(BACKWARD_STEPS[n])

    end_deal(p, res, res_back, s_res, r_res, l_res)
    end_deal(p, din, din_back, s_din, r_din, l_din)
    for g in (p.x * 2 + 1 - c, (1 - p.x) * 2 + 1 - c):
        for k in range(3):
            wait_for(grp.at[pl.ds(g * 24 + 8 * k, 8)], r_e.at[g * 3 + k])

    for n in range(RING):
        wait_for(ring.at[0], s_ring.at[n])
    for n in range(5):
        wait_for(vland.at[5 + n], s_v.at[n])

    wait_for(grp.at[pl.ds(0, 24)], s_e)
    wait_for(grp.at[pl.ds(0, 48)], s_e2)

    def drain(here):
        ways = [code // 1024 % 8 for codes in parts[here] for code in codes if code // 131072 == 1]
        for way, sem in enumerate((s_x, s_y, s_up, s_down)):
            if ways.count(way):
                wait_for(land_c.at[pl.ds(0, ways.count(way))], sem)

    for here in range(ZN):
        pl.when(z == here)(functools.partial(drain, here))


def backward(wm, l3, d2, acc, gp, xh, rs, p3, q3, res, vsum, vec):
    dma = pltpu.SemaphoreType.DMA
    rows = d2.shape[0]
    vmem = pl.BlockSpec(memory_space=pltpu.VMEM)
    far = pl.BlockSpec(memory_space=pl.ANY)
    out = jax.ShapeDtypeStruct
    return pl.pallas_call(
        backward_kernel,
        out_shape=(
            out((24, TB, TB), f32),
            out((96, TB, TB), bf),
            out((96, TB), f32),
            out(res.shape, bf),
            out(res.shape, bf),
        ),
        in_specs=[far] * 10 + [vmem] * 2,
        out_specs=(vmem,) * 3 + (far,) * 2,
        scratch_shapes=[
            pltpu.VMEM(l3.shape, bf), pltpu.VMEM((9, rows, D), bf), pltpu.VMEM(acc.shape, f32),
            pltpu.VMEM(gp.shape, f32), pltpu.VMEM(xh.shape, f32), pltpu.VMEM(rs.shape, f32),
            pltpu.VMEM(p3.shape, f32), pltpu.VMEM(q3.shape, bf), pltpu.VMEM((8, rows, TB), bf),
            pltpu.VMEM(res.shape, bf), pltpu.VMEM((2, 8, TB, D), bf), pltpu.VMEM((12, 8, D), f32),
            pltpu.VMEM((48, TB, D), bf), pltpu.VMEM((SPOTS, TB, D), bf),
            pltpu.VMEM((SPOTS, TB, D), bf), pltpu.VMEM((30, TB, D), bf), pltpu.VMEM((RING, TB, D), bf),
            pltpu.VMEM((10, 96, TB), f32), pltpu.VMEM((TB, D), f32),
            dma((11,)), dma((2,)), dma((48,)), dma((SPOTS,)), dma((SPOTS,)), dma((30,)), dma((12,)), dma((5,)),
            dma((RING,)), dma, dma, dma, dma, dma, dma, dma((5,)),
            dma, dma((2 * ZN,)), dma, dma, dma((2 * ZN,)), dma,
        ],
        compiler_params=pltpu.CompilerParams(
            collective_id=1, has_side_effects=True, vmem_limit_bytes=62 * 2**20
        ),
        name="backward",
    )(wm, l3, d2, acc, gp, xh, rs, p3, q3, res, vsum, vec)


GROUP = 8


def halves(a):
    high = a.astype(bf)
    return high, (a - high.astype(f32)).astype(bf)


def wide(b):
    return jnp.concatenate(
        [jnp.concatenate(b, 1), jnp.concatenate([b[0], jnp.zeros_like(b[0])], 1)], 0
    )


def fine(a, b_wide):
    out = mul(jnp.concatenate(a, 1), b_wide)
    return out[:, :TB] + out[:, TB:]


def fine_t(a, b):
    wide_t = jnp.concatenate(
        [jnp.concatenate([b[0], b[0]], 1), jnp.concatenate([b[1], jnp.zeros_like(b[1])], 1)], 0
    )
    out = mul_t(jnp.concatenate(a, 1), wide_t)
    return out[:, :TB] + out[:, TB:]


def moments(first, second, grad):
    first = BETA_ONE * first + (1.0 - BETA_ONE) * grad
    second = BETA_TWO * second + (1.0 - BETA_TWO) * grad * grad
    hat = (first * (1.0 / (1.0 - BETA_ONE**STEP))) / (
        jnp.sqrt(second * (1.0 / (1.0 - BETA_TWO**STEP))) + ADAM_EPS
    )
    return first, second, hat


def adam_kernel(owners, deal, *refs):
    masters = refs[:GROUP]
    (
        grads, left, right, first, second, vec, vec_first, vec_second, vec_total,
        tiles, res_back, din_back,
        new_first, new_second, new_tiles, new_low, vec_grad, vec_first_new, vec_second_new, new_vec,
        tile_grads, out_tokens, in_grad,
    ) = refs[GROUP:]
    step = pl.program_id(0)
    dp, fs = lax.axis_index("dp"), lax.axis_index("fsdp")
    seqs = res_back.shape[1]

    @pl.when(step == 0)
    def _():
        for b in range(res_back.shape[0]):
            for j in range(seqs):
                to = deal[b, j * 4 + fs] - fs * seqs
                out_tokens[b, to] = res_back[b, j]
                in_grad[b, to] = din_back[b, j]
        for i in range(3):
            m = (dp * 4 + fs) * 3 + i
            vec_grad[i : i + 1] = vec_total[pl.ds((m % 8) * 12 + m // 8, 1)]
        a, b, hat = moments(vec_first[...], vec_second[...], vec_grad[...])
        vec_first_new[...] = a
        vec_second_new[...] = b
        new_vec[...] = vec[...] - VEC_RATE * hat

    tile_grads[...] = tiles[...]
    span = range(GROUP)
    owner = [owners[step * GROUP + g] for g in span]
    ls = [halves(left[g]) for g in span]
    rs = [halves(right[g]) for g in span]
    grad = [grads[owner[g] - dp * 96] for g in span]
    inner = [t_mul(jnp.concatenate(ls[g], 0), jnp.concatenate([grad[g]] * 2, 0)) for g in span]
    rwide = [wide(rs[g]) for g in span]
    rotated = [fine(halves(inner[g]), rwide[g]) for g in span]
    hats = []
    for g in span:
        first_now, second_now, hat = moments(first[g], second[g], rotated[g])
        new_first[g] = first_now
        new_second[g] = second_now
        hats.append(hat)
    outer = [fine(ls[g], wide(halves(hats[g]))) for g in span]
    update = [fine_t(halves(outer[g]), rs[g]) for g in span]
    for g in span:
        master = masters[g][0].astype(f32)
        fresh = master - tile_rate(owner[g]) * (update[g] + DECAY * master)
        new_tiles[g] = fresh
        new_low[g] = fresh.astype(bf)


def adam(owners, deal, wm, grads, left, right, first, second, vec, vec_first, vec_second,
         vec_total, tiles, res_back, din_back):
    count = left.shape[0]
    out = jax.ShapeDtypeStruct

    def master_at(g, i, owners, *_):
        o = owners[i * GROUP + g]
        return octet_place(o // 8), 0, o % 8

    one = [pl.BlockSpec((1, TB, TB), functools.partial(master_at, g)) for g in range(GROUP)]
    stack = pl.BlockSpec((GROUP, TB, TB), lambda i, *_: (i, 0, 0))
    whole = pl.BlockSpec(grads.shape, lambda i, *_: (0, 0, 0))
    dealt = pl.BlockSpec(res_back.shape, lambda i, *_: (0, 0, 0, 0))

    def small(a):
        return pl.BlockSpec(a.shape, lambda i, *_: (0, 0))

    return pl.pallas_call(
        adam_kernel,
        out_shape=(out(left.shape, f32),) * 3
        + (out(left.shape, bf),)
        + (out(vec.shape, f32),) * 4
        + (out(tiles.shape, f32), out(res_back.shape, bf), out(din_back.shape, bf)),
        grid_spec=pltpu.PrefetchScalarGridSpec(
            num_scalar_prefetch=2,
            grid=(count // GROUP,),
            in_specs=one + [whole] + [stack] * 4 + [small(vec)] * 3 + [small(vec_total), stack, dealt, dealt],
            out_specs=[stack] * 4 + [small(vec)] * 4 + [stack, dealt, dealt],
        ),
        compiler_params=pltpu.CompilerParams(vmem_limit_bytes=60 * 2**20),
        name="adam",
    )(
        owners, deal, *([wm] * GROUP), grads, left, right, first, second,
        vec, vec_first, vec_second, vec_total, tiles, res_back, din_back,
    )


def per_device(
    tokens,
    cotangent,
    lengths,
    deal,
    weights,
    vectors,
    owners,
    left_basis,
    right_basis,
    first_moment,
    second_moment,
    vec_first,
    vec_second,
):
    rows = tokens.shape[0] * tokens.shape[2] * lax.axis_size("dp")
    vec_rows = vectors.reshape(3, TB)
    wm, l3, d2, acc, gp, xh, rs, p3, q3, res, vsum, vecs = forward(
        lengths, deal, weights, vec_rows, tokens, cotangent.reshape(rows, D)
    )
    tiles, group_grads, vec_total, res_back, din_back = backward(
        wm, l3, d2, acc, gp, xh, rs, p3, q3, res, vsum, vecs
    )
    (
        new_first, new_second, new_tiles, new_low, vec_grads, vec_first_new, vec_second_new,
        new_vectors, tile_grads, out_tokens, in_grad,
    ) = adam(
        owners, deal, wm, group_grads, left_basis, right_basis, first_moment, second_moment,
        vec_rows, vec_first.reshape(3, TB), vec_second.reshape(3, TB), vec_total, tiles,
        res_back, din_back,
    )
    return (
        out_tokens,
        in_grad,
        tile_grads,
        vec_grads.reshape(-1),
        new_first,
        new_second,
        new_tiles,
        new_low,
        vec_first_new.reshape(-1),
        vec_second_new.reshape(-1),
        new_vectors.reshape(-1),
    )


def solution(mesh):
    body = per_device if (mesh.shape["dp"], mesh.shape["fsdp"]) == (2 * ZN, 4) else per_device_any
    placed = (
        P(None, "fsdp", "dp", None),
        P(None, ("dp", "fsdp"), None, None),
        P(),
        P(),
        P(("dp", "fsdp"), None, None),
        P(("dp", "fsdp")),
        P(("dp", "fsdp")),
        P(("dp", "fsdp"), None, None),
        P(("dp", "fsdp"), None, None),
        P(("dp", "fsdp"), None, None),
        P(("dp", "fsdp"), None, None),
        P(("dp", "fsdp")),
        P(("dp", "fsdp")),
    )
    return jax.shard_map(
        body,
        mesh=mesh,
        in_specs=placed,
        out_specs=(
            P(None, "fsdp", "dp", None),
            P(None, "fsdp", "dp", None),
            P(("dp", "fsdp"), None, None),
            P(("dp", "fsdp")),
            P(("dp", "fsdp"), None, None),
            P(("dp", "fsdp"), None, None),
            P(("dp", "fsdp"), None, None),
            P(("dp", "fsdp"), None, None),
            P(("dp", "fsdp")),
            P(("dp", "fsdp")),
            P(("dp", "fsdp")),
        ),
        check_vma=False,
    )
```

```python
import functools

import jax
import jax.numpy as jnp
from jax import lax
from jax.experimental import pallas as pl
from jax.experimental.pallas import tpu as pltpu
from jax.sharding import PartitionSpec as P

D = 1024
HEADS = 16
HEAD_DIM = 64
FF = 4096
STEP = 10
TB = 128


EPS_NORM = 1e-05
BETA_ONE = 0.5
BETA_TWO = 0.6
ADAM_EPS = 1e-08
DECAY = 0.01
VEC_RATE = 0.2
PRECISION_HIGH = lax.Precision.HIGHEST


def cut_tiles(stacked, row_count, col_count, start_at):
    tile_count = row_count // TB * (col_count // TB)
    blocked = lax.slice_in_dim(stacked, start_at, start_at + tile_count, axis=0)
    blocked = blocked.reshape(row_count // TB, col_count // TB, TB, TB)
    return (blocked.transpose(0, 2, 1, 3).reshape(row_count, col_count), start_at + tile_count)


def unpack_mats(stacked):
    w_qkv, offset = cut_tiles(stacked, D, 3 * D, 0)
    w_out, offset = cut_tiles(stacked, D, D, offset)
    w_up, offset = cut_tiles(stacked, D, FF, offset)
    w_down, offset = cut_tiles(stacked, FF, D, offset)
    return (w_qkv, w_out, w_up, w_down)


def tiled_grad(left_rows, right_rows):
    row_total = left_rows.shape[0]
    left_split = left_rows.reshape(row_total, left_rows.shape[1] // TB, TB)
    right_split = right_rows.reshape(row_total, right_rows.shape[1] // TB, TB)
    blocked = jnp.einsum(
        "tai,tbj->abij", left_split, right_split, preferred_element_type=jnp.float32
    )
    return blocked.reshape(-1, TB, TB)


def unpack_vecs(vector):
    widths = [D, D, D, FF, D, D, D, D, D]
    pieces = []
    offset = 0
    for width_now in widths:
        pieces.append(vector[offset : offset + width_now])
        offset += width_now
    return tuple(pieces)


def tile_rate(tile_ids):
    qkv_end = 3 * D * D // (TB * TB)
    out_end = 4 * D * D // (TB * TB)
    up_end = (4 * D * D + D * FF) // (TB * TB)
    return jnp.where(
        tile_ids < qkv_end,
        D ** (-0.5),
        jnp.where(
            tile_ids < out_end,
            (HEAD_DIM / D) ** 0.5,
            jnp.where(tile_ids < up_end, D ** (-0.5), 1.5 * FF ** (-0.5)),
        ),
    ).astype(jnp.float32)


def norm_apply(values, gain_vec, shift_vec):
    center = values - jnp.mean(values, axis=-1, keepdims=True)
    spread = jnp.mean(center * center, axis=-1, keepdims=True)
    return center * lax.rsqrt(spread + EPS_NORM) * gain_vec + shift_vec


def exact_gelu(values):
    return jax.nn.gelu(values, approximate=False)


def split_heads(joined16):
    seq_rows = joined16.shape[0]
    query_heads = joined16[:, :D].reshape(seq_rows, HEADS, HEAD_DIM)
    key_heads = joined16[:, D : 2 * D].reshape(seq_rows, HEADS, HEAD_DIM)
    value_heads = joined16[:, 2 * D :].reshape(seq_rows, HEADS, HEAD_DIM)
    return (query_heads, key_heads, value_heads)


def masked_scores(query_heads, key_heads, in_length):
    scores = jnp.einsum(
        "qhd,khd->hqk", query_heads, key_heads, preferred_element_type=jnp.float32
    ) * HEAD_DIM ** (-0.5)
    return jnp.where(in_length[None, None, :], scores, -1e30)


def forward_pass(inputs16, length, matrices, vecs):
    w_qkv, w_out, w_up, w_down = matrices
    bias_q, bias_v, bias_out, bias_up, bias_down, gain_one, shift_one, gain_two, shift_two = vecs
    seq_rows = inputs16.shape[0]
    joined = jnp.dot(inputs16, w_qkv, preferred_element_type=jnp.float32)
    joined = joined + jnp.concatenate([bias_q, jnp.zeros_like(bias_q), bias_v])
    joined16 = joined.astype(jnp.bfloat16)
    query_heads, key_heads, value_heads = split_heads(joined16)
    in_length = jnp.arange(seq_rows) < length
    scores = masked_scores(query_heads, key_heads, in_length)
    row_top = jnp.max(scores, axis=-1, keepdims=True)
    exp_scores = jnp.exp(scores - row_top)
    row_total = jnp.sum(exp_scores, axis=-1, keepdims=True)
    attention16 = (exp_scores / row_total).astype(jnp.bfloat16)
    log_total = row_top + jnp.log(row_total)
    attended = jnp.einsum(
        "hqk,khd->qhd", attention16, value_heads, preferred_element_type=jnp.float32
    )
    attended16 = attended.reshape(seq_rows, D).astype(jnp.bfloat16)
    resid_one = (
        inputs16.astype(jnp.float32)
        + jnp.dot(attended16, w_out, preferred_element_type=jnp.float32)
        + bias_out
    )
    normed_one = norm_apply(resid_one, gain_one, shift_one)
    normed16 = normed_one.astype(jnp.bfloat16)
    hidden = jnp.dot(normed16, w_up, preferred_element_type=jnp.float32) + bias_up
    active16 = exact_gelu(hidden).astype(jnp.bfloat16)
    resid_two = (
        normed_one + jnp.dot(active16, w_down, preferred_element_type=jnp.float32) + bias_down
    )
    result = norm_apply(resid_two, gain_two, shift_two)
    result = jnp.where(in_length[:, None], result, 0.0).astype(jnp.bfloat16)
    kept = (
        joined16,
        log_total,
        attended16,
        resid_one,
        normed16,
        hidden,
        active16,
        resid_two,
        in_length,
    )
    return (result, kept)


def backward_pass(back16, inputs16, kept, matrices, vecs):
    w_qkv, w_out, w_up, w_down = matrices
    bias_q, bias_v, bias_out, bias_up, bias_down, gain_one, shift_one, gain_two, shift_two = vecs
    joined16, log_total, attended16, resid_one, normed16, hidden, active16, resid_two, in_length = (
        kept
    )
    seq_rows = inputs16.shape[0]
    back = jnp.where(in_length[:, None], back16.astype(jnp.float32), 0.0)
    unused_two, pull_two = jax.vjp(norm_apply, resid_two, gain_two, shift_two)
    d_resid_two, d_gain_two, d_shift_two = pull_two(back)
    d_down16 = d_resid_two.astype(jnp.bfloat16)
    d_active = jnp.einsum("to,io->ti", d_down16, w_down, preferred_element_type=jnp.float32)
    unused_gelu, pull_gelu = jax.vjp(exact_gelu, hidden)
    d_hidden = pull_gelu(d_active)[0]
    d_hidden16 = d_hidden.astype(jnp.bfloat16)
    d_normed = d_resid_two + jnp.einsum(
        "to,io->ti", d_hidden16, w_up, preferred_element_type=jnp.float32
    )
    unused_one, pull_one = jax.vjp(norm_apply, resid_one, gain_one, shift_one)
    d_resid_one, d_gain_one, d_shift_one = pull_one(d_normed)
    d_branch16 = d_resid_one.astype(jnp.bfloat16)
    d_attended = jnp.einsum("to,io->ti", d_branch16, w_out, preferred_element_type=jnp.float32)
    d_attended16 = d_attended.astype(jnp.bfloat16).reshape(seq_rows, HEADS, HEAD_DIM)
    query_heads, key_heads, value_heads = split_heads(joined16)
    scores = masked_scores(query_heads, key_heads, in_length)
    attention = jnp.exp(scores - log_total)
    attention16 = attention.astype(jnp.bfloat16)
    d_value = jnp.einsum(
        "hqk,qhd->khd", attention16, d_attended16, preferred_element_type=jnp.float32
    )
    d_attention = jnp.einsum(
        "qhd,khd->hqk", d_attended16, value_heads, preferred_element_type=jnp.float32
    )
    d_scores = attention * (d_attention - jnp.sum(attention * d_attention, axis=-1, keepdims=True))
    d_scores16 = d_scores.astype(jnp.bfloat16)
    d_query = jnp.einsum(
        "hqk,khd->qhd", d_scores16, key_heads, preferred_element_type=jnp.float32
    ) * HEAD_DIM ** (-0.5)
    d_key = jnp.einsum(
        "hqk,qhd->khd", d_scores16, query_heads, preferred_element_type=jnp.float32
    ) * HEAD_DIM ** (-0.5)
    d_query = d_query.reshape(seq_rows, D)
    d_key = d_key.reshape(seq_rows, D)
    d_value = d_value.reshape(seq_rows, D)
    d_joined16 = jnp.concatenate([d_query, d_key, d_value], axis=1).astype(jnp.bfloat16)
    d_inputs = d_resid_one + jnp.einsum(
        "to,io->ti", d_joined16, w_qkv, preferred_element_type=jnp.float32
    )
    vec_grad = jnp.concatenate(
        [
            jnp.sum(d_query, axis=0),
            jnp.sum(d_value, axis=0),
            jnp.sum(d_resid_one, axis=0),
            jnp.sum(d_hidden, axis=0),
            jnp.sum(d_resid_two, axis=0),
            d_gain_one,
            d_shift_one,
            d_gain_two,
            d_shift_two,
        ]
    )
    pairs = (d_joined16, attended16, d_branch16, normed16, d_hidden16, active16, d_down16)
    return (pairs, vec_grad, d_inputs.astype(jnp.bfloat16))


def rotate_in(left_side, matrix, right_side):
    inner = jnp.einsum(
        "pji,pjk->pik",
        left_side,
        matrix,
        precision=PRECISION_HIGH,
        preferred_element_type=jnp.float32,
    )
    return jnp.einsum(
        "pik,pkl->pil",
        inner,
        right_side,
        precision=PRECISION_HIGH,
        preferred_element_type=jnp.float32,
    )


def rotate_out(left_side, matrix, right_side):
    inner = jnp.einsum(
        "pij,pjk->pik",
        left_side,
        matrix,
        precision=PRECISION_HIGH,
        preferred_element_type=jnp.float32,
    )
    return jnp.einsum(
        "pik,plk->pil",
        inner,
        right_side,
        precision=PRECISION_HIGH,
        preferred_element_type=jnp.float32,
    )


def per_device_any(
    tokens,
    cotangent,
    lengths,
    deal,
    weights,
    vectors,
    owners,
    left_basis,
    right_basis,
    first_moment,
    second_moment,
    vec_first,
    vec_second,
):
    dp_count = lax.axis_size("dp")
    fsdp_count = lax.axis_size("fsdp")
    dp_place = lax.axis_index("dp")
    fsdp_place = lax.axis_index("fsdp")
    micro_count = tokens.shape[0]
    my_place = dp_place * fsdp_count + fsdp_place
    quarter = lax.dynamic_index_in_dim(
        deal.reshape(micro_count, dp_count, fsdp_count), fsdp_place, axis=2, keepdims=False
    )
    quarter = quarter - fsdp_place * dp_count
    ordered = jnp.take_along_axis(tokens, quarter[:, :, None, None], axis=1)
    dealt_rows = lax.all_to_all(ordered, "dp", split_axis=1, concat_axis=2, tiled=True)
    my_seq = lax.dynamic_index_in_dim(deal, my_place, axis=1, keepdims=False)
    my_length = jnp.take_along_axis(lengths, my_seq[:, None], axis=1)[:, 0]
    shard_low = (weights.astype(jnp.bfloat16), vectors.astype(jnp.bfloat16))
    whole_tiles, whole_vecs = (
        lax.all_gather(shard_low[0], ("dp", "fsdp"), axis=0, tiled=True),
        lax.all_gather(shard_low[1], ("dp", "fsdp"), axis=0, tiled=True),
    )
    mats_kept = unpack_mats(whole_tiles)
    vecs_kept = unpack_vecs(whole_vecs.astype(jnp.float32))
    all_pairs = []
    all_inputs = []
    vec_terms = []
    results = []
    input_grads = []
    for micro_index in range(micro_count):
        inputs16 = dealt_rows[micro_index, 0]
        matrices, vecs = (mats_kept, vecs_kept)
        result, kept = forward_pass(inputs16, my_length[micro_index], matrices, vecs)
        pairs, vec_term, d_inputs = backward_pass(
            cotangent[micro_index, 0], inputs16, kept, matrices, vecs
        )
        all_pairs.append(pairs)
        all_inputs.append(inputs16)
        vec_terms.append(vec_term)
        results.append(result)
        input_grads.append(d_inputs)

    def joined_rows(index):
        return jnp.concatenate([pairs[index] for pairs in all_pairs], axis=0)

    inputs_rows = jnp.concatenate(all_inputs, axis=0)
    tile_terms = jnp.concatenate(
        [
            tiled_grad(inputs_rows, joined_rows(0)),
            tiled_grad(joined_rows(1), joined_rows(2)),
            tiled_grad(joined_rows(3), joined_rows(4)),
            tiled_grad(joined_rows(5), joined_rows(6)),
        ],
        axis=0,
    )
    grad_vec = vec_terms[0]
    for vec_term in vec_terms[1:]:
        grad_vec = grad_vec + vec_term
    shard_tiles = weights.shape[0]
    tile_grads, vec_grads = (
        lax.psum_scatter(tile_terms, ("dp", "fsdp"), scatter_dimension=0, tiled=True),
        lax.psum_scatter(grad_vec, ("dp", "fsdp"), scatter_dimension=0, tiled=True),
    )
    group_grads, group_master = (
        lax.all_gather(tile_grads.astype(jnp.bfloat16), "fsdp", axis=0, tiled=True).astype(
            tile_grads.dtype
        ),
        lax.all_gather(weights.astype(jnp.bfloat16), "fsdp", axis=0, tiled=True).astype(
            weights.dtype
        ),
    )
    result_dealt = jnp.stack(results)[:, None]
    grads_dealt = jnp.stack(input_grads)[:, None]
    back_result, back_grads = (
        lax.all_to_all(result_dealt, "dp", split_axis=2, concat_axis=1, tiled=True),
        lax.all_to_all(grads_dealt, "dp", split_axis=2, concat_axis=1, tiled=True),
    )
    restore = jnp.argsort(quarter, axis=1)
    out_tokens = jnp.take_along_axis(back_result, restore[:, :, None, None], axis=1)
    in_grad = jnp.take_along_axis(back_grads, restore[:, :, None, None], axis=1)
    group_size = fsdp_count * shard_tiles
    pick_rows = owners - dp_place * group_size
    own_grads = jnp.take(group_grads, pick_rows, axis=0)
    own_master = jnp.take(group_master, pick_rows, axis=0)
    rates = tile_rate(owners)
    rotated = rotate_in(left_basis, own_grads, right_basis)
    new_first = BETA_ONE * first_moment + (1.0 - BETA_ONE) * rotated
    new_second = BETA_TWO * second_moment + (1.0 - BETA_TWO) * rotated * rotated
    first_hat = new_first / (1.0 - BETA_ONE**STEP)
    second_hat = new_second / (1.0 - BETA_TWO**STEP)
    step_rotated = first_hat / (jnp.sqrt(second_hat) + ADAM_EPS)
    update = rotate_out(left_basis, step_rotated, right_basis)
    new_tiles = own_master - rates[:, None, None] * (update + DECAY * own_master)
    vec_first_new = BETA_ONE * vec_first + (1.0 - BETA_ONE) * vec_grads
    vec_second_new = BETA_TWO * vec_second + (1.0 - BETA_TWO) * vec_grads * vec_grads
    vec_hat_one = vec_first_new / (1.0 - BETA_ONE**STEP)
    vec_hat_two = vec_second_new / (1.0 - BETA_TWO**STEP)
    new_vectors = vectors - VEC_RATE * vec_hat_one / (jnp.sqrt(vec_hat_two) + ADAM_EPS)
    return (
        out_tokens,
        in_grad,
        tile_grads,
        vec_grads,
        new_first,
        new_second,
        new_tiles,
        new_tiles.astype(jnp.bfloat16),
        vec_first_new,
        vec_second_new,
        new_vectors,
    )


CHUNK = 256
ROWS_AT_ONCE = 128
f32 = jnp.float32
bf = jnp.bfloat16


def mul(a, b):
    return jnp.dot(a, b, preferred_element_type=f32)


def mul_t(a, b):
    return lax.dot_general(a, b, (((1,), (1,)), ((), ())), preferred_element_type=f32)


def t_mul(a, b):
    return lax.dot_general(a, b, (((0,), (0,)), ((), ())), preferred_element_type=f32)


def column_chunks():
    return [slice(j * CHUNK, (j + 1) * CHUNK) for j in range(D // CHUNK)]


class Layer:
    def __init__(self, **refs):
        self.__dict__.update(refs)
        self.rows = self.l3.shape[1]
        self.seqs = self.rows // TB

    def left(self, first, count=8):
        return jnp.concatenate([self.l3[first + j] for j in range(count)], axis=1)

    def each_rows(self, fn):
        def body(i, _):
            fn(pl.ds(pl.multiple_of(i * ROWS_AT_ONCE, ROWS_AT_ONCE), ROWS_AT_ONCE), i)
            return 0

        lax.fori_loop(0, self.rows // ROWS_AT_ONCE, body, 0)

    def counted(self, i):
        per = TB // ROWS_AT_ONCE
        at = (i % per) * ROWS_AT_ONCE + lax.broadcasted_iota(jnp.int32, (ROWS_AT_ONCE, 1), 0)
        return at < self.lens[i // per]

    def add_sum(self, n, value, cols=slice(None)):
        self.vsum[n, :, cols] += value.reshape(value.shape[0] // 8, 8, value.shape[1]).sum(axis=0)

    def project(self, t):
        x = self.left(0)
        for j, cols in enumerate(column_chunks()):
            out = mul(x, self.wcols(t, cols))
            if t != 1:
                out = out + self.vec[pl.ds(0 if t == 0 else 1, 1), cols]
            out = out.astype(bf)
            for i in range(CHUNK // TB):
                self.q3[t, j * (CHUNK // TB) + i] = out[:, i * TB : (i + 1) * TB]

    def two(self, block):
        lane = lax.broadcasted_iota(jnp.int32, block.shape, 1)
        zero = jnp.zeros_like(block)
        return jnp.concatenate(
            [jnp.where(lane < HEAD_DIM, block, zero), jnp.where(lane < HEAD_DIM, zero, block)], axis=0
        )

    def one(self, stacked):
        top, low = stacked[:TB], stacked[TB:]
        lane = lax.broadcasted_iota(jnp.int32, top.shape, 1)
        return jnp.where(lane < HEAD_DIM, top, low)

    def attend(self):
        def body(b, _):
            at = pl.ds(pl.multiple_of(b * TB, TB), TB)
            key = lax.broadcasted_iota(jnp.int32, (2 * TB, TB), 1)
            seen = key < self.lens[b]
            for h in range(HEADS // 2):
                s = mul_t(self.two(self.q3[0, h, at]), self.q3[1, h, at]) * HEAD_DIM**-0.5
                s = jnp.where(seen, s, -1e30)
                e = jnp.exp(s - jnp.max(s, axis=1, keepdims=True))
                p = e * (1.0 / jnp.sum(e, axis=1, keepdims=True))
                self.p3[b, h] = p
                a = self.one(mul(p.astype(bf), self.q3[2, h, at]))
                self.l3[8 + h, at] = a.astype(bf)
            return 0

        lax.fori_loop(0, self.seqs, body, 0)

    def norm_one(self):
        a = self.left(8)
        for j, cols in enumerate(column_chunks()):
            x = jnp.concatenate([self.l3[2 * j], self.l3[2 * j + 1]], axis=1).astype(f32)
            self.xh[:, cols] = x + mul(a, self.wcols(3, cols)) + self.vec[pl.ds(2, 1), cols]

        def rows(at, i):
            r = self.xh[at]
            center = r - jnp.mean(r, axis=1, keepdims=True)
            scale = lax.rsqrt(jnp.mean(center * center, axis=1, keepdims=True) + EPS_NORM)
            hat = center * scale
            self.xh[at] = hat
            self.rs[at] = jnp.broadcast_to(scale, (ROWS_AT_ONCE, TB))
            u = hat * self.vec[pl.ds(8, 1)] + self.vec[pl.ds(9, 1)]
            self.acc[at] = u
            u16 = u.astype(bf)
            for j in range(8):
                self.l3[16 + j, at] = u16[:, j * TB : (j + 1) * TB]

        self.each_rows(rows)

    def up_begin(self, t):
        u = self.left(16, 4)
        for cols in column_chunks():
            self.gp[t, :, cols] = mul(u, self.wcols(4 + t, cols, 0)) + self.vec[pl.ds(3 + t, 1), cols]

    def up_end(self, t):
        u = self.left(20, 4)
        for cols in column_chunks():
            self.gp[t, :, cols] += mul(u, self.wcols(4 + t, cols, 1))

        def rows(at, i):
            h = self.gp[t, at]
            cdf = 0.5 + 0.5 * lax.erf(h * 0.7071067811865476)
            self.gp[t, at] = cdf + h * (0.3989422804014327 * jnp.exp(-0.5 * h * h))
            e = (h * cdf).astype(bf)
            for j in range(8):
                self.l3[24 + 8 * t + j, at] = e[:, j * TB : (j + 1) * TB]

        self.each_rows(rows)

    def down(self, t):
        e = self.left(24 + 8 * t)
        for cols in column_chunks():
            self.acc[:, cols] += mul(e, self.wcols(8 + t, cols))

    def norm_two(self):
        def rows(at, i):
            r = self.acc[at] + self.vec[pl.ds(7, 1)]
            center = r - jnp.mean(r, axis=1, keepdims=True)
            scale = lax.rsqrt(jnp.mean(center * center, axis=1, keepdims=True) + EPS_NORM)
            hat = center * scale
            live = self.counted(i)
            gain = self.vec[pl.ds(10, 1)]
            out = jnp.where(live, hat * gain + self.vec[pl.ds(11, 1)], 0.0).astype(bf)
            per = TB // ROWS_AT_ONCE
            slabs = ROWS_AT_ONCE // self.res.shape[2]
            self.res[i // per, pl.ds((i % per) * slabs, slabs)] = out.reshape(
                slabs, self.res.shape[2], D
            )
            dy = jnp.where(live, self.cot[at].astype(f32), 0.0)
            self.add_sum(10, dy * hat)
            self.add_sum(11, dy)
            g = dy * gain
            dr = scale * (
                g
                - jnp.mean(g, axis=1, keepdims=True)
                - hat * jnp.mean(g * hat, axis=1, keepdims=True)
            )
            self.add_sum(7, dr)
            self.acc[at] = dr
            self.d2[at] = dr.astype(bf)

        self.each_rows(rows)

    def down_back(self, t):
        d = self.r3[8]
        for cols in column_chunks():
            dh = mul_t(d, self.wrows(8 + t, cols)) * self.gp[t, :, cols]
            self.add_sum(3 + t, dh, cols)
            self.r3[4 + t, :, cols] = dh.astype(bf)

    def up_back(self, t):
        d = self.r3[4 + t]
        for cols in column_chunks():
            self.acc[:, cols] += mul_t(d, self.wrows(4 + t, cols))

    def norm_one_back(self):
        def rows(at, i):
            du, hat = self.acc[at], self.xh[at]
            self.add_sum(8, du * hat)
            self.add_sum(9, du)
            g = du * self.vec[pl.ds(8, 1)]
            dr = self.rs[at][:, :1] * (
                g
                - jnp.mean(g, axis=1, keepdims=True)
                - hat * jnp.mean(g * hat, axis=1, keepdims=True)
            )
            self.add_sum(2, dr)
            self.acc[at] = dr
            self.r3[3, at] = dr.astype(bf)

        self.each_rows(rows)

    def out_back(self):
        d = self.r3[3]
        for j, cols in enumerate(column_chunks()):
            da = mul_t(d, self.wrows(3, cols)).astype(bf)
            for i in range(CHUNK // TB):
                self.da3[j * (CHUNK // TB) + i] = da[:, i * TB : (i + 1) * TB]

    def attend_back(self):
        def body(b, _):
            at = pl.ds(pl.multiple_of(b * TB, TB), TB)
            for h in range(HEADS // 2):
                cols = slice(h * TB, (h + 1) * TB)
                p = self.p3[b, h]
                da = self.two(self.da3[h, at])
                dv = t_mul(p.astype(bf), da)
                pd = p * mul_t(da, self.q3[2, h, at])
                ds = (pd - p * jnp.sum(pd, axis=1, keepdims=True)).astype(bf)
                dq = self.one(mul(ds, self.q3[1, h, at])) * HEAD_DIM**-0.5
                dk = t_mul(ds, self.two(self.q3[0, h, at])) * HEAD_DIM**-0.5
                self.r3[0, at, cols] = dq.astype(bf)
                self.r3[1, at, cols] = dk.astype(bf)
                self.r3[2, at, cols] = dv.astype(bf)
                self.add_sum(0, dq, cols)
                self.add_sum(1, dv, cols)
            return 0

        lax.fori_loop(0, self.seqs, body, 0)

    def project_back(self, t):
        d = self.r3[t]
        for cols in column_chunks():
            value = self.acc[:, cols] + mul_t(d, self.wrows(t, cols))
            if t < 2:
                self.acc[:, cols] = value
            else:
                self.din[:, :, :, cols] = value.astype(bf).reshape(self.din.shape[:3] + (CHUNK,))


MESH = pl.DeviceIdType.MESH
ZN = 4
OCT = 96
RING = 8
SPOTS = 16


class Place:
    def __init__(self):
        self.dp = lax.axis_index("dp")
        self.fs = lax.axis_index("fsdp")
        self.z, self.y = self.dp // 2, self.dp % 2
        self.x, self.c = self.fs // 2, self.fs % 2
        self.to_x = (self.dp, (self.fs + 2) % 4)
        self.to_y = (self.z * 2 + 1 - self.y, self.fs)
        self.to_core = (self.dp, self.x * 2 + 1 - self.c)
        self.to_up = (self.dp + 2, self.fs)
        self.to_down = (self.dp - 2, self.fs)
        near = self.z + 1 - 2 * (self.z % 2)
        far = (self.z + 2) % ZN
        self.doubling = [
            self.to_core,
            self.to_x,
            self.to_y,
            (near * 2 + self.y, self.fs),
            (far * 2 + self.y, self.fs),
        ]

    def peer(self, j):
        return (self.dp + j) % (2 * ZN)

    def greet(self):
        bar = pltpu.get_barrier_semaphore()
        for dev in [self.to_x, self.to_core] + [(self.peer(j), self.fs) for j in range(1, 2 * ZN)]:
            pl.semaphore_signal(bar, inc=1, device_id=dev, device_id_type=MESH)

    def greeted(self):
        pl.semaphore_wait(pltpu.get_barrier_semaphore(), 1 + 2 * ZN)

    def octet(self, dx, dy, zp, k, c=None):
        yy = self.y if dy == 0 else 1 - self.y
        xx = self.x if dx == 0 else 1 - self.x
        return ((zp * 2 + yy) * 4 + xx * 2 + (self.c if c is None else c)) * 3 + k

    def plane(self, table, i):
        zp = table[0][i]
        for n in range(1, ZN):
            zp = jnp.where(self.z == n, table[n][i], zp)
        return zp


def octet_place(o):
    return jnp.where(
        o < 24,
        (o % 3) * 8 + o // 3,
        jnp.where((o >= 32) & (o < 64), 32 + ((o - 32) % 4) * 8 + (o - 32) // 4, o),
    )


def left_block(o):
    return jnp.where(
        o < 24, o // 3, jnp.where(o < 32, o - 16, jnp.where(o < 64, 16 + (o - 32) // 4, o - 40))
    )


def right_block(o):
    return jnp.where(o < 24, o % 3, jnp.where(o < 32, 3, jnp.where(o < 64, 4 + (o - 32) % 4, 8)))


def wait_for(ref, sem):
    pltpu.make_async_copy(ref, ref, sem).wait()


def remote(src, dst, send_sem, recv_sem, dev):
    return pltpu.make_async_remote_copy(
        src_ref=src,
        dst_ref=dst,
        send_sem=send_sem,
        recv_sem=recv_sem,
        device_id=dev,
        device_id_type=MESH,
    )


def start_deal(p, src, dst, s_sem, r_sem, l_sem):
    for j in range(1, 2 * ZN):
        d = p.peer(j)
        remote(src.at[:, d], dst.at[:, p.dp], s_sem, r_sem.at[p.dp], (d, p.fs)).start()
    pltpu.make_async_copy(src.at[:, p.dp], dst.at[:, p.dp], l_sem).start()


def end_deal(p, src, dst, s_sem, r_sem, l_sem):
    for j in range(1, 2 * ZN):
        d = p.peer(j)
        wait_for(dst.at[:, d], r_sem.at[d])
    wait_for(dst.at[:, p.dp], l_sem)
    wait_for(src.at[:, pl.ds(0, 2 * ZN - 1)], s_sem)


FORWARD_STEPS = [
    "P0", "P1", "P2", "ATT", "N1", "UA0", "UA1", "UA2", "UA3",
    "UB0", "UB1", "UB2", "UB3", "D0", "D1", "D2", "D3", "N2",
]
FORWARD_NEEDS = {"P0": (0,), "N1": (1,), "UB0": (2,), "D1": (3,)}
FORWARD_ROUTES = [
    ["xyx", "zzx", "zzy", "zxy"],
    ["zzz", "xyx", "zzz", "zzz"],
    ["zzz", "zzz", "xyx", "zzz"],
    ["zxy", "zzy", "zzx", "xyx"],
]
FORWARD_PLANS = [
    [
        0, 100, 1, 600, 2, 101, 102, 11, 200, 601, 111, 202, 602, 201, 22, 10,
        122, 110, 12, 301, 112, 300, 222, 212, 603, 604, 302, 605, 20, 120, 312, 31,
        32, 21, 311, 131, 220, 211, 132, 1000, 1001, 210, 310, 1002, 121, 1003, 322, 1004,
        1005, 232, 231, 30, 1006, 1007, 321, 130, 320, 1008, 221, 1009, 331, 1010, 332, 330,
        1011, 1012, 230, 1013, 1014, 1015, 1016, 1017,
    ],
    [
        11, 12, 112, 10, 110, 600, 111, 601, 22, 212, 122, 2, 602, 102, 1, 222,
        0, 20, 21, 210, 121, 202, 603, 31, 211, 301, 120, 300, 32, 311, 101, 100,
        310, 131, 302, 312, 200, 201, 221, 604, 30, 605, 1000, 322, 132, 130, 1001, 1002,
        220, 321, 1003, 1004, 1005, 320, 1006, 1007, 1008, 330, 232, 1009, 1010, 231, 1011, 331,
        1012, 1013, 230, 332, 1014, 1015, 1016, 1017,
    ],
    [
        600, 22, 122, 222, 601, 20, 11, 120, 31, 602, 12, 21, 121, 603, 30, 32,
        10, 111, 220, 110, 221, 322, 604, 132, 2, 1, 112, 211, 210, 331, 101, 0,
        330, 321, 100, 300, 232, 201, 311, 310, 320, 301, 102, 332, 130, 200, 605, 302,
        202, 1000, 1001, 131, 1002, 212, 312, 1003, 1004, 1005, 1006, 230, 1007, 1008, 1009, 1010,
        231, 1011, 1012, 1013, 1014, 1015, 1016, 1017,
    ],
    [
        32, 132, 31, 30, 130, 600, 131, 601, 230, 22, 122, 602, 231, 11, 20, 222,
        12, 112, 232, 120, 111, 603, 331, 2, 330, 604, 212, 102, 322, 0, 220, 1,
        332, 101, 100, 10, 201, 202, 211, 312, 300, 311, 21, 110, 200, 302, 121, 605,
        301, 1000, 1001, 1002, 321, 310, 210, 1003, 1004, 320, 1005, 221, 1006, 1007, 1008, 1009,
        1010, 1011, 1012, 1013, 1014, 1015, 1016, 1017,
    ],
]


def along_z(here, zp, k=None):
    up = zp <= here < ZN - 1 and (k is None or FORWARD_ROUTES[here + 1][zp][k] == "z")
    down = zp >= here > 0 and (k is None or FORWARD_ROUTES[here - 1][zp][k] == "z")
    return (["u"] if up else []) + (["d"] if down else [])


def split_plan(plan):
    parts = [[]]
    for code in plan:
        if code >= 1000:
            parts.append([])
        else:
            parts[-1].append(code)
    return parts


def forward_kernel(
    lengths, deal, weights, vec, tok, cot_in,
    wm, l3_out, d2_out, acc_out, gp_out, xh_out, rs_out, p3_out, q3_out, res_out, vsum, vecs,
    wbuf, vbuf, xl, xs, cot, l3, d2, q3, p3, xh, rs, acc, gp, res,
    r_w, s_x, s_y, s_up, s_down, s_core, s_local, s_vec, r_vec, s_tok, r_tok, l_tok, s_out, r_cot,
):
    p = Place()
    z = p.z
    p.greet()
    me = p.dp * 4 + p.fs
    get_cot = pltpu.make_async_copy(cot_in, cot, r_cot)
    get_cot.start()

    class Lens:
        def __getitem__(self, b):
            return lengths[b, jnp.clip(deal[b, me], 0, lengths.shape[1] - 1)]

    def wcols(n, cols, half=None):
        if half is None:
            return wbuf[8 * n : 8 * n + 8, :, cols].reshape(D, CHUNK)
        first = 8 * n + 4 * half
        return wbuf[first : first + 4, :, cols].reshape(D // 2, CHUNK)

    f = Layer(
        lens=Lens(), vec=vecs, l3=l3, d2=d2, vsum=vsum, q3=q3, p3=p3, xh=xh, rs=rs, acc=acc, gp=gp,
        res=res, cot=cot, wcols=wcols,
    )

    def ref_of(o):
        return wbuf.at[octet_place(o)]

    def wait(o):
        wait_for(ref_of(o), r_w.at[o])

    seqs = tok.shape[1]
    for b in range(tok.shape[0]):
        for j in range(seqs):
            xs[b, j] = tok[b, jnp.clip(deal[b, j * 4 + p.fs] - p.fs * seqs, 0, seqs - 1)]
    for k in range(3):
        place = octet_place(p.octet(0, 0, z, k))
        for j in range(8):
            wbuf[place, :, j * TB : (j + 1) * TB] = weights[8 * k + j].astype(bf)
    vbuf[me] = jnp.zeros(vbuf.shape[1:], f32)
    vbuf[me, :3] = vec[...].astype(bf).astype(f32)
    p.greeted()
    start_deal(p, xs, xl, s_tok, r_tok, l_tok)

    def vec_step(n):
        size = 2**n
        if n > 0:
            half = size // 2
            theirs = (me // half) * half
            theirs = theirs + half * (1 - 2 * (theirs // half % 2))
            wait_for(vbuf.at[pl.ds(theirs, half)], r_vec.at[n - 1])
        if n < 5:
            mine = vbuf.at[pl.ds((me // size) * size, size)]
            remote(mine, mine, s_vec.at[n], r_vec.at[n], p.doubling[n]).start()

    def vec_rows():
        for m in range(OCT):
            cols = slice((m % 8) * TB, (m % 8 + 1) * TB)
            vecs[m // 8 : m // 8 + 1, cols] = vbuf[m // 3, m % 3 : m % 3 + 1, :]

    sent = [dict(x=0, y=0, u=0, d=0, c=0) for _ in range(ZN)]
    way = dict(
        x=(p.to_x, s_x), y=(p.to_y, s_y), u=(p.to_up, s_up), d=(p.to_down, s_down),
        c=(p.to_core, s_core),
    )

    def item(here, kind, zp, k):
        if kind == 6:
            vec_step(k)
            return

        def send(o, *ways):
            ref = ref_of(o)
            for w in ways:
                dev, sem = way[w]
                remote(ref, ref, sem, r_w.at[o], dev).start()
                sent[here][w] += 1

        route = FORWARD_ROUTES[here][zp][k]
        if kind == 0:
            o = p.octet(0, 0, zp, k)
            if zp != here:
                wait(o)
            send(o, *along_z(here, zp))
        elif kind == 1:
            send(p.octet(0, 0, zp, k), "x", "y", "c")
        elif kind == 2:
            o = p.octet(0, 1, zp, k)
            wait(o)
            send(o, *(["x"] if route == "x" else []), "c")
            o = p.octet(1, 0, zp, k)
            wait(o)
            send(o, *(["y"] if route == "y" else []), "c")
        else:
            o = p.octet(1, 1, zp, k)
            wait(o)
            send(o, *along_z(here, zp, k), "c")

    def partner(zp):
        for dx in range(2):
            for dy in range(2):
                for k in range(3):
                    wait(p.octet(dx, dy, zp, k, 1 - p.c))

    outs = []

    def give(src, dst):
        copy = pltpu.make_async_copy(src, dst, s_out.at[len(outs)])
        copy.start()
        outs.append(copy)

    def give_square(n):
        give(wbuf.at[pl.ds(8 * n, 8)], wm.at[pl.ds(8 * n, 8)])

    def compute(name):
        t = int(name[-1]) if name[-1].isdigit() else 0
        if name == "P0":
            vec_rows()
            vsum[...] = jnp.zeros_like(vsum)
            end_deal(p, xs, xl, s_tok, r_tok, l_tok)
            for j in range(8):
                l3[j] = xl[:, :, :, j * TB : (j + 1) * TB].reshape(l3.shape[1], TB)
        if name[0] == "P":
            f.project(t)
            give_square(t)
        elif name == "ATT":
            f.attend()
            give(q3, q3_out)
            give(p3, p3_out)
        elif name == "N1":
            f.norm_one()
            give_square(3)
            give(xh, xh_out)
            give(rs, rs_out)
        elif name[:2] == "UA":
            f.up_begin(t)
        elif name[:2] == "UB":
            f.up_end(t)
            give_square(4 + t)
            give(gp.at[t], gp_out.at[t])
            if t == 3:
                give(l3, l3_out)
        elif name[0] == "D":
            f.down(t)
            give_square(8 + t)
        else:
            get_cot.wait()
            f.norm_two()
            give(d2, d2_out)
            give(acc, acc_out)
            give(res, res_out)

    parts = [split_plan(plan) for plan in FORWARD_PLANS]
    for n in range(len(FORWARD_STEPS) + 1):

        def run(here):
            for code in parts[here][n]:
                item(here, code // 100, code // 10 % 10, code % 10)

        for here in range(ZN):
            pl.when(z == here)(functools.partial(run, here))
        if n < len(FORWARD_STEPS):
            name = FORWARD_STEPS[n]
            for zp in FORWARD_NEEDS.get(name, ()):
                partner(zp)
            compute(name)

    for copy in outs:
        copy.wait()
    for n in range(5):
        wait_for(vbuf.at[pl.ds(0, 2**n)], s_vec.at[n])

    def drain(here):
        for w, n in sent[here].items():
            if n:
                wait_for(wbuf.at[pl.ds(0, n)], way[w][1])

    for here in range(ZN):
        pl.when(z == here)(functools.partial(drain, here))


def forward(lengths, deal, weights, vec, tok, cot):
    dma = pltpu.SemaphoreType.DMA
    rows = cot.shape[0]
    vmem = pl.BlockSpec(memory_space=pltpu.VMEM)
    far = pl.BlockSpec(memory_space=pl.ANY)
    out = jax.ShapeDtypeStruct
    stages = (
        out((56, rows, TB), bf),
        out((rows, D), bf),
        out((rows, D), f32),
        out((4, rows, D), f32),
        out((rows, D), f32),
        out((rows, TB), f32),
        out((rows // TB, 8, 2 * TB, TB), f32),
        out((3, 8, rows, TB), bf),
        out(tok.shape, bf),
    )
    scratch = [pltpu.VMEM(s.shape, s.dtype) for s in stages]
    l3, d2, acc, gp, xh, rs, p3, q3, res = scratch
    return pl.pallas_call(
        forward_kernel,
        out_shape=(out((OCT, TB, D), bf),) + stages + (out((12, 8, D), f32), out((12, D), f32)),
        in_specs=[pl.BlockSpec(memory_space=pltpu.SMEM)] * 2 + [vmem] * 3 + [far],
        out_specs=(far,) * 10 + (vmem,) * 2,
        scratch_shapes=[
            pltpu.VMEM((OCT, TB, D), bf), pltpu.VMEM((32, 8, TB), f32), pltpu.VMEM(tok.shape, bf),
            pltpu.VMEM(tok.shape, bf), pltpu.VMEM(cot.shape, bf),
            l3, d2, q3, p3, xh, rs, acc, gp, res,
            dma((OCT,)), dma, dma, dma, dma, dma, dma((3,)), dma((5,)), dma((5,)),
            dma, dma((2 * ZN,)), dma, dma((32,)), dma,
        ],
        compiler_params=pltpu.CompilerParams(
            collective_id=0, has_side_effects=True, vmem_limit_bytes=62 * 2**20
        ),
        name="forward",
    )(lengths, deal, weights, vec, tok, cot)


BACKWARD_STEPS = [
    "DB0", "DB1", "DB2", "DB3", "UB0", "UB1", "UB2", "UB3",
    "N1B", "OB", "ATB", "PB0", "PB1", "PB2",
]
BACKWARD_ROUTES = [
    ["xyy", "zzx", "zzy", "zzx"],
    ["zzz", "xyy", "zzz", "zzz"],
    ["zzz", "zzz", "xyy", "zzz"],
    ["zzx", "zzy", "zzx", "xyy"],
]
BACKWARD_PLANS = [
    [
        31, 30, 1000, 131, 231, 1001, 130, 1002, 32, 230, 1003, 1004, 1005, 21, 1006, 1007,
        121, 132, 221, 330, 20, 22, 120, 220, 1008, 331, 122, 232, 1009, 1010, 10, 110,
        210, 0, 222, 12, 600, 332, 11, 601, 2, 111, 320, 102, 321, 1011, 112, 310,
        211, 1, 322, 100, 602, 202, 212, 101, 603, 200, 311, 312, 201, 1012, 500, 1013,
        300, 301, 604, 400, 302, 501, 605, 401, 402,
    ],
    [
        500, 30, 1000, 32, 230, 1001, 1002, 1003, 22, 132, 1004, 31, 1005, 122, 1006, 222,
        20, 1007, 130, 21, 1008, 12, 1009, 220, 1010, 232, 0, 1011, 231, 131, 1012, 1013,
        121, 2, 120, 600, 221, 330, 601, 10, 200, 11, 102, 1, 201, 110, 202, 332,
        100, 331, 111, 112, 101, 320, 210, 300, 321, 211, 212, 322, 310, 602, 301, 311,
        302, 603, 501, 312, 401, 604, 605, 400, 402,
    ],
    [
        32, 30, 1000, 1001, 1002, 500, 230, 1003, 1004, 1005, 1006, 1007, 1008, 12, 11, 232,
        1009, 112, 1010, 0, 2, 200, 212, 31, 20, 102, 211, 1011, 111, 10, 132, 21,
        1, 1012, 110, 201, 22, 600, 131, 210, 121, 601, 100, 101, 130, 301, 120, 231,
        330, 220, 202, 300, 122, 332, 602, 331, 221, 311, 1013, 310, 302, 222, 603, 312,
        501, 320, 321, 322, 604, 401, 400, 402, 605,
    ],
    [
        500, 1000, 1001, 1002, 1003, 21, 1004, 221, 1005, 121, 20, 1006, 1007, 220, 1008, 11,
        120, 10, 211, 1009, 210, 111, 1010, 1, 110, 600, 201, 0, 12, 100, 2, 200,
        301, 22, 31, 112, 102, 122, 101, 310, 32, 30, 300, 132, 212, 202, 311, 601,
        1011, 320, 130, 232, 302, 1012, 312, 131, 1013, 231, 321, 602, 222, 603, 331, 230,
        332, 322, 401, 604, 501, 330, 402, 605, 400,
    ],
]


def backward_codes(here):
    routes = BACKWARD_ROUTES
    spots = {}
    for way in "xy":
        pairs = [(zp, k) for zp in range(ZN) for k in range(3) if routes[here][zp][k] == way]
        spots.update({pair: n for n, pair in enumerate(pairs)})

    def octet(side, zp, k):
        dx, dy = side % 2, side // 2
        own = zp == here
        route = routes[here][zp][k]
        code = k + 4 * zp + 16 * side + 131072
        along = "u" if zp > here else "d"
        if side == 0:
            code += 64 + 128
            way = "f" if own else along
        elif side == 1:
            code += 128 * (route == "y")
            way = "x"
        elif side == 2:
            code += 64 * (route == "x")
            way = "y"
        else:
            way = along if route == "z" else route
        if side in (0, 3):
            for step, there, bit in ((1, here - 1, 256), (-1, here + 1, 512)):
                if 0 <= there < ZN and (zp - here) * step >= 0:
                    code += bit * (side == 0 or routes[there][zp][k] == "z")
        return code + 1024 * "xyudf".index(way) + 8192 * spots.get((zp, k), 0)

    parts, first = [[]], 0
    for item in BACKWARD_PLANS[here]:
        if item >= 1000:
            parts.append([])
            continue
        kind, zp, k = item // 100, item // 10 % 10, item % 10
        if kind == 0:
            parts[-1].append(k + 4 * zp + 64 * (first >= 2) + 8192 * (first % 2))
            first += 1
        elif kind == 1:
            parts[-1].append(octet(3, zp, k))
        elif kind == 2:
            parts[-1] += [octet(2, zp, k), octet(1, zp, k)]
        elif kind == 3:
            parts[-1].append(octet(0, zp, k))
        elif kind == 4:
            parts[-1].append(131072 * 2 + k)
        elif kind == 5:
            parts[-1].append(131072 * (3 + k))
        else:
            parts[-1].append(131072 * (5 + k))
    return parts


def backward_kernel(
    wm, l3_in, d2_in, acc_in, gp_in, xh_in, rs_in, p3_in, q3_in, res, vsum_in, vec,
    tiles, grp, vout, res_back, din_back,
    l3, r3, acc, gp, xh, rs, p3, q3, da3, din, wb, vsum,
    land_c, land_x, land_y, land_z, ring, vland, total,
    r_in, r_wb, r_c, r_x, r_y, r_z, r_e, r_v, s_ring, s_x, s_y, s_up, s_down, s_e, s_e2, s_v,
    s_res, r_res, l_res, s_din, r_din, l_din,
):
    p = Place()
    z, c, fs = p.z, p.c, p.fs
    p.greet()
    weights = [8, 9, 10, 11, 4, 5, 6, 7, 3, 0, 1, 2]
    slots = wb.shape[0]

    def bring(n):
        if n < len(weights):
            pltpu.make_async_copy(
                wm.at[pl.ds(8 * weights[n], 8)], wb.at[n % slots], r_wb.at[n % slots]
            ).start()

    pairs = [(d2_in, r3.at[8]), (l3_in, l3)]
    pairs += [(gp_in.at[t], gp.at[t]) for t in range(4)]
    pairs += [(acc_in, acc), (xh_in, xh), (rs_in, rs), (p3_in, p3), (q3_in, q3)]
    takes = [pltpu.make_async_copy(src, dst, r_in.at[n]) for n, (src, dst) in enumerate(pairs)]
    for n, copy in enumerate(takes):
        copy.start()
        if 2 <= n < 2 + slots:
            bring(n - 2)
    vsum[...] = vsum_in[...]
    p.greeted()

    def wrows(n, rows):
        at = slice(rows.start // TB, rows.stop // TB)
        return wb[weights.index(n) % slots, at].reshape(CHUNK, D)

    f = Layer(
        vec=vec, l3=l3, r3=r3, vsum=vsum, q3=q3, p3=p3, da3=da3, xh=xh, rs=rs, acc=acc, gp=gp,
        din=din, wrows=wrows,
    )

    def part(o):
        return t_mul(l3[left_block(o)], r3[right_block(o)])

    def add(land, sem, n):
        wait_for(land.at[n], sem.at[n])
        total[...] += land[n].astype(f32)

    def to_partner(zp, k, slot, again):
        def body(j, _):
            yy, xx = j % 2, j // 2
            o = ((zp * 2 + yy) * 4 + xx * 2 + (1 - c)) * 3 + k
            n = slot * 4 + j
            value = part(o).astype(bf)
            pl.when(again == 1)(lambda: wait_for(ring.at[0], s_ring.at[n]))
            ring[n] = value
            q = ((jnp.where(yy == p.y, 0, 2) + jnp.where(xx == p.x, 0, 1)) * ZN + zp) * 3 + k
            remote(ring.at[n], land_c.at[q], s_ring.at[n], r_c.at[q], p.to_core).start()
            return 0

        lax.fori_loop(0, 4, body, 0)

    def octet_step(code, zp, k):
        side = code // 16 % 4
        dx, dy = side % 2, side // 2
        corner = side // 3
        q = (side * ZN + zp) * 3 + k
        yy = p.y + dy * (1 - 2 * p.y)
        xx = p.x + dx * (1 - 2 * p.x)
        o = ((zp * 2 + yy) * 4 + xx * 2 + c) * 3 + k
        wait_for(land_c.at[q], r_c.at[q])
        total[...] = part(o) + land_c[q].astype(f32)
        spot = 12 + code // 8192 % 16
        flat = zp * 3 + k
        column = jnp.where(side == 0, flat, spot)
        n = corner * 12 + flat
        mine = 24 + corner * 3 + k
        above = jnp.where(zp == z, mine, n)
        below_to = jnp.where(zp == z - 1, mine, n)
        pl.when(code // 64 % 2 == 1)(functools.partial(add, land_x, r_x, column))
        pl.when(code // 128 % 2 == 1)(functools.partial(add, land_y, r_y, column))
        pl.when(code // 256 % 2 == 1)(functools.partial(add, land_z, r_z, n))
        pl.when(code // 512 % 2 == 1)(functools.partial(add, land_z, r_z, above))
        way = code // 1024 % 8
        t = jnp.where(side == 3, spot, flat)

        @pl.when(way < 4)
        def _():
            land_c[q] = total[...].astype(bf)
            src = land_c.at[q]
            pl.when(way == 0)(lambda: remote(src, land_x.at[t], s_x, r_x.at[t], p.to_x).start())
            pl.when(way == 1)(lambda: remote(src, land_y.at[t], s_y, r_y.at[t], p.to_y).start())
            pl.when(way == 2)(lambda: remote(src, land_z.at[n], s_up, r_z.at[n], p.to_up).start())
            pl.when(way == 3)(
                lambda: remote(
                    src, land_z.at[below_to], s_down, r_z.at[below_to], p.to_down
                ).start()
            )

        @pl.when(way == 4)
        def _():
            for j in range(8):
                piece = total[:, j * TB : (j + 1) * TB]
                tiles[8 * k + j] = piece
                grp[fs * 24 + 8 * k + j] = piece.astype(bf)
            mine = grp.at[pl.ds(fs * 24 + 8 * k, 8)]
            remote(mine, mine, s_e, r_e.at[fs * 3 + k], p.to_x).start()
            remote(mine, mine, s_e2, r_e.at[fs * 3 + k], p.to_core).start()

    def hand_on(k):
        fx = (fs + 2) % 4
        block = grp.at[pl.ds(fx * 24 + 8 * k, 8)]
        wait_for(block, r_e.at[fx * 3 + k])
        remote(block, block, s_e2, r_e.at[fx * 3 + k], p.to_core).start()

    def vec_step(n):
        if n == 0:
            sums = vsum[...].sum(axis=1)
            for j in range(8):
                vout[pl.ds(12 * j, 12)] = sums[:, j * TB : (j + 1) * TB]
        else:
            wait_for(vland.at[n - 1], r_v.at[n - 1])
            vout[...] = vout[...] + vland[n - 1]
        if n < 5:
            vland[5 + n] = vout[...]
            remote(vland.at[5 + n], vland.at[n], s_v.at[n], r_v.at[n], p.doubling[n]).start()

    def run_codes(lists):
        longest = max(len(codes) for codes in lists)
        if longest == 0:
            return

        def of_plane(values):
            got = values[0]
            for here in range(1, ZN):
                if values[here] != values[0]:
                    got = jnp.where(z == here, values[here], got)
            return got

        count = of_plane([len(codes) for codes in lists])
        table = [of_plane([codes[i] if i < len(codes) else 0 for codes in lists]) for i in range(longest)]

        def body(i, _):
            code = table[0]
            for j in range(1, longest):
                code = jnp.where(i == j, table[j], code)
            kind = code // 131072
            zp, k = code // 4 % 4, code % 4
            pl.when(kind == 0)(lambda: to_partner(zp, k, code // 8192 % 16, code // 64 % 2))
            pl.when(kind == 1)(lambda: octet_step(code, zp, k))
            pl.when(kind == 2)(lambda: hand_on(k))
            pl.when(kind == 3)(lambda: start_deal(p, res, res_back, s_res, r_res, l_res))
            pl.when(kind == 4)(lambda: start_deal(p, din, din_back, s_din, r_din, l_din))
            for n in range(6):
                pl.when(kind == 5 + n)(functools.partial(vec_step, n))
            return 0

        lax.fori_loop(0, count, body, 0)

    used = [0]

    def square(step):
        n = used[0]
        used[0] += 1
        wait_for(wb.at[n % slots], r_wb.at[n % slots])
        step()
        bring(n + slots)

    def compute(name):
        t = int(name[-1]) if name[-1].isdigit() else 0
        if name[:2] == "DB":
            takes[2 + t].wait()
            square(lambda: f.down_back(t))
        elif name[:2] == "UB":
            if t == 0:
                takes[6].wait()
            square(lambda: f.up_back(t))
        elif name == "N1B":
            takes[7].wait()
            takes[8].wait()
            f.norm_one_back()
        elif name == "OB":
            square(f.out_back)
        elif name == "ATB":
            takes[9].wait()
            takes[10].wait()
            f.attend_back()
        else:
            square(lambda: f.project_back(t))

    takes[0].wait()
    takes[1].wait()
    parts = [backward_codes(here) for here in range(ZN)]
    for n in range(len(BACKWARD_STEPS) + 1):
        run_codes([codes[n] for codes in parts])
        if n < len(BACKWARD_STEPS):
            compute(BACKWARD_STEPS[n])

    end_deal(p, res, res_back, s_res, r_res, l_res)
    end_deal(p, din, din_back, s_din, r_din, l_din)
    for g in (p.x * 2 + 1 - c, (1 - p.x) * 2 + 1 - c):
        for k in range(3):
            wait_for(grp.at[pl.ds(g * 24 + 8 * k, 8)], r_e.at[g * 3 + k])

    for n in range(RING):
        wait_for(ring.at[0], s_ring.at[n])
    for n in range(5):
        wait_for(vland.at[5 + n], s_v.at[n])

    wait_for(grp.at[pl.ds(0, 24)], s_e)
    wait_for(grp.at[pl.ds(0, 48)], s_e2)

    def drain(here):
        ways = [code // 1024 % 8 for codes in parts[here] for code in codes if code // 131072 == 1]
        for way, sem in enumerate((s_x, s_y, s_up, s_down)):
            if ways.count(way):
                wait_for(land_c.at[pl.ds(0, ways.count(way))], sem)

    for here in range(ZN):
        pl.when(z == here)(functools.partial(drain, here))


def backward(wm, l3, d2, acc, gp, xh, rs, p3, q3, res, vsum, vec):
    dma = pltpu.SemaphoreType.DMA
    rows = d2.shape[0]
    vmem = pl.BlockSpec(memory_space=pltpu.VMEM)
    far = pl.BlockSpec(memory_space=pl.ANY)
    out = jax.ShapeDtypeStruct
    return pl.pallas_call(
        backward_kernel,
        out_shape=(
            out((24, TB, TB), f32),
            out((96, TB, TB), bf),
            out((96, TB), f32),
            out(res.shape, bf),
            out(res.shape, bf),
        ),
        in_specs=[far] * 10 + [vmem] * 2,
        out_specs=(vmem,) * 3 + (far,) * 2,
        scratch_shapes=[
            pltpu.VMEM(l3.shape, bf), pltpu.VMEM((9, rows, D), bf), pltpu.VMEM(acc.shape, f32),
            pltpu.VMEM(gp.shape, f32), pltpu.VMEM(xh.shape, f32), pltpu.VMEM(rs.shape, f32),
            pltpu.VMEM(p3.shape, f32), pltpu.VMEM(q3.shape, bf), pltpu.VMEM((8, rows, TB), bf),
            pltpu.VMEM(res.shape, bf), pltpu.VMEM((2, 8, TB, D), bf), pltpu.VMEM((12, 8, D), f32),
            pltpu.VMEM((48, TB, D), bf), pltpu.VMEM((SPOTS, TB, D), bf),
            pltpu.VMEM((SPOTS, TB, D), bf), pltpu.VMEM((30, TB, D), bf), pltpu.VMEM((RING, TB, D), bf),
            pltpu.VMEM((10, 96, TB), f32), pltpu.VMEM((TB, D), f32),
            dma((11,)), dma((2,)), dma((48,)), dma((SPOTS,)), dma((SPOTS,)), dma((30,)), dma((12,)), dma((5,)),
            dma((RING,)), dma, dma, dma, dma, dma, dma, dma((5,)),
            dma, dma((2 * ZN,)), dma, dma, dma((2 * ZN,)), dma,
        ],
        compiler_params=pltpu.CompilerParams(
            collective_id=1, has_side_effects=True, vmem_limit_bytes=62 * 2**20
        ),
        name="backward",
    )(wm, l3, d2, acc, gp, xh, rs, p3, q3, res, vsum, vec)


GROUP = 8


def halves(a):
    high = a.astype(bf)
    return high, (a - high.astype(f32)).astype(bf)


def wide(b):
    return jnp.concatenate(
        [jnp.concatenate(b, 1), jnp.concatenate([b[0], jnp.zeros_like(b[0])], 1)], 0
    )


def fine(a, b_wide):
    out = mul(jnp.concatenate(a, 1), b_wide)
    return out[:, :TB] + out[:, TB:]


def fine_t(a, b):
    wide_t = jnp.concatenate(
        [jnp.concatenate([b[0], b[0]], 1), jnp.concatenate([b[1], jnp.zeros_like(b[1])], 1)], 0
    )
    out = mul_t(jnp.concatenate(a, 1), wide_t)
    return out[:, :TB] + out[:, TB:]


def moments(first, second, grad):
    first = BETA_ONE * first + (1.0 - BETA_ONE) * grad
    second = BETA_TWO * second + (1.0 - BETA_TWO) * grad * grad
    hat = (first * (1.0 / (1.0 - BETA_ONE**STEP))) / (
        jnp.sqrt(second * (1.0 / (1.0 - BETA_TWO**STEP))) + ADAM_EPS
    )
    return first, second, hat


def adam_kernel(owners, deal, *refs):
    masters = refs[:GROUP]
    (
        grads, left, right, first, second, vec, vec_first, vec_second, vec_total,
        tiles, res_back, din_back,
        new_first, new_second, new_tiles, new_low, vec_grad, vec_first_new, vec_second_new, new_vec,
        tile_grads, out_tokens, in_grad,
    ) = refs[GROUP:]
    step = pl.program_id(0)
    dp, fs = lax.axis_index("dp"), lax.axis_index("fsdp")
    seqs = res_back.shape[1]

    @pl.when(step == 0)
    def _():
        for b in range(res_back.shape[0]):
            for j in range(seqs):
                to = deal[b, j * 4 + fs] - fs * seqs
                out_tokens[b, to] = res_back[b, j]
                in_grad[b, to] = din_back[b, j]
        for i in range(3):
            m = (dp * 4 + fs) * 3 + i
            vec_grad[i : i + 1] = vec_total[pl.ds((m % 8) * 12 + m // 8, 1)]
        a, b, hat = moments(vec_first[...], vec_second[...], vec_grad[...])
        vec_first_new[...] = a
        vec_second_new[...] = b
        new_vec[...] = vec[...] - VEC_RATE * hat

    tile_grads[...] = tiles[...]
    span = range(GROUP)
    owner = [owners[step * GROUP + g] for g in span]
    ls = [halves(left[g]) for g in span]
    rs = [halves(right[g]) for g in span]
    grad = [grads[owner[g] - dp * 96] for g in span]
    inner = [t_mul(jnp.concatenate(ls[g], 0), jnp.concatenate([grad[g]] * 2, 0)) for g in span]
    rwide = [wide(rs[g]) for g in span]
    rotated = [fine(halves(inner[g]), rwide[g]) for g in span]
    hats = []
    for g in span:
        first_now, second_now, hat = moments(first[g], second[g], rotated[g])
        new_first[g] = first_now
        new_second[g] = second_now
        hats.append(hat)
    outer = [fine(ls[g], wide(halves(hats[g]))) for g in span]
    update = [fine_t(halves(outer[g]), rs[g]) for g in span]
    for g in span:
        master = masters[g][0].astype(f32)
        fresh = master - tile_rate(owner[g]) * (update[g] + DECAY * master)
        new_tiles[g] = fresh
        new_low[g] = fresh.astype(bf)


def adam(owners, deal, wm, grads, left, right, first, second, vec, vec_first, vec_second,
         vec_total, tiles, res_back, din_back):
    count = left.shape[0]
    out = jax.ShapeDtypeStruct

    def master_at(g, i, owners, *_):
        o = owners[i * GROUP + g]
        return octet_place(o // 8), 0, o % 8

    one = [pl.BlockSpec((1, TB, TB), functools.partial(master_at, g)) for g in range(GROUP)]
    stack = pl.BlockSpec((GROUP, TB, TB), lambda i, *_: (i, 0, 0))
    whole = pl.BlockSpec(grads.shape, lambda i, *_: (0, 0, 0))
    dealt = pl.BlockSpec(res_back.shape, lambda i, *_: (0, 0, 0, 0))

    def small(a):
        return pl.BlockSpec(a.shape, lambda i, *_: (0, 0))

    return pl.pallas_call(
        adam_kernel,
        out_shape=(out(left.shape, f32),) * 3
        + (out(left.shape, bf),)
        + (out(vec.shape, f32),) * 4
        + (out(tiles.shape, f32), out(res_back.shape, bf), out(din_back.shape, bf)),
        grid_spec=pltpu.PrefetchScalarGridSpec(
            num_scalar_prefetch=2,
            grid=(count // GROUP,),
            in_specs=one + [whole] + [stack] * 4 + [small(vec)] * 3 + [small(vec_total), stack, dealt, dealt],
            out_specs=[stack] * 4 + [small(vec)] * 4 + [stack, dealt, dealt],
        ),
        compiler_params=pltpu.CompilerParams(vmem_limit_bytes=60 * 2**20),
        name="adam",
    )(
        owners, deal, *([wm] * GROUP), grads, left, right, first, second,
        vec, vec_first, vec_second, vec_total, tiles, res_back, din_back,
    )


def per_device(
    tokens,
    cotangent,
    lengths,
    deal,
    weights,
    vectors,
    owners,
    left_basis,
    right_basis,
    first_moment,
    second_moment,
    vec_first,
    vec_second,
):
    rows = tokens.shape[0] * tokens.shape[2] * lax.axis_size("dp")
    vec_rows = vectors.reshape(3, TB)
    wm, l3, d2, acc, gp, xh, rs, p3, q3, res, vsum, vecs = forward(
        lengths, deal, weights, vec_rows, tokens, cotangent.reshape(rows, D)
    )
    tiles, group_grads, vec_total, res_back, din_back = backward(
        wm, l3, d2, acc, gp, xh, rs, p3, q3, res, vsum, vecs
    )
    (
        new_first, new_second, new_tiles, new_low, vec_grads, vec_first_new, vec_second_new,
        new_vectors, tile_grads, out_tokens, in_grad,
    ) = adam(
        owners, deal, wm, group_grads, left_basis, right_basis, first_moment, second_moment,
        vec_rows, vec_first.reshape(3, TB), vec_second.reshape(3, TB), vec_total, tiles,
        res_back, din_back,
    )
    return (
        out_tokens,
        in_grad,
        tile_grads,
        vec_grads.reshape(-1),
        new_first,
        new_second,
        new_tiles,
        new_low,
        vec_first_new.reshape(-1),
        vec_second_new.reshape(-1),
        new_vectors.reshape(-1),
    )


def solution(mesh):
    body = per_device if (mesh.shape["dp"], mesh.shape["fsdp"]) == (2 * ZN, 4) else per_device_any
    placed = (
        P(None, "fsdp", "dp", None),
        P(None, ("dp", "fsdp"), None, None),
        P(),
        P(),
        P(("dp", "fsdp"), None, None),
        P(("dp", "fsdp")),
        P(("dp", "fsdp")),
        P(("dp", "fsdp"), None, None),
        P(("dp", "fsdp"), None, None),
        P(("dp", "fsdp"), None, None),
        P(("dp", "fsdp"), None, None),
        P(("dp", "fsdp")),
        P(("dp", "fsdp")),
    )
    return jax.shard_map(
        body,
        mesh=mesh,
        in_specs=placed,
        out_specs=(
            P(None, "fsdp", "dp", None),
            P(None, "fsdp", "dp", None),
            P(("dp", "fsdp"), None, None),
            P(("dp", "fsdp")),
            P(("dp", "fsdp"), None, None),
            P(("dp", "fsdp"), None, None),
            P(("dp", "fsdp"), None, None),
            P(("dp", "fsdp"), None, None),
            P(("dp", "fsdp")),
            P(("dp", "fsdp")),
            P(("dp", "fsdp")),
        ),
        check_vma=False,
    )
```

```python
import functools

import jax
import jax.numpy as jnp
from jax import lax
from jax.experimental import pallas as pl
from jax.experimental.pallas import tpu as pltpu
from jax.sharding import PartitionSpec as P

D = 1024
HEADS = 16
HEAD_DIM = 64
FF = 4096
STEP = 10
TB = 128


EPS_NORM = 1e-05
BETA_ONE = 0.5
BETA_TWO = 0.6
ADAM_EPS = 1e-08
DECAY = 0.01
VEC_RATE = 0.2
PRECISION_HIGH = lax.Precision.HIGHEST


def cut_tiles(stacked, row_count, col_count, start_at):
    tile_count = row_count // TB * (col_count // TB)
    blocked = lax.slice_in_dim(stacked, start_at, start_at + tile_count, axis=0)
    blocked = blocked.reshape(row_count // TB, col_count // TB, TB, TB)
    return (blocked.transpose(0, 2, 1, 3).reshape(row_count, col_count), start_at + tile_count)


def unpack_mats(stacked):
    w_qkv, offset = cut_tiles(stacked, D, 3 * D, 0)
    w_out, offset = cut_tiles(stacked, D, D, offset)
    w_up, offset = cut_tiles(stacked, D, FF, offset)
    w_down, offset = cut_tiles(stacked, FF, D, offset)
    return (w_qkv, w_out, w_up, w_down)


def tiled_grad(left_rows, right_rows):
    row_total = left_rows.shape[0]
    left_split = left_rows.reshape(row_total, left_rows.shape[1] // TB, TB)
    right_split = right_rows.reshape(row_total, right_rows.shape[1] // TB, TB)
    blocked = jnp.einsum(
        "tai,tbj->abij", left_split, right_split, preferred_element_type=jnp.float32
    )
    return blocked.reshape(-1, TB, TB)


def unpack_vecs(vector):
    widths = [D, D, D, FF, D, D, D, D, D]
    pieces = []
    offset = 0
    for width_now in widths:
        pieces.append(vector[offset : offset + width_now])
        offset += width_now
    return tuple(pieces)


def tile_rate(tile_ids):
    qkv_end = 3 * D * D // (TB * TB)
    out_end = 4 * D * D // (TB * TB)
    up_end = (4 * D * D + D * FF) // (TB * TB)
    return jnp.where(
        tile_ids < qkv_end,
        D ** (-0.5),
        jnp.where(
            tile_ids < out_end,
            (HEAD_DIM / D) ** 0.5,
            jnp.where(tile_ids < up_end, D ** (-0.5), 1.5 * FF ** (-0.5)),
        ),
    ).astype(jnp.float32)


def norm_apply(values, gain_vec, shift_vec):
    center = values - jnp.mean(values, axis=-1, keepdims=True)
    spread = jnp.mean(center * center, axis=-1, keepdims=True)
    return center * lax.rsqrt(spread + EPS_NORM) * gain_vec + shift_vec


def exact_gelu(values):
    return jax.nn.gelu(values, approximate=False)


def split_heads(joined16):
    seq_rows = joined16.shape[0]
    query_heads = joined16[:, :D].reshape(seq_rows, HEADS, HEAD_DIM)
    key_heads = joined16[:, D : 2 * D].reshape(seq_rows, HEADS, HEAD_DIM)
    value_heads = joined16[:, 2 * D :].reshape(seq_rows, HEADS, HEAD_DIM)
    return (query_heads, key_heads, value_heads)


def masked_scores(query_heads, key_heads, in_length):
    scores = jnp.einsum(
        "qhd,khd->hqk", query_heads, key_heads, preferred_element_type=jnp.float32
    ) * HEAD_DIM ** (-0.5)
    return jnp.where(in_length[None, None, :], scores, -1e30)


def forward_pass(inputs16, length, matrices, vecs):
    w_qkv, w_out, w_up, w_down = matrices
    bias_q, bias_v, bias_out, bias_up, bias_down, gain_one, shift_one, gain_two, shift_two = vecs
    seq_rows = inputs16.shape[0]
    joined = jnp.dot(inputs16, w_qkv, preferred_element_type=jnp.float32)
    joined = joined + jnp.concatenate([bias_q, jnp.zeros_like(bias_q), bias_v])
    joined16 = joined.astype(jnp.bfloat16)
    query_heads, key_heads, value_heads = split_heads(joined16)
    in_length = jnp.arange(seq_rows) < length
    scores = masked_scores(query_heads, key_heads, in_length)
    row_top = jnp.max(scores, axis=-1, keepdims=True)
    exp_scores = jnp.exp(scores - row_top)
    row_total = jnp.sum(exp_scores, axis=-1, keepdims=True)
    attention16 = (exp_scores / row_total).astype(jnp.bfloat16)
    log_total = row_top + jnp.log(row_total)
    attended = jnp.einsum(
        "hqk,khd->qhd", attention16, value_heads, preferred_element_type=jnp.float32
    )
    attended16 = attended.reshape(seq_rows, D).astype(jnp.bfloat16)
    resid_one = (
        inputs16.astype(jnp.float32)
        + jnp.dot(attended16, w_out, preferred_element_type=jnp.float32)
        + bias_out
    )
    normed_one = norm_apply(resid_one, gain_one, shift_one)
    normed16 = normed_one.astype(jnp.bfloat16)
    hidden = jnp.dot(normed16, w_up, preferred_element_type=jnp.float32) + bias_up
    active16 = exact_gelu(hidden).astype(jnp.bfloat16)
    resid_two = (
        normed_one + jnp.dot(active16, w_down, preferred_element_type=jnp.float32) + bias_down
    )
    result = norm_apply(resid_two, gain_two, shift_two)
    result = jnp.where(in_length[:, None], result, 0.0).astype(jnp.bfloat16)
    kept = (
        joined16,
        log_total,
        attended16,
        resid_one,
        normed16,
        hidden,
        active16,
        resid_two,
        in_length,
    )
    return (result, kept)


def backward_pass(back16, inputs16, kept, matrices, vecs):
    w_qkv, w_out, w_up, w_down = matrices
    bias_q, bias_v, bias_out, bias_up, bias_down, gain_one, shift_one, gain_two, shift_two = vecs
    joined16, log_total, attended16, resid_one, normed16, hidden, active16, resid_two, in_length = (
        kept
    )
    seq_rows = inputs16.shape[0]
    back = jnp.where(in_length[:, None], back16.astype(jnp.float32), 0.0)
    unused_two, pull_two = jax.vjp(norm_apply, resid_two, gain_two, shift_two)
    d_resid_two, d_gain_two, d_shift_two = pull_two(back)
    d_down16 = d_resid_two.astype(jnp.bfloat16)
    d_active = jnp.einsum("to,io->ti", d_down16, w_down, preferred_element_type=jnp.float32)
    unused_gelu, pull_gelu = jax.vjp(exact_gelu, hidden)
    d_hidden = pull_gelu(d_active)[0]
    d_hidden16 = d_hidden.astype(jnp.bfloat16)
    d_normed = d_resid_two + jnp.einsum(
        "to,io->ti", d_hidden16, w_up, preferred_element_type=jnp.float32
    )
    unused_one, pull_one = jax.vjp(norm_apply, resid_one, gain_one, shift_one)
    d_resid_one, d_gain_one, d_shift_one = pull_one(d_normed)
    d_branch16 = d_resid_one.astype(jnp.bfloat16)
    d_attended = jnp.einsum("to,io->ti", d_branch16, w_out, preferred_element_type=jnp.float32)
    d_attended16 = d_attended.astype(jnp.bfloat16).reshape(seq_rows, HEADS, HEAD_DIM)
    query_heads, key_heads, value_heads = split_heads(joined16)
    scores = masked_scores(query_heads, key_heads, in_length)
    attention = jnp.exp(scores - log_total)
    attention16 = attention.astype(jnp.bfloat16)
    d_value = jnp.einsum(
        "hqk,qhd->khd", attention16, d_attended16, preferred_element_type=jnp.float32
    )
    d_attention = jnp.einsum(
        "qhd,khd->hqk", d_attended16, value_heads, preferred_element_type=jnp.float32
    )
    d_scores = attention * (d_attention - jnp.sum(attention * d_attention, axis=-1, keepdims=True))
    d_scores16 = d_scores.astype(jnp.bfloat16)
    d_query = jnp.einsum(
        "hqk,khd->qhd", d_scores16, key_heads, preferred_element_type=jnp.float32
    ) * HEAD_DIM ** (-0.5)
    d_key = jnp.einsum(
        "hqk,qhd->khd", d_scores16, query_heads, preferred_element_type=jnp.float32
    ) * HEAD_DIM ** (-0.5)
    d_query = d_query.reshape(seq_rows, D)
    d_key = d_key.reshape(seq_rows, D)
    d_value = d_value.reshape(seq_rows, D)
    d_joined16 = jnp.concatenate([d_query, d_key, d_value], axis=1).astype(jnp.bfloat16)
    d_inputs = d_resid_one + jnp.einsum(
        "to,io->ti", d_joined16, w_qkv, preferred_element_type=jnp.float32
    )
    vec_grad = jnp.concatenate(
        [
            jnp.sum(d_query, axis=0),
            jnp.sum(d_value, axis=0),
            jnp.sum(d_resid_one, axis=0),
            jnp.sum(d_hidden, axis=0),
            jnp.sum(d_resid_two, axis=0),
            d_gain_one,
            d_shift_one,
            d_gain_two,
            d_shift_two,
        ]
    )
    pairs = (d_joined16, attended16, d_branch16, normed16, d_hidden16, active16, d_down16)
    return (pairs, vec_grad, d_inputs.astype(jnp.bfloat16))


def rotate_in(left_side, matrix, right_side):
    inner = jnp.einsum(
        "pji,pjk->pik",
        left_side,
        matrix,
        precision=PRECISION_HIGH,
        preferred_element_type=jnp.float32,
    )
    return jnp.einsum(
        "pik,pkl->pil",
        inner,
        right_side,
        precision=PRECISION_HIGH,
        preferred_element_type=jnp.float32,
    )


def rotate_out(left_side, matrix, right_side):
    inner = jnp.einsum(
        "pij,pjk->pik",
        left_side,
        matrix,
        precision=PRECISION_HIGH,
        preferred_element_type=jnp.float32,
    )
    return jnp.einsum(
        "pik,plk->pil",
        inner,
        right_side,
        precision=PRECISION_HIGH,
        preferred_element_type=jnp.float32,
    )


def per_device_any(
    tokens,
    cotangent,
    lengths,
    deal,
    weights,
    vectors,
    owners,
    left_basis,
    right_basis,
    first_moment,
    second_moment,
    vec_first,
    vec_second,
):
    dp_count = lax.axis_size("dp")
    fsdp_count = lax.axis_size("fsdp")
    dp_place = lax.axis_index("dp")
    fsdp_place = lax.axis_index("fsdp")
    micro_count = tokens.shape[0]
    my_place = dp_place * fsdp_count + fsdp_place
    quarter = lax.dynamic_index_in_dim(
        deal.reshape(micro_count, dp_count, fsdp_count), fsdp_place, axis=2, keepdims=False
    )
    quarter = quarter - fsdp_place * dp_count
    ordered = jnp.take_along_axis(tokens, quarter[:, :, None, None], axis=1)
    dealt_rows = lax.all_to_all(ordered, "dp", split_axis=1, concat_axis=2, tiled=True)
    my_seq = lax.dynamic_index_in_dim(deal, my_place, axis=1, keepdims=False)
    my_length = jnp.take_along_axis(lengths, my_seq[:, None], axis=1)[:, 0]
    shard_low = (weights.astype(jnp.bfloat16), vectors.astype(jnp.bfloat16))
    whole_tiles, whole_vecs = (
        lax.all_gather(shard_low[0], ("dp", "fsdp"), axis=0, tiled=True),
        lax.all_gather(shard_low[1], ("dp", "fsdp"), axis=0, tiled=True),
    )
    mats_kept = unpack_mats(whole_tiles)
    vecs_kept = unpack_vecs(whole_vecs.astype(jnp.float32))
    all_pairs = []
    all_inputs = []
    vec_terms = []
    results = []
    input_grads = []
    for micro_index in range(micro_count):
        inputs16 = dealt_rows[micro_index, 0]
        matrices, vecs = (mats_kept, vecs_kept)
        result, kept = forward_pass(inputs16, my_length[micro_index], matrices, vecs)
        pairs, vec_term, d_inputs = backward_pass(
            cotangent[micro_index, 0], inputs16, kept, matrices, vecs
        )
        all_pairs.append(pairs)
        all_inputs.append(inputs16)
        vec_terms.append(vec_term)
        results.append(result)
        input_grads.append(d_inputs)

    def joined_rows(index):
        return jnp.concatenate([pairs[index] for pairs in all_pairs], axis=0)

    inputs_rows = jnp.concatenate(all_inputs, axis=0)
    tile_terms = jnp.concatenate(
        [
            tiled_grad(inputs_rows, joined_rows(0)),
            tiled_grad(joined_rows(1), joined_rows(2)),
            tiled_grad(joined_rows(3), joined_rows(4)),
            tiled_grad(joined_rows(5), joined_rows(6)),
        ],
        axis=0,
    )
    grad_vec = vec_terms[0]
    for vec_term in vec_terms[1:]:
        grad_vec = grad_vec + vec_term
    shard_tiles = weights.shape[0]
    tile_grads, vec_grads = (
        lax.psum_scatter(tile_terms, ("dp", "fsdp"), scatter_dimension=0, tiled=True),
        lax.psum_scatter(grad_vec, ("dp", "fsdp"), scatter_dimension=0, tiled=True),
    )
    group_grads, group_master = (
        lax.all_gather(tile_grads.astype(jnp.bfloat16), "fsdp", axis=0, tiled=True).astype(
            tile_grads.dtype
        ),
        lax.all_gather(weights.astype(jnp.bfloat16), "fsdp", axis=0, tiled=True).astype(
            weights.dtype
        ),
    )
    result_dealt = jnp.stack(results)[:, None]
    grads_dealt = jnp.stack(input_grads)[:, None]
    back_result, back_grads = (
        lax.all_to_all(result_dealt, "dp", split_axis=2, concat_axis=1, tiled=True),
        lax.all_to_all(grads_dealt, "dp", split_axis=2, concat_axis=1, tiled=True),
    )
    restore = jnp.argsort(quarter, axis=1)
    out_tokens = jnp.take_along_axis(back_result, restore[:, :, None, None], axis=1)
    in_grad = jnp.take_along_axis(back_grads, restore[:, :, None, None], axis=1)
    group_size = fsdp_count * shard_tiles
    pick_rows = owners - dp_place * group_size
    own_grads = jnp.take(group_grads, pick_rows, axis=0)
    own_master = jnp.take(group_master, pick_rows, axis=0)
    rates = tile_rate(owners)
    rotated = rotate_in(left_basis, own_grads, right_basis)
    new_first = BETA_ONE * first_moment + (1.0 - BETA_ONE) * rotated
    new_second = BETA_TWO * second_moment + (1.0 - BETA_TWO) * rotated * rotated
    first_hat = new_first / (1.0 - BETA_ONE**STEP)
    second_hat = new_second / (1.0 - BETA_TWO**STEP)
    step_rotated = first_hat / (jnp.sqrt(second_hat) + ADAM_EPS)
    update = rotate_out(left_basis, step_rotated, right_basis)
    new_tiles = own_master - rates[:, None, None] * (update + DECAY * own_master)
    vec_first_new = BETA_ONE * vec_first + (1.0 - BETA_ONE) * vec_grads
    vec_second_new = BETA_TWO * vec_second + (1.0 - BETA_TWO) * vec_grads * vec_grads
    vec_hat_one = vec_first_new / (1.0 - BETA_ONE**STEP)
    vec_hat_two = vec_second_new / (1.0 - BETA_TWO**STEP)
    new_vectors = vectors - VEC_RATE * vec_hat_one / (jnp.sqrt(vec_hat_two) + ADAM_EPS)
    return (
        out_tokens,
        in_grad,
        tile_grads,
        vec_grads,
        new_first,
        new_second,
        new_tiles,
        new_tiles.astype(jnp.bfloat16),
        vec_first_new,
        vec_second_new,
        new_vectors,
    )


CHUNK = 256
ROWS_AT_ONCE = 128
f32 = jnp.float32
bf = jnp.bfloat16


def mul(a, b):
    return jnp.dot(a, b, preferred_element_type=f32)


def mul_t(a, b):
    return lax.dot_general(a, b, (((1,), (1,)), ((), ())), preferred_element_type=f32)


def t_mul(a, b):
    return lax.dot_general(a, b, (((0,), (0,)), ((), ())), preferred_element_type=f32)


def column_chunks():
    return [slice(j * CHUNK, (j + 1) * CHUNK) for j in range(D // CHUNK)]


class Layer:
    def __init__(self, **refs):
        self.__dict__.update(refs)
        self.rows = self.l3.shape[1]
        self.seqs = self.rows // TB

    def left(self, first, count=8):
        return jnp.concatenate([self.l3[first + j] for j in range(count)], axis=1)

    def each_rows(self, fn):
        def body(i, _):
            fn(pl.ds(pl.multiple_of(i * ROWS_AT_ONCE, ROWS_AT_ONCE), ROWS_AT_ONCE), i)
            return 0

        lax.fori_loop(0, self.rows // ROWS_AT_ONCE, body, 0)

    def counted(self, i):
        per = TB // ROWS_AT_ONCE
        at = (i % per) * ROWS_AT_ONCE + lax.broadcasted_iota(jnp.int32, (ROWS_AT_ONCE, 1), 0)
        return at < self.lens[i // per]

    def add_sum(self, n, value, cols=slice(None)):
        self.vsum[n, :, cols] += value.reshape(value.shape[0] // 8, 8, value.shape[1]).sum(axis=0)

    def project(self, t):
        x = self.left(0)
        for j, cols in enumerate(column_chunks()):
            out = mul(x, self.wcols(t, cols))
            if t != 1:
                out = out + self.vec[pl.ds(0 if t == 0 else 1, 1), cols]
            out = out.astype(bf)
            for i in range(CHUNK // TB):
                self.q3[t, j * (CHUNK // TB) + i] = out[:, i * TB : (i + 1) * TB]

    def two(self, block):
        lane = lax.broadcasted_iota(jnp.int32, block.shape, 1)
        zero = jnp.zeros_like(block)
        return jnp.concatenate(
            [jnp.where(lane < HEAD_DIM, block, zero), jnp.where(lane < HEAD_DIM, zero, block)], axis=0
        )

    def one(self, stacked):
        top, low = stacked[:TB], stacked[TB:]
        lane = lax.broadcasted_iota(jnp.int32, top.shape, 1)
        return jnp.where(lane < HEAD_DIM, top, low)

    def attend(self):
        def body(b, _):
            at = pl.ds(pl.multiple_of(b * TB, TB), TB)
            key = lax.broadcasted_iota(jnp.int32, (2 * TB, TB), 1)
            seen = key < self.lens[b]
            for h in range(HEADS // 2):
                s = mul_t(self.two(self.q3[0, h, at]), self.q3[1, h, at]) * HEAD_DIM**-0.5
                s = jnp.where(seen, s, -1e30)
                e = jnp.exp(s - jnp.max(s, axis=1, keepdims=True))
                p = e * (1.0 / jnp.sum(e, axis=1, keepdims=True))
                self.p3[b, h] = p
                a = self.one(mul(p.astype(bf), self.q3[2, h, at]))
                self.l3[8 + h, at] = a.astype(bf)
            return 0

        lax.fori_loop(0, self.seqs, body, 0)

    def norm_one(self):
        a = self.left(8)
        for j, cols in enumerate(column_chunks()):
            x = jnp.concatenate([self.l3[2 * j], self.l3[2 * j + 1]], axis=1).astype(f32)
            self.xh[:, cols] = x + mul(a, self.wcols(3, cols)) + self.vec[pl.ds(2, 1), cols]

        def rows(at, i):
            r = self.xh[at]
            center = r - jnp.mean(r, axis=1, keepdims=True)
            scale = lax.rsqrt(jnp.mean(center * center, axis=1, keepdims=True) + EPS_NORM)
            hat = center * scale
            self.xh[at] = hat
            self.rs[at] = jnp.broadcast_to(scale, (ROWS_AT_ONCE, TB))
            u = hat * self.vec[pl.ds(8, 1)] + self.vec[pl.ds(9, 1)]
            self.acc[at] = u
            u16 = u.astype(bf)
            for j in range(8):
                self.l3[16 + j, at] = u16[:, j * TB : (j + 1) * TB]

        self.each_rows(rows)

    def up_begin(self, t):
        u = self.left(16, 4)
        for cols in column_chunks():
            self.gp[t, :, cols] = mul(u, self.wcols(4 + t, cols, 0)) + self.vec[pl.ds(3 + t, 1), cols]

    def up_end(self, t):
        u = self.left(20, 4)
        for cols in column_chunks():
            self.gp[t, :, cols] += mul(u, self.wcols(4 + t, cols, 1))

        def rows(at, i):
            h = self.gp[t, at]
            cdf = 0.5 + 0.5 * lax.erf(h * 0.7071067811865476)
            self.gp[t, at] = cdf + h * (0.3989422804014327 * jnp.exp(-0.5 * h * h))
            e = (h * cdf).astype(bf)
            for j in range(8):
                self.l3[24 + 8 * t + j, at] = e[:, j * TB : (j + 1) * TB]

        self.each_rows(rows)

    def down(self, t):
        e = self.left(24 + 8 * t)
        for cols in column_chunks():
            self.acc[:, cols] += mul(e, self.wcols(8 + t, cols))

    def norm_two(self):
        def rows(at, i):
            r = self.acc[at] + self.vec[pl.ds(7, 1)]
            center = r - jnp.mean(r, axis=1, keepdims=True)
            scale = lax.rsqrt(jnp.mean(center * center, axis=1, keepdims=True) + EPS_NORM)
            hat = center * scale
            live = self.counted(i)
            gain = self.vec[pl.ds(10, 1)]
            out = jnp.where(live, hat * gain + self.vec[pl.ds(11, 1)], 0.0).astype(bf)
            per = TB // ROWS_AT_ONCE
            slabs = ROWS_AT_ONCE // self.res.shape[2]
            self.res[i // per, pl.ds((i % per) * slabs, slabs)] = out.reshape(
                slabs, self.res.shape[2], D
            )
            dy = jnp.where(live, self.cot[at].astype(f32), 0.0)
            self.add_sum(10, dy * hat)
            self.add_sum(11, dy)
            g = dy * gain
            dr = scale * (
                g
                - jnp.mean(g, axis=1, keepdims=True)
                - hat * jnp.mean(g * hat, axis=1, keepdims=True)
            )
            self.add_sum(7, dr)
            self.acc[at] = dr
            self.d2[at] = dr.astype(bf)

        self.each_rows(rows)

    def down_back(self, t):
        d = self.r3[8]
        for cols in column_chunks():
            dh = mul_t(d, self.wrows(8 + t, cols)) * self.gp[t, :, cols]
            self.add_sum(3 + t, dh, cols)
            self.r3[4 + t, :, cols] = dh.astype(bf)

    def up_back(self, t):
        d = self.r3[4 + t]
        for cols in column_chunks():
            self.acc[:, cols] += mul_t(d, self.wrows(4 + t, cols))

    def norm_one_back(self):
        def rows(at, i):
            du, hat = self.acc[at], self.xh[at]
            self.add_sum(8, du * hat)
            self.add_sum(9, du)
            g = du * self.vec[pl.ds(8, 1)]
            dr = self.rs[at][:, :1] * (
                g
                - jnp.mean(g, axis=1, keepdims=True)
                - hat * jnp.mean(g * hat, axis=1, keepdims=True)
            )
            self.add_sum(2, dr)
            self.acc[at] = dr
            self.r3[3, at] = dr.astype(bf)

        self.each_rows(rows)

    def out_back(self):
        d = self.r3[3]
        for j, cols in enumerate(column_chunks()):
            da = mul_t(d, self.wrows(3, cols)).astype(bf)
            for i in range(CHUNK // TB):
                self.da3[j * (CHUNK // TB) + i] = da[:, i * TB : (i + 1) * TB]

    def attend_back(self):
        def body(b, _):
            at = pl.ds(pl.multiple_of(b * TB, TB), TB)
            for h in range(HEADS // 2):
                cols = slice(h * TB, (h + 1) * TB)
                p = self.p3[b, h]
                da = self.two(self.da3[h, at])
                dv = t_mul(p.astype(bf), da)
                pd = p * mul_t(da, self.q3[2, h, at])
                ds = (pd - p * jnp.sum(pd, axis=1, keepdims=True)).astype(bf)
                dq = self.one(mul(ds, self.q3[1, h, at])) * HEAD_DIM**-0.5
                dk = t_mul(ds, self.two(self.q3[0, h, at])) * HEAD_DIM**-0.5
                self.r3[0, at, cols] = dq.astype(bf)
                self.r3[1, at, cols] = dk.astype(bf)
                self.r3[2, at, cols] = dv.astype(bf)
                self.add_sum(0, dq, cols)
                self.add_sum(1, dv, cols)
            return 0

        lax.fori_loop(0, self.seqs, body, 0)

    def project_back(self, t):
        d = self.r3[t]
        for cols in column_chunks():
            value = self.acc[:, cols] + mul_t(d, self.wrows(t, cols))
            if t < 2:
                self.acc[:, cols] = value
            else:
                self.din[:, :, :, cols] = value.astype(bf).reshape(self.din.shape[:3] + (CHUNK,))


MESH = pl.DeviceIdType.MESH
ZN = 4
OCT = 96
RING = 8
SPOTS = 16


class Place:
    def __init__(self):
        self.dp = lax.axis_index("dp")
        self.fs = lax.axis_index("fsdp")
        self.z, self.y = self.dp // 2, self.dp % 2
        self.x, self.c = self.fs // 2, self.fs % 2
        self.to_x = (self.dp, (self.fs + 2) % 4)
        self.to_y = (self.z * 2 + 1 - self.y, self.fs)
        self.to_core = (self.dp, self.x * 2 + 1 - self.c)
        self.to_up = (self.dp + 2, self.fs)
        self.to_down = (self.dp - 2, self.fs)
        near = self.z + 1 - 2 * (self.z % 2)
        far = (self.z + 2) % ZN
        self.doubling = [
            self.to_core,
            self.to_x,
            self.to_y,
            (near * 2 + self.y, self.fs),
            (far * 2 + self.y, self.fs),
        ]

    def peer(self, j):
        return (self.dp + j) % (2 * ZN)

    def greet(self):
        bar = pltpu.get_barrier_semaphore()
        for dev in [self.to_x, self.to_core] + [(self.peer(j), self.fs) for j in range(1, 2 * ZN)]:
            pl.semaphore_signal(bar, inc=1, device_id=dev, device_id_type=MESH)

    def greeted(self):
        pl.semaphore_wait(pltpu.get_barrier_semaphore(), 1 + 2 * ZN)

    def octet(self, dx, dy, zp, k, c=None):
        yy = self.y if dy == 0 else 1 - self.y
        xx = self.x if dx == 0 else 1 - self.x
        return ((zp * 2 + yy) * 4 + xx * 2 + (self.c if c is None else c)) * 3 + k

    def plane(self, table, i):
        zp = table[0][i]
        for n in range(1, ZN):
            zp = jnp.where(self.z == n, table[n][i], zp)
        return zp


def octet_place(o):
    return jnp.where(
        o < 24,
        (o % 3) * 8 + o // 3,
        jnp.where((o >= 32) & (o < 64), 32 + ((o - 32) % 4) * 8 + (o - 32) // 4, o),
    )


def left_block(o):
    return jnp.where(
        o < 24, o // 3, jnp.where(o < 32, o - 16, jnp.where(o < 64, 16 + (o - 32) // 4, o - 40))
    )


def right_block(o):
    return jnp.where(o < 24, o % 3, jnp.where(o < 32, 3, jnp.where(o < 64, 4 + (o - 32) % 4, 8)))


def wait_for(ref, sem):
    pltpu.make_async_copy(ref, ref, sem).wait()


def remote(src, dst, send_sem, recv_sem, dev):
    return pltpu.make_async_remote_copy(
        src_ref=src,
        dst_ref=dst,
        send_sem=send_sem,
        recv_sem=recv_sem,
        device_id=dev,
        device_id_type=MESH,
    )


def start_deal(p, src, dst, s_sem, r_sem, l_sem):
    for j in range(1, 2 * ZN):
        d = p.peer(j)
        remote(src.at[:, d], dst.at[:, p.dp], s_sem, r_sem.at[p.dp], (d, p.fs)).start()
    pltpu.make_async_copy(src.at[:, p.dp], dst.at[:, p.dp], l_sem).start()


def end_deal(p, src, dst, s_sem, r_sem, l_sem):
    for j in range(1, 2 * ZN):
        d = p.peer(j)
        wait_for(dst.at[:, d], r_sem.at[d])
    wait_for(dst.at[:, p.dp], l_sem)
    wait_for(src.at[:, pl.ds(0, 2 * ZN - 1)], s_sem)


FORWARD_STEPS = [
    "P0", "P1", "P2", "ATT", "N1", "UA0", "UA1", "UA2", "UA3",
    "UB0", "UB1", "UB2", "UB3", "D0", "D1", "D2", "D3", "N2",
]
FORWARD_NEEDS = {"P0": (0,), "N1": (1,), "UB0": (2,), "D1": (3,)}
FORWARD_ROUTES = [
    ["xyx", "zzx", "zzy", "zxy"],
    ["zzz", "xyx", "zzz", "zzz"],
    ["zzz", "zzz", "xyx", "zzz"],
    ["zxy", "zzy", "zzx", "xyx"],
]
FORWARD_PLANS = [
    [
        0, 100, 1, 600, 2, 101, 102, 11, 200, 601, 111, 202, 602, 201, 22, 10,
        122, 110, 12, 301, 112, 300, 222, 212, 603, 604, 302, 605, 20, 120, 312, 31,
        32, 21, 311, 131, 220, 211, 132, 1000, 1001, 210, 310, 1002, 121, 1003, 322, 1004,
        1005, 232, 231, 30, 1006, 1007, 321, 130, 320, 1008, 221, 1009, 331, 1010, 332, 330,
        1011, 1012, 230, 1013, 1014, 1015, 1016, 1017,
    ],
    [
        11, 12, 112, 10, 110, 600, 111, 601, 22, 212, 122, 2, 602, 102, 1, 222,
        0, 20, 21, 210, 121, 202, 603, 31, 211, 301, 120, 300, 32, 311, 101, 100,
        310, 131, 302, 312, 200, 201, 221, 604, 30, 605, 1000, 322, 132, 130, 1001, 1002,
        220, 321, 1003, 1004, 1005, 320, 1006, 1007, 1008, 330, 232, 1009, 1010, 231, 1011, 331,
        1012, 1013, 230, 332, 1014, 1015, 1016, 1017,
    ],
    [
        600, 22, 122, 222, 601, 20, 11, 120, 31, 602, 12, 21, 121, 603, 30, 32,
        10, 111, 220, 110, 221, 322, 604, 132, 2, 1, 112, 211, 210, 331, 101, 0,
        330, 321, 100, 300, 232, 201, 311, 310, 320, 301, 102, 332, 130, 200, 605, 302,
        202, 1000, 1001, 131, 1002, 212, 312, 1003, 1004, 1005, 1006, 230, 1007, 1008, 1009, 1010,
        231, 1011, 1012, 1013, 1014, 1015, 1016, 1017,
    ],
    [
        32, 132, 31, 30, 130, 600, 131, 601, 230, 22, 122, 602, 231, 11, 20, 222,
        12, 112, 232, 120, 111, 603, 331, 2, 330, 604, 212, 102, 322, 0, 220, 1,
        332, 101, 100, 10, 201, 202, 211, 312, 300, 311, 21, 110, 200, 302, 121, 605,
        301, 1000, 1001, 1002, 321, 310, 210, 1003, 1004, 320, 1005, 221, 1006, 1007, 1008, 1009,
        1010, 1011, 1012, 1013, 1014, 1015, 1016, 1017,
    ],
]


def along_z(here, zp, k=None):
    up = zp <= here < ZN - 1 and (k is None or FORWARD_ROUTES[here + 1][zp][k] == "z")
    down = zp >= here > 0 and (k is None or FORWARD_ROUTES[here - 1][zp][k] == "z")
    return (["u"] if up else []) + (["d"] if down else [])


def split_plan(plan):
    parts = [[]]
    for code in plan:
        if code >= 1000:
            parts.append([])
        else:
            parts[-1].append(code)
    return parts


def forward_kernel(
    lengths, deal, weights_in, vec, tok, cot_in,
    wm, l3_out, d2_out, acc_out, gp_out, xh_out, rs_out, p3_out, q3_out, res_out, vsum, vecs,
    wbuf, vbuf, xl, xs, cot, wf, l3, d2, q3, p3, xh, rs, acc, gp, res,
    r_w, s_x, s_y, s_up, s_down, s_core, s_local, s_vec, r_vec, s_tok, r_tok, l_tok, s_out, r_cot, r_wf,
):
    p = Place()
    z = p.z
    p.greet()
    me = p.dp * 4 + p.fs
    get_wf = pltpu.make_async_copy(weights_in, wf, r_wf)
    get_wf.start()
    get_cot = pltpu.make_async_copy(cot_in, cot, r_cot)
    get_cot.start()

    class Lens:
        def __getitem__(self, b):
            return lengths[b, jnp.clip(deal[b, me], 0, lengths.shape[1] - 1)]

    def wcols(n, cols, half=None):
        if half is None:
            return wbuf[8 * n : 8 * n + 8, :, cols].reshape(D, CHUNK)
        first = 8 * n + 4 * half
        return wbuf[first : first + 4, :, cols].reshape(D // 2, CHUNK)

    f = Layer(
        lens=Lens(), vec=vecs, l3=l3, d2=d2, vsum=vsum, q3=q3, p3=p3, xh=xh, rs=rs, acc=acc, gp=gp,
        res=res, cot=cot, wcols=wcols,
    )

    def ref_of(o):
        return wbuf.at[octet_place(o)]

    def wait(o):
        wait_for(ref_of(o), r_w.at[o])

    seqs = tok.shape[1]
    for b in range(tok.shape[0]):
        for j in range(seqs):
            xs[b, j] = tok[b, jnp.clip(deal[b, j * 4 + p.fs] - p.fs * seqs, 0, seqs - 1)]
    get_wf.wait()
    for k in range(3):
        place = octet_place(p.octet(0, 0, z, k))
        for j in range(8):
            wbuf[place, :, j * TB : (j + 1) * TB] = wf[8 * k + j].astype(bf)
    vbuf[me] = jnp.zeros(vbuf.shape[1:], f32)
    vbuf[me, :3] = vec[...].astype(bf).astype(f32)
    p.greeted()
    start_deal(p, xs, xl, s_tok, r_tok, l_tok)

    def vec_step(n):
        size = 2**n
        if n > 0:
            half = size // 2
            theirs = (me // half) * half
            theirs = theirs + half * (1 - 2 * (theirs // half % 2))
            wait_for(vbuf.at[pl.ds(theirs, half)], r_vec.at[n - 1])
        if n < 5:
            mine = vbuf.at[pl.ds((me // size) * size, size)]
            remote(mine, mine, s_vec.at[n], r_vec.at[n], p.doubling[n]).start()

    def vec_rows():
        for m in range(OCT):
            cols = slice((m % 8) * TB, (m % 8 + 1) * TB)
            vecs[m // 8 : m // 8 + 1, cols] = vbuf[m // 3, m % 3 : m % 3 + 1, :]

    sent = [dict(x=0, y=0, u=0, d=0, c=0) for _ in range(ZN)]
    way = dict(
        x=(p.to_x, s_x), y=(p.to_y, s_y), u=(p.to_up, s_up), d=(p.to_down, s_down),
        c=(p.to_core, s_core),
    )

    def item(here, kind, zp, k):
        if kind == 6:
            vec_step(k)
            return

        def send(o, *ways):
            ref = ref_of(o)
            for w in ways:
                dev, sem = way[w]
                remote(ref, ref, sem, r_w.at[o], dev).start()
                sent[here][w] += 1

        route = FORWARD_ROUTES[here][zp][k]
        if kind == 0:
            o = p.octet(0, 0, zp, k)
            if zp != here:
                wait(o)
            send(o, *along_z(here, zp))
        elif kind == 1:
            send(p.octet(0, 0, zp, k), "x", "y", "c")
        elif kind == 2:
            o = p.octet(0, 1, zp, k)
            wait(o)
            send(o, *(["x"] if route == "x" else []), "c")
            o = p.octet(1, 0, zp, k)
            wait(o)
            send(o, *(["y"] if route == "y" else []), "c")
        else:
            o = p.octet(1, 1, zp, k)
            wait(o)
            send(o, *along_z(here, zp, k), "c")

    def partner(zp):
        for dx in range(2):
            for dy in range(2):
                for k in range(3):
                    wait(p.octet(dx, dy, zp, k, 1 - p.c))

    outs = []

    def give(src, dst):
        copy = pltpu.make_async_copy(src, dst, s_out.at[len(outs)])
        copy.start()
        outs.append(copy)

    def give_square(n):
        give(wbuf.at[pl.ds(8 * n, 8)], wm.at[pl.ds(8 * n, 8)])

    def compute(name):
        t = int(name[-1]) if name[-1].isdigit() else 0
        if name == "P0":
            vec_rows()
            vsum[...] = jnp.zeros_like(vsum)
            end_deal(p, xs, xl, s_tok, r_tok, l_tok)
            for j in range(8):
                l3[j] = xl[:, :, :, j * TB : (j + 1) * TB].reshape(l3.shape[1], TB)
        if name[0] == "P":
            f.project(t)
            give_square(t)
        elif name == "ATT":
            f.attend()
            give(q3, q3_out)
            give(p3, p3_out)
        elif name == "N1":
            f.norm_one()
            give_square(3)
            give(xh, xh_out)
            give(rs, rs_out)
        elif name[:2] == "UA":
            f.up_begin(t)
        elif name[:2] == "UB":
            f.up_end(t)
            give_square(4 + t)
            give(gp.at[t], gp_out.at[t])
            if t == 3:
                give(l3, l3_out)
        elif name[0] == "D":
            f.down(t)
            give_square(8 + t)
        else:
            get_cot.wait()
            f.norm_two()
            give(d2, d2_out)
            give(acc, acc_out)
            give(res, res_out)

    parts = [split_plan(plan) for plan in FORWARD_PLANS]
    for n in range(len(FORWARD_STEPS) + 1):

        def run(here):
            for code in parts[here][n]:
                item(here, code // 100, code // 10 % 10, code % 10)

        for here in range(ZN):
            pl.when(z == here)(functools.partial(run, here))
        if n < len(FORWARD_STEPS):
            name = FORWARD_STEPS[n]
            for zp in FORWARD_NEEDS.get(name, ()):
                partner(zp)
            compute(name)

    for copy in outs:
        copy.wait()
    for n in range(5):
        wait_for(vbuf.at[pl.ds(0, 2**n)], s_vec.at[n])

    def drain(here):
        for w, n in sent[here].items():
            if n:
                wait_for(wbuf.at[pl.ds(0, n)], way[w][1])

    for here in range(ZN):
        pl.when(z == here)(functools.partial(drain, here))


def forward(lengths, deal, weights, vec, tok, cot):
    dma = pltpu.SemaphoreType.DMA
    rows = cot.shape[0]
    vmem = pl.BlockSpec(memory_space=pltpu.VMEM)
    far = pl.BlockSpec(memory_space=pl.ANY)
    out = jax.ShapeDtypeStruct
    stages = (
        out((56, rows, TB), bf),
        out((rows, D), bf),
        out((rows, D), f32),
        out((4, rows, D), f32),
        out((rows, D), f32),
        out((rows, TB), f32),
        out((rows // TB, 8, 2 * TB, TB), f32),
        out((3, 8, rows, TB), bf),
        out(tok.shape, bf),
    )
    scratch = [pltpu.VMEM(s.shape, s.dtype) for s in stages]
    l3, d2, acc, gp, xh, rs, p3, q3, res = scratch
    return pl.pallas_call(
        forward_kernel,
        out_shape=(out((OCT, TB, D), bf),) + stages + (out((12, 8, D), f32), out((12, D), f32)),
        in_specs=[pl.BlockSpec(memory_space=pltpu.SMEM)] * 2 + [far] + [vmem] * 2 + [far],
        out_specs=(far,) * 10 + (vmem,) * 2,
        scratch_shapes=[
            pltpu.VMEM((OCT, TB, D), bf), pltpu.VMEM((32, 8, TB), f32), pltpu.VMEM(tok.shape, bf),
            pltpu.VMEM(tok.shape, bf), pltpu.VMEM(cot.shape, bf),
            pltpu.VMEM(weights.shape, f32),
            l3, d2, q3, p3, xh, rs, acc, gp, res,
            dma((OCT,)), dma, dma, dma, dma, dma, dma((3,)), dma((5,)), dma((5,)),
            dma, dma((2 * ZN,)), dma, dma((32,)), dma, dma,
        ],
        compiler_params=pltpu.CompilerParams(
            collective_id=0, has_side_effects=True, vmem_limit_bytes=62 * 2**20
        ),
        name="forward",
    )(lengths, deal, weights, vec, tok, cot)


BACKWARD_STEPS = [
    "DB0", "DB1", "DB2", "DB3", "UB0", "UB1", "UB2", "UB3",
    "N1B", "OB", "ATB", "PB0", "PB1", "PB2",
]
BACKWARD_ROUTES = [
    ["xyy", "zzx", "zzy", "zzx"],
    ["zzz", "xyy", "zzz", "zzz"],
    ["zzz", "zzz", "xyy", "zzz"],
    ["zzx", "zzy", "zzx", "xyy"],
]
BACKWARD_PLANS = [
    [
        31, 30, 1000, 131, 231, 1001, 130, 1002, 32, 230, 1003, 1004, 1005, 21, 1006, 1007,
        121, 132, 221, 330, 20, 22, 120, 220, 1008, 331, 122, 232, 1009, 1010, 10, 110,
        210, 0, 222, 12, 600, 332, 11, 601, 2, 111, 320, 102, 321, 1011, 112, 310,
        211, 1, 322, 100, 602, 202, 212, 101, 603, 200, 311, 312, 201, 1012, 500, 1013,
        300, 301, 604, 400, 302, 501, 605, 401, 402,
    ],
    [
        500, 30, 1000, 32, 230, 1001, 1002, 1003, 22, 132, 1004, 31, 1005, 122, 1006, 222,
        20, 1007, 130, 21, 1008, 12, 1009, 220, 1010, 232, 0, 1011, 231, 131, 1012, 1013,
        121, 2, 120, 600, 221, 330, 601, 10, 200, 11, 102, 1, 201, 110, 202, 332,
        100, 331, 111, 112, 101, 320, 210, 300, 321, 211, 212, 322, 310, 602, 301, 311,
        302, 603, 501, 312, 401, 604, 605, 400, 402,
    ],
    [
        32, 30, 1000, 1001, 1002, 500, 230, 1003, 1004, 1005, 1006, 1007, 1008, 12, 11, 232,
        1009, 112, 1010, 0, 2, 200, 212, 31, 20, 102, 211, 1011, 111, 10, 132, 21,
        1, 1012, 110, 201, 22, 600, 131, 210, 121, 601, 100, 101, 130, 301, 120, 231,
        330, 220, 202, 300, 122, 332, 602, 331, 221, 311, 1013, 310, 302, 222, 603, 312,
        501, 320, 321, 322, 604, 401, 400, 402, 605,
    ],
    [
        500, 1000, 1001, 1002, 1003, 21, 1004, 221, 1005, 121, 20, 1006, 1007, 220, 1008, 11,
        120, 10, 211, 1009, 210, 111, 1010, 1, 110, 600, 201, 0, 12, 100, 2, 200,
        301, 22, 31, 112, 102, 122, 101, 310, 32, 30, 300, 132, 212, 202, 311, 601,
        1011, 320, 130, 232, 302, 1012, 312, 131, 1013, 231, 321, 602, 222, 603, 331, 230,
        332, 322, 401, 604, 501, 330, 402, 605, 400,
    ],
]


def backward_codes(here):
    routes = BACKWARD_ROUTES
    spots = {}
    for way in "xy":
        pairs = [(zp, k) for zp in range(ZN) for k in range(3) if routes[here][zp][k] == way]
        spots.update({pair: n for n, pair in enumerate(pairs)})

    def octet(side, zp, k):
        dx, dy = side % 2, side // 2
        own = zp == here
        route = routes[here][zp][k]
        code = k + 4 * zp + 16 * side + 131072
        along = "u" if zp > here else "d"
        if side == 0:
            code += 64 + 128
            way = "f" if own else along
        elif side == 1:
            code += 128 * (route == "y")
            way = "x"
        elif side == 2:
            code += 64 * (route == "x")
            way = "y"
        else:
            way = along if route == "z" else route
        if side in (0, 3):
            for step, there, bit in ((1, here - 1, 256), (-1, here + 1, 512)):
                if 0 <= there < ZN and (zp - here) * step >= 0:
                    code += bit * (side == 0 or routes[there][zp][k] == "z")
        return code + 1024 * "xyudf".index(way) + 8192 * spots.get((zp, k), 0)

    parts, first = [[]], 0
    for item in BACKWARD_PLANS[here]:
        if item >= 1000:
            parts.append([])
            continue
        kind, zp, k = item // 100, item // 10 % 10, item % 10
        if kind == 0:
            parts[-1].append(k + 4 * zp + 64 * (first >= 2) + 8192 * (first % 2))
            first += 1
        elif kind == 1:
            parts[-1].append(octet(3, zp, k))
        elif kind == 2:
            parts[-1] += [octet(2, zp, k), octet(1, zp, k)]
        elif kind == 3:
            parts[-1].append(octet(0, zp, k))
        elif kind == 4:
            parts[-1].append(131072 * 2 + k)
        elif kind == 5:
            parts[-1].append(131072 * (3 + k))
        else:
            parts[-1].append(131072 * (5 + k))
    return parts


def backward_kernel(
    wm, l3_in, d2_in, acc_in, gp_in, xh_in, rs_in, p3_in, q3_in, res, vsum_in, vec,
    tiles, grp, vout, res_back, din_back,
    l3, r3, acc, gp, xh, rs, p3, q3, da3, din, wb, vsum,
    land_c, land_x, land_y, land_z, ring, vland, total,
    r_in, r_wb, r_c, r_x, r_y, r_z, r_e, r_v, s_ring, s_x, s_y, s_up, s_down, s_e, s_e2, s_v,
    s_res, r_res, l_res, s_din, r_din, l_din,
):
    p = Place()
    z, c, fs = p.z, p.c, p.fs
    p.greet()
    weights = [8, 9, 10, 11, 4, 5, 6, 7, 3, 0, 1, 2]
    slots = wb.shape[0]

    def bring(n):
        if n < len(weights):
            pltpu.make_async_copy(
                wm.at[pl.ds(8 * weights[n], 8)], wb.at[n % slots], r_wb.at[n % slots]
            ).start()

    later = pl.ds(24, 32)
    pairs = [(d2_in, r3.at[8]), (l3_in.at[later], l3.at[later])]
    pairs += [(gp_in.at[t], gp.at[t]) for t in range(4)]
    pairs += [(acc_in, acc), (xh_in, xh), (rs_in, rs), (p3_in, p3), (q3_in, q3)]
    early = pl.ds(0, 24)
    pairs += [(l3_in.at[early], l3.at[early])]
    takes = [pltpu.make_async_copy(src, dst, r_in.at[n]) for n, (src, dst) in enumerate(pairs)]
    for n, copy in enumerate(takes):
        copy.start()
        if 2 <= n < 2 + slots:
            bring(n - 2)
    vsum[...] = vsum_in[...]
    p.greeted()

    def wrows(n, rows):
        at = slice(rows.start // TB, rows.stop // TB)
        return wb[weights.index(n) % slots, at].reshape(CHUNK, D)

    f = Layer(
        vec=vec, l3=l3, r3=r3, vsum=vsum, q3=q3, p3=p3, da3=da3, xh=xh, rs=rs, acc=acc, gp=gp,
        din=din, wrows=wrows,
    )

    def part(o):
        return t_mul(l3[left_block(o)], r3[right_block(o)])

    def add(land, sem, n):
        wait_for(land.at[n], sem.at[n])
        total[...] += land[n].astype(f32)

    def to_partner(zp, k, slot, again):
        def body(j, _):
            yy, xx = j % 2, j // 2
            o = ((zp * 2 + yy) * 4 + xx * 2 + (1 - c)) * 3 + k
            n = slot * 4 + j
            value = part(o).astype(bf)
            pl.when(again == 1)(lambda: wait_for(ring.at[0], s_ring.at[n]))
            ring[n] = value
            q = ((jnp.where(yy == p.y, 0, 2) + jnp.where(xx == p.x, 0, 1)) * ZN + zp) * 3 + k
            remote(ring.at[n], land_c.at[q], s_ring.at[n], r_c.at[q], p.to_core).start()
            return 0

        lax.fori_loop(0, 4, body, 0)

    def octet_step(code, zp, k):
        side = code // 16 % 4
        dx, dy = side % 2, side // 2
        corner = side // 3
        q = (side * ZN + zp) * 3 + k
        yy = p.y + dy * (1 - 2 * p.y)
        xx = p.x + dx * (1 - 2 * p.x)
        o = ((zp * 2 + yy) * 4 + xx * 2 + c) * 3 + k
        wait_for(land_c.at[q], r_c.at[q])
        total[...] = part(o) + land_c[q].astype(f32)
        spot = 12 + code // 8192 % 16
        flat = zp * 3 + k
        column = jnp.where(side == 0, flat, spot)
        n = corner * 12 + flat
        mine = 24 + corner * 3 + k
        above = jnp.where(zp == z, mine, n)
        below_to = jnp.where(zp == z - 1, mine, n)
        pl.when(code // 64 % 2 == 1)(functools.partial(add, land_x, r_x, column))
        pl.when(code // 128 % 2 == 1)(functools.partial(add, land_y, r_y, column))
        pl.when(code // 256 % 2 == 1)(functools.partial(add, land_z, r_z, n))
        pl.when(code // 512 % 2 == 1)(functools.partial(add, land_z, r_z, above))
        way = code // 1024 % 8
        t = jnp.where(side == 3, spot, flat)

        @pl.when(way < 4)
        def _():
            land_c[q] = total[...].astype(bf)
            src = land_c.at[q]
            pl.when(way == 0)(lambda: remote(src, land_x.at[t], s_x, r_x.at[t], p.to_x).start())
            pl.when(way == 1)(lambda: remote(src, land_y.at[t], s_y, r_y.at[t], p.to_y).start())
            pl.when(way == 2)(lambda: remote(src, land_z.at[n], s_up, r_z.at[n], p.to_up).start())
            pl.when(way == 3)(
                lambda: remote(
                    src, land_z.at[below_to], s_down, r_z.at[below_to], p.to_down
                ).start()
            )

        @pl.when(way == 4)
        def _():
            for j in range(8):
                piece = total[:, j * TB : (j + 1) * TB]
                tiles[8 * k + j] = piece
                grp[fs * 24 + 8 * k + j] = piece.astype(bf)
            mine = grp.at[pl.ds(fs * 24 + 8 * k, 8)]
            remote(mine, mine, s_e, r_e.at[fs * 3 + k], p.to_x).start()
            remote(mine, mine, s_e2, r_e.at[fs * 3 + k], p.to_core).start()

    def hand_on(k):
        fx = (fs + 2) % 4
        block = grp.at[pl.ds(fx * 24 + 8 * k, 8)]
        wait_for(block, r_e.at[fx * 3 + k])
        remote(block, block, s_e2, r_e.at[fx * 3 + k], p.to_core).start()

    def vec_step(n):
        if n == 0:
            sums = vsum[...].sum(axis=1)
            for j in range(8):
                vout[pl.ds(12 * j, 12)] = sums[:, j * TB : (j + 1) * TB]
        else:
            wait_for(vland.at[n - 1], r_v.at[n - 1])
            vout[...] = vout[...] + vland[n - 1]
        if n < 5:
            vland[5 + n] = vout[...]
            remote(vland.at[5 + n], vland.at[n], s_v.at[n], r_v.at[n], p.doubling[n]).start()

    def run_codes(lists):
        longest = max(len(codes) for codes in lists)
        if longest == 0:
            return

        def of_plane(values):
            got = values[0]
            for here in range(1, ZN):
                if values[here] != values[0]:
                    got = jnp.where(z == here, values[here], got)
            return got

        count = of_plane([len(codes) for codes in lists])
        table = [of_plane([codes[i] if i < len(codes) else 0 for codes in lists]) for i in range(longest)]

        def body(i, _):
            code = table[0]
            for j in range(1, longest):
                code = jnp.where(i == j, table[j], code)
            kind = code // 131072
            zp, k = code // 4 % 4, code % 4
            pl.when(kind == 0)(lambda: to_partner(zp, k, code // 8192 % 16, code // 64 % 2))
            pl.when(kind == 1)(lambda: octet_step(code, zp, k))
            pl.when(kind == 2)(lambda: hand_on(k))
            pl.when(kind == 3)(lambda: start_deal(p, res, res_back, s_res, r_res, l_res))
            pl.when(kind == 4)(lambda: start_deal(p, din, din_back, s_din, r_din, l_din))
            for n in range(6):
                pl.when(kind == 5 + n)(functools.partial(vec_step, n))
            return 0

        lax.fori_loop(0, count, body, 0)

    used = [0]

    def square(step):
        n = used[0]
        used[0] += 1
        wait_for(wb.at[n % slots], r_wb.at[n % slots])
        step()
        bring(n + slots)

    def compute(name):
        t = int(name[-1]) if name[-1].isdigit() else 0
        if name[:2] == "DB":
            takes[2 + t].wait()
            square(lambda: f.down_back(t))
            if t == 3:
                takes[11].wait()
        elif name[:2] == "UB":
            if t == 0:
                takes[6].wait()
            square(lambda: f.up_back(t))
        elif name == "N1B":
            takes[7].wait()
            takes[8].wait()
            f.norm_one_back()
        elif name == "OB":
            square(f.out_back)
        elif name == "ATB":
            takes[9].wait()
            takes[10].wait()
            f.attend_back()
        else:
            square(lambda: f.project_back(t))

    takes[0].wait()
    takes[1].wait()
    parts = [backward_codes(here) for here in range(ZN)]
    for n in range(len(BACKWARD_STEPS) + 1):
        run_codes([codes[n] for codes in parts])
        if n < len(BACKWARD_STEPS):
            compute(BACKWARD_STEPS[n])

    end_deal(p, res, res_back, s_res, r_res, l_res)
    end_deal(p, din, din_back, s_din, r_din, l_din)
    for g in (p.x * 2 + 1 - c, (1 - p.x) * 2 + 1 - c):
        for k in range(3):
            wait_for(grp.at[pl.ds(g * 24 + 8 * k, 8)], r_e.at[g * 3 + k])

    for n in range(RING):
        wait_for(ring.at[0], s_ring.at[n])
    for n in range(5):
        wait_for(vland.at[5 + n], s_v.at[n])

    wait_for(grp.at[pl.ds(0, 24)], s_e)
    wait_for(grp.at[pl.ds(0, 48)], s_e2)

    def drain(here):
        ways = [code // 1024 % 8 for codes in parts[here] for code in codes if code // 131072 == 1]
        for way, sem in enumerate((s_x, s_y, s_up, s_down)):
            if ways.count(way):
                wait_for(land_c.at[pl.ds(0, ways.count(way))], sem)

    for here in range(ZN):
        pl.when(z == here)(functools.partial(drain, here))


def backward(wm, l3, d2, acc, gp, xh, rs, p3, q3, res, vsum, vec):
    dma = pltpu.SemaphoreType.DMA
    rows = d2.shape[0]
    vmem = pl.BlockSpec(memory_space=pltpu.VMEM)
    far = pl.BlockSpec(memory_space=pl.ANY)
    out = jax.ShapeDtypeStruct
    return pl.pallas_call(
        backward_kernel,
        out_shape=(
            out((24, TB, TB), f32),
            out((96, TB, TB), bf),
            out((96, TB), f32),
            out(res.shape, bf),
            out(res.shape, bf),
        ),
        in_specs=[far] * 10 + [vmem] * 2,
        out_specs=(vmem,) * 3 + (far,) * 2,
        scratch_shapes=[
            pltpu.VMEM(l3.shape, bf), pltpu.VMEM((9, rows, D), bf), pltpu.VMEM(acc.shape, f32),
            pltpu.VMEM(gp.shape, f32), pltpu.VMEM(xh.shape, f32), pltpu.VMEM(rs.shape, f32),
            pltpu.VMEM(p3.shape, f32), pltpu.VMEM(q3.shape, bf), pltpu.VMEM((8, rows, TB), bf),
            pltpu.VMEM(res.shape, bf), pltpu.VMEM((2, 8, TB, D), bf), pltpu.VMEM((12, 8, D), f32),
            pltpu.VMEM((48, TB, D), bf), pltpu.VMEM((SPOTS, TB, D), bf),
            pltpu.VMEM((SPOTS, TB, D), bf), pltpu.VMEM((30, TB, D), bf), pltpu.VMEM((RING, TB, D), bf),
            pltpu.VMEM((10, 96, TB), f32), pltpu.VMEM((TB, D), f32),
            dma((12,)), dma((2,)), dma((48,)), dma((SPOTS,)), dma((SPOTS,)), dma((30,)), dma((12,)), dma((5,)),
            dma((RING,)), dma, dma, dma, dma, dma, dma, dma((5,)),
            dma, dma((2 * ZN,)), dma, dma, dma((2 * ZN,)), dma,
        ],
        compiler_params=pltpu.CompilerParams(
            collective_id=1, has_side_effects=True, vmem_limit_bytes=62 * 2**20
        ),
        name="backward",
    )(wm, l3, d2, acc, gp, xh, rs, p3, q3, res, vsum, vec)


GROUP = 8


def halves(a):
    high = a.astype(bf)
    return high, (a - high.astype(f32)).astype(bf)


def wide(b):
    return jnp.concatenate(
        [jnp.concatenate(b, 1), jnp.concatenate([b[0], jnp.zeros_like(b[0])], 1)], 0
    )


def fine(a, b_wide):
    out = mul(jnp.concatenate(a, 1), b_wide)
    return out[:, :TB] + out[:, TB:]


def fine_t(a, b):
    wide_t = jnp.concatenate(
        [jnp.concatenate([b[0], b[0]], 1), jnp.concatenate([b[1], jnp.zeros_like(b[1])], 1)], 0
    )
    out = mul_t(jnp.concatenate(a, 1), wide_t)
    return out[:, :TB] + out[:, TB:]


def moments(first, second, grad):
    first = BETA_ONE * first + (1.0 - BETA_ONE) * grad
    second = BETA_TWO * second + (1.0 - BETA_TWO) * grad * grad
    hat = (first * (1.0 / (1.0 - BETA_ONE**STEP))) / (
        jnp.sqrt(second * (1.0 / (1.0 - BETA_TWO**STEP))) + ADAM_EPS
    )
    return first, second, hat


def adam_kernel(owners, deal, *refs):
    masters = refs[:GROUP]
    (
        grads, left, right, first, second, vec, vec_first, vec_second, vec_total,
        tiles, res_back, din_back,
        new_first, new_second, new_tiles, new_low, vec_grad, vec_first_new, vec_second_new, new_vec,
        tile_grads, out_tokens, in_grad,
    ) = refs[GROUP:]
    step = pl.program_id(0)
    dp, fs = lax.axis_index("dp"), lax.axis_index("fsdp")
    seqs = res_back.shape[1]

    @pl.when(step == 0)
    def _():
        for b in range(res_back.shape[0]):
            for j in range(seqs):
                to = deal[b, j * 4 + fs] - fs * seqs
                out_tokens[b, to] = res_back[b, j]
                in_grad[b, to] = din_back[b, j]
        for i in range(3):
            m = (dp * 4 + fs) * 3 + i
            vec_grad[i : i + 1] = vec_total[pl.ds((m % 8) * 12 + m // 8, 1)]
        a, b, hat = moments(vec_first[...], vec_second[...], vec_grad[...])
        vec_first_new[...] = a
        vec_second_new[...] = b
        new_vec[...] = vec[...] - VEC_RATE * hat

    tile_grads[...] = tiles[...]
    span = range(GROUP)
    owner = [owners[step * GROUP + g] for g in span]
    ls = [halves(left[g]) for g in span]
    rs = [halves(right[g]) for g in span]
    grad = [grads[owner[g] - dp * 96] for g in span]
    inner = [t_mul(jnp.concatenate(ls[g], 0), jnp.concatenate([grad[g]] * 2, 0)) for g in span]
    rwide = [wide(rs[g]) for g in span]
    rotated = [fine(halves(inner[g]), rwide[g]) for g in span]
    hats = []
    for g in span:
        first_now, second_now, hat = moments(first[g], second[g], rotated[g])
        new_first[g] = first_now
        new_second[g] = second_now
        hats.append(hat)
    outer = [fine(ls[g], wide(halves(hats[g]))) for g in span]
    update = [fine_t(halves(outer[g]), rs[g]) for g in span]
    for g in span:
        master = masters[g][0].astype(f32)
        fresh = master - tile_rate(owner[g]) * (update[g] + DECAY * master)
        new_tiles[g] = fresh
        new_low[g] = fresh.astype(bf)


def adam(owners, deal, wm, grads, left, right, first, second, vec, vec_first, vec_second,
         vec_total, tiles, res_back, din_back):
    count = left.shape[0]
    out = jax.ShapeDtypeStruct

    def master_at(g, i, owners, *_):
        o = owners[i * GROUP + g]
        return octet_place(o // 8), 0, o % 8

    one = [pl.BlockSpec((1, TB, TB), functools.partial(master_at, g)) for g in range(GROUP)]
    stack = pl.BlockSpec((GROUP, TB, TB), lambda i, *_: (i, 0, 0))
    whole = pl.BlockSpec(grads.shape, lambda i, *_: (0, 0, 0))
    dealt = pl.BlockSpec(res_back.shape, lambda i, *_: (0, 0, 0, 0))

    def small(a):
        return pl.BlockSpec(a.shape, lambda i, *_: (0, 0))

    return pl.pallas_call(
        adam_kernel,
        out_shape=(out(left.shape, f32),) * 3
        + (out(left.shape, bf),)
        + (out(vec.shape, f32),) * 4
        + (out(tiles.shape, f32), out(res_back.shape, bf), out(din_back.shape, bf)),
        grid_spec=pltpu.PrefetchScalarGridSpec(
            num_scalar_prefetch=2,
            grid=(count // GROUP,),
            in_specs=one + [whole] + [stack] * 4 + [small(vec)] * 3 + [small(vec_total), stack, dealt, dealt],
            out_specs=[stack] * 4 + [small(vec)] * 4 + [stack, dealt, dealt],
        ),
        compiler_params=pltpu.CompilerParams(vmem_limit_bytes=60 * 2**20),
        name="adam",
    )(
        owners, deal, *([wm] * GROUP), grads, left, right, first, second,
        vec, vec_first, vec_second, vec_total, tiles, res_back, din_back,
    )


def per_device(
    tokens,
    cotangent,
    lengths,
    deal,
    weights,
    vectors,
    owners,
    left_basis,
    right_basis,
    first_moment,
    second_moment,
    vec_first,
    vec_second,
):
    rows = tokens.shape[0] * tokens.shape[2] * lax.axis_size("dp")
    vec_rows = vectors.reshape(3, TB)
    wm, l3, d2, acc, gp, xh, rs, p3, q3, res, vsum, vecs = forward(
        lengths, deal, weights, vec_rows, tokens, cotangent.reshape(rows, D)
    )
    tiles, group_grads, vec_total, res_back, din_back = backward(
        wm, l3, d2, acc, gp, xh, rs, p3, q3, res, vsum, vecs
    )
    (
        new_first, new_second, new_tiles, new_low, vec_grads, vec_first_new, vec_second_new,
        new_vectors, tile_grads, out_tokens, in_grad,
    ) = adam(
        owners, deal, wm, group_grads, left_basis, right_basis, first_moment, second_moment,
        vec_rows, vec_first.reshape(3, TB), vec_second.reshape(3, TB), vec_total, tiles,
        res_back, din_back,
    )
    return (
        out_tokens,
        in_grad,
        tile_grads,
        vec_grads.reshape(-1),
        new_first,
        new_second,
        new_tiles,
        new_low,
        vec_first_new.reshape(-1),
        vec_second_new.reshape(-1),
        new_vectors.reshape(-1),
    )


def solution(mesh):
    body = per_device if (mesh.shape["dp"], mesh.shape["fsdp"]) == (2 * ZN, 4) else per_device_any
    placed = (
        P(None, "fsdp", "dp", None),
        P(None, ("dp", "fsdp"), None, None),
        P(),
        P(),
        P(("dp", "fsdp"), None, None),
        P(("dp", "fsdp")),
        P(("dp", "fsdp")),
        P(("dp", "fsdp"), None, None),
        P(("dp", "fsdp"), None, None),
        P(("dp", "fsdp"), None, None),
        P(("dp", "fsdp"), None, None),
        P(("dp", "fsdp")),
        P(("dp", "fsdp")),
    )
    return jax.shard_map(
        body,
        mesh=mesh,
        in_specs=placed,
        out_specs=(
            P(None, "fsdp", "dp", None),
            P(None, "fsdp", "dp", None),
            P(("dp", "fsdp"), None, None),
            P(("dp", "fsdp")),
            P(("dp", "fsdp"), None, None),
            P(("dp", "fsdp"), None, None),
            P(("dp", "fsdp"), None, None),
            P(("dp", "fsdp"), None, None),
            P(("dp", "fsdp")),
            P(("dp", "fsdp")),
            P(("dp", "fsdp")),
        ),
        check_vma=False,
    )
```
